32 devices in a mesh: gx: 4 (over x, core), gy: 8 (over z, y).
Axes of the slice: x: 2, y: 2, z: 4, core: 2. Of those that a mesh axis runs over, the one named last changes fastest.
Arguments:
- flat_master: float32 [13326112], P(('gx', 'gy'))
- flat_first: float32 [13326112], P(('gx', 'gy'))
- flat_second: float32 [13326112], P(('gx', 'gy'))
- table: float32 [49408, 512], P('gy'), may hold values from -6 to 6
- table_first: float32 [49408, 512], P('gy')
- table_second: float32 [49408, 512], P('gy')
- pixels: bfloat16 [256, 49, 3072], P(('gx', 'gy')), may hold values from -6 to 6
- token_ids: int32 [256, 77], P(('gx', 'gy')), may hold values from 0 to 49407
- end_pos: int32 [256], P(('gx', 'gy')), may hold values from 19 to 76
- pair_counts: int32 [4, 8], replicated, may hold values from 1 to 8, as said below
- groups: int32 [256], replicated, may hold values from 0 to 169, as said below
- cached_image: bfloat16 [256, 512], P(('gx', 'gy')), may hold values from -0.625 to 0.625
- cached_text: bfloat16 [256, 512], P(('gx', 'gy')), may hold values from -0.625 to 0.625
Outputs:
- master_out: float32 [13326112], P(('gx', 'gy'))
- first_out: float32 [13326112], P(('gx', 'gy'))
- second_out: float32 [13326112], P(('gx', 'gy'))
- table_out: float32 [49408, 512], P('gy')
- table_first_out: float32 [49408, 512], P('gy')
- table_second_out: float32 [49408, 512], P('gy')
- loss_sum: float32 [], replicated
- positives: float32 [], replicated
- grad_norm: float32 [], replicated
The draws below stay inside these ranges and needn't reach their ends.
Inputs may be any that keep to these rules, and one draw needn't show every extreme that they name: `pair_counts`: each device's valid pairs fill its first slots; the last device is full. `groups`: pairs with equal ids are duplicates of one another. `end_pos`: tokens after a text's end token are padding.
All inputs are finite; a program needn't handle non-finite values.
Results may differ from the reference program's by a relative error of at most 0.0024.
The reference program's roundings to bfloat16 on the way count: a program that leaves them out, or rounds other values in their place, can miss the bound.
Values may be sent and summed in bfloat16 or wider, within the bound.
A program may use at most 384 MiB of HBM per device.

```python
import math
import jax
import jax.numpy as jnp
import numpy as np
from jax import lax

D_IMG = 768
IMG_HEADS = 12
IMG_MLP = 3072
PATCH_DIM = 3072
PATCHES = 49
D_TXT = 512
TXT_HEADS = 8
TXT_MLP = 2048
VOCAB = 49408
CTX = 77
EMBED = 512
PAIRS_DEV = 8
STEP = 10
IMG_TOK = 50
PAIRS = 256
CACHE = 256
N_PARAM = 13326081
FLAT = 13326112
N_GX = 4
N_GY = 8


clip_limit = 0.1


def segment_list_drawn():
    return [('patch_embed', PATCH_DIM, D_IMG), ('image_attn', D_IMG, 4 * D_IMG), ('image_up', D_IMG, IMG_MLP), ('image_down', IMG_MLP, D_IMG), ('image_proj', D_IMG, EMBED), ('text_attn', D_TXT, 4 * D_TXT), ('text_up', D_TXT, TXT_MLP), ('text_down', TXT_MLP, D_TXT), ('text_proj', D_TXT, EMBED), ('image_vec', IMG_TOK + 9, D_IMG), ('text_vec', CTX + 6, D_TXT), ('temper', 1, 1)]


def master_tables():
    bases = []
    spreads = []
    for seg_name, seg_rows, seg_cols in segment_list_drawn():
        if seg_name in ('image_attn', 'text_attn'):
            pattern = jnp.concatenate([jnp.full((3 * seg_rows,), seg_rows ** (-0.5), jnp.float32), jnp.full((seg_rows,), 4.0 * seg_rows ** (-0.5), jnp.float32)])
            bases.append(jnp.zeros((seg_rows * seg_cols,), jnp.float32))
            spreads.append(jnp.tile(pattern, seg_rows))
        elif seg_name == 'image_vec':
            row_base = [0.0] + [0.0] * IMG_TOK + [1.0, 0.0] * 4
            row_spread = [1.0] + [0.5] * IMG_TOK + [0.3, 0.3] * 4
            bases.append(jnp.repeat(jnp.array(row_base, jnp.float32), seg_cols))
            spreads.append(jnp.repeat(jnp.array(row_spread, jnp.float32), seg_cols))
        elif seg_name == 'text_vec':
            row_base = [0.0] * CTX + [1.0, 0.0] * 3
            row_spread = [0.5] * CTX + [0.3, 0.3] * 3
            bases.append(jnp.repeat(jnp.array(row_base, jnp.float32), seg_cols))
            spreads.append(jnp.repeat(jnp.array(row_spread, jnp.float32), seg_cols))
        elif seg_name == 'temper':
            bases.append(jnp.full((1,), 3.9, jnp.float32))
            spreads.append(jnp.full((1,), 0.12, jnp.float32))
        else:
            bases.append(jnp.zeros((seg_rows * seg_cols,), jnp.float32))
            spreads.append(jnp.full((seg_rows * seg_cols,), seg_rows ** (-0.5), jnp.float32))
    bases.append(jnp.zeros((FLAT - N_PARAM,), jnp.float32))
    spreads.append(jnp.zeros((FLAT - N_PARAM,), jnp.float32))
    return (jnp.concatenate(bases), jnp.concatenate(spreads))


def moment_scale():
    parts = []
    for seg_name, seg_rows, seg_cols in segment_list_drawn():
        if seg_name == 'temper':
            multiple = 20.0
        elif seg_name in ('image_vec', 'text_vec'):
            multiple = 4.0
        else:
            multiple = 1.0
        parts.append(jnp.full((seg_rows * seg_cols,), multiple, jnp.float32))
    parts.append(jnp.ones((FLAT - N_PARAM,), jnp.float32))
    grad_size = clip_limit * (N_PARAM + VOCAB * D_TXT) ** (-0.5)
    return jnp.concatenate(parts) * grad_size


def draw_flat_master(key, part):
    key = jax.random.fold_in(key, 1)
    bases, spreads = master_tables()
    noise_vals = jax.random.truncated_normal(key, -2.5, 2.5, (FLAT,), jnp.float32)
    return bases + spreads * noise_vals


def draw_flat_first(key, part):
    key = jax.random.fold_in(key, 2)
    noise_vals = jax.random.truncated_normal(key, -2.5, 2.5, (FLAT,), jnp.float32)
    return 0.1 / 0.9 * moment_scale() * noise_vals


def draw_flat_second(key, part):
    key = jax.random.fold_in(key, 3)
    key_one, key_two = jax.random.split(key)
    sizes_sq = moment_scale() ** 2
    first_factor = jax.random.uniform(key_one, (FLAT,), jnp.float32, 1.0, 4.0)
    second_factor = jax.random.uniform(key_two, (FLAT,), jnp.float32, 0.5, 2.0)
    return 0.001 / 0.999 * sizes_sq * first_factor * second_factor


def draw_table_first(key, part):
    key = jax.random.fold_in(key, 4)
    grad_size = 0.3 * clip_limit * (N_PARAM + VOCAB * D_TXT) ** (-0.5)
    noise_vals = jax.random.truncated_normal(key, -2.5, 2.5, (VOCAB, D_TXT), jnp.float32)
    return 0.1 / 0.9 * grad_size * noise_vals


def draw_table_second(key, part):
    key = jax.random.fold_in(key, 5)
    key_one, key_two = jax.random.split(key)
    grad_size = 0.3 * clip_limit * (N_PARAM + VOCAB * D_TXT) ** (-0.5)
    first_factor = jax.random.uniform(key_one, (VOCAB, D_TXT), jnp.float32, 1.0, 4.0)
    second_factor = jax.random.uniform(key_two, (VOCAB, D_TXT), jnp.float32, 0.5, 2.0)
    return 0.001 / 0.999 * grad_size * grad_size * first_factor * second_factor


def draw_pair_counts(key, part):
    key = jax.random.fold_in(key, 7)
    row_index = jnp.arange(N_GX)[:, None]
    col_index = jnp.arange(N_GY)[None, :]
    span_x = max(N_GX - 1, 1)
    span_y = max(N_GY - 1, 1)
    numerator = PAIRS_DEV * (span_x * span_y + row_index * span_y + col_index * span_x)
    denominator = 3 * span_x * span_y
    base_count = (numerator + denominator - 1) // denominator
    jitter = jax.random.randint(key, (N_GX, N_GY), 0, 2)
    last_one = (row_index == N_GX - 1) & (col_index == N_GY - 1)
    return jnp.where(last_one, PAIRS_DEV, jnp.clip(base_count - jitter, 1, PAIRS_DEV)).astype(jnp.int32)


def draw_groups(key, part):
    key = jax.random.fold_in(key, 11)
    key_one, key_two, key_three = jax.random.split(key, 3)
    top_group = max(PAIRS * 2 // 3, 1)
    picked = jax.random.randint(key_one, (PAIRS,), 0, top_group)
    half = PAIRS // 2
    low_slot = jax.random.randint(key_two, (), 0, max(half, 1))
    high_slot = jax.random.randint(key_three, (), half, PAIRS)
    slots = jnp.arange(PAIRS)
    picked = jnp.where(slots == low_slot, 0, picked)
    picked = jnp.where(slots == high_slot, top_group - 1, picked)
    return picked.astype(jnp.int32)


def set_ends(values, rng, smallest, top_value):
    spot = [jax.random.randint(jax.random.fold_in(rng, axis), (), 0, length) for axis, length in enumerate(values.shape)]
    longest = values.shape.index(max(values.shape))
    next_to = spot[:longest] + [(spot[longest] + 1) % values.shape[longest]] + spot[longest + 1:]
    return values.at[tuple(spot)].set(smallest).at[tuple(next_to)].set(top_value)


def level_of(stream_key, shape, cuts, smallest, top_value):
    def one(dim, blocks):
        draws = jax.random.uniform(jax.random.fold_in(jax.random.fold_in(stream_key, 6), dim), (blocks,), jnp.float32, smallest / len(cuts), top_value / len(cuts))
        return jnp.repeat(jnp.exp(draws), shape[dim] // blocks).reshape((-1,) + (1,) * (len(shape) - dim - 1))

    level = one(*cuts[0])
    for cut in cuts[1:]:
        level = level * one(*cut)
    return level


def rank_bounds(number_of, slope):
    loads = [(1 << 20) // math.isqrt(rank ** slope) + 1 for rank in range(1, number_of + 1)]
    scale = 1 + sum(loads) // (1 << 30)
    return np.cumsum(np.array([max(1, weight // scale) for weight in loads]))


def skewed_ids(rng, shape, count, lean):
    table = rank_bounds(count, lean)
    pick = jax.random.randint(jax.random.fold_in(rng, 1), shape, 0, int(table[count - 1]))
    standing = jnp.searchsorted(jnp.asarray(table, jnp.int32), pick, side="right")
    return jax.random.permutation(jax.random.fold_in(rng, 2), count)[standing].astype(jnp.int32)


def centred(key, extent, width, limit, cuts=(), held_as=jnp.bfloat16):
    gain = level_of(key, extent, cuts, -0.22, 0.18) if cuts else 1.0
    drawn = jax.random.normal(key, extent, jnp.float32) * width * gain
    return jnp.minimum(jnp.maximum(drawn, -limit), limit).astype(held_as)


def setup_inputs(seed: int = 0) -> dict:
    arg_keys = jax.random.split(jax.random.key(seed), 14)
    flat_master = draw_flat_master(jax.random.fold_in(arg_keys[13], 71), 0)
    flat_first = draw_flat_first(jax.random.fold_in(arg_keys[13], 71), 0)
    flat_second = draw_flat_second(jax.random.fold_in(arg_keys[13], 71), 0)
    table = centred(arg_keys[3], (VOCAB, D_TXT), 1.0, 6.0, ((0, 8),), jnp.float32)
    table_first = draw_table_first(jax.random.fold_in(arg_keys[13], 71), 0)
    table_second = draw_table_second(jax.random.fold_in(arg_keys[13], 71), 0)
    pixels = centred(arg_keys[6], (PAIRS, PATCHES, PATCH_DIM), 1.0, 6.0, ((0, 32),))
    token_ids = set_ends(skewed_ids(arg_keys[7], (PAIRS, CTX), VOCAB, 2), jax.random.fold_in(arg_keys[7], 3), 0, VOCAB - 1).astype(jnp.int32)
    end_pos = set_ends(jax.random.randint(arg_keys[8], (PAIRS,), CTX // 4, CTX), jax.random.fold_in(arg_keys[8], 1), CTX // 4, CTX - 1).astype(jnp.int32)
    pair_counts = draw_pair_counts(jax.random.fold_in(arg_keys[13], 71), 0)
    groups = draw_groups(jax.random.fold_in(arg_keys[13], 71), 0)
    cached_image = centred(arg_keys[11], (CACHE, EMBED), (EMBED ** -0.5), 0.625, ((0, 32),))
    cached_text = centred(arg_keys[12], (CACHE, EMBED), (EMBED ** -0.5), 0.625, ((0, 32),))
    return dict(flat_master=flat_master, flat_first=flat_first, flat_second=flat_second, table=table, table_first=table_first, table_second=table_second, pixels=pixels, token_ids=token_ids, end_pos=end_pos, pair_counts=pair_counts, groups=groups, cached_image=cached_image, cached_text=cached_text)


clip_limit = 0.1
beta_one = 0.9
beta_two = 0.999
adam_eps = 1e-08
decay_rate = 0.1
rate_matrix = 0.01
rate_vector = 0.2
rate_table = 0.2
norm_eps = 1e-05
highest = lax.Precision.HIGHEST

@jax.custom_vjp
def low(v):
    return lax.optimization_barrier(v.astype(jnp.bfloat16)).astype(jnp.float32)

@jax.custom_vjp
def low_back(v):
    return v

def low_keep(v):
    return (low(v), None)

def low_pass(kept, grad):
    return (grad,)

def back_keep(v):
    return (v, None)

def back_low(kept, grad):
    return (low(grad),)
low.defvjp(low_keep, low_pass)
low_back.defvjp(back_keep, back_low)

def segment_list():
    return [('patch_embed', PATCH_DIM, D_IMG), ('image_attn', D_IMG, 4 * D_IMG), ('image_up', D_IMG, IMG_MLP), ('image_down', IMG_MLP, D_IMG), ('image_proj', D_IMG, EMBED), ('text_attn', D_TXT, 4 * D_TXT), ('text_up', D_TXT, TXT_MLP), ('text_down', TXT_MLP, D_TXT), ('text_proj', D_TXT, EMBED), ('image_vec', IMG_TOK + 9, D_IMG), ('text_vec', CTX + 6, D_TXT), ('temper', 1, 1)]

def unpack(flat_vals):
    pieces = {}
    offset = 0
    for seg_name, seg_rows, seg_cols in segment_list():
        pieces[seg_name] = flat_vals[offset:offset + seg_rows * seg_cols].reshape(seg_rows, seg_cols)
        offset = offset + seg_rows * seg_cols
    return pieces

def matrix_end():
    return sum((seg_rows * seg_cols for seg_name, seg_rows, seg_cols in segment_list()[:9]))

def product_hi(left_side, right_side):
    return jnp.matmul(left_side, right_side, precision=highest)

def layer_norm(values, gain_vec, shift_vec):
    center = values - lax.optimization_barrier(jnp.mean(values, -1, keepdims=True))
    spread = lax.optimization_barrier(jnp.mean(center * center, -1, keepdims=True))
    return center * lax.rsqrt(spread + norm_eps) * gain_vec + shift_vec

def quick_gelu(values):
    return values * jax.nn.sigmoid(1.702 * values)

def unit_rows(values):
    return values * lax.rsqrt(lax.optimization_barrier(jnp.sum(values * values, -1, keepdims=True)) + 1e-06)

def block_forward(hidden, attn_w, up_w, down_w, gain_rows, head_count, causal):
    seq_count, length, model_width = hidden.shape
    head_dim = model_width // head_count
    normed = low(layer_norm(hidden, gain_rows[0], gain_rows[1]))
    triple = low(low_back(product_hi(normed, attn_w[:, :3 * model_width])))
    query_part = triple[..., :model_width].reshape(seq_count, length, head_count, head_dim)
    key_part = triple[..., model_width:2 * model_width].reshape(seq_count, length, head_count, head_dim)
    value_part = triple[..., 2 * model_width:].reshape(seq_count, length, head_count, head_dim)
    scores = low_back(jnp.einsum('slhd,smhd->shlm', query_part, key_part, precision=highest) * head_dim ** (-0.5))
    if causal:
        allowed = jnp.arange(length)[:, None] >= jnp.arange(length)[None, :]
        scores = jnp.where(allowed, scores, -1e+30)
    attn_probs = low(jax.nn.softmax(scores, axis=-1))
    attended = low(low_back(jnp.einsum('shlm,smhd->slhd', attn_probs, value_part, precision=highest)))
    attended = attended.reshape(seq_count, length, model_width)
    middle = hidden + low_back(product_hi(attended, attn_w[:, 3 * model_width:]))
    normed_two = low(layer_norm(middle, gain_rows[2], gain_rows[3]))
    upper = product_hi(normed_two, up_w)
    act_low = low(quick_gelu(low_back(upper)))
    return middle + low_back(product_hi(act_low, down_w))

def towers(pieces, pixel_vals, token_rows, end_pos):
    image_vec = pieces['image_vec']
    patch_out = low_back(product_hi(pixel_vals, pieces['patch_embed']))
    class_row = jnp.broadcast_to(image_vec[0], (pixel_vals.shape[0], 1, D_IMG))
    tokens = jnp.concatenate([class_row, patch_out], 1) + image_vec[1:IMG_TOK + 1]
    hidden = layer_norm(tokens, image_vec[IMG_TOK + 1], image_vec[IMG_TOK + 2])
    hidden = block_forward(hidden, pieces['image_attn'], pieces['image_up'], pieces['image_down'], image_vec[IMG_TOK + 3:IMG_TOK + 7], IMG_HEADS, False)
    head_in = low(layer_norm(hidden[:, 0], image_vec[IMG_TOK + 7], image_vec[IMG_TOK + 8]))
    image_emb = low(unit_rows(low_back(product_hi(head_in, pieces['image_proj']))))
    text_vec = pieces['text_vec']
    hidden = token_rows + text_vec[:CTX]
    hidden = block_forward(hidden, pieces['text_attn'], pieces['text_up'], pieces['text_down'], text_vec[CTX:CTX + 4], TXT_HEADS, True)
    final_rows = jnp.take_along_axis(hidden, end_pos[:, None, None], 1)[:, 0]
    head_in = low(layer_norm(final_rows, text_vec[CTX + 4], text_vec[CTX + 5]))
    text_emb = low(unit_rows(low_back(product_hi(head_in, pieces['text_proj']))))
    return (image_emb, text_emb)

def side_loss(row_embed, columns, column_ok, same_pad, logit_scale):
    logits = logit_scale * low_back(product_hi(row_embed, columns.T))
    masked = jnp.where(column_ok[None, :], logits, -1e+30)
    log_total = jax.scipy.special.logsumexp(masked, axis=1)
    return -jnp.sum(same_pad * (logits - log_total[:, None]))

def objective(flat_vals, table_vals, pixel_vals, token_ids, end_pos, valid_slot, groups, cached_image, cached_text):
    pieces = unpack(low(flat_vals))
    token_rows = low_back(jnp.take(low(table_vals), token_ids, axis=0))
    image_emb, text_emb = towers(pieces, pixel_vals, token_rows, end_pos)
    logit_scale = jnp.exp(pieces['temper'][0, 0])
    matches = ((groups[:, None] == groups[None, :]) & valid_slot[:, None] & valid_slot[None, :]).astype(jnp.float32)
    total_count = 2.0 * jnp.sum(matches)
    same_pad = jnp.concatenate([matches, jnp.zeros((PAIRS, CACHE), jnp.float32)], 1)
    column_ok = jnp.concatenate([valid_slot, jnp.ones((CACHE,), jnp.bool_)])
    loss_sum = side_loss(image_emb, jnp.concatenate([text_emb, cached_text]), column_ok, same_pad, logit_scale)
    loss_sum = loss_sum + side_loss(text_emb, jnp.concatenate([image_emb, cached_image]), column_ok, same_pad, logit_scale)
    return (loss_sum / total_count, (loss_sum, total_count))

def adam_step(weight, first, second, grad, rate, decay):
    first = beta_one * first + (1.0 - beta_one) * grad
    second = beta_two * second + (1.0 - beta_two) * grad * grad
    first_hat = first / (1.0 - beta_one ** STEP)
    second_hat = second / (1.0 - beta_two ** STEP)
    weight = weight - rate * (first_hat / (jnp.sqrt(second_hat) + adam_eps) + decay * weight)
    return (weight, first, second)

def reference(flat_master, flat_first, flat_second, table, table_first, table_second, pixels, token_ids, end_pos, pair_counts, groups, cached_image, cached_text):
    slot_ids = jnp.arange(PAIRS)
    valid_slot = slot_ids % PAIRS_DEV < jnp.repeat(pair_counts.reshape(-1), PAIRS_DEV)
    pixel_vals = pixels.astype(jnp.float32)
    cache_img = cached_image.astype(jnp.float32)
    cache_txt = cached_text.astype(jnp.float32)

    def wrapped(flat_vals, table_vals):
        return objective(flat_vals, table_vals, pixel_vals, token_ids, end_pos, valid_slot, groups, cache_img, cache_txt)
    mean_loss, pullback, aux_vals = jax.vjp(wrapped, flat_master, table, has_aux=True)
    loss_sum, total_count = aux_vals
    flat_grad, table_grad = pullback(jnp.ones_like(mean_loss))
    grad_norm = jnp.sqrt(jnp.sum(flat_grad * flat_grad) + jnp.sum(table_grad * table_grad))
    factor = jnp.minimum(1.0, clip_limit / (grad_norm + 1e-06))
    position = jnp.arange(flat_master.shape[0])
    is_matrix = position < matrix_end()
    rates = jnp.where(is_matrix, rate_matrix, rate_vector)
    decays = jnp.where(is_matrix, decay_rate, 0.0)
    master_out, first_out, second_out = adam_step(flat_master, flat_first, flat_second, flat_grad * factor, rates, decays)
    table_out, table_first_out, table_second_out = adam_step(table, table_first, table_second, table_grad * factor, rate_table, 0.0)
    return (master_out, first_out, second_out, table_out, table_first_out, table_second_out, loss_sum, total_count, grad_norm)
```

```python
import functools

import jax
import jax.numpy as jnp
from jax import lax
from jax.experimental import pallas as pl
from jax.experimental.pallas import tpu as pltpu
from jax.sharding import PartitionSpec as P

D_IMG = 768
IMG_HEADS = 12
IMG_MLP = 3072
PATCH_DIM = 3072
D_TXT = 512
TXT_HEADS = 8
TXT_MLP = 2048
CTX = 77
EMBED = 512
STEP = 10
IMG_TOK = 50


clip_limit = 0.1
beta_one = 0.9
beta_two = 0.999
adam_eps = 1e-08
decay_rate = 0.1
rate_matrix = 0.01
rate_vector = 0.2
rate_table = 0.2
norm_eps = 1e-05


def segment_list():
    return [
        ("patch_embed", PATCH_DIM, D_IMG),
        ("image_attn", D_IMG, 4 * D_IMG),
        ("image_up", D_IMG, IMG_MLP),
        ("image_down", IMG_MLP, D_IMG),
        ("image_proj", D_IMG, EMBED),
        ("text_attn", D_TXT, 4 * D_TXT),
        ("text_up", D_TXT, TXT_MLP),
        ("text_down", TXT_MLP, D_TXT),
        ("text_proj", D_TXT, EMBED),
        ("image_vec", IMG_TOK + 9, D_IMG),
        ("text_vec", CTX + 6, D_TXT),
        ("temper", 1, 1),
    ]


LANES = 128
GROUP = 16
CHUNKS = 16
GATHER_CHUNKS = 14
CACHED_ROWS = 64
ID_ROWS = 16
MESH = pl.DeviceIdType.MESH


def dot_nn(left_side, right_side):
    return lax.dot_general(
        left_side, right_side, (((1,), (0,)), ((), ())), preferred_element_type=jnp.float32
    )


def dot_nt(left_side, right_side):
    return lax.dot_general(
        left_side, right_side, (((1,), (1,)), ((), ())), preferred_element_type=jnp.float32
    )


def dot_tn(left_side, right_side):
    return lax.dot_general(
        left_side, right_side, (((0,), (0,)), ((), ())), preferred_element_type=jnp.float32
    )


def back_dot(left_side, right_side):
    return dot_nt(left_side, right_side)


def fwd_dot(left_side, right_side):
    return dot_nn(left_side, right_side)


def weight_grad(left_side, right_side):
    return dot_tn(left_side, right_side)


def norm_parts(values):
    center = values - jnp.mean(values, -1, keepdims=True)
    scale = lax.rsqrt(jnp.mean(center * center, -1, keepdims=True) + norm_eps)
    return center * scale, scale


def layer_norm(values, gain_vec, shift_vec):
    return norm_parts(values)[0] * gain_vec + shift_vec


def layer_norm_back(values, gain_vec, grad):
    unit, scale = norm_parts(values)
    grad_unit = grad * gain_vec
    inner = jnp.mean(grad_unit, -1, keepdims=True)
    along = jnp.mean(grad_unit * unit, -1, keepdims=True)
    return scale * (grad_unit - inner - unit * along), grad * unit


def sum_rows(values):
    return jnp.sum(values, 0, keepdims=True)


def low16(values):
    return jnp.concatenate([values, jnp.zeros_like(values)], 0).astype(jnp.bfloat16)


SEQS = 8


class Tower:
    def __init__(self, image):
        self.image = image
        self.width = D_IMG if image else D_TXT
        self.heads = IMG_HEADS if image else TXT_HEADS
        self.length = IMG_TOK if image else CTX
        self.rows = -(-SEQS * self.length // GROUP) * GROUP
        self.lanes = 16 if image else 8
        self.queries = SEQS * self.lanes
        self.block = 80 if image else 48
        self.names = ("patch", "attn", "up", "down", "proj") if image else ("attn", "up", "down", "proj")

    def shapes(self):
        width = self.width
        found = dict(attn=(width, 4 * width), up=(width, 4 * width), down=(4 * width, width), proj=(width, EMBED))
        if self.image:
            found["patch"] = (PATCH_DIM, width)
        return found

    def head_mask(self):
        lane = lax.broadcasted_iota(jnp.int32, (self.lanes, self.width), 1)
        row = lax.broadcasted_iota(jnp.int32, (self.lanes, self.width), 0)
        return lane // (self.width // self.heads) == row

    def spread_heads(self, values, wide_ref):
        mask = self.head_mask()
        for s in range(SEQS):
            row = jnp.broadcast_to(values[s : s + 1].astype(jnp.float32), mask.shape)
            wide_ref[s * self.lanes : (s + 1) * self.lanes, :] = jnp.where(mask, row, 0.0)
        return wide_ref[...].astype(jnp.bfloat16)

    def join_heads(self, values, wide_ref):
        mask = self.head_mask()
        wide_ref[...] = values
        rows = [
            sum_rows(jnp.where(mask, wide_ref[s * self.lanes : (s + 1) * self.lanes, :], 0.0))
            for s in range(SEQS)
        ]
        return jnp.concatenate(rows, 0)

    def row_of(self, s, ends_ref):
        return s * self.length + (0 if self.image else ends_ref[s])

    def each_block(self, function, start):
        return lax.fori_loop(
            0,
            self.rows // self.block,
            lambda i, carry: function(pl.ds(pl.multiple_of(i * self.block, GROUP), self.block), carry),
            start,
        )


def tower_fetch(names, sources, landed, sems):
    copies = {
        name: pltpu.make_async_copy(source, ref, sems.at[i])
        for i, (name, source, ref) in enumerate(zip(names, sources, landed))
    }
    for copy in copies.values():
        copy.start()
    return copies, dict(zip(names, landed))


def tower_forward_kernel(tower, *refs):
    count = len(tower.names)
    ends_ref, gains_ref, base_ref, input_ref = refs[:4]
    sources = refs[4 : 4 + count]
    (tokens_ref, normed_ref, pair_ref, normed_own_ref, query_ref, probs_ref, attended_ref, middle_ref, normed_two_ref,
     upper_ref, act_ref, output_ref, head_ref, raw_ref, emb_ref) = refs[4 + count : 19 + count]
    hidden_ref, wide_ref = refs[19 + count : 21 + count]
    landed, sems = refs[21 + count : 21 + 2 * count], refs[21 + 2 * count]
    copies, weights = tower_fetch(tower.names, sources, landed, sems)
    width = tower.width
    gains = [gains_ref[i : i + 1, :] for i in range(8)]
    if tower.image:
        copies["patch"].wait()

        def patch(j, carry):
            cols = pl.ds(pl.multiple_of(j * 256, 256), 256)
            tokens_ref[:, cols] = dot_nn(input_ref[...], weights["patch"][:, cols]) + base_ref[:, cols]
            return carry

        lax.fori_loop(0, width // 256, patch, 0)

    def first(rows, carry):
        if tower.image:
            hidden = layer_norm(tokens_ref[rows, :], gains[0], gains[1])
        else:
            hidden = input_ref[rows, :].astype(jnp.float32) + base_ref[rows, :]
            tokens_ref[rows, :] = hidden
        hidden_ref[rows, :] = hidden
        normed_ref[rows, :] = layer_norm(hidden, gains[2], gains[3]).astype(jnp.bfloat16)
        return carry

    tower.each_block(first, 0)
    copies["attn"].wait()

    def pair(j, carry):
        at = pl.multiple_of(j * 256, 256)
        product = dot_nn(normed_ref[...], weights["attn"][:, pl.ds(width + at, 256)])
        pair_ref[:, pl.ds(at, 256)] = product.astype(jnp.bfloat16)
        return carry

    lax.fori_loop(0, 2 * width // 256, pair, 0)
    hidden_own = jnp.concatenate(
        [hidden_ref[pl.ds(tower.row_of(s, ends_ref), 1), :] for s in range(SEQS)], 0
    )
    normed_own = low16(layer_norm(hidden_own, gains[2], gains[3]))
    normed_own_ref[...] = normed_own
    query = dot_nn(normed_own, weights["attn"][:, :width]).astype(jnp.bfloat16)
    query_ref[...] = query
    queries = tower.spread_heads(query, wide_ref)
    scores = dot_nt(queries, pair_ref[:, :width]) * (width // tower.heads) ** (-0.5)
    row = lax.broadcasted_iota(jnp.int32, scores.shape, 0) // tower.lanes
    spot = lax.broadcasted_iota(jnp.int32, scores.shape, 1) - row * tower.length
    last = jnp.full(scores.shape, tower.length - 1, jnp.int32)
    if not tower.image:
        for s in range(SEQS):
            last = jnp.where(row == s, ends_ref[s], last)
    scores = jnp.where((spot >= 0) & (spot <= last), scores, -1e30)
    powers = jnp.exp(scores - jnp.max(scores, -1, keepdims=True))
    probs = powers / jnp.sum(powers, -1, keepdims=True)
    probs_ref[...] = probs
    attended = low16(tower.join_heads(dot_nn(probs.astype(jnp.bfloat16), pair_ref[:, width:]), wide_ref))
    attended_ref[...] = attended
    middle = hidden_own + dot_nn(attended, weights["attn"][:, 3 * width :])[:SEQS]
    middle_ref[...] = middle
    normed_two_ref[...] = low16(layer_norm(middle, gains[4], gains[5]))
    copies["up"].wait()

    def rise(j, carry):
        cols = pl.ds(pl.multiple_of(j * 512, 512), 512)
        upper = dot_nn(normed_two_ref[...], weights["up"][:, cols])[:SEQS]
        upper_ref[:, cols] = upper
        act_ref[:, cols] = low16(upper * jax.nn.sigmoid(1.702 * upper))
        return carry

    lax.fori_loop(0, 4 * width // 512, rise, 0)
    copies["down"].wait()

    def fall(j, carry):
        cols = pl.ds(pl.multiple_of(j * 256, 256), 256)
        output_ref[:, cols] = middle_ref[:, cols] + dot_nn(act_ref[...], weights["down"][:, cols])[:SEQS]
        return carry

    lax.fori_loop(0, width // 256, fall, 0)
    head_in = low16(layer_norm(output_ref[...], gains[6], gains[7]))
    head_ref[...] = head_in
    copies["proj"].wait()
    raw = dot_nn(head_in, weights["proj"][...])[:SEQS]
    raw_ref[...] = raw
    emb_ref[...] = raw * lax.rsqrt(jnp.sum(raw * raw, -1, keepdims=True) + 1e-06)


def tower_forward(tower, ends, gains, base, inputs, weights):
    width, rows = tower.width, tower.rows
    low, full = jnp.bfloat16, jnp.float32
    outs = [
        ((rows, width), full),
        ((rows, width), low),
        ((rows, 2 * width), low),
        ((GROUP, width), low),
        ((GROUP, width), low),
        ((tower.queries, rows), full),
        ((GROUP, width), low),
        ((SEQS, width), full),
        ((GROUP, width), low),
        ((SEQS, 4 * width), full),
        ((GROUP, 4 * width), low),
        ((SEQS, width), full),
        ((GROUP, width), low),
        ((SEQS, EMBED), full),
        ((SEQS, EMBED), full),
    ]
    vmem = pl.BlockSpec(memory_space=pltpu.VMEM)
    shapes = tower.shapes()
    return pl.pallas_call(
        functools.partial(tower_forward_kernel, tower),
        out_shape=[jax.ShapeDtypeStruct(shape, kind) for shape, kind in outs],
        in_specs=[pl.BlockSpec(memory_space=pltpu.SMEM)]
        + [vmem] * 3
        + [pl.BlockSpec(memory_space=pl.ANY)] * len(tower.names),
        out_specs=[vmem] * len(outs),
        scratch_shapes=[pltpu.VMEM((rows, width), full), pltpu.VMEM((tower.queries, width), full)]
        + [pltpu.VMEM(shapes[name], low) for name in tower.names]
        + [pltpu.SemaphoreType.DMA((len(tower.names),))],
        compiler_params=pltpu.CompilerParams(vmem_limit_bytes=58 << 20),
        name="image_forward" if tower.image else "text_forward",
    )(ends, gains, base, inputs, *[weights[name] for name in tower.names])


def tower_backward_kernel(tower, *refs):
    names = tower.names[-4:]
    count = len(names)
    ends_ref, gains_ref, grad_ref = refs[:3]
    (tokens_ref, normed_ref, pair_ref, normed_own_ref, query_ref, probs_ref, attended_ref, middle_ref, normed_two_ref,
     upper_ref, act_ref, output_ref, head_ref, raw_ref) = refs[3:17]
    sources = refs[17 : 17 + count]
    (grad_raw_ref, grad_mlp_ref, grad_upper_ref, grad_att_ref, grad_query_ref, grad_pair_ref, grad_rows_ref,
     places_ref, gain_grads_ref) = refs[17 + count : 26 + count]
    grad_ref_wide, wide_ref, grad_middle_ref = refs[26 + count : 29 + count]
    landed, sems = refs[29 + count : 29 + 2 * count], refs[29 + 2 * count]
    copies, weights = tower_fetch(names, sources, landed, sems)
    width, rows = tower.width, tower.rows
    scale = (width // tower.heads) ** (-0.5)
    gains = [gains_ref[i : i + 1, :] for i in range(8)]
    raw, grad_emb = raw_ref[...], grad_ref[...]
    norm = lax.rsqrt(jnp.sum(raw * raw, -1, keepdims=True) + 1e-06)
    along = jnp.sum(raw * grad_emb, -1, keepdims=True)
    grad_raw = low16(grad_emb * norm - raw * (norm * norm * norm * along))
    grad_raw_ref[...] = grad_raw
    copies["proj"].wait()
    grad_head = dot_nt(grad_raw, weights["proj"][...])[:SEQS]
    grad_out, gain_part = layer_norm_back(output_ref[...], gains[6], grad_head)
    gain_grads_ref[6:7, :] = sum_rows(gain_part)
    gain_grads_ref[7:8, :] = sum_rows(grad_head)
    grad_mlp_ref[...] = low16(grad_out)
    copies["down"].wait()

    def rise(j, carry):
        cols = pl.ds(pl.multiple_of(j * 512, 512), 512)
        grad_act = dot_nt(grad_mlp_ref[...], weights["down"][cols, :])[:SEQS]
        upper = upper_ref[:, cols]
        sig = jax.nn.sigmoid(1.702 * upper)
        grad_upper_ref[:, cols] = low16(grad_act * (sig + upper * (1.702 * (sig * (1.0 - sig)))))
        return carry

    lax.fori_loop(0, 4 * width // 512, rise, 0)
    copies["up"].wait()

    def fall(j, carry):
        cols = pl.ds(pl.multiple_of(j * 256, 256), 256)
        grad_middle_ref[:, cols] = dot_nt(grad_upper_ref[...], weights["up"][cols, :])[:SEQS]
        return carry

    lax.fori_loop(0, width // 256, fall, 0)
    grad_norm_two = grad_middle_ref[...]
    grad_mid, gain_part = layer_norm_back(middle_ref[...], gains[4], grad_norm_two)
    gain_grads_ref[4:5, :] = sum_rows(gain_part)
    gain_grads_ref[5:6, :] = sum_rows(grad_norm_two)
    grad_middle = grad_out + grad_mid
    grad_middle_ref[...] = grad_middle
    grad_att = low16(grad_middle)
    grad_att_ref[...] = grad_att
    copies["attn"].wait()
    grad_attended = dot_nt(grad_att, weights["attn"][:, 3 * width :]).astype(jnp.bfloat16)
    grads_heads = tower.spread_heads(grad_attended, wide_ref)
    queries = tower.spread_heads(query_ref[...], wide_ref)
    probs = probs_ref[...]
    grad_probs = dot_nt(grads_heads, pair_ref[:, width:])
    grad_scores = probs * (grad_probs - jnp.sum(grad_probs * probs, -1, keepdims=True))
    grad_scores = grad_scores.astype(jnp.bfloat16)
    grad_query = low16(tower.join_heads(dot_nn(grad_scores, pair_ref[:, :width]), wide_ref) * scale)
    grad_query_ref[...] = grad_query
    grad_pair_ref[:, :width] = (dot_tn(grad_scores, queries) * scale).astype(jnp.bfloat16)
    grad_pair_ref[:, width:] = dot_tn(probs.astype(jnp.bfloat16), grads_heads).astype(jnp.bfloat16)

    def inner(j, carry):
        at = pl.multiple_of(j * 256, 256)
        grad_ref_wide[:, pl.ds(at, 256)] = dot_nt(
            grad_pair_ref[...], weights["attn"][pl.ds(at, 256), width : 3 * width]
        )
        return carry

    lax.fori_loop(0, width // 256, inner, 0)
    grad_own = dot_nt(grad_query, weights["attn"][:, :width])
    for s in range(SEQS):
        grad_ref_wide[pl.ds(tower.row_of(s, ends_ref), 1), :] += grad_own[s : s + 1]

    def first(at, carry):
        grad = grad_ref_wide[at, :]
        hidden = tokens_ref[at, :]
        if tower.image:
            hidden = layer_norm(hidden, gains[0], gains[1])
        grad_in, gain_part = layer_norm_back(hidden, gains[2], grad)
        grad_ref_wide[at, :] = grad_in
        return carry[0] + sum_rows(gain_part), carry[1] + sum_rows(grad)

    nothing = jnp.zeros((1, width), jnp.float32)
    gain_one, shift_one = tower.each_block(first, (nothing, nothing))
    gain_grads_ref[2:3, :] = gain_one
    gain_grads_ref[3:4, :] = shift_one
    for s in range(SEQS):
        grad_ref_wide[pl.ds(tower.row_of(s, ends_ref), 1), :] += grad_middle_ref[s : s + 1, :]

    def second(at, carry):
        grad = grad_ref_wide[at, :]
        if not tower.image:
            grad_rows_ref[at, :] = grad.astype(jnp.bfloat16)
            return carry
        grad_in, gain_part = layer_norm_back(tokens_ref[at, :], gains[0], grad)
        grad_ref_wide[at, :] = grad_in
        grad_rows_ref[at, :] = grad_in.astype(jnp.bfloat16)
        return carry[0] + sum_rows(gain_part), carry[1] + sum_rows(grad)

    gain_pre, shift_pre = tower.each_block(second, (nothing, nothing))
    gain_grads_ref[0:1, :] = gain_pre
    gain_grads_ref[1:2, :] = shift_pre
    places = grad_ref_wide[0 : tower.length, :]
    for s in range(1, SEQS):
        places = places + grad_ref_wide[s * tower.length : (s + 1) * tower.length, :]
    places_ref[...] = places


def tower_backward(tower, ends, gains, grad_emb, kept, weights):
    width, rows = tower.width, tower.rows
    low, full = jnp.bfloat16, jnp.float32
    outs = [
        ((GROUP, EMBED), low),
        ((GROUP, width), low),
        ((GROUP, 4 * width), low),
        ((GROUP, width), low),
        ((GROUP, width), low),
        ((rows, 2 * width), low),
        ((rows, width), low),
        ((tower.length, width), full),
        ((8, width), full),
    ]
    vmem = pl.BlockSpec(memory_space=pltpu.VMEM)
    shapes, names = tower.shapes(), tower.names[-4:]
    return pl.pallas_call(
        functools.partial(tower_backward_kernel, tower),
        out_shape=[jax.ShapeDtypeStruct(shape, kind) for shape, kind in outs],
        in_specs=[pl.BlockSpec(memory_space=pltpu.SMEM)]
        + [vmem] * (2 + len(kept))
        + [pl.BlockSpec(memory_space=pl.ANY)] * len(names),
        out_specs=[vmem] * len(outs),
        scratch_shapes=[
            pltpu.VMEM((rows, width), full),
            pltpu.VMEM((tower.queries, width), full),
            pltpu.VMEM((SEQS, width), full),
        ]
        + [pltpu.VMEM(shapes[name], low) for name in names]
        + [pltpu.SemaphoreType.DMA((len(names),))],
        compiler_params=pltpu.CompilerParams(vmem_limit_bytes=58 << 20),
        name="image_backward" if tower.image else "text_backward",
    )(ends, gains, grad_emb, *kept, *[weights[name] for name in names])


def grad_pairs(kept, grads):
    (normed, normed_own, attended, normed_two, act_low, head_in) = (
        kept[1], kept[3], kept[6], kept[8], kept[10], kept[12]
    )
    grad_raw, grad_mlp, grad_upper, grad_att, grad_query, grad_pair = grads[:6]
    return (
        [(normed_own, grad_query), (normed, grad_pair), (attended, grad_att)],
        [(normed_two, grad_upper)],
        [(act_low, grad_mlp)],
        [(head_in, grad_raw)],
    )


def image_inputs(image_vec, pixels):
    pixels = jnp.pad(pixels, ((0, 0), (1, 0), (0, 0))).reshape(-1, PATCH_DIM)
    base = image_vec[1 : IMG_TOK + 1] + jnp.pad(image_vec[:1], ((0, IMG_TOK - 1), (0, 0)))
    return image_vec[IMG_TOK + 1 :], jnp.tile(base, (SEQS, 1)), pixels


def text_inputs(text_vec, token_rows):
    gains = jnp.pad(text_vec[CTX:], ((2, 0), (0, 0)))
    extra = TEXT.rows - SEQS * CTX
    base = jnp.pad(jnp.tile(text_vec[:CTX], (SEQS, 1)), ((0, extra), (0, 0)))
    return gains, base, jnp.pad(token_rows, ((0, extra), (0, 0)))


def adam_step(weight, first, second, grad, rate, decay):
    first = beta_one * first + (1.0 - beta_one) * grad
    second = beta_two * second + (1.0 - beta_two) * grad * grad
    first_hat = first / (1.0 - beta_one**STEP)
    second_hat = second / (1.0 - beta_two**STEP)
    weight = weight - rate * (first_hat / (jnp.sqrt(second_hat) + adam_eps) + decay * weight)
    return (weight, first, second)


IMAGE, TEXT = Tower(True), Tower(False)


def matrix_rows():
    return sum(seg_rows * seg_cols for seg_name, seg_rows, seg_cols in segment_list()[:9]) // LANES


def window_rows(shard, step=GROUP):
    need = -(-(GROUP * LANES - 1 + shard) // LANES)
    return -(-need // step) * step


def window_start(shard, index):
    return (shard * index // (GROUP * LANES)) * GROUP


def linear_index(gy_size):
    return lax.axis_index("gx") * gy_size + lax.axis_index("gy")


def place_kernel(shard, gy_size, flat_ref, out_ref, rolled):
    rows = flat_ref.shape[0]
    offset = lax.rem(shard * linear_index(gy_size), GROUP * LANES)
    down, right = offset // LANES, lax.rem(offset, LANES)
    pad = 2 * GROUP
    rolled[0:pad, :] = jnp.zeros((pad, LANES), jnp.float32)
    parts = 5 if rows % (5 * GROUP) == 0 else 1
    step = rows // parts

    def roll_rows(i, carry):
        at = pl.multiple_of(i * step, GROUP)
        rolled[pl.ds(pad + at, step), :] = pltpu.roll(flat_ref[pl.ds(at, step), :], right, 1)
        return carry

    lax.fori_loop(0, parts, roll_rows, 0)
    lane = lax.broadcasted_iota(jnp.int32, (step, LANES), 1)

    def put_rows(i, carry):
        at = pl.multiple_of(i * step, GROUP)
        upper = rolled[pl.ds(pad + at - down - 1, step), :]
        lower = rolled[pl.ds(pad + at - down, step), :]
        out_ref[pl.ds(at, step), :] = jnp.where(lane < right, upper, lower).astype(jnp.bfloat16)
        return carry

    lax.fori_loop(0, parts, put_rows, 0)


def place_window(flat, gy_size):
    shard = flat.shape[0]
    rows = window_rows(shard)
    padded = jnp.pad(flat, (0, rows * LANES - shard)).reshape(rows, LANES)
    return pl.pallas_call(
        functools.partial(place_kernel, shard, gy_size),
        out_shape=jax.ShapeDtypeStruct((rows, LANES), jnp.bfloat16),
        in_specs=[pl.BlockSpec(memory_space=pltpu.VMEM)],
        out_specs=pl.BlockSpec(memory_space=pltpu.VMEM),
        scratch_shapes=[pltpu.VMEM((rows + 2 * GROUP, LANES), jnp.float32)],
        compiler_params=pltpu.CompilerParams(vmem_limit_bytes=32 << 20),
        name="place_window",
    )(padded)


def lift_kernel(shard, gy_size, window_ref, out_ref, rolled):
    rows = window_ref.shape[0]
    offset = lax.rem(shard * linear_index(gy_size), GROUP * LANES)
    up, left = offset // LANES, lax.rem(offset, LANES)
    pad = 2 * GROUP
    step = rows // CHUNKS
    rolled[rows:, :] = jnp.zeros((pad, LANES), jnp.float32)

    def roll_rows(i, carry):
        at = pl.multiple_of(i * step, GROUP)
        rolled[pl.ds(at, step), :] = pltpu.roll(
            window_ref[pl.ds(at, step), :], lax.rem(LANES - left, LANES), 1
        )
        return carry

    lax.fori_loop(0, CHUNKS, roll_rows, 0)
    lane = lax.broadcasted_iota(jnp.int32, (step, LANES), 1)

    def put_rows(i, carry):
        at = pl.multiple_of(i * step, GROUP)
        first = rolled[pl.ds(at + up, step), :]
        second = rolled[pl.ds(at + up + 1, step), :]
        out_ref[pl.ds(at, step), :] = jnp.where(lane < LANES - left, first, second)
        return carry

    lax.fori_loop(0, CHUNKS, put_rows, 0)


def lift_window(window, shard, gy_size):
    rows = window.shape[0]
    lifted = pl.pallas_call(
        functools.partial(lift_kernel, shard, gy_size),
        out_shape=jax.ShapeDtypeStruct((rows, LANES), jnp.float32),
        in_specs=[pl.BlockSpec(memory_space=pltpu.VMEM)],
        out_specs=pl.BlockSpec(memory_space=pltpu.VMEM),
        scratch_shapes=[pltpu.VMEM((rows + 2 * GROUP, LANES), jnp.float32)],
        compiler_params=pltpu.CompilerParams(vmem_limit_bytes=32 << 20),
        name="lift_window",
    )(window)
    return lifted.reshape(-1)[:shard]


def spread_steps():
    steps = []
    base = 0
    for number, (seg_name, seg_rows, seg_cols) in enumerate(segment_list()[:9]):
        wide = seg_cols // LANES
        take = seg_rows
        while take * wide > 4608:
            take //= 2
        for start in range(0, seg_rows, take):
            steps.append((number, start, take, seg_cols, base + start * wide))
        base += seg_rows * wide
    return steps


def window_pieces(shard, count, stride, first, length):
    pieces, shared = [], []
    for index in range(count):
        low = window_start(shard, index)
        high = window_start(shard, index + 1) if index + 1 < count else low + window_rows(shard)
        start, stop = max(low, first), min(high, first + length)
        if start < stop:
            pieces.append((index * stride + start - low, start - first, stop - start))
        if index + 1 < count and first <= high < first + length:
            shared.append((index * stride + high - low, high - first))
    return pieces, shared


def spread_kernel(shard, count, vec_rows, gathered_ref, *refs):
    outs, vec_ref = refs[:9], refs[9]
    landed, edges, wide_rows, ready, in_sem, out_sem = refs[10:]
    rows = gathered_ref.shape[0] // count
    steps = spread_steps()
    steps.append((9, 0, vec_rows, LANES, matrix_rows()))

    def copies_in(number):
        seg, start, take, cols, base = steps[number]
        slot = number % 2
        pieces, shared = window_pieces(shard, count, rows, base, take * cols // LANES)
        found = [
            pltpu.make_async_copy(
                gathered_ref.at[pl.ds(src, size)], landed.at[slot, pl.ds(dst, size)], in_sem.at[slot]
            )
            for src, dst, size in pieces
        ]
        found += [
            pltpu.make_async_copy(
                gathered_ref.at[pl.ds(src, GROUP)], edges.at[slot, order], in_sem.at[slot]
            )
            for order, (src, dst) in enumerate(shared)
        ]
        return found, shared

    def copy_out(number):
        seg, start, take, cols, base = steps[number]
        slot = number % 2
        if seg == 9:
            return pltpu.make_async_copy(wide_rows.at[pl.ds(0, take)], vec_ref, out_sem.at[slot])
        return pltpu.make_async_copy(
            ready[cols].at[slot, pl.ds(0, take)], outs[seg].at[pl.ds(start, take)], out_sem.at[slot]
        )

    for copy in copies_in(0)[0]:
        copy.start()
    for number, (seg, start, take, cols, base) in enumerate(steps):
        slot = number % 2
        wide = cols // LANES
        total = take * wide
        if number + 1 < len(steps):
            for copy in copies_in(number + 1)[0]:
                copy.start()
        found, shared = copies_in(number)
        for copy in found:
            copy.wait()
        if number >= 2:
            copy_out(number - 2).wait()
        block = 256 if total % 256 == 0 else GROUP

        def widen(i, carry, slot=slot, block=block):
            at = pl.multiple_of(i * block, GROUP)
            wide_rows[pl.ds(at, block), :] = landed[slot, pl.ds(at, block), :].astype(jnp.float32)
            return carry

        lax.fori_loop(0, total // block, widen, 0)
        for order, (src, dst) in enumerate(shared):
            wide_rows[dst : dst + GROUP, :] += edges[slot, order].astype(jnp.float32)
        if seg < 9:

            def tile(i, carry, slot=slot, wide=wide, cols=cols):
                at = pl.multiple_of(i * GROUP, GROUP)
                for j in range(wide):
                    ready[cols][slot, pl.ds(at, GROUP), j * LANES : (j + 1) * LANES] = wide_rows[
                        pl.ds(at * wide + j, GROUP, stride=wide), :
                    ].astype(jnp.bfloat16)
                return carry

            lax.fori_loop(0, take // GROUP, tile, 0)
        copy_out(number).start()
    copy_out(len(steps) - 2).wait()
    copy_out(len(steps) - 1).wait()


def spread_entry(shard, count, vec_rows, gathered_ref, *refs):
    outs = refs[:10]
    landed, edges, wide_rows, ready_a, ready_b, ready_c, ready_d, in_sem, out_sem = refs[10:]
    ready = {D_IMG: ready_a, 4 * D_IMG: ready_b, D_TXT: ready_c, 4 * D_TXT: ready_d}
    spread_kernel(
        shard, count, vec_rows, gathered_ref, *outs, landed, edges, wide_rows, ready, in_sem, out_sem
    )


def spread_weights(gathered, shard, count):
    rows = gathered.shape[0] // count
    steps = spread_steps()
    tallest = {}
    for seg, start, take, cols, base in steps:
        tallest[cols] = max(tallest.get(cols, 0), take)
    most = max(take * cols // LANES for seg, start, take, cols, base in steps)
    vec_rows = -(-(sum(r * c for name, r, c in segment_list()[9:])) // (LANES * GROUP)) * GROUP
    edge_count = max(
        len(window_pieces(shard, count, rows, base, take * cols // LANES)[1])
        for seg, start, take, cols, base in steps
    )
    ready = [
        pltpu.VMEM((2, tallest[cols], cols), jnp.bfloat16)
        for cols in (D_IMG, 4 * D_IMG, D_TXT, 4 * D_TXT)
    ]
    return pl.pallas_call(
        functools.partial(spread_entry, shard, count, vec_rows),
        out_shape=[
            jax.ShapeDtypeStruct((seg_rows, seg_cols), jnp.bfloat16)
            for seg_name, seg_rows, seg_cols in segment_list()[:9]
        ]
        + [jax.ShapeDtypeStruct((vec_rows, LANES), jnp.float32)],
        in_specs=[pl.BlockSpec(memory_space=pl.ANY)],
        out_specs=[pl.BlockSpec(memory_space=pl.ANY)] * 10,
        scratch_shapes=[
            pltpu.VMEM((2, most, LANES), jnp.bfloat16),
            pltpu.VMEM((2, edge_count + 1, GROUP, LANES), jnp.bfloat16),
            pltpu.VMEM((most, LANES), jnp.float32),
        ]
        + ready
        + [pltpu.SemaphoreType.DMA((2,)), pltpu.SemaphoreType.DMA((2,))],
        compiler_params=pltpu.CompilerParams(vmem_limit_bytes=48 << 20),
        name="spread_weights",
    )(gathered)


def split_vectors(vec_rows):
    image_count, text_count = (IMG_TOK + 9) * D_IMG // LANES, (CTX + 6) * D_TXT // LANES
    image_vec = vec_rows[:image_count].reshape(IMG_TOK + 9, D_IMG)
    text_vec = vec_rows[image_count : image_count + text_count].reshape(CTX + 6, D_TXT)
    return image_vec, text_vec, vec_rows[image_count + text_count, 0]


def grads_kernel(parts, total_rows, *refs):
    operand_count = sum(2 * len(pairs) for seg_rows, seg_cols, take, pairs in parts)
    operands = refs[:operand_count]
    vec_ref, out_ref, flat_rows, vec_sem, out_sem = refs[operand_count:]
    tail = pltpu.make_async_copy(vec_ref, out_ref.at[pl.ds(matrix_rows(), vec_ref.shape[0])], vec_sem)
    tail.start()
    base = 0
    steps_before = 0
    for seg_rows, seg_cols, take, pairs in parts:
        wide = seg_cols // LANES
        size = take * wide
        count = seg_rows // take

        def step(i, carry, base=base, before=steps_before, size=size, take=take, wide=wide, pairs=pairs):
            slot = lax.rem(i + before, 2)

            def written(number):
                at = pl.multiple_of(base + number * size, 8)
                return pltpu.make_async_copy(
                    flat_rows.at[slot, pl.ds(0, size)], out_ref.at[pl.ds(at, size)], out_sem.at[slot]
                )

            @pl.when(i >= 2)
            def _():
                written(i - 2).wait()

            for left_number, right_number, first in pairs:
                left_ref, right_ref = operands[left_number], operands[right_number]
                at = pl.multiple_of(i * take, LANES)
                product = lax.dot_general(
                    left_ref[:, pl.ds(at, take)],
                    right_ref[...],
                    (((0,), (0,)), ((), ())),
                    preferred_element_type=jnp.float32,
                )
                for j in range(right_ref.shape[1] // LANES):
                    flat_rows[slot, pl.ds(first + j, take, stride=wide), :] = product[
                        :, j * LANES : (j + 1) * LANES
                    ]
            written(i).start()
            return carry

        lax.fori_loop(0, count, step, 0)
        for number in range(max(count - 2, 0), count):
            slot = (number + steps_before) % 2
            at = base + number * size
            pltpu.make_async_copy(
                flat_rows.at[slot, pl.ds(0, size)], out_ref.at[pl.ds(at, size)], out_sem.at[slot]
            ).wait()
        base += seg_rows * wide
        steps_before += count
    tail.wait()


def weight_grads(pair_lists, vec_rows):
    operands, parts = [], []
    for (seg_name, seg_rows, seg_cols), pairs in zip(segment_list()[:9], pair_lists):
        numbered, first = [], 0
        for left_side, right_side in pairs:
            numbered.append((len(operands), len(operands) + 1, first))
            for side in (left_side, right_side):
                side = side.reshape(-1, side.shape[-1])
                operands.append(jnp.pad(side, ((0, -side.shape[0] % GROUP), (0, 0))))
            first += right_side.shape[-1] // LANES
        parts.append((seg_rows, seg_cols, min(seg_rows, 256 if seg_cols <= 768 else 128), numbered))
    total_rows = matrix_rows() + vec_rows.shape[0]
    most = max(take * seg_cols // LANES for seg_rows, seg_cols, take, pairs in parts)
    return pl.pallas_call(
        functools.partial(grads_kernel, parts, total_rows),
        out_shape=jax.ShapeDtypeStruct((total_rows, LANES), jnp.float32),
        in_specs=[pl.BlockSpec(memory_space=pltpu.VMEM)] * (len(operands) + 1),
        out_specs=pl.BlockSpec(memory_space=pl.ANY),
        scratch_shapes=[
            pltpu.VMEM((2, most, LANES), jnp.float32),
            pltpu.SemaphoreType.DMA,
            pltpu.SemaphoreType.DMA((2,)),
        ],
        compiler_params=pltpu.CompilerParams(vmem_limit_bytes=56 << 20),
        name="weight_grads",
    )(*operands, vec_rows)


def exchange_kernel(gx_size, gy_size, many, *refs):
    blocks, outs = refs[:many], refs[many : 2 * many]
    send_sem, recv_sem, own_sem = refs[2 * many :]
    count = gx_size * gy_size
    me = linear_index(gy_size)
    barrier = pltpu.get_barrier_semaphore()

    def device(step):
        other = lax.rem(me + step, count)
        return (other // gy_size, lax.rem(other, gy_size))

    def greet(step, carry):
        pl.semaphore_signal(barrier, inc=1, device_id=device(step), device_id_type=MESH)
        return carry

    lax.fori_loop(1, count, greet, 0)
    own = [
        pltpu.make_async_copy(block, out.at[me], own_sem.at[i])
        for i, (block, out) in enumerate(zip(blocks, outs))
    ]
    for copy in own:
        copy.start()
    pl.semaphore_wait(barrier, count - 1)

    def send(step, carry):
        for i, (block, out) in enumerate(zip(blocks, outs)):
            pltpu.make_async_remote_copy(
                src_ref=block,
                dst_ref=out.at[me],
                send_sem=send_sem.at[i],
                recv_sem=recv_sem.at[i],
                device_id=device(step),
                device_id_type=MESH,
            ).start()
        return carry

    lax.fori_loop(1, count, send, 0)
    for i, out in enumerate(outs):
        own[i].wait()
        others = out.at[pl.ds(0, count - 1)]
        both = pltpu.make_async_remote_copy(
            src_ref=others,
            dst_ref=others,
            send_sem=send_sem.at[i],
            recv_sem=recv_sem.at[i],
            device_id=device(1),
            device_id_type=MESH,
        )
        both.wait_send()
        both.wait_recv()


def exchange_all(blocks, gx_size, gy_size, number, name):
    count, many = gx_size * gy_size, len(blocks)
    return pl.pallas_call(
        functools.partial(exchange_kernel, gx_size, gy_size, many),
        out_shape=[jax.ShapeDtypeStruct((count,) + block.shape, block.dtype) for block in blocks],
        in_specs=[pl.BlockSpec(memory_space=pltpu.VMEM)] * many,
        out_specs=[pl.BlockSpec(memory_space=pltpu.VMEM)] * many,
        scratch_shapes=[pltpu.SemaphoreType.DMA((many,))] * 3,
        compiler_params=pltpu.CompilerParams(
            collective_id=number, has_side_effects=True, vmem_limit_bytes=32 << 20
        ),
        name=name,
    )(*blocks)


class Places:
    def __init__(self, sizes):
        self.x_size, self.low_size, self.high_size = sizes
        self.mixed = self.x_size == self.low_size
        self.gy_size = self.high_size * self.low_size
        gx, gy = lax.axis_index("gx"), lax.axis_index("gy")
        self.core, x = lax.rem(gx, 2), gx // 2
        self.h, low = gy // self.low_size, lax.rem(gy, self.low_size)
        self.a, self.b = self.turned(self.core, x, low)
        self.a_size, self.b_size = self.x_size, self.low_size

    def turned(self, side, a, b):
        if not self.mixed:
            return a, b
        return a * (1 - side) + b * side, b * (1 - side) + a * side

    def device(self, side, a, b, h):
        dev_x, dev_low = self.turned(side, a, b)
        return (dev_x * 2 + side, h * self.low_size + dev_low)

    def linear(self, side, a, b, h):
        gx, gy = self.device(side, a, b, h)
        return gx * self.gy_size + gy

    def sibling(self):
        a, b = (self.b, self.a) if self.mixed else (self.a, self.b)
        return self.device(1 - self.core, a, b, self.h)

    def along_a(self):
        return [
            self.device(self.core, lax.rem(self.a + d, self.a_size), self.b, self.h)
            for d in range(1, self.a_size)
        ]

    def along_b(self):
        return [
            self.device(self.core, self.a, lax.rem(self.b + d, self.b_size), self.h)
            for d in range(1, self.b_size)
        ]

    def along_h(self):
        return [
            self.device(self.core, self.a, self.b, lax.rem(self.h + d, self.high_size))
            for d in range(1, self.high_size)
        ]


def greet_all(others):
    barrier = pltpu.get_barrier_semaphore()
    for other in others:
        pl.semaphore_signal(barrier, inc=1, device_id=other, device_id_type=MESH)
    pl.semaphore_wait(barrier, len(others))


def remote(src, dst, send_sem, recv_sem, other):
    return pltpu.make_async_remote_copy(
        src_ref=src, dst_ref=dst, send_sem=send_sem, recv_sem=recv_sem, device_id=other, device_id_type=MESH
    )


def axis_sizes(gx_size, gy_size):
    return gx_size // 2, gy_size // 4, 4


def route_capacity(tokens, gy_size):
    return max(5 * tokens // (2 * gy_size * GROUP), 1) * GROUP


def share_kernel(gx_size, gy_size, everyone, send_ref, out_ref, own_sem, row_send, row_recv, x_send, x_recv, core_send,
                 core_recv):
    gx, gy = lax.axis_index("gx"), lax.axis_index("gy")
    x_size = gx_size // 2
    core, x = lax.rem(gx, 2), gx // 2
    rows = [(gx, lax.rem(gy + d, gy_size)) for d in range(1, gy_size)]
    along_x = [(lax.rem(x + d, x_size) * 2 + core, gy) for d in range(1, x_size)] if everyone else []
    sibling = [(x * 2 + 1 - core, gy)] if everyone else []
    greet_all(rows + along_x + sibling)
    mine = out_ref.at[gx] if everyone else out_ref.at[0]
    own = pltpu.make_async_copy(send_ref.at[gy], mine.at[gy], own_sem)
    own.start()
    for d, other in enumerate(rows):
        remote(send_ref.at[other[1]], mine.at[gy], row_send.at[d], row_recv.at[d], other).start()
    own.wait()
    for d, other in enumerate(rows):
        copy = remote(send_ref.at[other[1]], mine.at[gy], row_send.at[d], row_recv.at[d], other)
        copy.wait_recv()
    for d, other in enumerate(along_x):
        remote(mine, mine, x_send.at[d], x_recv.at[d], other).start()
    for other in sibling:
        remote(mine, mine, core_send.at[0], core_recv.at[0], other).start()
    for d, other in enumerate(along_x):
        remote(mine, mine, x_send.at[d], x_recv.at[d], other).wait_recv()
        source = out_ref.at[lax.rem(x + x_size - d - 1, x_size) * 2 + core]
        remote(source, source, core_send.at[d + 1], core_recv.at[d + 1], sibling[0]).start()
    for d, other in enumerate(rows):
        remote(send_ref.at[other[1]], mine.at[gy], row_send.at[d], row_recv.at[d], other).wait_send()
    for d, other in enumerate(along_x):
        remote(mine, mine, x_send.at[d], x_recv.at[d], other).wait_send()
    for i in range(x_size if everyone else 0):
        copy = remote(mine, mine, core_send.at[i], core_recv.at[i], sibling[0])
        copy.wait_send()
        copy.wait_recv()


def share_rows(rows, gx_size, gy_size, everyone, number, name):
    groups, dma = (gx_size if everyone else 1), pltpu.SemaphoreType.DMA
    x_size = gx_size // 2
    return pl.pallas_call(
        functools.partial(share_kernel, gx_size, gy_size, everyone),
        out_shape=jax.ShapeDtypeStruct((groups,) + rows.shape, rows.dtype),
        in_specs=[pl.BlockSpec(memory_space=pltpu.VMEM)],
        out_specs=pl.BlockSpec(memory_space=pltpu.VMEM),
        scratch_shapes=[dma, dma((gy_size - 1,)), dma((gy_size - 1,)), dma((x_size,)), dma((x_size,)), dma((x_size,)),
                        dma((x_size,))],
        compiler_params=pltpu.CompilerParams(
            collective_id=number, has_side_effects=True, vmem_limit_bytes=48 << 20
        ),
        name=name,
    )(rows)


def table_sum_kernel(cap, counts_ref, index_ref, rows_ref, out_ref, square_ref, wide, row_sem):
    sources = rows_ref.shape[0]
    vocab = out_ref.shape[0]

    def fetch(source):
        slot = lax.rem(source, 2)
        return pltpu.make_async_copy(rows_ref.at[source], wide.at[slot], row_sem.at[slot])

    fetch(0).start()
    block = 32 if vocab % 32 == 0 else 8

    def clear(i, carry):
        out_ref[pl.ds(pl.multiple_of(i * block, 8), block), :] = jnp.zeros((block, D_TXT), jnp.float32)
        return carry

    lax.fori_loop(0, vocab // block, clear, 0)

    def one_source(source, carry):
        slot = lax.rem(source, 2)

        @pl.when(source + 1 < sources)
        def _():
            fetch(source + 1).start()

        fetch(source).wait()
        count = counts_ref[source]
        widened = wide.at[slot]

        def add(group, carry):
            rows = widened[pl.ds(pl.multiple_of(group * GROUP, GROUP), GROUP), :].astype(jnp.float32)
            for i in range(GROUP):
                @pl.when(group * GROUP + i < count)
                def _(i=i):
                    place = pl.ds(index_ref[source * cap + group * GROUP + i], 1)
                    out_ref[place, :] = out_ref[place, :] + rows[i : i + 1, :]

            return carry

        lax.fori_loop(0, (count + GROUP - 1) // GROUP, add, 0)
        return carry

    lax.fori_loop(0, sources, one_source, 0)

    def square(i, carry):
        part = out_ref[pl.ds(pl.multiple_of(i * block, 8), block), :]
        part = part * part
        total = carry
        for r in range(0, block, 8):
            total = total + part[r : r + 8]
        return total

    square_ref[...] = lax.fori_loop(0, vocab // block, square, jnp.zeros((8, D_TXT), jnp.float32))


def table_sum(counts, index, rows, vocab):
    sources, cap = rows.shape[0], rows.shape[1]
    return pl.pallas_call(
        functools.partial(table_sum_kernel, cap),
        out_shape=[
            jax.ShapeDtypeStruct((vocab, D_TXT), jnp.float32),
            jax.ShapeDtypeStruct((8, D_TXT), jnp.float32),
        ],
        in_specs=[pl.BlockSpec(memory_space=pltpu.SMEM)] * 2 + [pl.BlockSpec(memory_space=pl.ANY)],
        out_specs=[pl.BlockSpec(memory_space=pltpu.VMEM)] * 2,
        scratch_shapes=[pltpu.VMEM((2, cap, D_TXT), jnp.bfloat16), pltpu.SemaphoreType.DMA((2,))],
        compiler_params=pltpu.CompilerParams(vmem_limit_bytes=40 << 20),
        name="table_sum",
    )(counts, index, rows)


def ranks(flags):
    tokens = flags.shape[-1]
    before = (jnp.arange(tokens)[:, None] < jnp.arange(tokens)[None, :]).astype(jnp.bfloat16)
    return fwd_dot(flags.astype(jnp.bfloat16), before).astype(jnp.int32)


def pick_matrix(slots, count):
    return (jnp.arange(count)[:, None] == slots[None, :]).astype(jnp.bfloat16)


def gather_kernel(sizes, window_ref, out_ref, own_sem, h_send, h_recv, b_send, b_recv, a_send, a_recv, core_send,
                  core_recv):
    at = Places(sizes)
    rows = window_ref.shape[0]
    chunk = rows // GATHER_CHUNKS
    me = at.linear(at.core, at.a, at.b, at.h)
    sibling, peers_a, peers_b, peers_h = at.sibling(), at.along_a(), at.along_b(), at.along_h()
    greet_all([sibling] + peers_a + peers_b + peers_h)

    def part(block, t):
        return out_ref.at[pl.ds(pl.multiple_of(block * rows + t * chunk, GROUP), chunk)]

    def many(count):
        return out_ref.at[pl.ds(0, count * chunk)]

    def own_copy(t):
        src = window_ref.at[pl.ds(pl.multiple_of(t * chunk, GROUP), chunk)]
        return src, pltpu.make_async_copy(src, part(me, t), own_sem.at[t])

    def stage_h(t):
        src, own = own_copy(t)
        for d, other in enumerate(peers_h):
            remote(src, part(me, t), h_send.at[d], h_recv.at[t, d], other).start()
        own.start()

    def stage_b(t):
        own_copy(t)[1].wait()
        for d, other in enumerate(peers_h):
            remote(many(1), many(1), h_send.at[d], h_recv.at[t, d], other).wait_recv()
        for d, other in enumerate(peers_b):
            for h in range(at.high_size):
                block = part(at.linear(at.core, at.a, at.b, h), t)
                remote(block, block, b_send.at[d], b_recv.at[t, d], other).start()

    def stage_a(t):
        for d, other in enumerate(peers_b):
            remote(many(at.high_size), many(at.high_size), b_send.at[d], b_recv.at[t, d], other).wait_recv()
        for d, other in enumerate(peers_a):
            for b in range(at.b_size):
                for h in range(at.high_size):
                    block = part(at.linear(at.core, at.a, b, h), t)
                    remote(block, block, a_send.at[d], a_recv.at[t, d], other).start()

    plane = at.b_size * at.high_size

    def stage_core(t):
        for d, other in enumerate(peers_a):
            remote(many(plane), many(plane), a_send.at[d], a_recv.at[t, d], other).wait_recv()
        for a in range(at.a_size):
            for b in range(at.b_size):
                for h in range(at.high_size):
                    block = part(at.linear(at.core, a, b, h), t)
                    remote(block, block, core_send, core_recv, sibling).start()

    def turn(t, carry):
        for depth, stage in enumerate((stage_h, stage_b, stage_a, stage_core)):
            @pl.when((t >= depth) & (t < GATHER_CHUNKS + depth))
            def _():
                stage(t - depth)

        return carry

    lax.fori_loop(0, GATHER_CHUNKS + 3, turn, 0)

    def whole(count):
        return out_ref.at[pl.ds(0, count * rows)]

    for d, other in enumerate(peers_h):
        remote(whole(1), whole(1), h_send.at[d], h_recv.at[0, d], other).wait_send()
    for d, other in enumerate(peers_b):
        remote(whole(at.high_size), whole(at.high_size), b_send.at[d], b_recv.at[0, d], other).wait_send()
    for d, other in enumerate(peers_a):
        remote(whole(plane), whole(plane), a_send.at[d], a_recv.at[0, d], other).wait_send()
    half = whole(at.a_size * plane)
    last = remote(half, half, core_send, core_recv, sibling)
    last.wait_send()
    last.wait_recv()


def gather_windows(window, gx_size, gy_size, number):
    sizes = axis_sizes(gx_size, gy_size)
    a, b, h = sizes[0] - 1, sizes[1] - 1, sizes[2] - 1
    dma = pltpu.SemaphoreType.DMA
    return pl.pallas_call(
        functools.partial(gather_kernel, sizes),
        out_shape=jax.ShapeDtypeStruct((gx_size * gy_size * window.shape[0], LANES), window.dtype),
        in_specs=[pl.BlockSpec(memory_space=pltpu.VMEM)],
        out_specs=pl.BlockSpec(memory_space=pl.ANY),
        scratch_shapes=[dma((GATHER_CHUNKS,)), dma((h,)), dma((GATHER_CHUNKS, h)), dma((b,)), dma((GATHER_CHUNKS, b)), dma((a,)),
                        dma((GATHER_CHUNKS, a)), dma, dma],
        compiler_params=pltpu.CompilerParams(
            collective_id=number, has_side_effects=True, vmem_limit_bytes=32 << 20
        ),
        name="gather_windows",
    )(window)


def reduce_kernel(shard, sizes, grads_ref, out_ref, own, landed, keep_one, send_one, recv_one, keep_two, send_two,
                  recv_two, keep_three, send_three, recv_three, load_sem, pair_send, pair_recv, credit,
                  one_send, one_recv, two_send, two_recv, three_send, three_recv):
    at = Places(sizes)
    a_size, b_size, high_size = at.a_size, at.b_size, at.high_size
    core, my_a, my_b, high = at.core, at.a, at.b, at.h
    plane = b_size * high_size
    chunk = own.shape[2]
    chunks = out_ref.shape[0] // chunk

    def start_row(side, number):
        a, rest = number // plane, lax.rem(number, plane)
        return window_start(shard, at.linear(side, a, rest // high_size, lax.rem(rest, high_size)))

    sibling, peers, peers_two, peers_three = at.sibling(), at.along_a(), at.along_b(), at.along_h()
    greet_all([sibling] + peers + peers_two + peers_three)
    blocks = a_size * plane

    def pair_stage(t):
        slot = lax.rem(t, 2)

        @pl.when(t >= 2)
        def _():
            pl.semaphore_wait(credit, 1)

        def each(number, carry):
            theirs = pl.multiple_of(start_row(1 - core, number) + t * chunk, GROUP)
            mine = pl.multiple_of(start_row(core, number) + t * chunk, GROUP)
            remote(
                grads_ref.at[pl.ds(theirs, chunk)], landed.at[slot, number], pair_send.at[slot], pair_recv.at[slot], sibling
            ).start()
            pltpu.make_async_copy(
                grads_ref.at[pl.ds(mine, chunk)], own.at[slot, number], load_sem.at[slot]
            ).start()
            return carry

        lax.fori_loop(0, blocks, each, 0)

    def first_stage(u):
        slot = lax.rem(u, 2)
        both = remote(landed.at[slot], landed.at[slot], pair_send.at[slot], pair_recv.at[slot], sibling)
        pltpu.make_async_copy(own.at[slot], own.at[slot], load_sem.at[slot]).wait()
        both.wait_send()
        both.wait_recv()
        for d in range(1, a_size):
            @pl.when(u >= 2)
            def _():
                remote(send_one.at[slot, d - 1], recv_one.at[u - 2, d - 1], one_send.at[slot, d - 1],
                       one_recv.at[u - 2, d - 1], peers[d - 1]).wait_send()

            first = lax.rem(my_a + d, a_size) * plane

            def give(i, carry):
                send_one[slot, d - 1, i] = (own[slot, first + i] + landed[slot, first + i]).astype(jnp.bfloat16)
                return carry

            lax.fori_loop(0, plane, give, 0)
            remote(send_one.at[slot, d - 1], recv_one.at[u, d - 1], one_send.at[slot, d - 1],
                   one_recv.at[u, d - 1], peers[d - 1]).start()

        def hold(i, carry):
            keep_one[slot, i] = own[slot, my_a * plane + i] + landed[slot, my_a * plane + i]
            return carry

        lax.fori_loop(0, plane, hold, 0)

        @pl.when(u < chunks - 2)
        def _():
            pl.semaphore_signal(credit, inc=1, device_id=sibling, device_id_type=MESH)

    def second_stage(u):
        slot = lax.rem(u, 2)
        for d in range(1, a_size):
            remote(recv_one.at[u, d - 1], recv_one.at[u, d - 1], one_send.at[slot, d - 1], one_recv.at[u, d - 1],
                   peers[d - 1]).wait_recv()

        def total(number):
            value = keep_one[slot, number]
            for d in range(1, a_size):
                value = value + recv_one[u, d - 1, number].astype(jnp.float32)
            return value

        for d in range(1, b_size):
            @pl.when(u >= 2)
            def _():
                remote(send_two.at[slot, d - 1], recv_two.at[u - 2, d - 1], two_send.at[slot, d - 1],
                       two_recv.at[u - 2, d - 1], peers_two[d - 1]).wait_send()

            first = lax.rem(my_b + d, b_size) * high_size

            def give(i, carry):
                send_two[slot, d - 1, i] = total(first + i).astype(jnp.bfloat16)
                return carry

            lax.fori_loop(0, high_size, give, 0)
            remote(send_two.at[slot, d - 1], recv_two.at[u, d - 1], two_send.at[slot, d - 1],
                   two_recv.at[u, d - 1], peers_two[d - 1]).start()

        def hold(i, carry):
            keep_two[slot, i] = total(my_b * high_size + i)
            return carry

        lax.fori_loop(0, high_size, hold, 0)

    def third_stage(u):
        slot = lax.rem(u, 2)
        for d in range(1, b_size):
            remote(recv_two.at[u, d - 1], recv_two.at[u, d - 1], two_send.at[slot, d - 1], two_recv.at[u, d - 1],
                   peers_two[d - 1]).wait_recv()

        def total(number):
            value = keep_two[slot, number]
            for d in range(1, b_size):
                value = value + recv_two[u, d - 1, number].astype(jnp.float32)
            return value

        for d in range(1, high_size):
            @pl.when(u >= 2)
            def _():
                remote(send_three.at[slot, d - 1], recv_three.at[u - 2, d - 1], three_send.at[slot, d - 1],
                       three_recv.at[u - 2, d - 1], peers_three[d - 1]).wait_send()

            send_three[slot, d - 1] = total(lax.rem(high + d, high_size)).astype(jnp.bfloat16)
            remote(send_three.at[slot, d - 1], recv_three.at[u, d - 1], three_send.at[slot, d - 1],
                   three_recv.at[u, d - 1], peers_three[d - 1]).start()
        keep_three[slot] = total(high)

    def last_stage(u):
        slot = lax.rem(u, 2)
        value = keep_three[slot]
        for d in range(1, high_size):
            remote(recv_three.at[u, d - 1], recv_three.at[u, d - 1], three_send.at[slot, d - 1],
                   three_recv.at[u, d - 1], peers_three[d - 1]).wait_recv()
            value = value + recv_three[u, d - 1].astype(jnp.float32)
        out_ref[pl.ds(pl.multiple_of(u * chunk, GROUP), chunk), :] = value

    def turn(t, carry):
        stages = (pair_stage, first_stage, second_stage, third_stage, last_stage)
        for depth, stage in enumerate(stages):
            @pl.when((t >= depth) & (t < chunks + depth))
            def _():
                stage(t - depth)

        return carry

    lax.fori_loop(0, chunks + 4, turn, 0)
    for u in range(max(chunks - 2, 0), chunks):
        slot = u % 2
        for d in range(1, a_size):
            remote(send_one.at[slot, d - 1], recv_one.at[u, d - 1], one_send.at[slot, d - 1],
                   one_recv.at[u, d - 1], peers[d - 1]).wait_send()
        for d in range(1, b_size):
            remote(send_two.at[slot, d - 1], recv_two.at[u, d - 1], two_send.at[slot, d - 1],
                   two_recv.at[u, d - 1], peers_two[d - 1]).wait_send()
        for d in range(1, high_size):
            remote(send_three.at[slot, d - 1], recv_three.at[u, d - 1], three_send.at[slot, d - 1],
                   three_recv.at[u, d - 1], peers_three[d - 1]).wait_send()


def reduce_windows(grads, shard, gx_size, gy_size, number):
    rows = window_rows(shard, GROUP * CHUNKS)
    chunk = rows // CHUNKS
    x_size, low_size, high_size = axis_sizes(gx_size, gy_size)
    plane = low_size * high_size
    blocks = x_size * plane
    low_type, dma = jnp.bfloat16, pltpu.SemaphoreType.DMA
    a, b, h = x_size - 1, low_size - 1, high_size - 1
    return pl.pallas_call(
        functools.partial(reduce_kernel, shard, (x_size, low_size, high_size)),
        out_shape=jax.ShapeDtypeStruct((rows, LANES), jnp.float32),
        in_specs=[pl.BlockSpec(memory_space=pl.ANY)],
        out_specs=pl.BlockSpec(memory_space=pltpu.VMEM),
        scratch_shapes=[
            pltpu.VMEM((2, blocks, chunk, LANES), jnp.float32),
            pltpu.VMEM((2, blocks, chunk, LANES), jnp.float32),
            pltpu.VMEM((2, plane, chunk, LANES), jnp.float32),
            pltpu.VMEM((2, a, plane, chunk, LANES), low_type),
            pltpu.VMEM((CHUNKS, a, plane, chunk, LANES), low_type),
            pltpu.VMEM((2, high_size, chunk, LANES), jnp.float32),
            pltpu.VMEM((2, b, high_size, chunk, LANES), low_type),
            pltpu.VMEM((CHUNKS, b, high_size, chunk, LANES), low_type),
            pltpu.VMEM((2, chunk, LANES), jnp.float32),
            pltpu.VMEM((2, h, chunk, LANES), low_type),
            pltpu.VMEM((CHUNKS, h, chunk, LANES), low_type),
            dma((2,)),
            dma((2,)),
            dma((2,)),
            pltpu.SemaphoreType.REGULAR,
            dma((2, a)),
            dma((CHUNKS, a)),
            dma((2, b)),
            dma((CHUNKS, b)),
            dma((2, h)),
            dma((CHUNKS, h)),
        ],
        compiler_params=pltpu.CompilerParams(
            collective_id=number, has_side_effects=True, vmem_limit_bytes=60 << 20
        ),
        name="reduce_windows",
    )(grads)


def log_sums(rows, columns, column_ok, logit_scale, matches):
    total, taken = rows.shape[0], min(rows.shape[0], 256)

    def some(args):
        row_part, match_part = args
        logits = logit_scale * back_dot(row_part, columns)
        masked = jnp.where(column_ok[None, :], logits, -1e30)
        row_max = jnp.max(masked, 1, keepdims=True)
        log_total = row_max[:, 0] + jnp.log(jnp.sum(jnp.exp(masked - row_max), 1))
        gap = jnp.where(match_part > 0.0, logits[:, :total] - log_total[:, None], 0.0)
        return log_total, -jnp.sum(gap)

    if taken == total:
        return some((rows, matches))
    logs, parts = lax.map(
        some, (rows.reshape(-1, taken, rows.shape[1]), matches.reshape(-1, taken, total))
    )
    return logs.reshape(-1), jnp.sum(parts)


def side_grads(row_embed, columns, column_ok, same_own, positives_own, log_own, logit_scale, total_count):
    dot_vals = back_dot(row_embed, columns)
    masked = jnp.where(column_ok[None, :], logit_scale * dot_vals, -1e30)
    extra = columns.shape[0] - same_own.shape[1]
    weights_pos = jnp.concatenate(
        [same_own, jnp.zeros((same_own.shape[0], extra), jnp.float32)], 1
    )
    grad_logits = (
        positives_own[:, None] * jnp.exp(masked - log_own[:, None]) - weights_pos
    ) / total_count
    grad_dots = (logit_scale * grad_logits).astype(jnp.bfloat16)
    grad_temper = logit_scale * jnp.sum(grad_logits * dot_vals)
    return fwd_dot(grad_dots, columns), grad_temper


def cross_grads(rows, own, valid_own, same_own, positives_all, logs, logit_scale, total_count):
    logits = logit_scale * back_dot(rows, own)
    masked = jnp.where(valid_own[None, :], logits, -1e30)
    grad_logits = (
        positives_all[:, None] * jnp.exp(masked - logs[:, None]) - same_own.T
    ) / total_count
    grad_dots = (logit_scale * grad_logits).astype(jnp.bfloat16)
    return weight_grad(grad_dots, rows)


def body(
    flat_master,
    flat_first,
    flat_second,
    table,
    table_first,
    table_second,
    pixels,
    token_ids,
    end_pos,
    pair_counts,
    groups,
    cached_image,
    cached_text,
):
    gx_size, gy_size = lax.axis_size("gx"), lax.axis_size("gy")
    device_count = gx_size * gy_size
    my_index = linear_index(gy_size)
    pairs_dev = pixels.shape[0]
    shard = flat_master.shape[0]
    tokens = token_ids.size
    vocab_dev = table.shape[0]
    cap = route_capacity(tokens, gy_size)
    flat_ids = jnp.pad(token_ids.reshape(-1), (0, ID_ROWS * LANES // 2 - tokens)).reshape(-1, LANES)
    payload = [
        place_window(flat_master, gy_size),
        jnp.concatenate([cached_image, cached_text], 0).reshape(CACHED_ROWS, LANES),
        jnp.concatenate([flat_ids // 256, flat_ids % 256], 0).astype(jnp.bfloat16),
    ]
    used = sum(part.shape[0] for part in payload)
    step = GROUP * GATHER_CHUNKS
    payload = jnp.pad(jnp.concatenate(payload, 0), ((0, -used % step), (0, 0)))
    gathered = gather_windows(payload, gx_size, gy_size, 4)
    every_part = gathered.reshape(device_count, -1, LANES)
    cached = every_part[:, used - ID_ROWS - CACHED_ROWS : used - ID_ROWS].reshape(device_count, -1, EMBED)
    cache_img, cache_txt = lax.optimization_barrier((cached[:, :pairs_dev], cached[:, pairs_dev:]))
    cache_img, cache_txt = cache_img.reshape(-1, EMBED), cache_txt.reshape(-1, EMBED)
    coded = every_part[:, used - ID_ROWS : used].astype(jnp.int32)
    ids_all = coded[:, : ID_ROWS // 2] * 256 + coded[:, ID_ROWS // 2 :]
    ids_all = ids_all.reshape(device_count, -1)[:, :tokens]
    holders = ids_all // vocab_dev
    pair_rows = jnp.sum(holders[:, :, None] == jnp.arange(gy_size), 1)
    rounds = (jnp.max(pair_rows) + cap - 1) // cap
    me_y = lax.axis_index("gy")
    held = holders == me_y
    held_rank = jnp.where(held, ranks(held), -1)
    held_row = ids_all - me_y * vocab_dev
    held_count = jnp.sum(held, 1)
    own_holder = lax.dynamic_slice_in_dim(holders, my_index, 1, 0)[0]
    own_flags = jnp.arange(gy_size)[:, None] == own_holder[None, :]
    own_rank = jnp.sum(jnp.where(own_flags, ranks(own_flags), 0), 0)

    def held_rows(turn):
        slots = held_rank - turn * cap
        found = slots[:, None, :] == jnp.arange(cap)[None, :, None]
        return jnp.sum(jnp.where(found, held_row[:, None, :], 0), 2)

    def own_slots(turn):
        rank = own_rank - turn * cap
        return jnp.where((rank >= 0) & (rank < cap), own_holder * cap + rank, -1)

    first_rows = held_rows(0)
    group_start = lax.axis_index("gx") * gy_size

    def rows_to_send(index):
        index = lax.dynamic_slice_in_dim(index, group_start, gy_size, 0)
        return lax.optimization_barrier(jnp.take(table, index.reshape(-1), axis=0)).astype(jnp.bfloat16)

    landed = share_rows(
        rows_to_send(first_rows).reshape(gy_size, cap, D_TXT), gx_size, gy_size, False, 5, "token_rows"
    )
    slot_count = gy_size * cap
    picks = pick_matrix(own_slots(0), slot_count)
    token_rows = weight_grad(picks, landed.reshape(slot_count, D_TXT)).astype(jnp.bfloat16)

    def more_rows(turn, found):
        rows = rows_to_send(held_rows(turn)).reshape(gy_size, cap, D_TXT)
        rows = lax.all_to_all(rows, "gy", 0, 0, tiled=True).reshape(slot_count, D_TXT)
        return found + weight_grad(pick_matrix(own_slots(turn), slot_count), rows).astype(jnp.bfloat16)

    token_rows = lax.fori_loop(1, rounds, more_rows, token_rows)
    spread = spread_weights(gathered, shard, device_count)
    image_weights = dict(zip(IMAGE.names, spread[:5]))
    text_weights = dict(zip(TEXT.names, spread[5:9]))
    image_vec, text_vec, temper = split_vectors(spread[9])
    image_gains, image_base, image_rows = image_inputs(image_vec, pixels)
    text_gains, text_base, text_rows = text_inputs(text_vec, token_rows)
    image_kept = tower_forward(IMAGE, end_pos, image_gains, image_base, image_rows, image_weights)
    text_kept = tower_forward(TEXT, end_pos, text_gains, text_base, text_rows, text_weights)
    image_emb = image_kept[14].astype(jnp.bfloat16)
    text_emb = text_kept[14].astype(jnp.bfloat16)
    (embeds,) = exchange_all(
        [jnp.concatenate([image_emb, text_emb], 0)], gx_size, gy_size, 0, "embeddings"
    )
    all_img, all_txt = lax.optimization_barrier((embeds[:, :pairs_dev], embeds[:, pairs_dev:]))
    all_img, all_txt = all_img.reshape(-1, EMBED), all_txt.reshape(-1, EMBED)
    total_pairs = all_img.shape[0]
    valid_all = jnp.arange(total_pairs) % pairs_dev < jnp.repeat(pair_counts.reshape(-1), pairs_dev)
    matches = (
        (groups[:, None] == groups[None, :]) & valid_all[:, None] & valid_all[None, :]
    ).astype(jnp.float32)
    positives_all = jnp.sum(matches, 1)
    total_count = 2.0 * jnp.sum(positives_all)
    own_start = my_index * pairs_dev
    own_part = functools.partial(
        lax.dynamic_slice_in_dim, start_index=own_start, slice_size=pairs_dev, axis=0
    )
    same_own, positives_own, valid_own = own_part(matches), own_part(positives_all), own_part(valid_all)
    logit_scale = jnp.exp(temper)
    column_ok = jnp.concatenate([valid_all, jnp.ones((cache_img.shape[0],), jnp.bool_)])
    columns_txt = jnp.concatenate([all_txt, cache_txt])
    columns_img = jnp.concatenate([all_img, cache_img])
    log_img, loss_one = log_sums(all_img, columns_txt, column_ok, logit_scale, matches)
    log_txt, loss_two = log_sums(all_txt, columns_img, column_ok, logit_scale, matches)
    loss_sum = loss_one + loss_two
    grad_img, temper_one = side_grads(
        image_emb, columns_txt, column_ok, same_own, positives_own, own_part(log_img), logit_scale, total_count
    )
    grad_txt, temper_two = side_grads(
        text_emb, columns_img, column_ok, same_own, positives_own, own_part(log_txt), logit_scale, total_count
    )
    grad_img = grad_img + cross_grads(
        all_txt, image_emb, valid_own, same_own, positives_all, log_txt, logit_scale, total_count
    )
    grad_txt = grad_txt + cross_grads(
        all_img, text_emb, valid_own, same_own, positives_all, log_img, logit_scale, total_count
    )
    text_grads = tower_backward(TEXT, end_pos, text_gains, grad_txt, text_kept[:14], text_weights)
    grad_rows = text_grads[6][: SEQS * CTX]
    to_holders = fwd_dot(picks, grad_rows).astype(jnp.bfloat16).reshape(gy_size, cap, D_TXT)
    arrived = share_rows(to_holders, gx_size, gy_size, True, 6, "token_grads")
    image_grads = tower_backward(IMAGE, end_pos, image_gains, grad_img, image_kept[:14], image_weights)
    pair_lists = ([(image_rows, image_grads[6])],) + grad_pairs(image_kept, image_grads)
    pair_lists = pair_lists + grad_pairs(text_kept, text_grads)
    table_grad, table_square = table_sum(
        jnp.minimum(held_count, cap),
        first_rows.reshape(-1),
        arrived.reshape(device_count, cap, D_TXT),
        vocab_dev,
    )

    def more_grads(turn, total):
        rows = fwd_dot(pick_matrix(own_slots(turn), slot_count), grad_rows).astype(jnp.bfloat16)
        rows = lax.all_to_all(rows.reshape(gy_size, cap, D_TXT), "gy", 0, 0, tiled=True)
        rows = lax.all_gather(rows, "gx", axis=0).reshape(device_count * cap, D_TXT).astype(jnp.float32)
        taken = jnp.arange(cap)[None, :] < (held_count - turn * cap)[:, None]
        rows = jnp.where(taken.reshape(-1)[:, None], rows, 0.0)
        return total.at[held_rows(turn).reshape(-1)].add(rows)

    table_grad, table_squares = lax.cond(
        rounds > 1,
        lambda total, square: (
            lambda whole: (whole, jnp.sum(whole * whole))
        )(lax.fori_loop(1, rounds, more_grads, total)),
        lambda total, square: (total, jnp.sum(square)),
        table_grad,
        table_square,
    )
    total_rows = window_start(shard, device_count - 1) + window_rows(shard, GROUP * CHUNKS)
    vec_rows = jnp.concatenate(
        [
            image_grads[7][:1].reshape(-1, LANES),
            image_grads[7].reshape(-1, LANES),
            image_grads[8].reshape(-1, LANES),
            text_grads[7].reshape(-1, LANES),
            text_grads[8][2:].reshape(-1, LANES),
            jnp.pad((temper_one + temper_two).reshape(1, 1), ((0, 0), (0, LANES - 1))),
        ]
    )
    vec_rows = jnp.pad(vec_rows, ((0, total_rows - matrix_rows() - vec_rows.shape[0]), (0, 0)))
    local_grads = weight_grads(pair_lists, vec_rows)
    grad_window = reduce_windows(local_grads, shard, gx_size, gy_size, 1)
    grad_shard = lift_window(grad_window, shard, gy_size)
    table_squares = jnp.where(lax.axis_index("gx") == 0, table_squares, 0.0)
    squares = jnp.sum(grad_shard * grad_shard) + table_squares
    (every,) = exchange_all([jnp.full((8, LANES), squares)], gx_size, gy_size, 2, "squares")
    grad_norm = jnp.sqrt(jnp.sum(every[:, 0, 0]))
    factor = jnp.minimum(1.0, clip_limit / (grad_norm + 1e-06))
    matrix_stop = matrix_rows() * LANES
    position = my_index * shard + jnp.arange(shard)
    is_matrix = position < matrix_stop
    rates = jnp.where(is_matrix, rate_matrix, rate_vector)
    decays = jnp.where(is_matrix, decay_rate, 0.0)
    master_out, first_out, second_out = adam_step(
        flat_master, flat_first, flat_second, grad_shard * factor, rates, decays
    )
    table_out, table_first_out, table_second_out = adam_step(
        table, table_first, table_second, table_grad * factor, rate_table, 0.0
    )
    return (
        master_out,
        first_out,
        second_out,
        table_out,
        table_first_out,
        table_second_out,
        loss_sum,
        total_count,
        grad_norm,
    )


def solution(mesh):
    placed = (
        P(("gx", "gy")),
        P(("gx", "gy")),
        P(("gx", "gy")),
        P("gy", None),
        P("gy", None),
        P("gy", None),
        P(("gx", "gy"), None, None),
        P(("gx", "gy"), None),
        P(("gx", "gy")),
        P(),
        P(),
        P(("gx", "gy"), None),
        P(("gx", "gy"), None),
    )
    return jax.shard_map(
        body,
        mesh=mesh,
        in_specs=placed,
        out_specs=(
            P(("gx", "gy")),
            P(("gx", "gy")),
            P(("gx", "gy")),
            P("gy", None),
            P("gy", None),
            P("gy", None),
            P(),
            P(),
            P(),
        ),
        check_vma=False,
    )
```

```python
import functools

import jax
import jax.numpy as jnp
from jax import lax
from jax.experimental import pallas as pl
from jax.experimental.pallas import tpu as pltpu
from jax.sharding import PartitionSpec as P

D_IMG = 768
IMG_HEADS = 12
IMG_MLP = 3072
PATCH_DIM = 3072
D_TXT = 512
TXT_HEADS = 8
TXT_MLP = 2048
CTX = 77
EMBED = 512
STEP = 10
IMG_TOK = 50


clip_limit = 0.1
beta_one = 0.9
beta_two = 0.999
adam_eps = 1e-08
decay_rate = 0.1
rate_matrix = 0.01
rate_vector = 0.2
rate_table = 0.2
norm_eps = 1e-05


def segment_list():
    return [
        ("patch_embed", PATCH_DIM, D_IMG),
        ("image_attn", D_IMG, 4 * D_IMG),
        ("image_up", D_IMG, IMG_MLP),
        ("image_down", IMG_MLP, D_IMG),
        ("image_proj", D_IMG, EMBED),
        ("text_attn", D_TXT, 4 * D_TXT),
        ("text_up", D_TXT, TXT_MLP),
        ("text_down", TXT_MLP, D_TXT),
        ("text_proj", D_TXT, EMBED),
        ("image_vec", IMG_TOK + 9, D_IMG),
        ("text_vec", CTX + 6, D_TXT),
        ("temper", 1, 1),
    ]


LANES = 128
GROUP = 16
CHUNKS = 16
GATHER_CHUNKS = 14
CACHED_ROWS = 64
ID_ROWS = 16
MESH = pl.DeviceIdType.MESH


def dot_nn(left_side, right_side):
    return lax.dot_general(
        left_side, right_side, (((1,), (0,)), ((), ())), preferred_element_type=jnp.float32
    )


def dot_nt(left_side, right_side):
    return lax.dot_general(
        left_side, right_side, (((1,), (1,)), ((), ())), preferred_element_type=jnp.float32
    )


def dot_tn(left_side, right_side):
    return lax.dot_general(
        left_side, right_side, (((0,), (0,)), ((), ())), preferred_element_type=jnp.float32
    )


def back_dot(left_side, right_side):
    return dot_nt(left_side, right_side)


def fwd_dot(left_side, right_side):
    return dot_nn(left_side, right_side)


def weight_grad(left_side, right_side):
    return dot_tn(left_side, right_side)


def norm_parts(values):
    center = values - jnp.mean(values, -1, keepdims=True)
    scale = lax.rsqrt(jnp.mean(center * center, -1, keepdims=True) + norm_eps)
    return center * scale, scale


def layer_norm(values, gain_vec, shift_vec):
    return norm_parts(values)[0] * gain_vec + shift_vec


def layer_norm_back(values, gain_vec, grad):
    unit, scale = norm_parts(values)
    grad_unit = grad * gain_vec
    inner = jnp.mean(grad_unit, -1, keepdims=True)
    along = jnp.mean(grad_unit * unit, -1, keepdims=True)
    return scale * (grad_unit - inner - unit * along), grad * unit


def sum_rows(values):
    return jnp.sum(values, 0, keepdims=True)


def low16(values):
    return jnp.concatenate([values, jnp.zeros_like(values)], 0).astype(jnp.bfloat16)


SEQS = 8


class Tower:
    def __init__(self, image):
        self.image = image
        self.width = D_IMG if image else D_TXT
        self.heads = IMG_HEADS if image else TXT_HEADS
        self.length = IMG_TOK if image else CTX
        self.rows = -(-SEQS * self.length // GROUP) * GROUP
        self.lanes = 16 if image else 8
        self.queries = SEQS * self.lanes
        self.block = 80 if image else 48
        self.names = ("patch", "attn", "up", "down", "proj") if image else ("attn", "up", "down", "proj")

    def shapes(self):
        width = self.width
        found = dict(attn=(width, 4 * width), up=(width, 4 * width), down=(4 * width, width), proj=(width, EMBED))
        if self.image:
            found["patch"] = (PATCH_DIM, width)
        return found

    def head_mask(self):
        lane = lax.broadcasted_iota(jnp.int32, (self.lanes, self.width), 1)
        row = lax.broadcasted_iota(jnp.int32, (self.lanes, self.width), 0)
        return lane // (self.width // self.heads) == row

    def spread_heads(self, values, wide_ref):
        mask = self.head_mask()
        for s in range(SEQS):
            row = jnp.broadcast_to(values[s : s + 1].astype(jnp.float32), mask.shape)
            wide_ref[s * self.lanes : (s + 1) * self.lanes, :] = jnp.where(mask, row, 0.0)
        return wide_ref[...].astype(jnp.bfloat16)

    def join_heads(self, values, wide_ref):
        mask = self.head_mask()
        wide_ref[...] = values
        rows = [
            sum_rows(jnp.where(mask, wide_ref[s * self.lanes : (s + 1) * self.lanes, :], 0.0))
            for s in range(SEQS)
        ]
        return jnp.concatenate(rows, 0)

    def row_of(self, s, ends_ref):
        return s * self.length + (0 if self.image else ends_ref[s])

    def each_block(self, function, start):
        return lax.fori_loop(
            0,
            self.rows // self.block,
            lambda i, carry: function(pl.ds(pl.multiple_of(i * self.block, GROUP), self.block), carry),
            start,
        )


def tower_fetch(names, sources, landed, sems):
    copies = {
        name: pltpu.make_async_copy(source, ref, sems.at[i])
        for i, (name, source, ref) in enumerate(zip(names, sources, landed))
    }
    for copy in copies.values():
        copy.start()
    return copies, dict(zip(names, landed))


def tower_forward_kernel(tower, *refs):
    count = len(tower.names)
    ends_ref, gains_ref, base_ref, input_ref = refs[:4]
    sources = refs[4 : 4 + count]
    (tokens_ref, normed_ref, pair_ref, normed_own_ref, query_ref, probs_ref, attended_ref, middle_ref, normed_two_ref,
     upper_ref, act_ref, output_ref, head_ref, raw_ref, emb_ref) = refs[4 + count : 19 + count]
    hidden_ref, wide_ref = refs[19 + count : 21 + count]
    landed, sems = refs[21 + count : 21 + 2 * count], refs[21 + 2 * count]
    copies, weights = tower_fetch(tower.names, sources, landed, sems)
    width = tower.width
    gains = [gains_ref[i : i + 1, :] for i in range(8)]
    if tower.image:
        copies["patch"].wait()

        def patch(j, carry):
            cols = pl.ds(pl.multiple_of(j * 256, 256), 256)
            tokens_ref[:, cols] = dot_nn(input_ref[...], weights["patch"][:, cols]) + base_ref[:, cols]
            return carry

        lax.fori_loop(0, width // 256, patch, 0)

    def first(rows, carry):
        if tower.image:
            hidden = layer_norm(tokens_ref[rows, :], gains[0], gains[1])
        else:
            hidden = input_ref[rows, :].astype(jnp.float32) + base_ref[rows, :]
            tokens_ref[rows, :] = hidden
        hidden_ref[rows, :] = hidden
        normed_ref[rows, :] = layer_norm(hidden, gains[2], gains[3]).astype(jnp.bfloat16)
        return carry

    tower.each_block(first, 0)
    copies["attn"].wait()

    def pair(j, carry):
        at = pl.multiple_of(j * 256, 256)
        product = dot_nn(normed_ref[...], weights["attn"][:, pl.ds(width + at, 256)])
        pair_ref[:, pl.ds(at, 256)] = product.astype(jnp.bfloat16)
        return carry

    lax.fori_loop(0, 2 * width // 256, pair, 0)
    hidden_own = jnp.concatenate(
        [hidden_ref[pl.ds(tower.row_of(s, ends_ref), 1), :] for s in range(SEQS)], 0
    )
    normed_own = low16(layer_norm(hidden_own, gains[2], gains[3]))
    normed_own_ref[...] = normed_own
    query = dot_nn(normed_own, weights["attn"][:, :width]).astype(jnp.bfloat16)
    query_ref[...] = query
    queries = tower.spread_heads(query, wide_ref)
    scores = dot_nt(queries, pair_ref[:, :width]) * (width // tower.heads) ** (-0.5)
    row = lax.broadcasted_iota(jnp.int32, scores.shape, 0) // tower.lanes
    spot = lax.broadcasted_iota(jnp.int32, scores.shape, 1) - row * tower.length
    last = jnp.full(scores.shape, tower.length - 1, jnp.int32)
    if not tower.image:
        for s in range(SEQS):
            last = jnp.where(row == s, ends_ref[s], last)
    scores = jnp.where((spot >= 0) & (spot <= last), scores, -1e30)
    powers = jnp.exp(scores - jnp.max(scores, -1, keepdims=True))
    probs = powers / jnp.sum(powers, -1, keepdims=True)
    probs_ref[...] = probs
    attended = low16(tower.join_heads(dot_nn(probs.astype(jnp.bfloat16), pair_ref[:, width:]), wide_ref))
    attended_ref[...] = attended
    middle = hidden_own + dot_nn(attended, weights["attn"][:, 3 * width :])[:SEQS]
    middle_ref[...] = middle
    normed_two_ref[...] = low16(layer_norm(middle, gains[4], gains[5]))
    copies["up"].wait()

    def rise(j, carry):
        cols = pl.ds(pl.multiple_of(j * 512, 512), 512)
        upper = dot_nn(normed_two_ref[...], weights["up"][:, cols])[:SEQS]
        upper_ref[:, cols] = upper
        act_ref[:, cols] = low16(upper * jax.nn.sigmoid(1.702 * upper))
        return carry

    lax.fori_loop(0, 4 * width // 512, rise, 0)
    copies["down"].wait()

    def fall(j, carry):
        cols = pl.ds(pl.multiple_of(j * 256, 256), 256)
        output_ref[:, cols] = middle_ref[:, cols] + dot_nn(act_ref[...], weights["down"][:, cols])[:SEQS]
        return carry

    lax.fori_loop(0, width // 256, fall, 0)
    head_in = low16(layer_norm(output_ref[...], gains[6], gains[7]))
    head_ref[...] = head_in
    copies["proj"].wait()
    raw = dot_nn(head_in, weights["proj"][...])[:SEQS]
    raw_ref[...] = raw
    emb_ref[...] = raw * lax.rsqrt(jnp.sum(raw * raw, -1, keepdims=True) + 1e-06)


def tower_forward(tower, ends, gains, base, inputs, weights):
    width, rows = tower.width, tower.rows
    low, full = jnp.bfloat16, jnp.float32
    outs = [
        ((rows, width), full),
        ((rows, width), low),
        ((rows, 2 * width), low),
        ((GROUP, width), low),
        ((GROUP, width), low),
        ((tower.queries, rows), full),
        ((GROUP, width), low),
        ((SEQS, width), full),
        ((GROUP, width), low),
        ((SEQS, 4 * width), full),
        ((GROUP, 4 * width), low),
        ((SEQS, width), full),
        ((GROUP, width), low),
        ((SEQS, EMBED), full),
        ((SEQS, EMBED), full),
    ]
    vmem = pl.BlockSpec(memory_space=pltpu.VMEM)
    shapes = tower.shapes()
    return pl.pallas_call(
        functools.partial(tower_forward_kernel, tower),
        out_shape=[jax.ShapeDtypeStruct(shape, kind) for shape, kind in outs],
        in_specs=[pl.BlockSpec(memory_space=pltpu.SMEM)]
        + [vmem] * 3
        + [pl.BlockSpec(memory_space=pl.ANY)] * len(tower.names),
        out_specs=[vmem] * len(outs),
        scratch_shapes=[pltpu.VMEM((rows, width), full), pltpu.VMEM((tower.queries, width), full)]
        + [pltpu.VMEM(shapes[name], low) for name in tower.names]
        + [pltpu.SemaphoreType.DMA((len(tower.names),))],
        compiler_params=pltpu.CompilerParams(vmem_limit_bytes=58 << 20),
        name="image_forward" if tower.image else "text_forward",
    )(ends, gains, base, inputs, *[weights[name] for name in tower.names])


def tower_backward_kernel(tower, *refs):
    names = tower.names[-4:]
    count = len(names)
    ends_ref, gains_ref, grad_ref = refs[:3]
    (tokens_ref, normed_ref, pair_ref, normed_own_ref, query_ref, probs_ref, attended_ref, middle_ref, normed_two_ref,
     upper_ref, act_ref, output_ref, head_ref, raw_ref) = refs[3:17]
    sources = refs[17 : 17 + count]
    (grad_raw_ref, grad_mlp_ref, grad_upper_ref, grad_att_ref, grad_query_ref, grad_pair_ref, grad_rows_ref,
     places_ref, gain_grads_ref) = refs[17 + count : 26 + count]
    grad_ref_wide, wide_ref, grad_middle_ref = refs[26 + count : 29 + count]
    landed, sems = refs[29 + count : 29 + 2 * count], refs[29 + 2 * count]
    copies, weights = tower_fetch(names, sources, landed, sems)
    width, rows = tower.width, tower.rows
    scale = (width // tower.heads) ** (-0.5)
    gains = [gains_ref[i : i + 1, :] for i in range(8)]
    raw, grad_emb = raw_ref[...], grad_ref[...]
    norm = lax.rsqrt(jnp.sum(raw * raw, -1, keepdims=True) + 1e-06)
    along = jnp.sum(raw * grad_emb, -1, keepdims=True)
    grad_raw = low16(grad_emb * norm - raw * (norm * norm * norm * along))
    grad_raw_ref[...] = grad_raw
    copies["proj"].wait()
    grad_head = dot_nt(grad_raw, weights["proj"][...])[:SEQS]
    grad_out, gain_part = layer_norm_back(output_ref[...], gains[6], grad_head)
    gain_grads_ref[6:7, :] = sum_rows(gain_part)
    gain_grads_ref[7:8, :] = sum_rows(grad_head)
    grad_mlp_ref[...] = low16(grad_out)
    copies["down"].wait()

    def rise(j, carry):
        cols = pl.ds(pl.multiple_of(j * 512, 512), 512)
        grad_act = dot_nt(grad_mlp_ref[...], weights["down"][cols, :])[:SEQS]
        upper = upper_ref[:, cols]
        sig = jax.nn.sigmoid(1.702 * upper)
        grad_upper_ref[:, cols] = low16(grad_act * (sig + upper * (1.702 * (sig * (1.0 - sig)))))
        return carry

    lax.fori_loop(0, 4 * width // 512, rise, 0)
    copies["up"].wait()

    def fall(j, carry):
        cols = pl.ds(pl.multiple_of(j * 256, 256), 256)
        grad_middle_ref[:, cols] = dot_nt(grad_upper_ref[...], weights["up"][cols, :])[:SEQS]
        return carry

    lax.fori_loop(0, width // 256, fall, 0)
    grad_norm_two = grad_middle_ref[...]
    grad_mid, gain_part = layer_norm_back(middle_ref[...], gains[4], grad_norm_two)
    gain_grads_ref[4:5, :] = sum_rows(gain_part)
    gain_grads_ref[5:6, :] = sum_rows(grad_norm_two)
    grad_middle = grad_out + grad_mid
    grad_middle_ref[...] = grad_middle
    grad_att = low16(grad_middle)
    grad_att_ref[...] = grad_att
    copies["attn"].wait()
    grad_attended = dot_nt(grad_att, weights["attn"][:, 3 * width :]).astype(jnp.bfloat16)
    grads_heads = tower.spread_heads(grad_attended, wide_ref)
    queries = tower.spread_heads(query_ref[...], wide_ref)
    probs = probs_ref[...]
    grad_probs = dot_nt(grads_heads, pair_ref[:, width:])
    grad_scores = probs * (grad_probs - jnp.sum(grad_probs * probs, -1, keepdims=True))
    grad_scores = grad_scores.astype(jnp.bfloat16)
    grad_query = low16(tower.join_heads(dot_nn(grad_scores, pair_ref[:, :width]), wide_ref) * scale)
    grad_query_ref[...] = grad_query
    grad_pair_ref[:, :width] = (dot_tn(grad_scores, queries) * scale).astype(jnp.bfloat16)
    grad_pair_ref[:, width:] = dot_tn(probs.astype(jnp.bfloat16), grads_heads).astype(jnp.bfloat16)

    def inner(j, carry):
        at = pl.multiple_of(j * 256, 256)
        grad_ref_wide[:, pl.ds(at, 256)] = dot_nt(
            grad_pair_ref[...], weights["attn"][pl.ds(at, 256), width : 3 * width]
        )
        return carry

    lax.fori_loop(0, width // 256, inner, 0)
    grad_own = dot_nt(grad_query, weights["attn"][:, :width])
    for s in range(SEQS):
        grad_ref_wide[pl.ds(tower.row_of(s, ends_ref), 1), :] += grad_own[s : s + 1]

    def first(at, carry):
        grad = grad_ref_wide[at, :]
        hidden = tokens_ref[at, :]
        if tower.image:
            hidden = layer_norm(hidden, gains[0], gains[1])
        grad_in, gain_part = layer_norm_back(hidden, gains[2], grad)
        grad_ref_wide[at, :] = grad_in
        return carry[0] + sum_rows(gain_part), carry[1] + sum_rows(grad)

    nothing = jnp.zeros((1, width), jnp.float32)
    gain_one, shift_one = tower.each_block(first, (nothing, nothing))
    gain_grads_ref[2:3, :] = gain_one
    gain_grads_ref[3:4, :] = shift_one
    for s in range(SEQS):
        grad_ref_wide[pl.ds(tower.row_of(s, ends_ref), 1), :] += grad_middle_ref[s : s + 1, :]

    def second(at, carry):
        grad = grad_ref_wide[at, :]
        if not tower.image:
            grad_rows_ref[at, :] = grad.astype(jnp.bfloat16)
            return carry
        grad_in, gain_part = layer_norm_back(tokens_ref[at, :], gains[0], grad)
        grad_ref_wide[at, :] = grad_in
        grad_rows_ref[at, :] = grad_in.astype(jnp.bfloat16)
        return carry[0] + sum_rows(gain_part), carry[1] + sum_rows(grad)

    gain_pre, shift_pre = tower.each_block(second, (nothing, nothing))
    gain_grads_ref[0:1, :] = gain_pre
    gain_grads_ref[1:2, :] = shift_pre
    places = grad_ref_wide[0 : tower.length, :]
    for s in range(1, SEQS):
        places = places + grad_ref_wide[s * tower.length : (s + 1) * tower.length, :]
    places_ref[...] = places


def tower_backward(tower, ends, gains, grad_emb, kept, weights):
    width, rows = tower.width, tower.rows
    low, full = jnp.bfloat16, jnp.float32
    outs = [
        ((GROUP, EMBED), low),
        ((GROUP, width), low),
        ((GROUP, 4 * width), low),
        ((GROUP, width), low),
        ((GROUP, width), low),
        ((rows, 2 * width), low),
        ((rows, width), low),
        ((tower.length, width), full),
        ((8, width), full),
    ]
    vmem = pl.BlockSpec(memory_space=pltpu.VMEM)
    shapes, names = tower.shapes(), tower.names[-4:]
    return pl.pallas_call(
        functools.partial(tower_backward_kernel, tower),
        out_shape=[jax.ShapeDtypeStruct(shape, kind) for shape, kind in outs],
        in_specs=[pl.BlockSpec(memory_space=pltpu.SMEM)]
        + [vmem] * (2 + len(kept))
        + [pl.BlockSpec(memory_space=pl.ANY)] * len(names),
        out_specs=[vmem] * len(outs),
        scratch_shapes=[
            pltpu.VMEM((rows, width), full),
            pltpu.VMEM((tower.queries, width), full),
            pltpu.VMEM((SEQS, width), full),
        ]
        + [pltpu.VMEM(shapes[name], low) for name in names]
        + [pltpu.SemaphoreType.DMA((len(names),))],
        compiler_params=pltpu.CompilerParams(vmem_limit_bytes=58 << 20),
        name="image_backward" if tower.image else "text_backward",
    )(ends, gains, grad_emb, *kept, *[weights[name] for name in names])


def grad_pairs(kept, grads):
    (normed, normed_own, attended, normed_two, act_low, head_in) = (
        kept[1], kept[3], kept[6], kept[8], kept[10], kept[12]
    )
    grad_raw, grad_mlp, grad_upper, grad_att, grad_query, grad_pair = grads[:6]
    return (
        [(normed_own, grad_query), (normed, grad_pair), (attended, grad_att)],
        [(normed_two, grad_upper)],
        [(act_low, grad_mlp)],
        [(head_in, grad_raw)],
    )


def image_inputs(image_vec, pixels):
    pixels = jnp.pad(pixels, ((0, 0), (1, 0), (0, 0))).reshape(-1, PATCH_DIM)
    base = image_vec[1 : IMG_TOK + 1] + jnp.pad(image_vec[:1], ((0, IMG_TOK - 1), (0, 0)))
    return image_vec[IMG_TOK + 1 :], jnp.tile(base, (SEQS, 1)), pixels


def text_inputs(text_vec, token_rows):
    gains = jnp.pad(text_vec[CTX:], ((2, 0), (0, 0)))
    extra = TEXT.rows - SEQS * CTX
    base = jnp.pad(jnp.tile(text_vec[:CTX], (SEQS, 1)), ((0, extra), (0, 0)))
    return gains, base, jnp.pad(token_rows, ((0, extra), (0, 0)))


def adam_step(weight, first, second, grad, rate, decay):
    first = beta_one * first + (1.0 - beta_one) * grad
    second = beta_two * second + (1.0 - beta_two) * grad * grad
    first_hat = first / (1.0 - beta_one**STEP)
    second_hat = second / (1.0 - beta_two**STEP)
    weight = weight - rate * (first_hat / (jnp.sqrt(second_hat) + adam_eps) + decay * weight)
    return (weight, first, second)


IMAGE, TEXT = Tower(True), Tower(False)


def matrix_rows():
    return sum(seg_rows * seg_cols for seg_name, seg_rows, seg_cols in segment_list()[:9]) // LANES


def window_rows(shard, step=GROUP):
    need = -(-(GROUP * LANES - 1 + shard) // LANES)
    return -(-need // step) * step


def window_start(shard, index):
    return (shard * index // (GROUP * LANES)) * GROUP


def linear_index(gy_size):
    return lax.axis_index("gx") * gy_size + lax.axis_index("gy")


def place_kernel(shard, gy_size, flat_ref, out_ref, rolled):
    rows = flat_ref.shape[0]
    offset = lax.rem(shard * linear_index(gy_size), GROUP * LANES)
    down, right = offset // LANES, lax.rem(offset, LANES)
    pad = 2 * GROUP
    rolled[0:pad, :] = jnp.zeros((pad, LANES), jnp.float32)
    parts = 5 if rows % (5 * GROUP) == 0 else 1
    step = rows // parts

    def roll_rows(i, carry):
        at = pl.multiple_of(i * step, GROUP)
        rolled[pl.ds(pad + at, step), :] = pltpu.roll(flat_ref[pl.ds(at, step), :], right, 1)
        return carry

    lax.fori_loop(0, parts, roll_rows, 0)
    lane = lax.broadcasted_iota(jnp.int32, (step, LANES), 1)

    def put_rows(i, carry):
        at = pl.multiple_of(i * step, GROUP)
        upper = rolled[pl.ds(pad + at - down - 1, step), :]
        lower = rolled[pl.ds(pad + at - down, step), :]
        out_ref[pl.ds(at, step), :] = jnp.where(lane < right, upper, lower).astype(jnp.bfloat16)
        return carry

    lax.fori_loop(0, parts, put_rows, 0)


def place_window(flat, gy_size):
    shard = flat.shape[0]
    rows = window_rows(shard)
    padded = jnp.pad(flat, (0, rows * LANES - shard)).reshape(rows, LANES)
    return pl.pallas_call(
        functools.partial(place_kernel, shard, gy_size),
        out_shape=jax.ShapeDtypeStruct((rows, LANES), jnp.bfloat16),
        in_specs=[pl.BlockSpec(memory_space=pltpu.VMEM)],
        out_specs=pl.BlockSpec(memory_space=pltpu.VMEM),
        scratch_shapes=[pltpu.VMEM((rows + 2 * GROUP, LANES), jnp.float32)],
        compiler_params=pltpu.CompilerParams(vmem_limit_bytes=32 << 20),
        name="place_window",
    )(padded)


def lift_kernel(shard, gy_size, window_ref, out_ref, rolled):
    rows = window_ref.shape[0]
    offset = lax.rem(shard * linear_index(gy_size), GROUP * LANES)
    up, left = offset // LANES, lax.rem(offset, LANES)
    pad = 2 * GROUP
    step = rows // CHUNKS
    rolled[rows:, :] = jnp.zeros((pad, LANES), jnp.float32)

    def roll_rows(i, carry):
        at = pl.multiple_of(i * step, GROUP)
        rolled[pl.ds(at, step), :] = pltpu.roll(
            window_ref[pl.ds(at, step), :], lax.rem(LANES - left, LANES), 1
        )
        return carry

    lax.fori_loop(0, CHUNKS, roll_rows, 0)
    lane = lax.broadcasted_iota(jnp.int32, (step, LANES), 1)

    def put_rows(i, carry):
        at = pl.multiple_of(i * step, GROUP)
        first = rolled[pl.ds(at + up, step), :]
        second = rolled[pl.ds(at + up + 1, step), :]
        out_ref[pl.ds(at, step), :] = jnp.where(lane < LANES - left, first, second)
        return carry

    lax.fori_loop(0, CHUNKS, put_rows, 0)


def lift_window(window, shard, gy_size):
    rows = window.shape[0]
    lifted = pl.pallas_call(
        functools.partial(lift_kernel, shard, gy_size),
        out_shape=jax.ShapeDtypeStruct((rows, LANES), jnp.float32),
        in_specs=[pl.BlockSpec(memory_space=pltpu.VMEM)],
        out_specs=pl.BlockSpec(memory_space=pltpu.VMEM),
        scratch_shapes=[pltpu.VMEM((rows + 2 * GROUP, LANES), jnp.float32)],
        compiler_params=pltpu.CompilerParams(vmem_limit_bytes=32 << 20),
        name="lift_window",
    )(window)
    return lifted.reshape(-1)[:shard]


def spread_steps():
    steps = []
    base = 0
    for number, (seg_name, seg_rows, seg_cols) in enumerate(segment_list()[:9]):
        wide = seg_cols // LANES
        take = seg_rows
        while take * wide > 4608:
            take //= 2
        for start in range(0, seg_rows, take):
            steps.append((number, start, take, seg_cols, base + start * wide))
        base += seg_rows * wide
    return steps


def window_pieces(shard, count, stride, first, length):
    pieces, shared = [], []
    for index in range(count):
        low = window_start(shard, index)
        high = window_start(shard, index + 1) if index + 1 < count else low + window_rows(shard)
        start, stop = max(low, first), min(high, first + length)
        if start < stop:
            pieces.append((index * stride + start - low, start - first, stop - start))
        if index + 1 < count and first <= high < first + length:
            shared.append((index * stride + high - low, high - first))
    return pieces, shared


def spread_kernel(shard, count, vec_rows, gathered_ref, *refs):
    outs, vec_ref = refs[:9], refs[9]
    landed, edges, wide_rows, ready, in_sem, out_sem = refs[10:]
    rows = gathered_ref.shape[0] // count
    steps = spread_steps()
    steps.append((9, 0, vec_rows, LANES, matrix_rows()))

    def copies_in(number):
        seg, start, take, cols, base = steps[number]
        slot = number % 2
        pieces, shared = window_pieces(shard, count, rows, base, take * cols // LANES)
        found = [
            pltpu.make_async_copy(
                gathered_ref.at[pl.ds(src, size)], landed.at[slot, pl.ds(dst, size)], in_sem.at[slot]
            )
            for src, dst, size in pieces
        ]
        found += [
            pltpu.make_async_copy(
                gathered_ref.at[pl.ds(src, GROUP)], edges.at[slot, order], in_sem.at[slot]
            )
            for order, (src, dst) in enumerate(shared)
        ]
        return found, shared

    def copy_out(number):
        seg, start, take, cols, base = steps[number]
        slot = number % 2
        if seg == 9:
            return pltpu.make_async_copy(wide_rows.at[pl.ds(0, take)], vec_ref, out_sem.at[slot])
        return pltpu.make_async_copy(
            ready[cols].at[slot, pl.ds(0, take)], outs[seg].at[pl.ds(start, take)], out_sem.at[slot]
        )

    for copy in copies_in(0)[0]:
        copy.start()
    for number, (seg, start, take, cols, base) in enumerate(steps):
        slot = number % 2
        wide = cols // LANES
        total = take * wide
        if number + 1 < len(steps):
            for copy in copies_in(number + 1)[0]:
                copy.start()
        found, shared = copies_in(number)
        for copy in found:
            copy.wait()
        if number >= 2:
            copy_out(number - 2).wait()
        block = 256 if total % 256 == 0 else GROUP

        def widen(i, carry, slot=slot, block=block):
            at = pl.multiple_of(i * block, GROUP)
            wide_rows[pl.ds(at, block), :] = landed[slot, pl.ds(at, block), :].astype(jnp.float32)
            return carry

        lax.fori_loop(0, total // block, widen, 0)
        for order, (src, dst) in enumerate(shared):
            wide_rows[dst : dst + GROUP, :] += edges[slot, order].astype(jnp.float32)
        if seg < 9:

            def tile(i, carry, slot=slot, wide=wide, cols=cols):
                at = pl.multiple_of(i * GROUP, GROUP)
                for j in range(wide):
                    ready[cols][slot, pl.ds(at, GROUP), j * LANES : (j + 1) * LANES] = wide_rows[
                        pl.ds(at * wide + j, GROUP, stride=wide), :
                    ].astype(jnp.bfloat16)
                return carry

            lax.fori_loop(0, take // GROUP, tile, 0)
        copy_out(number).start()
    copy_out(len(steps) - 2).wait()
    copy_out(len(steps) - 1).wait()


def spread_entry(shard, count, vec_rows, gathered_ref, *refs):
    outs = refs[:10]
    landed, edges, wide_rows, ready_a, ready_b, ready_c, ready_d, in_sem, out_sem = refs[10:]
    ready = {D_IMG: ready_a, 4 * D_IMG: ready_b, D_TXT: ready_c, 4 * D_TXT: ready_d}
    spread_kernel(
        shard, count, vec_rows, gathered_ref, *outs, landed, edges, wide_rows, ready, in_sem, out_sem
    )


def spread_weights(gathered, shard, count):
    rows = gathered.shape[0] // count
    steps = spread_steps()
    tallest = {}
    for seg, start, take, cols, base in steps:
        tallest[cols] = max(tallest.get(cols, 0), take)
    most = max(take * cols // LANES for seg, start, take, cols, base in steps)
    vec_rows = -(-(sum(r * c for name, r, c in segment_list()[9:])) // (LANES * GROUP)) * GROUP
    edge_count = max(
        len(window_pieces(shard, count, rows, base, take * cols // LANES)[1])
        for seg, start, take, cols, base in steps
    )
    ready = [
        pltpu.VMEM((2, tallest[cols], cols), jnp.bfloat16)
        for cols in (D_IMG, 4 * D_IMG, D_TXT, 4 * D_TXT)
    ]
    return pl.pallas_call(
        functools.partial(spread_entry, shard, count, vec_rows),
        out_shape=[
            jax.ShapeDtypeStruct((seg_rows, seg_cols), jnp.bfloat16)
            for seg_name, seg_rows, seg_cols in segment_list()[:9]
        ]
        + [jax.ShapeDtypeStruct((vec_rows, LANES), jnp.float32)],
        in_specs=[pl.BlockSpec(memory_space=pl.ANY)],
        out_specs=[pl.BlockSpec(memory_space=pl.ANY)] * 10,
        scratch_shapes=[
            pltpu.VMEM((2, most, LANES), jnp.bfloat16),
            pltpu.VMEM((2, edge_count + 1, GROUP, LANES), jnp.bfloat16),
            pltpu.VMEM((most, LANES), jnp.float32),
        ]
        + ready
        + [pltpu.SemaphoreType.DMA((2,)), pltpu.SemaphoreType.DMA((2,))],
        compiler_params=pltpu.CompilerParams(vmem_limit_bytes=48 << 20),
        name="spread_weights",
    )(gathered)


def split_vectors(vec_rows):
    image_count, text_count = (IMG_TOK + 9) * D_IMG // LANES, (CTX + 6) * D_TXT // LANES
    image_vec = vec_rows[:image_count].reshape(IMG_TOK + 9, D_IMG)
    text_vec = vec_rows[image_count : image_count + text_count].reshape(CTX + 6, D_TXT)
    return image_vec, text_vec, vec_rows[image_count + text_count, 0]


def grads_kernel(parts, total_rows, *refs):
    operand_count = sum(2 * len(pairs) for seg_rows, seg_cols, take, pairs in parts)
    operands = refs[:operand_count]
    vec_ref, out_ref, flat_rows, vec_sem, out_sem = refs[operand_count:]
    tail = pltpu.make_async_copy(vec_ref, out_ref.at[pl.ds(matrix_rows(), vec_ref.shape[0])], vec_sem)
    tail.start()
    base = 0
    steps_before = 0
    for seg_rows, seg_cols, take, pairs in parts:
        wide = seg_cols // LANES
        size = take * wide
        count = seg_rows // take

        def step(i, carry, base=base, before=steps_before, size=size, take=take, wide=wide, pairs=pairs):
            slot = lax.rem(i + before, 2)

            def written(number):
                at = pl.multiple_of(base + number * size, 8)
                return pltpu.make_async_copy(
                    flat_rows.at[slot, pl.ds(0, size)], out_ref.at[pl.ds(at, size)], out_sem.at[slot]
                )

            @pl.when(i >= 2)
            def _():
                written(i - 2).wait()

            for left_number, right_number, first in pairs:
                left_ref, right_ref = operands[left_number], operands[right_number]
                at = pl.multiple_of(i * take, LANES)
                product = lax.dot_general(
                    left_ref[:, pl.ds(at, take)],
                    right_ref[...],
                    (((0,), (0,)), ((), ())),
                    preferred_element_type=jnp.float32,
                )
                for j in range(right_ref.shape[1] // LANES):
                    flat_rows[slot, pl.ds(first + j, take, stride=wide), :] = product[
                        :, j * LANES : (j + 1) * LANES
                    ]
            written(i).start()
            return carry

        lax.fori_loop(0, count, step, 0)
        for number in range(max(count - 2, 0), count):
            slot = (number + steps_before) % 2
            at = base + number * size
            pltpu.make_async_copy(
                flat_rows.at[slot, pl.ds(0, size)], out_ref.at[pl.ds(at, size)], out_sem.at[slot]
            ).wait()
        base += seg_rows * wide
        steps_before += count
    tail.wait()


def weight_grads(pair_lists, vec_rows):
    operands, parts = [], []
    for (seg_name, seg_rows, seg_cols), pairs in zip(segment_list()[:9], pair_lists):
        numbered, first = [], 0
        for left_side, right_side in pairs:
            numbered.append((len(operands), len(operands) + 1, first))
            for side in (left_side, right_side):
                side = side.reshape(-1, side.shape[-1])
                operands.append(jnp.pad(side, ((0, -side.shape[0] % GROUP), (0, 0))))
            first += right_side.shape[-1] // LANES
        parts.append((seg_rows, seg_cols, min(seg_rows, 256 if seg_cols <= 768 else 128), numbered))
    total_rows = matrix_rows() + vec_rows.shape[0]
    most = max(take * seg_cols // LANES for seg_rows, seg_cols, take, pairs in parts)
    return pl.pallas_call(
        functools.partial(grads_kernel, parts, total_rows),
        out_shape=jax.ShapeDtypeStruct((total_rows, LANES), jnp.float32),
        in_specs=[pl.BlockSpec(memory_space=pltpu.VMEM)] * (len(operands) + 1),
        out_specs=pl.BlockSpec(memory_space=pl.ANY),
        scratch_shapes=[
            pltpu.VMEM((2, most, LANES), jnp.float32),
            pltpu.SemaphoreType.DMA,
            pltpu.SemaphoreType.DMA((2,)),
        ],
        compiler_params=pltpu.CompilerParams(vmem_limit_bytes=56 << 20),
        name="weight_grads",
    )(*operands, vec_rows)


def exchange_kernel(gx_size, gy_size, many, *refs):
    blocks, outs = refs[:many], refs[many : 2 * many]
    send_sem, recv_sem, own_sem = refs[2 * many :]
    count = gx_size * gy_size
    me = linear_index(gy_size)
    barrier = pltpu.get_barrier_semaphore()

    def device(step):
        other = lax.rem(me + step, count)
        return (other // gy_size, lax.rem(other, gy_size))

    def greet(step, carry):
        pl.semaphore_signal(barrier, inc=1, device_id=device(step), device_id_type=MESH)
        return carry

    lax.fori_loop(1, count, greet, 0)
    own = [
        pltpu.make_async_copy(block, out.at[me], own_sem.at[i])
        for i, (block, out) in enumerate(zip(blocks, outs))
    ]
    for copy in own:
        copy.start()
    pl.semaphore_wait(barrier, count - 1)

    def send(step, carry):
        for i, (block, out) in enumerate(zip(blocks, outs)):
            pltpu.make_async_remote_copy(
                src_ref=block,
                dst_ref=out.at[me],
                send_sem=send_sem.at[i],
                recv_sem=recv_sem.at[i],
                device_id=device(step),
                device_id_type=MESH,
            ).start()
        return carry

    lax.fori_loop(1, count, send, 0)
    for i, out in enumerate(outs):
        own[i].wait()
        others = out.at[pl.ds(0, count - 1)]
        both = pltpu.make_async_remote_copy(
            src_ref=others,
            dst_ref=others,
            send_sem=send_sem.at[i],
            recv_sem=recv_sem.at[i],
            device_id=device(1),
            device_id_type=MESH,
        )
        both.wait_send()
        both.wait_recv()


def exchange_all(blocks, gx_size, gy_size, number, name):
    count, many = gx_size * gy_size, len(blocks)
    return pl.pallas_call(
        functools.partial(exchange_kernel, gx_size, gy_size, many),
        out_shape=[jax.ShapeDtypeStruct((count,) + block.shape, block.dtype) for block in blocks],
        in_specs=[pl.BlockSpec(memory_space=pltpu.VMEM)] * many,
        out_specs=[pl.BlockSpec(memory_space=pltpu.VMEM)] * many,
        scratch_shapes=[pltpu.SemaphoreType.DMA((many,))] * 3,
        compiler_params=pltpu.CompilerParams(
            collective_id=number, has_side_effects=True, vmem_limit_bytes=32 << 20
        ),
        name=name,
    )(*blocks)


class Places:
    def __init__(self, sizes):
        self.x_size, self.low_size, self.high_size = sizes
        self.mixed = self.x_size == self.low_size
        self.gy_size = self.high_size * self.low_size
        gx, gy = lax.axis_index("gx"), lax.axis_index("gy")
        self.core, x = lax.rem(gx, 2), gx // 2
        self.h, low = gy // self.low_size, lax.rem(gy, self.low_size)
        self.a, self.b = self.turned(self.core, x, low)
        self.a_size, self.b_size = self.x_size, self.low_size

    def turned(self, side, a, b):
        if not self.mixed:
            return a, b
        return a * (1 - side) + b * side, b * (1 - side) + a * side

    def device(self, side, a, b, h):
        dev_x, dev_low = self.turned(side, a, b)
        return (dev_x * 2 + side, h * self.low_size + dev_low)

    def linear(self, side, a, b, h):
        gx, gy = self.device(side, a, b, h)
        return gx * self.gy_size + gy

    def sibling(self):
        a, b = (self.b, self.a) if self.mixed else (self.a, self.b)
        return self.device(1 - self.core, a, b, self.h)

    def along_a(self):
        return [
            self.device(self.core, lax.rem(self.a + d, self.a_size), self.b, self.h)
            for d in range(1, self.a_size)
        ]

    def along_b(self):
        return [
            self.device(self.core, self.a, lax.rem(self.b + d, self.b_size), self.h)
            for d in range(1, self.b_size)
        ]

    def along_h(self):
        return [
            self.device(self.core, self.a, self.b, lax.rem(self.h + d, self.high_size))
            for d in range(1, self.high_size)
        ]


def greet_all(others):
    barrier = pltpu.get_barrier_semaphore()
    for other in others:
        pl.semaphore_signal(barrier, inc=1, device_id=other, device_id_type=MESH)
    pl.semaphore_wait(barrier, len(others))


def remote(src, dst, send_sem, recv_sem, other):
    return pltpu.make_async_remote_copy(
        src_ref=src, dst_ref=dst, send_sem=send_sem, recv_sem=recv_sem, device_id=other, device_id_type=MESH
    )


def axis_sizes(gx_size, gy_size):
    return gx_size // 2, gy_size // 4, 4


NO_TOKEN = 65535


def route_capacity(tokens, gy_size):
    return GROUP * (1 + 17 * tokens // (16 * gy_size * GROUP))


def share_kernel(gx_size, gy_size, everyone, send_ref, out_ref, own_sem, row_send, row_recv, x_send, x_recv, core_send,
                 core_recv):
    gx, gy = lax.axis_index("gx"), lax.axis_index("gy")
    x_size = gx_size // 2
    core, x = lax.rem(gx, 2), gx // 2
    rows = [(gx, lax.rem(gy + d, gy_size)) for d in range(1, gy_size)]
    along_x = [(lax.rem(x + d, x_size) * 2 + core, gy) for d in range(1, x_size)] if everyone else []
    sibling = [(x * 2 + 1 - core, gy)] if everyone else []
    greet_all(rows + along_x + sibling)
    mine = out_ref.at[gx] if everyone else out_ref.at[0]
    own = pltpu.make_async_copy(send_ref.at[gy], mine.at[gy], own_sem)
    own.start()
    for d, other in enumerate(rows):
        remote(send_ref.at[other[1]], mine.at[gy], row_send.at[d], row_recv.at[d], other).start()
    own.wait()
    for d, other in enumerate(rows):
        copy = remote(send_ref.at[other[1]], mine.at[gy], row_send.at[d], row_recv.at[d], other)
        copy.wait_recv()
    for d, other in enumerate(along_x):
        remote(mine, mine, x_send.at[d], x_recv.at[d], other).start()
    for other in sibling:
        remote(mine, mine, core_send.at[0], core_recv.at[0], other).start()
    for d, other in enumerate(along_x):
        remote(mine, mine, x_send.at[d], x_recv.at[d], other).wait_recv()
        source = out_ref.at[lax.rem(x + x_size - d - 1, x_size) * 2 + core]
        remote(source, source, core_send.at[d + 1], core_recv.at[d + 1], sibling[0]).start()
    for d, other in enumerate(rows):
        remote(send_ref.at[other[1]], mine.at[gy], row_send.at[d], row_recv.at[d], other).wait_send()
    for d, other in enumerate(along_x):
        remote(mine, mine, x_send.at[d], x_recv.at[d], other).wait_send()
    for i in range(x_size if everyone else 0):
        copy = remote(mine, mine, core_send.at[i], core_recv.at[i], sibling[0])
        copy.wait_send()
        copy.wait_recv()


def share_rows(rows, gx_size, gy_size, everyone, number, name):
    groups, dma = (gx_size if everyone else 1), pltpu.SemaphoreType.DMA
    x_size = gx_size // 2
    return pl.pallas_call(
        functools.partial(share_kernel, gx_size, gy_size, everyone),
        out_shape=jax.ShapeDtypeStruct((groups,) + rows.shape, rows.dtype),
        in_specs=[pl.BlockSpec(memory_space=pltpu.VMEM)],
        out_specs=pl.BlockSpec(memory_space=pltpu.VMEM),
        scratch_shapes=[dma, dma((gy_size - 1,)), dma((gy_size - 1,)), dma((x_size,)), dma((x_size,)), dma((x_size,)),
                        dma((x_size,))],
        compiler_params=pltpu.CompilerParams(
            collective_id=number, has_side_effects=True, vmem_limit_bytes=48 << 20
        ),
        name=name,
    )(rows)


def table_sum_kernel(cap, counts_ref, index_ref, rows_ref, out_ref, square_ref, wide, row_sem):
    sources = rows_ref.shape[0]
    vocab = out_ref.shape[0] - 8

    def fetch(source):
        slot = lax.rem(source, 2)
        return pltpu.make_async_copy(rows_ref.at[source], wide.at[slot], row_sem.at[slot])

    fetch(0).start()
    block = 32 if vocab % 32 == 0 else 8

    def clear(i, carry):
        out_ref[pl.ds(pl.multiple_of(i * block, 8), block), :] = jnp.zeros((block, D_TXT), jnp.float32)
        return carry

    lax.fori_loop(0, vocab // block, clear, 0)
    out_ref[vocab:, :] = jnp.zeros((8, D_TXT), jnp.float32)

    def one_source(source, carry):
        slot = lax.rem(source, 2)

        @pl.when(source + 1 < sources)
        def _():
            fetch(source + 1).start()

        fetch(source).wait()
        widened = wide.at[slot]

        def add(group, carry):
            rows = widened[pl.ds(pl.multiple_of(group * GROUP, GROUP), GROUP), :].astype(jnp.float32)
            for half in range(0, GROUP, 8):
                places = [
                    pl.ds(index_ref[source * cap + group * GROUP + half + i], 1) for i in range(8)
                ]
                sums = [out_ref[place, :] + rows[half + i : half + i + 1, :] for i, place in enumerate(places)]
                for place, value in zip(places, sums):
                    out_ref[place, :] = value
            return carry

        lax.fori_loop(0, (counts_ref[source] + GROUP - 1) // GROUP, add, 0)
        return carry

    lax.fori_loop(0, sources, one_source, 0)

    def square(i, carry):
        part = out_ref[pl.ds(pl.multiple_of(i * block, 8), block), :]
        part = part * part
        total = carry
        for r in range(0, block, 8):
            total = total + part[r : r + 8]
        return total

    square_ref[...] = lax.fori_loop(0, vocab // block, square, jnp.zeros((8, D_TXT), jnp.float32))


def table_sum(counts, index, rows, vocab):
    sources, cap = rows.shape[0], rows.shape[1]
    return pl.pallas_call(
        functools.partial(table_sum_kernel, cap),
        out_shape=[
            jax.ShapeDtypeStruct((vocab + 8, D_TXT), jnp.float32),
            jax.ShapeDtypeStruct((8, D_TXT), jnp.float32),
        ],
        in_specs=[pl.BlockSpec(memory_space=pltpu.SMEM)] * 2 + [pl.BlockSpec(memory_space=pl.ANY)],
        out_specs=[pl.BlockSpec(memory_space=pltpu.VMEM)] * 2,
        scratch_shapes=[pltpu.VMEM((2, cap, D_TXT), jnp.bfloat16), pltpu.SemaphoreType.DMA((2,))],
        compiler_params=pltpu.CompilerParams(vmem_limit_bytes=40 << 20),
        name="table_sum",
    )(counts, index, rows)


def ranks(flags):
    tokens = flags.shape[-1]
    before = (jnp.arange(tokens)[:, None] < jnp.arange(tokens)[None, :]).astype(jnp.bfloat16)
    return fwd_dot(flags.astype(jnp.bfloat16), before).astype(jnp.int32)


def pick_matrix(slots, count):
    return (jnp.arange(count)[:, None] == slots[None, :]).astype(jnp.bfloat16)


def gather_kernel(sizes, chunks, window_ref, out_ref, own_sem, h_send, h_recv, b_send, b_recv, a_send, a_recv, core_send,
                  core_recv):
    at = Places(sizes)
    rows = window_ref.shape[0]
    chunk = rows // chunks
    me = at.linear(at.core, at.a, at.b, at.h)
    sibling, peers_a, peers_b, peers_h = at.sibling(), at.along_a(), at.along_b(), at.along_h()
    greet_all([sibling] + peers_a + peers_b + peers_h)

    def part(block, t):
        return out_ref.at[pl.ds(pl.multiple_of(block * rows + t * chunk, GROUP), chunk)]

    def many(count):
        return out_ref.at[pl.ds(0, count * chunk)]

    def own_copy(t):
        src = window_ref.at[pl.ds(pl.multiple_of(t * chunk, GROUP), chunk)]
        return src, pltpu.make_async_copy(src, part(me, t), own_sem.at[t])

    def stage_h(t):
        src, own = own_copy(t)
        for d, other in enumerate(peers_h):
            remote(src, part(me, t), h_send.at[d], h_recv.at[t, d], other).start()
        own.start()

    def stage_b(t):
        own_copy(t)[1].wait()
        for d, other in enumerate(peers_h):
            remote(many(1), many(1), h_send.at[d], h_recv.at[t, d], other).wait_recv()
        for d, other in enumerate(peers_b):
            for h in range(at.high_size):
                block = part(at.linear(at.core, at.a, at.b, h), t)
                remote(block, block, b_send.at[d], b_recv.at[t, d], other).start()

    def stage_a(t):
        for d, other in enumerate(peers_b):
            remote(many(at.high_size), many(at.high_size), b_send.at[d], b_recv.at[t, d], other).wait_recv()
        for d, other in enumerate(peers_a):
            for b in range(at.b_size):
                for h in range(at.high_size):
                    block = part(at.linear(at.core, at.a, b, h), t)
                    remote(block, block, a_send.at[d], a_recv.at[t, d], other).start()

    plane = at.b_size * at.high_size

    def stage_core(t):
        for d, other in enumerate(peers_a):
            remote(many(plane), many(plane), a_send.at[d], a_recv.at[t, d], other).wait_recv()
        for a in range(at.a_size):
            for b in range(at.b_size):
                for h in range(at.high_size):
                    block = part(at.linear(at.core, a, b, h), t)
                    remote(block, block, core_send, core_recv, sibling).start()

    def turn(t, carry):
        for depth, stage in enumerate((stage_h, stage_b, stage_a, stage_core)):
            @pl.when((t >= depth) & (t < chunks + depth))
            def _():
                stage(t - depth)

        return carry

    lax.fori_loop(0, chunks + 3, turn, 0)

    def whole(count):
        return out_ref.at[pl.ds(0, count * rows)]

    for d, other in enumerate(peers_h):
        remote(whole(1), whole(1), h_send.at[d], h_recv.at[0, d], other).wait_send()
    for d, other in enumerate(peers_b):
        remote(whole(at.high_size), whole(at.high_size), b_send.at[d], b_recv.at[0, d], other).wait_send()
    for d, other in enumerate(peers_a):
        remote(whole(plane), whole(plane), a_send.at[d], a_recv.at[0, d], other).wait_send()
    half = whole(at.a_size * plane)
    last = remote(half, half, core_send, core_recv, sibling)
    last.wait_send()
    last.wait_recv()


def gather_windows(window, gx_size, gy_size, chunks, number, name):
    sizes = axis_sizes(gx_size, gy_size)
    a, b, h = sizes[0] - 1, sizes[1] - 1, sizes[2] - 1
    dma = pltpu.SemaphoreType.DMA
    return pl.pallas_call(
        functools.partial(gather_kernel, sizes, chunks),
        out_shape=jax.ShapeDtypeStruct((gx_size * gy_size * window.shape[0], LANES), window.dtype),
        in_specs=[pl.BlockSpec(memory_space=pltpu.VMEM)],
        out_specs=pl.BlockSpec(memory_space=pl.ANY),
        scratch_shapes=[dma((chunks,)), dma((h,)), dma((chunks, h)), dma((b,)), dma((chunks, b)), dma((a,)),
                        dma((chunks, a)), dma, dma],
        compiler_params=pltpu.CompilerParams(
            collective_id=number, has_side_effects=True, vmem_limit_bytes=32 << 20
        ),
        name=name,
    )(window)


def reduce_kernel(shard, sizes, grads_ref, out_ref, own, landed, keep_one, send_one, recv_one, keep_two, send_two,
                  recv_two, keep_three, send_three, recv_three, load_sem, pair_send, pair_recv, credit,
                  one_send, one_recv, two_send, two_recv, three_send, three_recv):
    at = Places(sizes)
    a_size, b_size, high_size = at.a_size, at.b_size, at.high_size
    core, my_a, my_b, high = at.core, at.a, at.b, at.h
    plane = b_size * high_size
    chunk = own.shape[2]
    chunks = out_ref.shape[0] // chunk

    def start_row(side, number):
        a, rest = number // plane, lax.rem(number, plane)
        return window_start(shard, at.linear(side, a, rest // high_size, lax.rem(rest, high_size)))

    sibling, peers, peers_two, peers_three = at.sibling(), at.along_a(), at.along_b(), at.along_h()
    greet_all([sibling] + peers + peers_two + peers_three)
    blocks = a_size * plane

    def pair_stage(t):
        slot = lax.rem(t, 2)

        @pl.when(t >= 2)
        def _():
            pl.semaphore_wait(credit, 1)

        def each(number, carry):
            theirs = pl.multiple_of(start_row(1 - core, number) + t * chunk, GROUP)
            mine = pl.multiple_of(start_row(core, number) + t * chunk, GROUP)
            remote(
                grads_ref.at[pl.ds(theirs, chunk)], landed.at[slot, number], pair_send.at[slot], pair_recv.at[slot], sibling
            ).start()
            pltpu.make_async_copy(
                grads_ref.at[pl.ds(mine, chunk)], own.at[slot, number], load_sem.at[slot]
            ).start()
            return carry

        lax.fori_loop(0, blocks, each, 0)

    def first_stage(u):
        slot = lax.rem(u, 2)
        both = remote(landed.at[slot], landed.at[slot], pair_send.at[slot], pair_recv.at[slot], sibling)
        pltpu.make_async_copy(own.at[slot], own.at[slot], load_sem.at[slot]).wait()
        both.wait_send()
        both.wait_recv()
        for d in range(1, a_size):
            @pl.when(u >= 2)
            def _():
                remote(send_one.at[slot, d - 1], recv_one.at[u - 2, d - 1], one_send.at[slot, d - 1],
                       one_recv.at[u - 2, d - 1], peers[d - 1]).wait_send()

            first = lax.rem(my_a + d, a_size) * plane

            def give(i, carry):
                send_one[slot, d - 1, i] = (own[slot, first + i] + landed[slot, first + i]).astype(jnp.bfloat16)
                return carry

            lax.fori_loop(0, plane, give, 0)
            remote(send_one.at[slot, d - 1], recv_one.at[u, d - 1], one_send.at[slot, d - 1],
                   one_recv.at[u, d - 1], peers[d - 1]).start()

        def hold(i, carry):
            keep_one[slot, i] = own[slot, my_a * plane + i] + landed[slot, my_a * plane + i]
            return carry

        lax.fori_loop(0, plane, hold, 0)

        @pl.when(u < chunks - 2)
        def _():
            pl.semaphore_signal(credit, inc=1, device_id=sibling, device_id_type=MESH)

    def second_stage(u):
        slot = lax.rem(u, 2)
        for d in range(1, a_size):
            remote(recv_one.at[u, d - 1], recv_one.at[u, d - 1], one_send.at[slot, d - 1], one_recv.at[u, d - 1],
                   peers[d - 1]).wait_recv()

        def total(number):
            value = keep_one[slot, number]
            for d in range(1, a_size):
                value = value + recv_one[u, d - 1, number].astype(jnp.float32)
            return value

        for d in range(1, b_size):
            @pl.when(u >= 2)
            def _():
                remote(send_two.at[slot, d - 1], recv_two.at[u - 2, d - 1], two_send.at[slot, d - 1],
                       two_recv.at[u - 2, d - 1], peers_two[d - 1]).wait_send()

            first = lax.rem(my_b + d, b_size) * high_size

            def give(i, carry):
                send_two[slot, d - 1, i] = total(first + i).astype(jnp.bfloat16)
                return carry

            lax.fori_loop(0, high_size, give, 0)
            remote(send_two.at[slot, d - 1], recv_two.at[u, d - 1], two_send.at[slot, d - 1],
                   two_recv.at[u, d - 1], peers_two[d - 1]).start()

        def hold(i, carry):
            keep_two[slot, i] = total(my_b * high_size + i)
            return carry

        lax.fori_loop(0, high_size, hold, 0)

    def third_stage(u):
        slot = lax.rem(u, 2)
        for d in range(1, b_size):
            remote(recv_two.at[u, d - 1], recv_two.at[u, d - 1], two_send.at[slot, d - 1], two_recv.at[u, d - 1],
                   peers_two[d - 1]).wait_recv()

        def total(number):
            value = keep_two[slot, number]
            for d in range(1, b_size):
                value = value + recv_two[u, d - 1, number].astype(jnp.float32)
            return value

        for d in range(1, high_size):
            @pl.when(u >= 2)
            def _():
                remote(send_three.at[slot, d - 1], recv_three.at[u - 2, d - 1], three_send.at[slot, d - 1],
                       three_recv.at[u - 2, d - 1], peers_three[d - 1]).wait_send()

            send_three[slot, d - 1] = total(lax.rem(high + d, high_size)).astype(jnp.bfloat16)
            remote(send_three.at[slot, d - 1], recv_three.at[u, d - 1], three_send.at[slot, d - 1],
                   three_recv.at[u, d - 1], peers_three[d - 1]).start()
        keep_three[slot] = total(high)

    def last_stage(u):
        slot = lax.rem(u, 2)
        value = keep_three[slot]
        for d in range(1, high_size):
            remote(recv_three.at[u, d - 1], recv_three.at[u, d - 1], three_send.at[slot, d - 1],
                   three_recv.at[u, d - 1], peers_three[d - 1]).wait_recv()
            value = value + recv_three[u, d - 1].astype(jnp.float32)
        out_ref[pl.ds(pl.multiple_of(u * chunk, GROUP), chunk), :] = value

    def turn(t, carry):
        stages = (pair_stage, first_stage, second_stage, third_stage, last_stage)
        for depth, stage in enumerate(stages):
            @pl.when((t >= depth) & (t < chunks + depth))
            def _():
                stage(t - depth)

        return carry

    lax.fori_loop(0, chunks + 4, turn, 0)
    for u in range(max(chunks - 2, 0), chunks):
        slot = u % 2
        for d in range(1, a_size):
            remote(send_one.at[slot, d - 1], recv_one.at[u, d - 1], one_send.at[slot, d - 1],
                   one_recv.at[u, d - 1], peers[d - 1]).wait_send()
        for d in range(1, b_size):
            remote(send_two.at[slot, d - 1], recv_two.at[u, d - 1], two_send.at[slot, d - 1],
                   two_recv.at[u, d - 1], peers_two[d - 1]).wait_send()
        for d in range(1, high_size):
            remote(send_three.at[slot, d - 1], recv_three.at[u, d - 1], three_send.at[slot, d - 1],
                   three_recv.at[u, d - 1], peers_three[d - 1]).wait_send()


def reduce_windows(grads, shard, gx_size, gy_size, number):
    rows = window_rows(shard, GROUP * CHUNKS)
    chunk = rows // CHUNKS
    x_size, low_size, high_size = axis_sizes(gx_size, gy_size)
    plane = low_size * high_size
    blocks = x_size * plane
    low_type, dma = jnp.bfloat16, pltpu.SemaphoreType.DMA
    a, b, h = x_size - 1, low_size - 1, high_size - 1
    return pl.pallas_call(
        functools.partial(reduce_kernel, shard, (x_size, low_size, high_size)),
        out_shape=jax.ShapeDtypeStruct((rows, LANES), jnp.float32),
        in_specs=[pl.BlockSpec(memory_space=pl.ANY)],
        out_specs=pl.BlockSpec(memory_space=pltpu.VMEM),
        scratch_shapes=[
            pltpu.VMEM((2, blocks, chunk, LANES), jnp.float32),
            pltpu.VMEM((2, blocks, chunk, LANES), jnp.float32),
            pltpu.VMEM((2, plane, chunk, LANES), jnp.float32),
            pltpu.VMEM((2, a, plane, chunk, LANES), low_type),
            pltpu.VMEM((CHUNKS, a, plane, chunk, LANES), low_type),
            pltpu.VMEM((2, high_size, chunk, LANES), jnp.float32),
            pltpu.VMEM((2, b, high_size, chunk, LANES), low_type),
            pltpu.VMEM((CHUNKS, b, high_size, chunk, LANES), low_type),
            pltpu.VMEM((2, chunk, LANES), jnp.float32),
            pltpu.VMEM((2, h, chunk, LANES), low_type),
            pltpu.VMEM((CHUNKS, h, chunk, LANES), low_type),
            dma((2,)),
            dma((2,)),
            dma((2,)),
            pltpu.SemaphoreType.REGULAR,
            dma((2, a)),
            dma((CHUNKS, a)),
            dma((2, b)),
            dma((CHUNKS, b)),
            dma((2, h)),
            dma((CHUNKS, h)),
        ],
        compiler_params=pltpu.CompilerParams(
            collective_id=number, has_side_effects=True, vmem_limit_bytes=60 << 20
        ),
        name="reduce_windows",
    )(grads)


def log_sums(rows, columns, column_ok, logit_scale, matches):
    total, taken = rows.shape[0], min(rows.shape[0], 256)

    def some(args):
        row_part, match_part = args
        logits = logit_scale * back_dot(row_part, columns)
        masked = jnp.where(column_ok[None, :], logits, -1e30)
        row_max = jnp.max(masked, 1, keepdims=True)
        log_total = row_max[:, 0] + jnp.log(jnp.sum(jnp.exp(masked - row_max), 1))
        gap = jnp.where(match_part > 0.0, logits[:, :total] - log_total[:, None], 0.0)
        return log_total, -jnp.sum(gap)

    if taken == total:
        return some((rows, matches))
    logs, parts = lax.map(
        some, (rows.reshape(-1, taken, rows.shape[1]), matches.reshape(-1, taken, total))
    )
    return logs.reshape(-1), jnp.sum(parts)


def side_grads(row_embed, columns, column_ok, same_own, positives_own, log_own, logit_scale, total_count):
    dot_vals = back_dot(row_embed, columns)
    masked = jnp.where(column_ok[None, :], logit_scale * dot_vals, -1e30)
    extra = columns.shape[0] - same_own.shape[1]
    weights_pos = jnp.concatenate(
        [same_own, jnp.zeros((same_own.shape[0], extra), jnp.float32)], 1
    )
    grad_logits = (
        positives_own[:, None] * jnp.exp(masked - log_own[:, None]) - weights_pos
    ) / total_count
    grad_dots = (logit_scale * grad_logits).astype(jnp.bfloat16)
    grad_temper = logit_scale * jnp.sum(grad_logits * dot_vals)
    return fwd_dot(grad_dots, columns), grad_temper


def cross_grads(rows, own, valid_own, same_own, positives_all, logs, logit_scale, total_count):
    logits = logit_scale * back_dot(rows, own)
    masked = jnp.where(valid_own[None, :], logits, -1e30)
    grad_logits = (
        positives_all[:, None] * jnp.exp(masked - logs[:, None]) - same_own.T
    ) / total_count
    grad_dots = (logit_scale * grad_logits).astype(jnp.bfloat16)
    return weight_grad(grad_dots, rows)


def body(
    flat_master,
    flat_first,
    flat_second,
    table,
    table_first,
    table_second,
    pixels,
    token_ids,
    end_pos,
    pair_counts,
    groups,
    cached_image,
    cached_text,
):
    gx_size, gy_size = lax.axis_size("gx"), lax.axis_size("gy")
    device_count = gx_size * gy_size
    my_index = linear_index(gy_size)
    pairs_dev = pixels.shape[0]
    shard = flat_master.shape[0]
    tokens = token_ids.size
    vocab_dev = table.shape[0]
    cap = route_capacity(tokens, gy_size)
    own_ids = token_ids.reshape(-1)
    same = own_ids[:, None] == own_ids[None, :]
    order = jnp.arange(tokens)
    leading = ~jnp.any(same & (order[None, :] < order[:, None]), 1)
    flat_ids = jnp.where(leading, own_ids, NO_TOKEN)
    flat_ids = jnp.pad(flat_ids, (0, ID_ROWS * LANES // 2 - tokens)).reshape(-1, LANES)
    payload = [
        place_window(flat_master, gy_size),
        jnp.concatenate([cached_image, cached_text], 0).reshape(CACHED_ROWS, LANES),
        jnp.concatenate([flat_ids // 256, flat_ids % 256], 0).astype(jnp.bfloat16),
    ]
    used = sum(part.shape[0] for part in payload)
    step = GROUP * GATHER_CHUNKS
    payload = jnp.pad(jnp.concatenate(payload, 0), ((0, -used % step), (0, 0)))
    gathered = gather_windows(payload, gx_size, gy_size, GATHER_CHUNKS, 4, "gather_weights")
    every_part = gathered.reshape(device_count, -1, LANES)
    cached = every_part[:, used - ID_ROWS - CACHED_ROWS : used - ID_ROWS].reshape(device_count, -1, EMBED)
    cache_img, cache_txt = lax.optimization_barrier((cached[:, :pairs_dev], cached[:, pairs_dev:]))
    cache_img, cache_txt = cache_img.reshape(-1, EMBED), cache_txt.reshape(-1, EMBED)
    coded = every_part[:, used - ID_ROWS : used].astype(jnp.int32)
    ids_all = coded[:, : ID_ROWS // 2] * 256 + coded[:, ID_ROWS // 2 :]
    ids_all = ids_all.reshape(device_count, -1)[:, :tokens]
    holders = ids_all // vocab_dev
    pair_rows = jnp.sum(holders[:, :, None] == jnp.arange(gy_size), 1)
    rounds = (jnp.max(pair_rows) + cap - 1) // cap
    me_y = lax.axis_index("gy")
    held = holders == me_y
    held_rank = jnp.where(held, ranks(held), -1)
    held_row = ids_all - me_y * vocab_dev
    held_count = jnp.sum(held, 1)
    own_flags = (jnp.arange(gy_size)[:, None] == own_ids[None, :] // vocab_dev) & leading[None, :]
    own_place = jnp.arange(gy_size)[:, None] * tokens + ranks(own_flags)
    own_place = jnp.sum(jnp.where(own_flags, own_place, 0), 0)
    own_place = jnp.sum(jnp.where(same & leading[None, :], own_place[None, :], 0), 1)
    own_holder, own_rank = own_place // tokens, own_place % tokens

    def held_rows(turn):
        slots = held_rank - turn * cap
        found = slots[:, None, :] == jnp.arange(cap)[None, :, None]
        return vocab_dev + jnp.sum(jnp.where(found, held_row[:, None, :] - vocab_dev, 0), 2)

    def own_slots(turn):
        rank = own_rank - turn * cap
        return jnp.where((rank >= 0) & (rank < cap), own_holder * cap + rank, -1)

    first_rows = held_rows(0)
    group_start = lax.axis_index("gx") * gy_size

    def rows_to_send(index):
        index = lax.dynamic_slice_in_dim(index, group_start, gy_size, 0)
        return lax.optimization_barrier(jnp.take(table, index.reshape(-1), axis=0, mode="clip")).astype(jnp.bfloat16)

    landed = share_rows(
        rows_to_send(first_rows).reshape(gy_size, cap, D_TXT), gx_size, gy_size, False, 5, "token_rows"
    )
    slot_count = gy_size * cap
    picks = pick_matrix(own_slots(0), slot_count)
    token_rows = weight_grad(picks, landed.reshape(slot_count, D_TXT)).astype(jnp.bfloat16)

    def more_rows(turn, found):
        rows = rows_to_send(held_rows(turn)).reshape(gy_size, cap, D_TXT)
        rows = lax.all_to_all(rows, "gy", 0, 0, tiled=True).reshape(slot_count, D_TXT)
        return found + weight_grad(pick_matrix(own_slots(turn), slot_count), rows).astype(jnp.bfloat16)

    token_rows = lax.fori_loop(1, rounds, more_rows, token_rows)
    spread = spread_weights(gathered, shard, device_count)
    image_weights = dict(zip(IMAGE.names, spread[:5]))
    text_weights = dict(zip(TEXT.names, spread[5:9]))
    image_vec, text_vec, temper = split_vectors(spread[9])
    image_gains, image_base, image_rows = image_inputs(image_vec, pixels)
    text_gains, text_base, text_rows = text_inputs(text_vec, token_rows)
    image_kept = tower_forward(IMAGE, end_pos, image_gains, image_base, image_rows, image_weights)
    text_kept = tower_forward(TEXT, end_pos, text_gains, text_base, text_rows, text_weights)
    image_emb = image_kept[14].astype(jnp.bfloat16)
    text_emb = text_kept[14].astype(jnp.bfloat16)
    embeds = jnp.concatenate([image_emb, text_emb], 0).reshape(-1, LANES)
    embeds = gather_windows(embeds, gx_size, gy_size, 1, 0, "embeddings")
    embeds = embeds.reshape(device_count, 2 * pairs_dev, EMBED)
    all_img, all_txt = lax.optimization_barrier((embeds[:, :pairs_dev], embeds[:, pairs_dev:]))
    all_img, all_txt = all_img.reshape(-1, EMBED), all_txt.reshape(-1, EMBED)
    total_pairs = all_img.shape[0]
    valid_all = jnp.arange(total_pairs) % pairs_dev < jnp.repeat(pair_counts.reshape(-1), pairs_dev)
    matches = (
        (groups[:, None] == groups[None, :]) & valid_all[:, None] & valid_all[None, :]
    ).astype(jnp.float32)
    positives_all = jnp.sum(matches, 1)
    total_count = 2.0 * jnp.sum(positives_all)
    own_start = my_index * pairs_dev
    own_part = functools.partial(
        lax.dynamic_slice_in_dim, start_index=own_start, slice_size=pairs_dev, axis=0
    )
    same_own, positives_own, valid_own = own_part(matches), own_part(positives_all), own_part(valid_all)
    logit_scale = jnp.exp(temper)
    column_ok = jnp.concatenate([valid_all, jnp.ones((cache_img.shape[0],), jnp.bool_)])
    columns_txt = jnp.concatenate([all_txt, cache_txt])
    columns_img = jnp.concatenate([all_img, cache_img])
    log_img, loss_one = log_sums(all_img, columns_txt, column_ok, logit_scale, matches)
    log_txt, loss_two = log_sums(all_txt, columns_img, column_ok, logit_scale, matches)
    loss_sum = loss_one + loss_two
    grad_img, temper_one = side_grads(
        image_emb, columns_txt, column_ok, same_own, positives_own, own_part(log_img), logit_scale, total_count
    )
    grad_txt, temper_two = side_grads(
        text_emb, columns_img, column_ok, same_own, positives_own, own_part(log_txt), logit_scale, total_count
    )
    grad_img = grad_img + cross_grads(
        all_txt, image_emb, valid_own, same_own, positives_all, log_txt, logit_scale, total_count
    )
    grad_txt = grad_txt + cross_grads(
        all_img, text_emb, valid_own, same_own, positives_all, log_img, logit_scale, total_count
    )
    text_grads = tower_backward(TEXT, end_pos, text_gains, grad_txt, text_kept[:14], text_weights)
    grad_rows = text_grads[6][: SEQS * CTX]
    to_holders = fwd_dot(picks, grad_rows).astype(jnp.bfloat16).reshape(gy_size, cap, D_TXT)
    arrived = share_rows(to_holders, gx_size, gy_size, True, 6, "token_grads")
    image_grads = tower_backward(IMAGE, end_pos, image_gains, grad_img, image_kept[:14], image_weights)
    pair_lists = ([(image_rows, image_grads[6])],) + grad_pairs(image_kept, image_grads)
    pair_lists = pair_lists + grad_pairs(text_kept, text_grads)
    table_grad, table_square = table_sum(
        jnp.minimum(held_count, cap),
        first_rows.reshape(-1),
        arrived.reshape(device_count, cap, D_TXT),
        vocab_dev,
    )

    def more_grads(turn, total):
        rows = fwd_dot(pick_matrix(own_slots(turn), slot_count), grad_rows).astype(jnp.bfloat16)
        rows = lax.all_to_all(rows.reshape(gy_size, cap, D_TXT), "gy", 0, 0, tiled=True)
        rows = lax.all_gather(rows, "gx", axis=0).reshape(device_count * cap, D_TXT).astype(jnp.float32)
        return total.at[held_rows(turn).reshape(-1)].add(rows)

    table_grad, table_squares = lax.cond(
        rounds > 1,
        lambda total, square: (
            lambda whole: (whole, jnp.sum(whole[:vocab_dev] * whole[:vocab_dev]))
        )(lax.fori_loop(1, rounds, more_grads, total)),
        lambda total, square: (total, jnp.sum(square)),
        table_grad,
        table_square,
    )
    total_rows = window_start(shard, device_count - 1) + window_rows(shard, GROUP * CHUNKS)
    vec_rows = jnp.concatenate(
        [
            image_grads[7][:1].reshape(-1, LANES),
            image_grads[7].reshape(-1, LANES),
            image_grads[8].reshape(-1, LANES),
            text_grads[7].reshape(-1, LANES),
            text_grads[8][2:].reshape(-1, LANES),
            jnp.pad((temper_one + temper_two).reshape(1, 1), ((0, 0), (0, LANES - 1))),
        ]
    )
    vec_rows = jnp.pad(vec_rows, ((0, total_rows - matrix_rows() - vec_rows.shape[0]), (0, 0)))
    local_grads = weight_grads(pair_lists, vec_rows)
    grad_window = reduce_windows(local_grads, shard, gx_size, gy_size, 1)
    grad_shard = lift_window(grad_window, shard, gy_size)
    table_squares = jnp.where(lax.axis_index("gx") == 0, table_squares, 0.0)
    squares = jnp.sum(grad_shard * grad_shard) + table_squares
    (every,) = exchange_all([jnp.full((8, LANES), squares)], gx_size, gy_size, 2, "squares")
    grad_norm = jnp.sqrt(jnp.sum(every[:, 0, 0]))
    factor = jnp.minimum(1.0, clip_limit / (grad_norm + 1e-06))
    matrix_stop = matrix_rows() * LANES
    position = my_index * shard + jnp.arange(shard)
    is_matrix = position < matrix_stop
    rates = jnp.where(is_matrix, rate_matrix, rate_vector)
    decays = jnp.where(is_matrix, decay_rate, 0.0)
    master_out, first_out, second_out = adam_step(
        flat_master, flat_first, flat_second, grad_shard * factor, rates, decays
    )
    table_out, table_first_out, table_second_out = adam_step(
        table, table_first, table_second, table_grad[:vocab_dev] * factor, rate_table, 0.0
    )
    return (
        master_out,
        first_out,
        second_out,
        table_out,
        table_first_out,
        table_second_out,
        loss_sum,
        total_count,
        grad_norm,
    )


def solution(mesh):
    placed = (
        P(("gx", "gy")),
        P(("gx", "gy")),
        P(("gx", "gy")),
        P("gy", None),
        P("gy", None),
        P("gy", None),
        P(("gx", "gy"), None, None),
        P(("gx", "gy"), None),
        P(("gx", "gy")),
        P(),
        P(),
        P(("gx", "gy"), None),
        P(("gx", "gy"), None),
    )
    return jax.shard_map(
        body,
        mesh=mesh,
        in_specs=placed,
        out_specs=(
            P(("gx", "gy")),
            P(("gx", "gy")),
            P(("gx", "gy")),
            P("gy", None),
            P("gy", None),
            P("gy", None),
            P(),
            P(),
            P(),
        ),
        check_vma=False,
    )
```

```python
import functools

import jax
import jax.numpy as jnp
from jax import lax
from jax.experimental import pallas as pl
from jax.experimental.pallas import tpu as pltpu
from jax.sharding import PartitionSpec as P

D_IMG = 768
IMG_HEADS = 12
IMG_MLP = 3072
PATCH_DIM = 3072
D_TXT = 512
TXT_HEADS = 8
TXT_MLP = 2048
CTX = 77
EMBED = 512
STEP = 10
IMG_TOK = 50


clip_limit = 0.1
beta_one = 0.9
beta_two = 0.999
adam_eps = 1e-08
decay_rate = 0.1
rate_matrix = 0.01
rate_vector = 0.2
rate_table = 0.2
norm_eps = 1e-05


def segment_list():
    return [
        ("patch_embed", PATCH_DIM, D_IMG),
        ("image_attn", D_IMG, 4 * D_IMG),
        ("image_up", D_IMG, IMG_MLP),
        ("image_down", IMG_MLP, D_IMG),
        ("image_proj", D_IMG, EMBED),
        ("text_attn", D_TXT, 4 * D_TXT),
        ("text_up", D_TXT, TXT_MLP),
        ("text_down", TXT_MLP, D_TXT),
        ("text_proj", D_TXT, EMBED),
        ("image_vec", IMG_TOK + 9, D_IMG),
        ("text_vec", CTX + 6, D_TXT),
        ("temper", 1, 1),
    ]


LANES = 128
GROUP = 16
CHUNKS = 16
GATHER_CHUNKS = 14
CACHED_ROWS = 64
ID_ROWS = 16
MESH = pl.DeviceIdType.MESH


def dot_nn(left_side, right_side):
    return lax.dot_general(
        left_side, right_side, (((1,), (0,)), ((), ())), preferred_element_type=jnp.float32
    )


def dot_nt(left_side, right_side):
    return lax.dot_general(
        left_side, right_side, (((1,), (1,)), ((), ())), preferred_element_type=jnp.float32
    )


def dot_tn(left_side, right_side):
    return lax.dot_general(
        left_side, right_side, (((0,), (0,)), ((), ())), preferred_element_type=jnp.float32
    )


def back_dot(left_side, right_side):
    return dot_nt(left_side, right_side)


def fwd_dot(left_side, right_side):
    return dot_nn(left_side, right_side)


def weight_grad(left_side, right_side):
    return dot_tn(left_side, right_side)


def norm_parts(values):
    center = values - jnp.mean(values, -1, keepdims=True)
    scale = lax.rsqrt(jnp.mean(center * center, -1, keepdims=True) + norm_eps)
    return center * scale, scale


def layer_norm(values, gain_vec, shift_vec):
    return norm_parts(values)[0] * gain_vec + shift_vec


def layer_norm_back(values, gain_vec, grad):
    unit, scale = norm_parts(values)
    grad_unit = grad * gain_vec
    inner = jnp.mean(grad_unit, -1, keepdims=True)
    along = jnp.mean(grad_unit * unit, -1, keepdims=True)
    return scale * (grad_unit - inner - unit * along), grad * unit


def sum_rows(values):
    return jnp.sum(values, 0, keepdims=True)


def low16(values):
    return jnp.concatenate([values, jnp.zeros_like(values)], 0).astype(jnp.bfloat16)


SEQS = 8


class Tower:
    def __init__(self, image):
        self.image = image
        self.width = D_IMG if image else D_TXT
        self.heads = IMG_HEADS if image else TXT_HEADS
        self.length = IMG_TOK if image else CTX
        self.rows = -(-SEQS * self.length // GROUP) * GROUP
        self.lanes = 16 if image else 8
        self.queries = SEQS * self.lanes
        self.block = 80 if image else 48
        self.names = ("patch", "attn", "up", "down", "proj") if image else ("attn", "up", "down", "proj")

    def shapes(self):
        width = self.width
        found = dict(attn=(width, 4 * width), up=(width, 4 * width), down=(4 * width, width), proj=(width, EMBED))
        if self.image:
            found["patch"] = (PATCH_DIM, width)
        return found

    def head_mask(self):
        lane = lax.broadcasted_iota(jnp.int32, (self.lanes, self.width), 1)
        row = lax.broadcasted_iota(jnp.int32, (self.lanes, self.width), 0)
        return lane // (self.width // self.heads) == row

    def spread_heads(self, values, wide_ref):
        mask = self.head_mask()
        for s in range(SEQS):
            row = jnp.broadcast_to(values[s : s + 1].astype(jnp.float32), mask.shape)
            wide_ref[s * self.lanes : (s + 1) * self.lanes, :] = jnp.where(mask, row, 0.0)
        return wide_ref[...].astype(jnp.bfloat16)

    def join_heads(self, values, wide_ref):
        mask = self.head_mask()
        wide_ref[...] = values
        rows = [
            sum_rows(jnp.where(mask, wide_ref[s * self.lanes : (s + 1) * self.lanes, :], 0.0))
            for s in range(SEQS)
        ]
        return jnp.concatenate(rows, 0)

    def row_of(self, s, ends_ref):
        return s * self.length + (0 if self.image else ends_ref[s])

    def each_block(self, function, start):
        return lax.fori_loop(
            0,
            self.rows // self.block,
            lambda i, carry: function(pl.ds(pl.multiple_of(i * self.block, GROUP), self.block), carry),
            start,
        )


def tower_fetch(names, sources, landed, sems):
    copies = {
        name: pltpu.make_async_copy(source, ref, sems.at[i])
        for i, (name, source, ref) in enumerate(zip(names, sources, landed))
    }
    for copy in copies.values():
        copy.start()
    return copies, dict(zip(names, landed))


def tower_forward_kernel(tower, *refs):
    count = len(tower.names)
    ends_ref, gains_ref, base_ref, input_ref = refs[:4]
    sources = refs[4 : 4 + count]
    (tokens_ref, normed_ref, pair_ref, normed_own_ref, query_ref, probs_ref, attended_ref, middle_ref, normed_two_ref,
     upper_ref, act_ref, output_ref, head_ref, raw_ref, emb_ref) = refs[4 + count : 19 + count]
    hidden_ref, wide_ref = refs[19 + count : 21 + count]
    landed, sems = refs[21 + count : 21 + 2 * count], refs[21 + 2 * count]
    copies, weights = tower_fetch(tower.names, sources, landed, sems)
    width = tower.width
    gains = [gains_ref[i : i + 1, :] for i in range(8)]
    if tower.image:
        copies["patch"].wait()

        def patch(j, carry):
            cols = pl.ds(pl.multiple_of(j * 256, 256), 256)
            tokens_ref[:, cols] = dot_nn(input_ref[...], weights["patch"][:, cols]) + base_ref[:, cols]
            return carry

        lax.fori_loop(0, width // 256, patch, 0)

    def first(rows, carry):
        if tower.image:
            hidden = layer_norm(tokens_ref[rows, :], gains[0], gains[1])
        else:
            hidden = input_ref[rows, :].astype(jnp.float32) + base_ref[rows, :]
            tokens_ref[rows, :] = hidden
        hidden_ref[rows, :] = hidden
        normed_ref[rows, :] = layer_norm(hidden, gains[2], gains[3]).astype(jnp.bfloat16)
        return carry

    tower.each_block(first, 0)
    copies["attn"].wait()

    def pair(j, carry):
        at = pl.multiple_of(j * 256, 256)
        product = dot_nn(normed_ref[...], weights["attn"][:, pl.ds(width + at, 256)])
        pair_ref[:, pl.ds(at, 256)] = product.astype(jnp.bfloat16)
        return carry

    lax.fori_loop(0, 2 * width // 256, pair, 0)
    hidden_own = jnp.concatenate(
        [hidden_ref[pl.ds(tower.row_of(s, ends_ref), 1), :] for s in range(SEQS)], 0
    )
    normed_own = low16(layer_norm(hidden_own, gains[2], gains[3]))
    normed_own_ref[...] = normed_own
    query = dot_nn(normed_own, weights["attn"][:, :width]).astype(jnp.bfloat16)
    query_ref[...] = query
    queries = tower.spread_heads(query, wide_ref)
    scores = dot_nt(queries, pair_ref[:, :width]) * (width // tower.heads) ** (-0.5)
    row = lax.broadcasted_iota(jnp.int32, scores.shape, 0) // tower.lanes
    spot = lax.broadcasted_iota(jnp.int32, scores.shape, 1) - row * tower.length
    last = jnp.full(scores.shape, tower.length - 1, jnp.int32)
    if not tower.image:
        for s in range(SEQS):
            last = jnp.where(row == s, ends_ref[s], last)
    scores = jnp.where((spot >= 0) & (spot <= last), scores, -1e30)
    powers = jnp.exp(scores - jnp.max(scores, -1, keepdims=True))
    probs = powers / jnp.sum(powers, -1, keepdims=True)
    probs_ref[...] = probs
    attended = low16(tower.join_heads(dot_nn(probs.astype(jnp.bfloat16), pair_ref[:, width:]), wide_ref))
    attended_ref[...] = attended
    middle = hidden_own + dot_nn(attended, weights["attn"][:, 3 * width :])[:SEQS]
    middle_ref[...] = middle
    normed_two_ref[...] = low16(layer_norm(middle, gains[4], gains[5]))
    copies["up"].wait()

    def rise(j, carry):
        cols = pl.ds(pl.multiple_of(j * 512, 512), 512)
        upper = dot_nn(normed_two_ref[...], weights["up"][:, cols])[:SEQS]
        upper_ref[:, cols] = upper
        act_ref[:, cols] = low16(upper * jax.nn.sigmoid(1.702 * upper))
        return carry

    lax.fori_loop(0, 4 * width // 512, rise, 0)
    copies["down"].wait()

    def fall(j, carry):
        cols = pl.ds(pl.multiple_of(j * 256, 256), 256)
        output_ref[:, cols] = middle_ref[:, cols] + dot_nn(act_ref[...], weights["down"][:, cols])[:SEQS]
        return carry

    lax.fori_loop(0, width // 256, fall, 0)
    head_in = low16(layer_norm(output_ref[...], gains[6], gains[7]))
    head_ref[...] = head_in
    copies["proj"].wait()
    raw = dot_nn(head_in, weights["proj"][...])[:SEQS]
    raw_ref[...] = raw
    emb_ref[...] = raw * lax.rsqrt(jnp.sum(raw * raw, -1, keepdims=True) + 1e-06)


def tower_forward(tower, ends, gains, base, inputs, weights):
    width, rows = tower.width, tower.rows
    low, full = jnp.bfloat16, jnp.float32
    outs = [
        ((rows, width), full),
        ((rows, width), low),
        ((rows, 2 * width), low),
        ((GROUP, width), low),
        ((GROUP, width), low),
        ((tower.queries, rows), full),
        ((GROUP, width), low),
        ((SEQS, width), full),
        ((GROUP, width), low),
        ((SEQS, 4 * width), full),
        ((GROUP, 4 * width), low),
        ((SEQS, width), full),
        ((GROUP, width), low),
        ((SEQS, EMBED), full),
        ((SEQS, EMBED), full),
    ]
    vmem = pl.BlockSpec(memory_space=pltpu.VMEM)
    shapes = tower.shapes()
    return pl.pallas_call(
        functools.partial(tower_forward_kernel, tower),
        out_shape=[jax.ShapeDtypeStruct(shape, kind) for shape, kind in outs],
        in_specs=[pl.BlockSpec(memory_space=pltpu.SMEM)]
        + [vmem] * 3
        + [pl.BlockSpec(memory_space=pl.ANY)] * len(tower.names),
        out_specs=[vmem] * len(outs),
        scratch_shapes=[pltpu.VMEM((rows, width), full), pltpu.VMEM((tower.queries, width), full)]
        + [pltpu.VMEM(shapes[name], low) for name in tower.names]
        + [pltpu.SemaphoreType.DMA((len(tower.names),))],
        compiler_params=pltpu.CompilerParams(vmem_limit_bytes=58 << 20),
        name="image_forward" if tower.image else "text_forward",
    )(ends, gains, base, inputs, *[weights[name] for name in tower.names])


def tower_backward_kernel(tower, *refs):
    names = tower.names[-4:]
    count = len(names)
    ends_ref, gains_ref, grad_ref = refs[:3]
    (tokens_ref, normed_ref, pair_ref, normed_own_ref, query_ref, probs_ref, attended_ref, middle_ref, normed_two_ref,
     upper_ref, act_ref, output_ref, head_ref, raw_ref) = refs[3:17]
    sources = refs[17 : 17 + count]
    (grad_raw_ref, grad_mlp_ref, grad_upper_ref, grad_att_ref, grad_query_ref, grad_pair_ref, grad_rows_ref,
     places_ref, gain_grads_ref) = refs[17 + count : 26 + count]
    grad_ref_wide, wide_ref, grad_middle_ref = refs[26 + count : 29 + count]
    landed, sems = refs[29 + count : 29 + 2 * count], refs[29 + 2 * count]
    copies, weights = tower_fetch(names, sources, landed, sems)
    width, rows = tower.width, tower.rows
    scale = (width // tower.heads) ** (-0.5)
    gains = [gains_ref[i : i + 1, :] for i in range(8)]
    raw, grad_emb = raw_ref[...], grad_ref[...]
    norm = lax.rsqrt(jnp.sum(raw * raw, -1, keepdims=True) + 1e-06)
    along = jnp.sum(raw * grad_emb, -1, keepdims=True)
    grad_raw = low16(grad_emb * norm - raw * (norm * norm * norm * along))
    grad_raw_ref[...] = grad_raw
    copies["proj"].wait()
    grad_head = dot_nt(grad_raw, weights["proj"][...])[:SEQS]
    grad_out, gain_part = layer_norm_back(output_ref[...], gains[6], grad_head)
    gain_grads_ref[6:7, :] = sum_rows(gain_part)
    gain_grads_ref[7:8, :] = sum_rows(grad_head)
    grad_mlp_ref[...] = low16(grad_out)
    copies["down"].wait()

    def rise(j, carry):
        cols = pl.ds(pl.multiple_of(j * 512, 512), 512)
        grad_act = dot_nt(grad_mlp_ref[...], weights["down"][cols, :])[:SEQS]
        upper = upper_ref[:, cols]
        sig = jax.nn.sigmoid(1.702 * upper)
        grad_upper_ref[:, cols] = low16(grad_act * (sig + upper * (1.702 * (sig * (1.0 - sig)))))
        return carry

    lax.fori_loop(0, 4 * width // 512, rise, 0)
    copies["up"].wait()

    def fall(j, carry):
        cols = pl.ds(pl.multiple_of(j * 256, 256), 256)
        grad_middle_ref[:, cols] = dot_nt(grad_upper_ref[...], weights["up"][cols, :])[:SEQS]
        return carry

    lax.fori_loop(0, width // 256, fall, 0)
    grad_norm_two = grad_middle_ref[...]
    grad_mid, gain_part = layer_norm_back(middle_ref[...], gains[4], grad_norm_two)
    gain_grads_ref[4:5, :] = sum_rows(gain_part)
    gain_grads_ref[5:6, :] = sum_rows(grad_norm_two)
    grad_middle = grad_out + grad_mid
    grad_middle_ref[...] = grad_middle
    grad_att = low16(grad_middle)
    grad_att_ref[...] = grad_att
    copies["attn"].wait()
    grad_attended = dot_nt(grad_att, weights["attn"][:, 3 * width :]).astype(jnp.bfloat16)
    grads_heads = tower.spread_heads(grad_attended, wide_ref)
    queries = tower.spread_heads(query_ref[...], wide_ref)
    probs = probs_ref[...]
    grad_probs = dot_nt(grads_heads, pair_ref[:, width:])
    grad_scores = probs * (grad_probs - jnp.sum(grad_probs * probs, -1, keepdims=True))
    grad_scores = grad_scores.astype(jnp.bfloat16)
    grad_query = low16(tower.join_heads(dot_nn(grad_scores, pair_ref[:, :width]), wide_ref) * scale)
    grad_query_ref[...] = grad_query
    grad_pair_ref[:, :width] = (dot_tn(grad_scores, queries) * scale).astype(jnp.bfloat16)
    grad_pair_ref[:, width:] = dot_tn(probs.astype(jnp.bfloat16), grads_heads).astype(jnp.bfloat16)

    def inner(j, carry):
        at = pl.multiple_of(j * 256, 256)
        grad_ref_wide[:, pl.ds(at, 256)] = dot_nt(
            grad_pair_ref[...], weights["attn"][pl.ds(at, 256), width : 3 * width]
        )
        return carry

    lax.fori_loop(0, width // 256, inner, 0)
    grad_own = dot_nt(grad_query, weights["attn"][:, :width])
    for s in range(SEQS):
        grad_ref_wide[pl.ds(tower.row_of(s, ends_ref), 1), :] += grad_own[s : s + 1]

    def first(at, carry):
        grad = grad_ref_wide[at, :]
        hidden = tokens_ref[at, :]
        if tower.image:
            hidden = layer_norm(hidden, gains[0], gains[1])
        grad_in, gain_part = layer_norm_back(hidden, gains[2], grad)
        grad_ref_wide[at, :] = grad_in
        return carry[0] + sum_rows(gain_part), carry[1] + sum_rows(grad)

    nothing = jnp.zeros((1, width), jnp.float32)
    gain_one, shift_one = tower.each_block(first, (nothing, nothing))
    gain_grads_ref[2:3, :] = gain_one
    gain_grads_ref[3:4, :] = shift_one
    for s in range(SEQS):
        grad_ref_wide[pl.ds(tower.row_of(s, ends_ref), 1), :] += grad_middle_ref[s : s + 1, :]

    def second(at, carry):
        grad = grad_ref_wide[at, :]
        if not tower.image:
            grad_rows_ref[at, :] = grad.astype(jnp.bfloat16)
            return carry
        grad_in, gain_part = layer_norm_back(tokens_ref[at, :], gains[0], grad)
        grad_ref_wide[at, :] = grad_in
        grad_rows_ref[at, :] = grad_in.astype(jnp.bfloat16)
        return carry[0] + sum_rows(gain_part), carry[1] + sum_rows(grad)

    gain_pre, shift_pre = tower.each_block(second, (nothing, nothing))
    gain_grads_ref[0:1, :] = gain_pre
    gain_grads_ref[1:2, :] = shift_pre
    places = grad_ref_wide[0 : tower.length, :]
    for s in range(1, SEQS):
        places = places + grad_ref_wide[s * tower.length : (s + 1) * tower.length, :]
    places_ref[...] = places


def tower_backward(tower, ends, gains, grad_emb, kept, weights):
    width, rows = tower.width, tower.rows
    low, full = jnp.bfloat16, jnp.float32
    outs = [
        ((GROUP, EMBED), low),
        ((GROUP, width), low),
        ((GROUP, 4 * width), low),
        ((GROUP, width), low),
        ((GROUP, width), low),
        ((rows, 2 * width), low),
        ((rows, width), low),
        ((tower.length, width), full),
        ((8, width), full),
    ]
    vmem = pl.BlockSpec(memory_space=pltpu.VMEM)
    shapes, names = tower.shapes(), tower.names[-4:]
    return pl.pallas_call(
        functools.partial(tower_backward_kernel, tower),
        out_shape=[jax.ShapeDtypeStruct(shape, kind) for shape, kind in outs],
        in_specs=[pl.BlockSpec(memory_space=pltpu.SMEM)]
        + [vmem] * (2 + len(kept))
        + [pl.BlockSpec(memory_space=pl.ANY)] * len(names),
        out_specs=[vmem] * len(outs),
        scratch_shapes=[
            pltpu.VMEM((rows, width), full),
            pltpu.VMEM((tower.queries, width), full),
            pltpu.VMEM((SEQS, width), full),
        ]
        + [pltpu.VMEM(shapes[name], low) for name in names]
        + [pltpu.SemaphoreType.DMA((len(names),))],
        compiler_params=pltpu.CompilerParams(vmem_limit_bytes=58 << 20),
        name="image_backward" if tower.image else "text_backward",
    )(ends, gains, grad_emb, *kept, *[weights[name] for name in names])


def grad_pairs(kept, grads):
    (normed, normed_own, attended, normed_two, act_low, head_in) = (
        kept[1], kept[3], kept[6], kept[8], kept[10], kept[12]
    )
    grad_raw, grad_mlp, grad_upper, grad_att, grad_query, grad_pair = grads[:6]
    return (
        [(normed_own, grad_query), (normed, grad_pair), (attended, grad_att)],
        [(normed_two, grad_upper)],
        [(act_low, grad_mlp)],
        [(head_in, grad_raw)],
    )


def image_inputs(image_vec, pixels):
    pixels = jnp.pad(pixels, ((0, 0), (1, 0), (0, 0))).reshape(-1, PATCH_DIM)
    base = image_vec[1 : IMG_TOK + 1] + jnp.pad(image_vec[:1], ((0, IMG_TOK - 1), (0, 0)))
    return image_vec[IMG_TOK + 1 :], jnp.tile(base, (SEQS, 1)), pixels


def text_inputs(text_vec, token_rows):
    gains = jnp.pad(text_vec[CTX:], ((2, 0), (0, 0)))
    extra = TEXT.rows - SEQS * CTX
    base = jnp.pad(jnp.tile(text_vec[:CTX], (SEQS, 1)), ((0, extra), (0, 0)))
    return gains, base, jnp.pad(token_rows, ((0, extra), (0, 0)))


def adam_step(weight, first, second, grad, rate, decay):
    first = beta_one * first + (1.0 - beta_one) * grad
    second = beta_two * second + (1.0 - beta_two) * grad * grad
    first_hat = first / (1.0 - beta_one**STEP)
    second_hat = second / (1.0 - beta_two**STEP)
    weight = weight - rate * (first_hat / (jnp.sqrt(second_hat) + adam_eps) + decay * weight)
    return (weight, first, second)


IMAGE, TEXT = Tower(True), Tower(False)


def matrix_rows():
    return sum(seg_rows * seg_cols for seg_name, seg_rows, seg_cols in segment_list()[:9]) // LANES


def window_rows(shard, step=GROUP):
    need = -(-(GROUP * LANES - 1 + shard) // LANES)
    return -(-need // step) * step


def window_start(shard, index):
    return (shard * index // (GROUP * LANES)) * GROUP


def linear_index(gy_size):
    return lax.axis_index("gx") * gy_size + lax.axis_index("gy")


def place_kernel(shard, gy_size, flat_ref, out_ref, rolled):
    rows = flat_ref.shape[0]
    offset = lax.rem(shard * linear_index(gy_size), GROUP * LANES)
    down, right = offset // LANES, lax.rem(offset, LANES)
    pad = 2 * GROUP
    rolled[0:pad, :] = jnp.zeros((pad, LANES), jnp.float32)
    parts = 5 if rows % (5 * GROUP) == 0 else 1
    step = rows // parts

    def roll_rows(i, carry):
        at = pl.multiple_of(i * step, GROUP)
        rolled[pl.ds(pad + at, step), :] = pltpu.roll(flat_ref[pl.ds(at, step), :], right, 1)
        return carry

    lax.fori_loop(0, parts, roll_rows, 0)
    lane = lax.broadcasted_iota(jnp.int32, (step, LANES), 1)

    def put_rows(i, carry):
        at = pl.multiple_of(i * step, GROUP)
        upper = rolled[pl.ds(pad + at - down - 1, step), :]
        lower = rolled[pl.ds(pad + at - down, step), :]
        out_ref[pl.ds(at, step), :] = jnp.where(lane < right, upper, lower).astype(jnp.bfloat16)
        return carry

    lax.fori_loop(0, parts, put_rows, 0)


def place_window(flat, gy_size):
    shard = flat.shape[0]
    rows = window_rows(shard)
    padded = jnp.pad(flat, (0, rows * LANES - shard)).reshape(rows, LANES)
    return pl.pallas_call(
        functools.partial(place_kernel, shard, gy_size),
        out_shape=jax.ShapeDtypeStruct((rows, LANES), jnp.bfloat16),
        in_specs=[pl.BlockSpec(memory_space=pltpu.VMEM)],
        out_specs=pl.BlockSpec(memory_space=pltpu.VMEM),
        scratch_shapes=[pltpu.VMEM((rows + 2 * GROUP, LANES), jnp.float32)],
        compiler_params=pltpu.CompilerParams(vmem_limit_bytes=32 << 20),
        name="place_window",
    )(padded)


def lift_kernel(shard, gy_size, window_ref, out_ref, rolled):
    rows = window_ref.shape[0]
    offset = lax.rem(shard * linear_index(gy_size), GROUP * LANES)
    up, left = offset // LANES, lax.rem(offset, LANES)
    pad = 2 * GROUP
    step = rows // CHUNKS
    rolled[rows:, :] = jnp.zeros((pad, LANES), jnp.float32)

    def roll_rows(i, carry):
        at = pl.multiple_of(i * step, GROUP)
        rolled[pl.ds(at, step), :] = pltpu.roll(
            window_ref[pl.ds(at, step), :], lax.rem(LANES - left, LANES), 1
        )
        return carry

    lax.fori_loop(0, CHUNKS, roll_rows, 0)
    lane = lax.broadcasted_iota(jnp.int32, (step, LANES), 1)

    def put_rows(i, carry):
        at = pl.multiple_of(i * step, GROUP)
        first = rolled[pl.ds(at + up, step), :]
        second = rolled[pl.ds(at + up + 1, step), :]
        out_ref[pl.ds(at, step), :] = jnp.where(lane < LANES - left, first, second)
        return carry

    lax.fori_loop(0, CHUNKS, put_rows, 0)


def lift_window(window, shard, gy_size):
    rows = window.shape[0]
    lifted = pl.pallas_call(
        functools.partial(lift_kernel, shard, gy_size),
        out_shape=jax.ShapeDtypeStruct((rows, LANES), jnp.float32),
        in_specs=[pl.BlockSpec(memory_space=pltpu.VMEM)],
        out_specs=pl.BlockSpec(memory_space=pltpu.VMEM),
        scratch_shapes=[pltpu.VMEM((rows + 2 * GROUP, LANES), jnp.float32)],
        compiler_params=pltpu.CompilerParams(vmem_limit_bytes=32 << 20),
        name="lift_window",
    )(window)
    return lifted.reshape(-1)[:shard]


def spread_steps():
    steps = []
    base = 0
    for number, (seg_name, seg_rows, seg_cols) in enumerate(segment_list()[:9]):
        wide = seg_cols // LANES
        take = seg_rows
        while take * wide > 4608:
            take //= 2
        for start in range(0, seg_rows, take):
            steps.append((number, start, take, seg_cols, base + start * wide))
        base += seg_rows * wide
    return steps


def window_pieces(shard, count, stride, first, length):
    pieces, shared = [], []
    for index in range(count):
        low = window_start(shard, index)
        high = window_start(shard, index + 1) if index + 1 < count else low + window_rows(shard)
        start, stop = max(low, first), min(high, first + length)
        if start < stop:
            pieces.append((index * stride + start - low, start - first, stop - start))
        if index + 1 < count and first <= high < first + length:
            shared.append((index * stride + high - low, high - first))
    return pieces, shared


def spread_kernel(shard, count, vec_rows, gathered_ref, *refs):
    outs, vec_ref = refs[:9], refs[9]
    landed, edges, wide_rows, ready, in_sem, out_sem = refs[10:]
    rows = gathered_ref.shape[0] // count
    steps = spread_steps()
    steps.append((9, 0, vec_rows, LANES, matrix_rows()))

    def copies_in(number):
        seg, start, take, cols, base = steps[number]
        slot = number % 2
        pieces, shared = window_pieces(shard, count, rows, base, take * cols // LANES)
        found = [
            pltpu.make_async_copy(
                gathered_ref.at[pl.ds(src, size)], landed.at[slot, pl.ds(dst, size)], in_sem.at[slot]
            )
            for src, dst, size in pieces
        ]
        found += [
            pltpu.make_async_copy(
                gathered_ref.at[pl.ds(src, GROUP)], edges.at[slot, order], in_sem.at[slot]
            )
            for order, (src, dst) in enumerate(shared)
        ]
        return found, shared

    def copy_out(number):
        seg, start, take, cols, base = steps[number]
        slot = number % 2
        if seg == 9:
            return pltpu.make_async_copy(wide_rows.at[pl.ds(0, take)], vec_ref, out_sem.at[slot])
        return pltpu.make_async_copy(
            ready[cols].at[slot, pl.ds(0, take)], outs[seg].at[pl.ds(start, take)], out_sem.at[slot]
        )

    for copy in copies_in(0)[0]:
        copy.start()
    for number, (seg, start, take, cols, base) in enumerate(steps):
        slot = number % 2
        wide = cols // LANES
        total = take * wide
        if number + 1 < len(steps):
            for copy in copies_in(number + 1)[0]:
                copy.start()
        found, shared = copies_in(number)
        for copy in found:
            copy.wait()
        if number >= 2:
            copy_out(number - 2).wait()
        block = 256 if total % 256 == 0 else GROUP

        def widen(i, carry, slot=slot, block=block):
            at = pl.multiple_of(i * block, GROUP)
            wide_rows[pl.ds(at, block), :] = landed[slot, pl.ds(at, block), :].astype(jnp.float32)
            return carry

        lax.fori_loop(0, total // block, widen, 0)
        for order, (src, dst) in enumerate(shared):
            wide_rows[dst : dst + GROUP, :] += edges[slot, order].astype(jnp.float32)
        if seg < 9:

            def tile(i, carry, slot=slot, wide=wide, cols=cols):
                at = pl.multiple_of(i * GROUP, GROUP)
                for j in range(wide):
                    ready[cols][slot, pl.ds(at, GROUP), j * LANES : (j + 1) * LANES] = wide_rows[
                        pl.ds(at * wide + j, GROUP, stride=wide), :
                    ].astype(jnp.bfloat16)
                return carry

            lax.fori_loop(0, take // GROUP, tile, 0)
        copy_out(number).start()
    copy_out(len(steps) - 2).wait()
    copy_out(len(steps) - 1).wait()


def spread_entry(shard, gx_size, gy_size, vec_rows, gathered_ref, rows_ref, *refs):
    outs, landed_rows = refs[:10], refs[10]
    landed, edges, wide_rows, ready_a, ready_b, ready_c, ready_d, in_sem, out_sem = refs[11:20]
    ready = {D_IMG: ready_a, 4 * D_IMG: ready_b, D_TXT: ready_c, 4 * D_TXT: ready_d}
    share = Share(gx_size, gy_size, False, rows_ref, landed_rows, refs[20:])
    share.greet()
    share.begin()
    spread_kernel(
        shard, gx_size * gy_size, vec_rows, gathered_ref, *outs, landed, edges, wide_rows, ready, in_sem, out_sem
    )
    share.middle()
    share.finish()


def spread_weights(gathered, rows_to_send, shard, gx_size, gy_size, number):
    count = gx_size * gy_size
    rows = gathered.shape[0] // count
    steps = spread_steps()
    tallest = {}
    for seg, start, take, cols, base in steps:
        tallest[cols] = max(tallest.get(cols, 0), take)
    most = max(take * cols // LANES for seg, start, take, cols, base in steps)
    vec_rows = -(-(sum(r * c for name, r, c in segment_list()[9:])) // (LANES * GROUP)) * GROUP
    edge_count = max(
        len(window_pieces(shard, count, rows, base, take * cols // LANES)[1])
        for seg, start, take, cols, base in steps
    )
    ready = [
        pltpu.VMEM((2, tallest[cols], cols), jnp.bfloat16)
        for cols in (D_IMG, 4 * D_IMG, D_TXT, 4 * D_TXT)
    ]
    return pl.pallas_call(
        functools.partial(spread_entry, shard, gx_size, gy_size, vec_rows),
        out_shape=[
            jax.ShapeDtypeStruct((seg_rows, seg_cols), jnp.bfloat16)
            for seg_name, seg_rows, seg_cols in segment_list()[:9]
        ]
        + [
            jax.ShapeDtypeStruct((vec_rows, LANES), jnp.float32),
            jax.ShapeDtypeStruct((1,) + rows_to_send.shape, rows_to_send.dtype),
        ],
        in_specs=[pl.BlockSpec(memory_space=pl.ANY), pl.BlockSpec(memory_space=pltpu.VMEM)],
        out_specs=[pl.BlockSpec(memory_space=pl.ANY)] * 10 + [pl.BlockSpec(memory_space=pltpu.VMEM)],
        scratch_shapes=[
            pltpu.VMEM((2, most, LANES), jnp.bfloat16),
            pltpu.VMEM((2, edge_count + 1, GROUP, LANES), jnp.bfloat16),
            pltpu.VMEM((most, LANES), jnp.float32),
        ]
        + ready
        + [pltpu.SemaphoreType.DMA((2,)), pltpu.SemaphoreType.DMA((2,))]
        + share_sems(gx_size, gy_size),
        compiler_params=pltpu.CompilerParams(
            collective_id=number, has_side_effects=True, vmem_limit_bytes=48 << 20
        ),
        name="spread_weights",
    )(gathered, rows_to_send)


def split_vectors(vec_rows):
    image_count, text_count = (IMG_TOK + 9) * D_IMG // LANES, (CTX + 6) * D_TXT // LANES
    image_vec = vec_rows[:image_count].reshape(IMG_TOK + 9, D_IMG)
    text_vec = vec_rows[image_count : image_count + text_count].reshape(CTX + 6, D_TXT)
    return image_vec, text_vec, vec_rows[image_count + text_count, 0]


def grads_kernel(parts, gx_size, gy_size, *refs):
    operand_count = sum(2 * len(pairs) for seg_rows, seg_cols, take, pairs in parts)
    operands = refs[:operand_count]
    vec_ref, token_ref, out_ref, arrived_ref, flat_rows, vec_sem, out_sem = refs[operand_count : operand_count + 7]
    share = Share(gx_size, gy_size, True, token_ref, arrived_ref, refs[operand_count + 7 :])
    share.greet()
    share.begin()
    tail = pltpu.make_async_copy(vec_ref, out_ref.at[pl.ds(matrix_rows(), vec_ref.shape[0])], vec_sem)
    tail.start()
    base = 0
    steps_before = 0
    for number, (seg_rows, seg_cols, take, pairs) in enumerate(parts):
        if number == 2:
            share.middle()
        if number == 6:
            share.rest()
        wide = seg_cols // LANES
        size = take * wide
        count = seg_rows // take

        def step(i, carry, base=base, before=steps_before, size=size, take=take, wide=wide, pairs=pairs):
            slot = lax.rem(i + before, 2)

            def written(number):
                at = pl.multiple_of(base + number * size, 8)
                return pltpu.make_async_copy(
                    flat_rows.at[slot, pl.ds(0, size)], out_ref.at[pl.ds(at, size)], out_sem.at[slot]
                )

            @pl.when(i >= 2)
            def _():
                written(i - 2).wait()

            for left_number, right_number, first in pairs:
                left_ref, right_ref = operands[left_number], operands[right_number]
                at = pl.multiple_of(i * take, LANES)
                product = lax.dot_general(
                    left_ref[:, pl.ds(at, take)],
                    right_ref[...],
                    (((0,), (0,)), ((), ())),
                    preferred_element_type=jnp.float32,
                )
                for j in range(right_ref.shape[1] // LANES):
                    flat_rows[slot, pl.ds(first + j, take, stride=wide), :] = product[
                        :, j * LANES : (j + 1) * LANES
                    ]
            written(i).start()
            return carry

        lax.fori_loop(0, count, step, 0)
        for number in range(max(count - 2, 0), count):
            slot = (number + steps_before) % 2
            at = base + number * size
            pltpu.make_async_copy(
                flat_rows.at[slot, pl.ds(0, size)], out_ref.at[pl.ds(at, size)], out_sem.at[slot]
            ).wait()
        base += seg_rows * wide
        steps_before += count
    tail.wait()
    share.finish()


def weight_grads(pair_lists, vec_rows, token_grads, gx_size, gy_size, number):
    operands, parts = [], []
    for (seg_name, seg_rows, seg_cols), pairs in zip(segment_list()[:9], pair_lists):
        numbered, first = [], 0
        for left_side, right_side in pairs:
            numbered.append((len(operands), len(operands) + 1, first))
            for side in (left_side, right_side):
                side = side.reshape(-1, side.shape[-1])
                operands.append(jnp.pad(side, ((0, -side.shape[0] % GROUP), (0, 0))))
            first += right_side.shape[-1] // LANES
        parts.append((seg_rows, seg_cols, min(seg_rows, 256 if seg_cols <= 768 else 128), numbered))
    total_rows = matrix_rows() + vec_rows.shape[0]
    most = max(take * seg_cols // LANES for seg_rows, seg_cols, take, pairs in parts)
    return pl.pallas_call(
        functools.partial(grads_kernel, parts, gx_size, gy_size),
        out_shape=[
            jax.ShapeDtypeStruct((total_rows, LANES), jnp.float32),
            jax.ShapeDtypeStruct((gx_size,) + token_grads.shape, token_grads.dtype),
        ],
        in_specs=[pl.BlockSpec(memory_space=pltpu.VMEM)] * (len(operands) + 2),
        out_specs=[pl.BlockSpec(memory_space=pl.ANY)] * 2,
        scratch_shapes=[
            pltpu.VMEM((2, most, LANES), jnp.float32),
            pltpu.SemaphoreType.DMA,
            pltpu.SemaphoreType.DMA((2,)),
        ]
        + share_sems(gx_size, gy_size),
        compiler_params=pltpu.CompilerParams(
            collective_id=number, has_side_effects=True, vmem_limit_bytes=56 << 20
        ),
        name="weight_grads",
    )(*operands, vec_rows, token_grads)


def exchange_kernel(gx_size, gy_size, many, *refs):
    blocks, outs = refs[:many], refs[many : 2 * many]
    send_sem, recv_sem, own_sem = refs[2 * many :]
    count = gx_size * gy_size
    me = linear_index(gy_size)
    barrier = pltpu.get_barrier_semaphore()

    def device(step):
        other = lax.rem(me + step, count)
        return (other // gy_size, lax.rem(other, gy_size))

    def greet(step, carry):
        pl.semaphore_signal(barrier, inc=1, device_id=device(step), device_id_type=MESH)
        return carry

    lax.fori_loop(1, count, greet, 0)
    own = [
        pltpu.make_async_copy(block, out.at[me], own_sem.at[i])
        for i, (block, out) in enumerate(zip(blocks, outs))
    ]
    for copy in own:
        copy.start()
    pl.semaphore_wait(barrier, count - 1)

    def send(step, carry):
        for i, (block, out) in enumerate(zip(blocks, outs)):
            pltpu.make_async_remote_copy(
                src_ref=block,
                dst_ref=out.at[me],
                send_sem=send_sem.at[i],
                recv_sem=recv_sem.at[i],
                device_id=device(step),
                device_id_type=MESH,
            ).start()
        return carry

    lax.fori_loop(1, count, send, 0)
    for i, out in enumerate(outs):
        own[i].wait()
        others = out.at[pl.ds(0, count - 1)]
        both = pltpu.make_async_remote_copy(
            src_ref=others,
            dst_ref=others,
            send_sem=send_sem.at[i],
            recv_sem=recv_sem.at[i],
            device_id=device(1),
            device_id_type=MESH,
        )
        both.wait_send()
        both.wait_recv()


def exchange_all(blocks, gx_size, gy_size, number, name):
    count, many = gx_size * gy_size, len(blocks)
    return pl.pallas_call(
        functools.partial(exchange_kernel, gx_size, gy_size, many),
        out_shape=[jax.ShapeDtypeStruct((count,) + block.shape, block.dtype) for block in blocks],
        in_specs=[pl.BlockSpec(memory_space=pltpu.VMEM)] * many,
        out_specs=[pl.BlockSpec(memory_space=pltpu.VMEM)] * many,
        scratch_shapes=[pltpu.SemaphoreType.DMA((many,))] * 3,
        compiler_params=pltpu.CompilerParams(
            collective_id=number, has_side_effects=True, vmem_limit_bytes=32 << 20
        ),
        name=name,
    )(*blocks)


class Share:
    def __init__(self, gx_size, gy_size, everyone, send_ref, out_ref, sems):
        gx, self.gy = lax.axis_index("gx"), lax.axis_index("gy")
        self.x_size, self.send_ref, self.out_ref = gx_size // 2, send_ref, out_ref
        self.core, self.x = lax.rem(gx, 2), gx // 2
        (self.own_sem, self.row_send, self.row_recv, self.x_send, self.x_recv, self.core_send, self.core_recv) = sems
        self.rows = [(gx, lax.rem(self.gy + d, gy_size)) for d in range(1, gy_size)]
        self.along_x, self.sibling = [], []
        if everyone:
            self.along_x = [
                (lax.rem(self.x + d, self.x_size) * 2 + self.core, self.gy) for d in range(1, self.x_size)
            ]
            self.sibling = [(self.x * 2 + 1 - self.core, self.gy)]
        self.mine = out_ref.at[gx if everyone else 0]

    def greet(self):
        greet_all(self.rows + self.along_x + self.sibling)

    def own(self):
        return pltpu.make_async_copy(self.send_ref.at[self.gy], self.mine.at[self.gy], self.own_sem)

    def row(self, d):
        other = self.rows[d]
        return remote(self.send_ref.at[other[1]], self.mine.at[self.gy], self.row_send.at[d], self.row_recv.at[d], other)

    def group(self, d):
        return remote(self.mine, self.mine, self.x_send.at[d], self.x_recv.at[d], self.along_x[d])

    def across(self, i, source):
        return remote(source, source, self.core_send.at[i], self.core_recv.at[i], self.sibling[0])

    def begin(self):
        self.own().start()
        for d in range(len(self.rows)):
            self.row(d).start()

    def middle(self):
        self.own().wait()
        for d in range(len(self.rows)):
            self.row(d).wait_recv()
        for d in range(len(self.along_x)):
            self.group(d).start()
        if self.sibling:
            self.across(0, self.mine).start()

    def rest(self):
        for d in range(len(self.along_x)):
            self.group(d).wait_recv()
            sender = lax.rem(self.x + self.x_size - d - 1, self.x_size) * 2 + self.core
            self.across(d + 1, self.out_ref.at[sender]).start()

    def finish(self):
        for d in range(len(self.rows)):
            self.row(d).wait_send()
        for d in range(len(self.along_x)):
            self.group(d).wait_send()
        for i in range(self.x_size if self.sibling else 0):
            self.across(i, self.mine).wait_send()
            self.across(i, self.mine).wait_recv()


def share_sems(gx_size, gy_size):
    dma, x_size = pltpu.SemaphoreType.DMA, gx_size // 2
    return [dma, dma((gy_size - 1,)), dma((gy_size - 1,)), dma((x_size,)), dma((x_size,)), dma((x_size,)), dma((x_size,))]


class Places:
    def __init__(self, sizes):
        self.x_size, self.low_size, self.high_size = sizes
        self.mixed = self.x_size == self.low_size
        self.gy_size = self.high_size * self.low_size
        gx, gy = lax.axis_index("gx"), lax.axis_index("gy")
        self.core, x = lax.rem(gx, 2), gx // 2
        self.h, low = gy // self.low_size, lax.rem(gy, self.low_size)
        self.a, self.b = self.turned(self.core, x, low)
        self.a_size, self.b_size = self.x_size, self.low_size

    def turned(self, side, a, b):
        if not self.mixed:
            return a, b
        return a * (1 - side) + b * side, b * (1 - side) + a * side

    def device(self, side, a, b, h):
        dev_x, dev_low = self.turned(side, a, b)
        return (dev_x * 2 + side, h * self.low_size + dev_low)

    def linear(self, side, a, b, h):
        gx, gy = self.device(side, a, b, h)
        return gx * self.gy_size + gy

    def sibling(self):
        a, b = (self.b, self.a) if self.mixed else (self.a, self.b)
        return self.device(1 - self.core, a, b, self.h)

    def along_a(self):
        return [
            self.device(self.core, lax.rem(self.a + d, self.a_size), self.b, self.h)
            for d in range(1, self.a_size)
        ]

    def along_b(self):
        return [
            self.device(self.core, self.a, lax.rem(self.b + d, self.b_size), self.h)
            for d in range(1, self.b_size)
        ]

    def along_h(self):
        return [
            self.device(self.core, self.a, self.b, lax.rem(self.h + d, self.high_size))
            for d in range(1, self.high_size)
        ]


def greet_all(others):
    barrier = pltpu.get_barrier_semaphore()
    for other in others:
        pl.semaphore_signal(barrier, inc=1, device_id=other, device_id_type=MESH)
    pl.semaphore_wait(barrier, len(others))


def remote(src, dst, send_sem, recv_sem, other):
    return pltpu.make_async_remote_copy(
        src_ref=src, dst_ref=dst, send_sem=send_sem, recv_sem=recv_sem, device_id=other, device_id_type=MESH
    )


def axis_sizes(gx_size, gy_size):
    return gx_size // 2, gy_size // 4, 4


NO_TOKEN = 65535


def route_capacity(tokens, gy_size):
    return GROUP * (1 + 17 * tokens // (16 * gy_size * GROUP))


def table_sum_kernel(cap, counts_ref, index_ref, rows_ref, out_ref, square_ref, wide, row_sem):
    sources = rows_ref.shape[0]
    vocab = out_ref.shape[0] - 8

    def fetch(source):
        slot = lax.rem(source, 2)
        return pltpu.make_async_copy(rows_ref.at[source], wide.at[slot], row_sem.at[slot])

    fetch(0).start()
    block = 32 if vocab % 32 == 0 else 8

    def clear(i, carry):
        out_ref[pl.ds(pl.multiple_of(i * block, 8), block), :] = jnp.zeros((block, D_TXT), jnp.float32)
        return carry

    lax.fori_loop(0, vocab // block, clear, 0)
    out_ref[vocab:, :] = jnp.zeros((8, D_TXT), jnp.float32)

    def one_source(source, carry):
        slot = lax.rem(source, 2)

        @pl.when(source + 1 < sources)
        def _():
            fetch(source + 1).start()

        fetch(source).wait()
        widened = wide.at[slot]

        def add(group, carry):
            rows = widened[pl.ds(pl.multiple_of(group * GROUP, GROUP), GROUP), :].astype(jnp.float32)
            for half in range(0, GROUP, 8):
                places = [
                    pl.ds(index_ref[source * cap + group * GROUP + half + i], 1) for i in range(8)
                ]
                sums = [out_ref[place, :] + rows[half + i : half + i + 1, :] for i, place in enumerate(places)]
                for place, value in zip(places, sums):
                    out_ref[place, :] = value
            return carry

        lax.fori_loop(0, (counts_ref[source] + GROUP - 1) // GROUP, add, 0)
        return carry

    lax.fori_loop(0, sources, one_source, 0)

    def square(i, carry):
        part = out_ref[pl.ds(pl.multiple_of(i * block, 8), block), :]
        part = part * part
        total = carry
        for r in range(0, block, 8):
            total = total + part[r : r + 8]
        return total

    square_ref[...] = lax.fori_loop(0, vocab // block, square, jnp.zeros((8, D_TXT), jnp.float32))


def table_sum(counts, index, rows, vocab):
    sources, cap = rows.shape[0], rows.shape[1]
    return pl.pallas_call(
        functools.partial(table_sum_kernel, cap),
        out_shape=[
            jax.ShapeDtypeStruct((vocab + 8, D_TXT), jnp.float32),
            jax.ShapeDtypeStruct((8, D_TXT), jnp.float32),
        ],
        in_specs=[pl.BlockSpec(memory_space=pltpu.SMEM)] * 2 + [pl.BlockSpec(memory_space=pl.ANY)],
        out_specs=[pl.BlockSpec(memory_space=pltpu.VMEM)] * 2,
        scratch_shapes=[pltpu.VMEM((2, cap, D_TXT), jnp.bfloat16), pltpu.SemaphoreType.DMA((2,))],
        compiler_params=pltpu.CompilerParams(vmem_limit_bytes=40 << 20),
        name="table_sum",
    )(counts, index, rows)


def ranks(flags):
    tokens = flags.shape[-1]
    before = (jnp.arange(tokens)[:, None] < jnp.arange(tokens)[None, :]).astype(jnp.bfloat16)
    return fwd_dot(flags.astype(jnp.bfloat16), before).astype(jnp.int32)


def pick_matrix(slots, count):
    return (jnp.arange(count)[:, None] == slots[None, :]).astype(jnp.bfloat16)


def gather_kernel(sizes, chunks, window_ref, out_ref, own_sem, h_send, h_recv, b_send, b_recv, a_send, a_recv, core_send,
                  core_recv):
    at = Places(sizes)
    rows = window_ref.shape[0]
    chunk = rows // chunks
    me = at.linear(at.core, at.a, at.b, at.h)
    sibling, peers_a, peers_b, peers_h = at.sibling(), at.along_a(), at.along_b(), at.along_h()
    greet_all([sibling] + peers_a + peers_b + peers_h)

    def part(block, t):
        return out_ref.at[pl.ds(pl.multiple_of(block * rows + t * chunk, GROUP), chunk)]

    def many(count):
        return out_ref.at[pl.ds(0, count * chunk)]

    def own_copy(t):
        src = window_ref.at[pl.ds(pl.multiple_of(t * chunk, GROUP), chunk)]
        return src, pltpu.make_async_copy(src, part(me, t), own_sem.at[t])

    def stage_h(t):
        src, own = own_copy(t)
        for d, other in enumerate(peers_h):
            remote(src, part(me, t), h_send.at[d], h_recv.at[t, d], other).start()
        own.start()

    def stage_b(t):
        own_copy(t)[1].wait()
        for d, other in enumerate(peers_h):
            remote(many(1), many(1), h_send.at[d], h_recv.at[t, d], other).wait_recv()
        for d, other in enumerate(peers_b):
            for h in range(at.high_size):
                block = part(at.linear(at.core, at.a, at.b, h), t)
                remote(block, block, b_send.at[d], b_recv.at[t, d], other).start()

    def stage_a(t):
        for d, other in enumerate(peers_b):
            remote(many(at.high_size), many(at.high_size), b_send.at[d], b_recv.at[t, d], other).wait_recv()
        for d, other in enumerate(peers_a):
            for b in range(at.b_size):
                for h in range(at.high_size):
                    block = part(at.linear(at.core, at.a, b, h), t)
                    remote(block, block, a_send.at[d], a_recv.at[t, d], other).start()

    plane = at.b_size * at.high_size

    def stage_core(t):
        for d, other in enumerate(peers_a):
            remote(many(plane), many(plane), a_send.at[d], a_recv.at[t, d], other).wait_recv()
        for a in range(at.a_size):
            for b in range(at.b_size):
                for h in range(at.high_size):
                    block = part(at.linear(at.core, a, b, h), t)
                    remote(block, block, core_send, core_recv, sibling).start()

    def turn(t, carry):
        for depth, stage in enumerate((stage_h, stage_b, stage_a, stage_core)):
            @pl.when((t >= depth) & (t < chunks + depth))
            def _():
                stage(t - depth)

        return carry

    lax.fori_loop(0, chunks + 3, turn, 0)

    def whole(count):
        return out_ref.at[pl.ds(0, count * rows)]

    for d, other in enumerate(peers_h):
        remote(whole(1), whole(1), h_send.at[d], h_recv.at[0, d], other).wait_send()
    for d, other in enumerate(peers_b):
        remote(whole(at.high_size), whole(at.high_size), b_send.at[d], b_recv.at[0, d], other).wait_send()
    for d, other in enumerate(peers_a):
        remote(whole(plane), whole(plane), a_send.at[d], a_recv.at[0, d], other).wait_send()
    half = whole(at.a_size * plane)
    last = remote(half, half, core_send, core_recv, sibling)
    last.wait_send()
    last.wait_recv()


def gather_windows(window, gx_size, gy_size, chunks, number, name):
    sizes = axis_sizes(gx_size, gy_size)
    a, b, h = sizes[0] - 1, sizes[1] - 1, sizes[2] - 1
    dma = pltpu.SemaphoreType.DMA
    return pl.pallas_call(
        functools.partial(gather_kernel, sizes, chunks),
        out_shape=jax.ShapeDtypeStruct((gx_size * gy_size * window.shape[0], LANES), window.dtype),
        in_specs=[pl.BlockSpec(memory_space=pltpu.VMEM)],
        out_specs=pl.BlockSpec(memory_space=pl.ANY),
        scratch_shapes=[dma((chunks,)), dma((h,)), dma((chunks, h)), dma((b,)), dma((chunks, b)), dma((a,)),
                        dma((chunks, a)), dma, dma],
        compiler_params=pltpu.CompilerParams(
            collective_id=number, has_side_effects=True, vmem_limit_bytes=32 << 20
        ),
        name=name,
    )(window)


def reduce_kernel(shard, sizes, grads_ref, out_ref, own, landed, keep_one, send_one, recv_one, keep_two, send_two,
                  recv_two, keep_three, send_three, recv_three, load_sem, pair_send, pair_recv, credit,
                  one_send, one_recv, two_send, two_recv, three_send, three_recv):
    at = Places(sizes)
    a_size, b_size, high_size = at.a_size, at.b_size, at.high_size
    core, my_a, my_b, high = at.core, at.a, at.b, at.h
    plane = b_size * high_size
    chunk = own.shape[2]
    chunks = out_ref.shape[0] // chunk

    def start_row(side, number):
        a, rest = number // plane, lax.rem(number, plane)
        return window_start(shard, at.linear(side, a, rest // high_size, lax.rem(rest, high_size)))

    sibling, peers, peers_two, peers_three = at.sibling(), at.along_a(), at.along_b(), at.along_h()
    greet_all([sibling] + peers + peers_two + peers_three)
    blocks = a_size * plane

    def pair_stage(t):
        slot = lax.rem(t, 2)

        @pl.when(t >= 2)
        def _():
            pl.semaphore_wait(credit, 1)

        def each(number, carry):
            theirs = pl.multiple_of(start_row(1 - core, number) + t * chunk, GROUP)
            mine = pl.multiple_of(start_row(core, number) + t * chunk, GROUP)
            remote(
                grads_ref.at[pl.ds(theirs, chunk)], landed.at[slot, number], pair_send.at[slot], pair_recv.at[slot], sibling
            ).start()
            pltpu.make_async_copy(
                grads_ref.at[pl.ds(mine, chunk)], own.at[slot, number], load_sem.at[slot]
            ).start()
            return carry

        lax.fori_loop(0, blocks, each, 0)

    def first_stage(u):
        slot = lax.rem(u, 2)
        both = remote(landed.at[slot], landed.at[slot], pair_send.at[slot], pair_recv.at[slot], sibling)
        pltpu.make_async_copy(own.at[slot], own.at[slot], load_sem.at[slot]).wait()
        both.wait_send()
        both.wait_recv()
        for d in range(1, a_size):
            @pl.when(u >= 2)
            def _():
                remote(send_one.at[slot, d - 1], recv_one.at[u - 2, d - 1], one_send.at[slot, d - 1],
                       one_recv.at[u - 2, d - 1], peers[d - 1]).wait_send()

            first = lax.rem(my_a + d, a_size) * plane

            def give(i, carry):
                send_one[slot, d - 1, i] = (own[slot, first + i] + landed[slot, first + i]).astype(jnp.bfloat16)
                return carry

            lax.fori_loop(0, plane, give, 0)
            remote(send_one.at[slot, d - 1], recv_one.at[u, d - 1], one_send.at[slot, d - 1],
                   one_recv.at[u, d - 1], peers[d - 1]).start()

        def hold(i, carry):
            keep_one[slot, i] = own[slot, my_a * plane + i] + landed[slot, my_a * plane + i]
            return carry

        lax.fori_loop(0, plane, hold, 0)

        @pl.when(u < chunks - 2)
        def _():
            pl.semaphore_signal(credit, inc=1, device_id=sibling, device_id_type=MESH)

    def second_stage(u):
        slot = lax.rem(u, 2)
        for d in range(1, a_size):
            remote(recv_one.at[u, d - 1], recv_one.at[u, d - 1], one_send.at[slot, d - 1], one_recv.at[u, d - 1],
                   peers[d - 1]).wait_recv()

        def total(number):
            value = keep_one[slot, number]
            for d in range(1, a_size):
                value = value + recv_one[u, d - 1, number].astype(jnp.float32)
            return value

        for d in range(1, b_size):
            @pl.when(u >= 2)
            def _():
                remote(send_two.at[slot, d - 1], recv_two.at[u - 2, d - 1], two_send.at[slot, d - 1],
                       two_recv.at[u - 2, d - 1], peers_two[d - 1]).wait_send()

            first = lax.rem(my_b + d, b_size) * high_size

            def give(i, carry):
                send_two[slot, d - 1, i] = total(first + i).astype(jnp.bfloat16)
                return carry

            lax.fori_loop(0, high_size, give, 0)
            remote(send_two.at[slot, d - 1], recv_two.at[u, d - 1], two_send.at[slot, d - 1],
                   two_recv.at[u, d - 1], peers_two[d - 1]).start()

        def hold(i, carry):
            keep_two[slot, i] = total(my_b * high_size + i)
            return carry

        lax.fori_loop(0, high_size, hold, 0)

    def third_stage(u):
        slot = lax.rem(u, 2)
        for d in range(1, b_size):
            remote(recv_two.at[u, d - 1], recv_two.at[u, d - 1], two_send.at[slot, d - 1], two_recv.at[u, d - 1],
                   peers_two[d - 1]).wait_recv()

        def total(number):
            value = keep_two[slot, number]
            for d in range(1, b_size):
                value = value + recv_two[u, d - 1, number].astype(jnp.float32)
            return value

        for d in range(1, high_size):
            @pl.when(u >= 2)
            def _():
                remote(send_three.at[slot, d - 1], recv_three.at[u - 2, d - 1], three_send.at[slot, d - 1],
                       three_recv.at[u - 2, d - 1], peers_three[d - 1]).wait_send()

            send_three[slot, d - 1] = total(lax.rem(high + d, high_size)).astype(jnp.bfloat16)
            remote(send_three.at[slot, d - 1], recv_three.at[u, d - 1], three_send.at[slot, d - 1],
                   three_recv.at[u, d - 1], peers_three[d - 1]).start()
        keep_three[slot] = total(high)

    def last_stage(u):
        slot = lax.rem(u, 2)
        value = keep_three[slot]
        for d in range(1, high_size):
            remote(recv_three.at[u, d - 1], recv_three.at[u, d - 1], three_send.at[slot, d - 1],
                   three_recv.at[u, d - 1], peers_three[d - 1]).wait_recv()
            value = value + recv_three[u, d - 1].astype(jnp.float32)
        out_ref[pl.ds(pl.multiple_of(u * chunk, GROUP), chunk), :] = value

    def turn(t, carry):
        stages = (pair_stage, first_stage, second_stage, third_stage, last_stage)
        for depth, stage in enumerate(stages):
            @pl.when((t >= depth) & (t < chunks + depth))
            def _():
                stage(t - depth)

        return carry

    lax.fori_loop(0, chunks + 4, turn, 0)
    for u in range(max(chunks - 2, 0), chunks):
        slot = u % 2
        for d in range(1, a_size):
            remote(send_one.at[slot, d - 1], recv_one.at[u, d - 1], one_send.at[slot, d - 1],
                   one_recv.at[u, d - 1], peers[d - 1]).wait_send()
        for d in range(1, b_size):
            remote(send_two.at[slot, d - 1], recv_two.at[u, d - 1], two_send.at[slot, d - 1],
                   two_recv.at[u, d - 1], peers_two[d - 1]).wait_send()
        for d in range(1, high_size):
            remote(send_three.at[slot, d - 1], recv_three.at[u, d - 1], three_send.at[slot, d - 1],
                   three_recv.at[u, d - 1], peers_three[d - 1]).wait_send()


def reduce_windows(grads, shard, gx_size, gy_size, number):
    rows = window_rows(shard, GROUP * CHUNKS)
    chunk = rows // CHUNKS
    x_size, low_size, high_size = axis_sizes(gx_size, gy_size)
    plane = low_size * high_size
    blocks = x_size * plane
    low_type, dma = jnp.bfloat16, pltpu.SemaphoreType.DMA
    a, b, h = x_size - 1, low_size - 1, high_size - 1
    return pl.pallas_call(
        functools.partial(reduce_kernel, shard, (x_size, low_size, high_size)),
        out_shape=jax.ShapeDtypeStruct((rows, LANES), jnp.float32),
        in_specs=[pl.BlockSpec(memory_space=pl.ANY)],
        out_specs=pl.BlockSpec(memory_space=pltpu.VMEM),
        scratch_shapes=[
            pltpu.VMEM((2, blocks, chunk, LANES), jnp.float32),
            pltpu.VMEM((2, blocks, chunk, LANES), jnp.float32),
            pltpu.VMEM((2, plane, chunk, LANES), jnp.float32),
            pltpu.VMEM((2, a, plane, chunk, LANES), low_type),
            pltpu.VMEM((CHUNKS, a, plane, chunk, LANES), low_type),
            pltpu.VMEM((2, high_size, chunk, LANES), jnp.float32),
            pltpu.VMEM((2, b, high_size, chunk, LANES), low_type),
            pltpu.VMEM((CHUNKS, b, high_size, chunk, LANES), low_type),
            pltpu.VMEM((2, chunk, LANES), jnp.float32),
            pltpu.VMEM((2, h, chunk, LANES), low_type),
            pltpu.VMEM((CHUNKS, h, chunk, LANES), low_type),
            dma((2,)),
            dma((2,)),
            dma((2,)),
            pltpu.SemaphoreType.REGULAR,
            dma((2, a)),
            dma((CHUNKS, a)),
            dma((2, b)),
            dma((CHUNKS, b)),
            dma((2, h)),
            dma((CHUNKS, h)),
        ],
        compiler_params=pltpu.CompilerParams(
            collective_id=number, has_side_effects=True, vmem_limit_bytes=60 << 20
        ),
        name="reduce_windows",
    )(grads)


def log_sums(rows, columns, column_ok, logit_scale, matches):
    total, taken = rows.shape[0], min(rows.shape[0], 256)

    def some(args):
        row_part, match_part = args
        logits = logit_scale * back_dot(row_part, columns)
        masked = jnp.where(column_ok[None, :], logits, -1e30)
        row_max = jnp.max(masked, 1, keepdims=True)
        log_total = row_max[:, 0] + jnp.log(jnp.sum(jnp.exp(masked - row_max), 1))
        gap = jnp.where(match_part > 0.0, logits[:, :total] - log_total[:, None], 0.0)
        return log_total, -jnp.sum(gap)

    if taken == total:
        return some((rows, matches))
    logs, parts = lax.map(
        some, (rows.reshape(-1, taken, rows.shape[1]), matches.reshape(-1, taken, total))
    )
    return logs.reshape(-1), jnp.sum(parts)


def side_grads(row_embed, columns, column_ok, same_own, positives_own, log_own, logit_scale, total_count):
    dot_vals = back_dot(row_embed, columns)
    masked = jnp.where(column_ok[None, :], logit_scale * dot_vals, -1e30)
    extra = columns.shape[0] - same_own.shape[1]
    weights_pos = jnp.concatenate(
        [same_own, jnp.zeros((same_own.shape[0], extra), jnp.float32)], 1
    )
    grad_logits = (
        positives_own[:, None] * jnp.exp(masked - log_own[:, None]) - weights_pos
    ) / total_count
    grad_dots = (logit_scale * grad_logits).astype(jnp.bfloat16)
    grad_temper = logit_scale * jnp.sum(grad_logits * dot_vals)
    return fwd_dot(grad_dots, columns), grad_temper


def cross_grads(rows, own, valid_own, same_own, positives_all, logs, logit_scale, total_count):
    logits = logit_scale * back_dot(rows, own)
    masked = jnp.where(valid_own[None, :], logits, -1e30)
    grad_logits = (
        positives_all[:, None] * jnp.exp(masked - logs[:, None]) - same_own.T
    ) / total_count
    grad_dots = (logit_scale * grad_logits).astype(jnp.bfloat16)
    return weight_grad(grad_dots, rows)


def body(
    flat_master,
    flat_first,
    flat_second,
    table,
    table_first,
    table_second,
    pixels,
    token_ids,
    end_pos,
    pair_counts,
    groups,
    cached_image,
    cached_text,
):
    gx_size, gy_size = lax.axis_size("gx"), lax.axis_size("gy")
    device_count = gx_size * gy_size
    my_index = linear_index(gy_size)
    pairs_dev = pixels.shape[0]
    shard = flat_master.shape[0]
    tokens = token_ids.size
    vocab_dev = table.shape[0]
    cap = route_capacity(tokens, gy_size)
    own_ids = token_ids.reshape(-1)
    same = own_ids[:, None] == own_ids[None, :]
    order = jnp.arange(tokens)
    leading = ~jnp.any(same & (order[None, :] < order[:, None]), 1)
    flat_ids = jnp.where(leading, own_ids, NO_TOKEN)
    flat_ids = jnp.pad(flat_ids, (0, ID_ROWS * LANES // 2 - tokens)).reshape(-1, LANES)
    payload = [
        place_window(flat_master, gy_size),
        jnp.concatenate([cached_image, cached_text], 0).reshape(CACHED_ROWS, LANES),
        jnp.concatenate([flat_ids // 256, flat_ids % 256], 0).astype(jnp.bfloat16),
    ]
    used = sum(part.shape[0] for part in payload)
    step = GROUP * GATHER_CHUNKS
    payload = jnp.pad(jnp.concatenate(payload, 0), ((0, -used % step), (0, 0)))
    gathered = gather_windows(payload, gx_size, gy_size, GATHER_CHUNKS, 4, "gather_weights")
    every_part = gathered.reshape(device_count, -1, LANES)
    cached = every_part[:, used - ID_ROWS - CACHED_ROWS : used - ID_ROWS].reshape(device_count, -1, EMBED)
    cache_img, cache_txt = lax.optimization_barrier((cached[:, :pairs_dev], cached[:, pairs_dev:]))
    cache_img, cache_txt = cache_img.reshape(-1, EMBED), cache_txt.reshape(-1, EMBED)
    coded = every_part[:, used - ID_ROWS : used].astype(jnp.int32)
    ids_all = coded[:, : ID_ROWS // 2] * 256 + coded[:, ID_ROWS // 2 :]
    ids_all = ids_all.reshape(device_count, -1)[:, :tokens]
    holders = ids_all // vocab_dev
    pair_rows = jnp.sum(holders[:, :, None] == jnp.arange(gy_size), 1)
    rounds = (jnp.max(pair_rows) + cap - 1) // cap
    me_y = lax.axis_index("gy")
    held = holders == me_y
    held_rank = jnp.where(held, ranks(held), -1)
    held_row = ids_all - me_y * vocab_dev
    held_count = jnp.sum(held, 1)
    own_flags = (jnp.arange(gy_size)[:, None] == own_ids[None, :] // vocab_dev) & leading[None, :]
    own_place = jnp.arange(gy_size)[:, None] * tokens + ranks(own_flags)
    own_place = jnp.sum(jnp.where(own_flags, own_place, 0), 0)
    own_place = jnp.sum(jnp.where(same & leading[None, :], own_place[None, :], 0), 1)
    own_holder, own_rank = own_place // tokens, own_place % tokens

    def held_rows(turn):
        slots = held_rank - turn * cap
        found = slots[:, None, :] == jnp.arange(cap)[None, :, None]
        return vocab_dev + jnp.sum(jnp.where(found, held_row[:, None, :] - vocab_dev, 0), 2)

    def own_slots(turn):
        rank = own_rank - turn * cap
        return jnp.where((rank >= 0) & (rank < cap), own_holder * cap + rank, -1)

    first_rows = held_rows(0)
    group_start = lax.axis_index("gx") * gy_size

    def rows_to_send(index):
        index = lax.dynamic_slice_in_dim(index, group_start, gy_size, 0)
        return lax.optimization_barrier(jnp.take(table, index.reshape(-1), axis=0, mode="clip")).astype(jnp.bfloat16)

    sent = rows_to_send(first_rows).reshape(gy_size, cap, D_TXT)
    *spread, landed = spread_weights(gathered, sent, shard, gx_size, gy_size, 5)
    slot_count = gy_size * cap
    picks = pick_matrix(own_slots(0), slot_count)
    token_rows = weight_grad(picks, landed.reshape(slot_count, D_TXT)).astype(jnp.bfloat16)

    def more_rows(turn, found):
        rows = rows_to_send(held_rows(turn)).reshape(gy_size, cap, D_TXT)
        rows = lax.all_to_all(rows, "gy", 0, 0, tiled=True).reshape(slot_count, D_TXT)
        return found + weight_grad(pick_matrix(own_slots(turn), slot_count), rows).astype(jnp.bfloat16)

    token_rows = lax.cond(
        rounds > 1, lambda rows: lax.fori_loop(1, rounds, more_rows, rows), lambda rows: rows, token_rows
    )
    image_weights = dict(zip(IMAGE.names, spread[:5]))
    text_weights = dict(zip(TEXT.names, spread[5:9]))
    image_vec, text_vec, temper = split_vectors(spread[9])
    image_gains, image_base, image_rows = image_inputs(image_vec, pixels)
    text_gains, text_base, text_rows = text_inputs(text_vec, token_rows)
    image_kept = tower_forward(IMAGE, end_pos, image_gains, image_base, image_rows, image_weights)
    text_kept = tower_forward(TEXT, end_pos, text_gains, text_base, text_rows, text_weights)
    image_emb = image_kept[14].astype(jnp.bfloat16)
    text_emb = text_kept[14].astype(jnp.bfloat16)
    embeds = jnp.concatenate([image_emb, text_emb], 0).reshape(-1, LANES)
    embeds = gather_windows(embeds, gx_size, gy_size, 1, 0, "embeddings")
    embeds = embeds.reshape(device_count, 2 * pairs_dev, EMBED)
    all_img, all_txt = lax.optimization_barrier((embeds[:, :pairs_dev], embeds[:, pairs_dev:]))
    all_img, all_txt = all_img.reshape(-1, EMBED), all_txt.reshape(-1, EMBED)
    total_pairs = all_img.shape[0]
    valid_all = jnp.arange(total_pairs) % pairs_dev < jnp.repeat(pair_counts.reshape(-1), pairs_dev)
    matches = (
        (groups[:, None] == groups[None, :]) & valid_all[:, None] & valid_all[None, :]
    ).astype(jnp.float32)
    positives_all = jnp.sum(matches, 1)
    total_count = 2.0 * jnp.sum(positives_all)
    own_start = my_index * pairs_dev
    own_part = functools.partial(
        lax.dynamic_slice_in_dim, start_index=own_start, slice_size=pairs_dev, axis=0
    )
    same_own, positives_own, valid_own = own_part(matches), own_part(positives_all), own_part(valid_all)
    logit_scale = jnp.exp(temper)
    column_ok = jnp.concatenate([valid_all, jnp.ones((cache_img.shape[0],), jnp.bool_)])
    columns_txt = jnp.concatenate([all_txt, cache_txt])
    columns_img = jnp.concatenate([all_img, cache_img])
    log_img, loss_one = log_sums(all_img, columns_txt, column_ok, logit_scale, matches)
    log_txt, loss_two = log_sums(all_txt, columns_img, column_ok, logit_scale, matches)
    loss_sum = loss_one + loss_two
    grad_img, temper_one = side_grads(
        image_emb, columns_txt, column_ok, same_own, positives_own, own_part(log_img), logit_scale, total_count
    )
    grad_txt, temper_two = side_grads(
        text_emb, columns_img, column_ok, same_own, positives_own, own_part(log_txt), logit_scale, total_count
    )
    grad_img = grad_img + cross_grads(
        all_txt, image_emb, valid_own, same_own, positives_all, log_txt, logit_scale, total_count
    )
    grad_txt = grad_txt + cross_grads(
        all_img, text_emb, valid_own, same_own, positives_all, log_img, logit_scale, total_count
    )
    text_grads = tower_backward(TEXT, end_pos, text_gains, grad_txt, text_kept[:14], text_weights)
    grad_rows = text_grads[6][: SEQS * CTX]
    to_holders = fwd_dot(picks, grad_rows).astype(jnp.bfloat16).reshape(gy_size, cap, D_TXT)
    image_grads = tower_backward(IMAGE, end_pos, image_gains, grad_img, image_kept[:14], image_weights)
    pair_lists = ([(image_rows, image_grads[6])],) + grad_pairs(image_kept, image_grads)
    pair_lists = pair_lists + grad_pairs(text_kept, text_grads)
    total_rows = window_start(shard, device_count - 1) + window_rows(shard, GROUP * CHUNKS)
    vec_rows = jnp.concatenate(
        [
            image_grads[7][:1].reshape(-1, LANES),
            image_grads[7].reshape(-1, LANES),
            image_grads[8].reshape(-1, LANES),
            text_grads[7].reshape(-1, LANES),
            text_grads[8][2:].reshape(-1, LANES),
            jnp.pad((temper_one + temper_two).reshape(1, 1), ((0, 0), (0, LANES - 1))),
        ]
    )
    vec_rows = jnp.pad(vec_rows, ((0, total_rows - matrix_rows() - vec_rows.shape[0]), (0, 0)))
    local_grads, arrived = weight_grads(pair_lists, vec_rows, to_holders, gx_size, gy_size, 6)
    table_grad, table_square = table_sum(
        jnp.minimum(held_count, cap),
        first_rows.reshape(-1),
        arrived.reshape(device_count, cap, D_TXT),
        vocab_dev,
    )

    def more_grads(turn, total):
        rows = fwd_dot(pick_matrix(own_slots(turn), slot_count), grad_rows).astype(jnp.bfloat16)
        rows = lax.all_to_all(rows.reshape(gy_size, cap, D_TXT), "gy", 0, 0, tiled=True)
        rows = lax.all_gather(rows, "gx", axis=0).reshape(device_count * cap, D_TXT).astype(jnp.float32)
        return total.at[held_rows(turn).reshape(-1)].add(rows)

    table_grad, table_squares = lax.cond(
        rounds > 1,
        lambda total, square: (
            lambda whole: (whole, jnp.sum(whole[:vocab_dev] * whole[:vocab_dev]))
        )(lax.fori_loop(1, rounds, more_grads, total)),
        lambda total, square: (total, jnp.sum(square)),
        table_grad,
        table_square,
    )
    grad_window = reduce_windows(local_grads, shard, gx_size, gy_size, 1)
    grad_shard = lift_window(grad_window, shard, gy_size)
    table_squares = jnp.where(lax.axis_index("gx") == 0, table_squares, 0.0)
    squares = jnp.sum(grad_shard * grad_shard) + table_squares
    (every,) = exchange_all([jnp.full((8, LANES), squares)], gx_size, gy_size, 2, "squares")
    grad_norm = jnp.sqrt(jnp.sum(every[:, 0, 0]))
    factor = jnp.minimum(1.0, clip_limit / (grad_norm + 1e-06))
    matrix_stop = matrix_rows() * LANES
    position = my_index * shard + jnp.arange(shard)
    is_matrix = position < matrix_stop
    rates = jnp.where(is_matrix, rate_matrix, rate_vector)
    decays = jnp.where(is_matrix, decay_rate, 0.0)
    master_out, first_out, second_out = adam_step(
        flat_master, flat_first, flat_second, grad_shard * factor, rates, decays
    )
    table_out, table_first_out, table_second_out = adam_step(
        table, table_first, table_second, table_grad[:vocab_dev] * factor, rate_table, 0.0
    )
    return (
        master_out,
        first_out,
        second_out,
        table_out,
        table_first_out,
        table_second_out,
        loss_sum,
        total_count,
        grad_norm,
    )


def solution(mesh):
    placed = (
        P(("gx", "gy")),
        P(("gx", "gy")),
        P(("gx", "gy")),
        P("gy", None),
        P("gy", None),
        P("gy", None),
        P(("gx", "gy"), None, None),
        P(("gx", "gy"), None),
        P(("gx", "gy")),
        P(),
        P(),
        P(("gx", "gy"), None),
        P(("gx", "gy"), None),
    )
    return jax.shard_map(
        body,
        mesh=mesh,
        in_specs=placed,
        out_specs=(
            P(("gx", "gy")),
            P(("gx", "gy")),
            P(("gx", "gy")),
            P("gy", None),
            P("gy", None),
            P("gy", None),
            P(),
            P(),
            P(),
        ),
        check_vma=False,
    )
```

```python
import functools

import jax
import jax.numpy as jnp
from jax import lax
from jax.experimental import pallas as pl
from jax.experimental.pallas import tpu as pltpu
from jax.sharding import PartitionSpec as P

D_IMG = 768
IMG_HEADS = 12
IMG_MLP = 3072
PATCH_DIM = 3072
D_TXT = 512
TXT_HEADS = 8
TXT_MLP = 2048
CTX = 77
EMBED = 512
STEP = 10
IMG_TOK = 50


clip_limit = 0.1
beta_one = 0.9
beta_two = 0.999
adam_eps = 1e-08
decay_rate = 0.1
rate_matrix = 0.01
rate_vector = 0.2
rate_table = 0.2
norm_eps = 1e-05


def segment_list():
    return [
        ("patch_embed", PATCH_DIM, D_IMG),
        ("image_attn", D_IMG, 4 * D_IMG),
        ("image_up", D_IMG, IMG_MLP),
        ("image_down", IMG_MLP, D_IMG),
        ("image_proj", D_IMG, EMBED),
        ("text_attn", D_TXT, 4 * D_TXT),
        ("text_up", D_TXT, TXT_MLP),
        ("text_down", TXT_MLP, D_TXT),
        ("text_proj", D_TXT, EMBED),
        ("image_vec", IMG_TOK + 9, D_IMG),
        ("text_vec", CTX + 6, D_TXT),
        ("temper", 1, 1),
    ]


LANES = 128
GROUP = 16
CHUNKS = 16
GATHER_CHUNKS = 14
CACHED_ROWS = 64
ID_ROWS = 16
MESH = pl.DeviceIdType.MESH


def dot_nn(left_side, right_side):
    return lax.dot_general(
        left_side, right_side, (((1,), (0,)), ((), ())), preferred_element_type=jnp.float32
    )


def dot_nt(left_side, right_side):
    return lax.dot_general(
        left_side, right_side, (((1,), (1,)), ((), ())), preferred_element_type=jnp.float32
    )


def dot_tn(left_side, right_side):
    return lax.dot_general(
        left_side, right_side, (((0,), (0,)), ((), ())), preferred_element_type=jnp.float32
    )


def back_dot(left_side, right_side):
    return dot_nt(left_side, right_side)


def fwd_dot(left_side, right_side):
    return dot_nn(left_side, right_side)


def weight_grad(left_side, right_side):
    return dot_tn(left_side, right_side)


def norm_parts(values):
    center = values - jnp.mean(values, -1, keepdims=True)
    scale = lax.rsqrt(jnp.mean(center * center, -1, keepdims=True) + norm_eps)
    return center * scale, scale


def layer_norm(values, gain_vec, shift_vec):
    return norm_parts(values)[0] * gain_vec + shift_vec


def layer_norm_back(values, gain_vec, grad):
    unit, scale = norm_parts(values)
    grad_unit = grad * gain_vec
    inner = jnp.mean(grad_unit, -1, keepdims=True)
    along = jnp.mean(grad_unit * unit, -1, keepdims=True)
    return scale * (grad_unit - inner - unit * along), grad * unit


def sum_rows(values):
    return jnp.sum(values, 0, keepdims=True)


def low16(values):
    return jnp.concatenate([values, jnp.zeros_like(values)], 0).astype(jnp.bfloat16)


SEQS = 8


class Tower:
    def __init__(self, image):
        self.image = image
        self.width = D_IMG if image else D_TXT
        self.heads = IMG_HEADS if image else TXT_HEADS
        self.length = IMG_TOK if image else CTX
        self.rows = -(-SEQS * self.length // GROUP) * GROUP
        self.lanes = 16 if image else 8
        self.queries = SEQS * self.lanes
        self.block = 80 if image else 48
        self.names = ("patch", "attn", "up", "down", "proj") if image else ("attn", "up", "down", "proj")

    def shapes(self):
        width = self.width
        found = dict(attn=(width, 4 * width), up=(width, 4 * width), down=(4 * width, width), proj=(width, EMBED))
        if self.image:
            found["patch"] = (PATCH_DIM, width)
        return found

    def head_mask(self):
        lane = lax.broadcasted_iota(jnp.int32, (self.lanes, self.width), 1)
        row = lax.broadcasted_iota(jnp.int32, (self.lanes, self.width), 0)
        return lane // (self.width // self.heads) == row

    def spread_heads(self, values, wide_ref):
        mask = self.head_mask()
        for s in range(SEQS):
            row = jnp.broadcast_to(values[s : s + 1].astype(jnp.float32), mask.shape)
            wide_ref[s * self.lanes : (s + 1) * self.lanes, :] = jnp.where(mask, row, 0.0)
        return wide_ref[...].astype(jnp.bfloat16)

    def join_heads(self, values, wide_ref):
        mask = self.head_mask()
        wide_ref[...] = values
        rows = [
            sum_rows(jnp.where(mask, wide_ref[s * self.lanes : (s + 1) * self.lanes, :], 0.0))
            for s in range(SEQS)
        ]
        return jnp.concatenate(rows, 0)

    def row_of(self, s, ends_ref):
        return s * self.length + (0 if self.image else ends_ref[s])

    def each_block(self, function, start):
        return lax.fori_loop(
            0,
            self.rows // self.block,
            lambda i, carry: function(pl.ds(pl.multiple_of(i * self.block, GROUP), self.block), carry),
            start,
        )


def tower_fetch(names, sources, landed, sems):
    copies = {
        name: pltpu.make_async_copy(source, ref, sems.at[i])
        for i, (name, source, ref) in enumerate(zip(names, sources, landed))
    }
    for copy in copies.values():
        copy.start()
    return copies, dict(zip(names, landed))


def tower_forward_kernel(tower, *refs):
    count = len(tower.names)
    ends_ref, gains_ref, base_ref, input_ref = refs[:4]
    sources = refs[4 : 4 + count]
    (tokens_ref, normed_ref, pair_ref, normed_own_ref, query_ref, probs_ref, attended_ref, middle_ref, normed_two_ref,
     upper_ref, act_ref, output_ref, head_ref, raw_ref, emb_ref) = refs[4 + count : 19 + count]
    hidden_ref, wide_ref = refs[19 + count : 21 + count]
    landed, sems = refs[21 + count : 21 + 2 * count], refs[21 + 2 * count]
    copies, weights = tower_fetch(tower.names, sources, landed, sems)
    width = tower.width
    gains = [gains_ref[i : i + 1, :] for i in range(8)]
    if tower.image:
        copies["patch"].wait()

        def patch(j, carry):
            cols = pl.ds(pl.multiple_of(j * 256, 256), 256)
            tokens_ref[:, cols] = dot_nn(input_ref[...], weights["patch"][:, cols]) + base_ref[:, cols]
            return carry

        lax.fori_loop(0, width // 256, patch, 0)

    def first(rows, carry):
        if tower.image:
            hidden = layer_norm(tokens_ref[rows, :], gains[0], gains[1])
        else:
            hidden = input_ref[rows, :].astype(jnp.float32) + base_ref[rows, :]
            tokens_ref[rows, :] = hidden
        hidden_ref[rows, :] = hidden
        normed_ref[rows, :] = layer_norm(hidden, gains[2], gains[3]).astype(jnp.bfloat16)
        return carry

    tower.each_block(first, 0)
    copies["attn"].wait()

    def pair(j, carry):
        at = pl.multiple_of(j * 256, 256)
        product = dot_nn(normed_ref[...], weights["attn"][:, pl.ds(width + at, 256)])
        pair_ref[:, pl.ds(at, 256)] = product.astype(jnp.bfloat16)
        return carry

    lax.fori_loop(0, 2 * width // 256, pair, 0)
    hidden_own = jnp.concatenate(
        [hidden_ref[pl.ds(tower.row_of(s, ends_ref), 1), :] for s in range(SEQS)], 0
    )
    normed_own = low16(layer_norm(hidden_own, gains[2], gains[3]))
    normed_own_ref[...] = normed_own
    query = dot_nn(normed_own, weights["attn"][:, :width]).astype(jnp.bfloat16)
    query_ref[...] = query
    queries = tower.spread_heads(query, wide_ref)
    scores = dot_nt(queries, pair_ref[:, :width]) * (width // tower.heads) ** (-0.5)
    row = lax.broadcasted_iota(jnp.int32, scores.shape, 0) // tower.lanes
    spot = lax.broadcasted_iota(jnp.int32, scores.shape, 1) - row * tower.length
    last = jnp.full(scores.shape, tower.length - 1, jnp.int32)
    if not tower.image:
        for s in range(SEQS):
            last = jnp.where(row == s, ends_ref[s], last)
    scores = jnp.where((spot >= 0) & (spot <= last), scores, -1e30)
    powers = jnp.exp(scores - jnp.max(scores, -1, keepdims=True))
    probs = powers / jnp.sum(powers, -1, keepdims=True)
    probs_ref[...] = probs
    attended = low16(tower.join_heads(dot_nn(probs.astype(jnp.bfloat16), pair_ref[:, width:]), wide_ref))
    attended_ref[...] = attended
    middle = hidden_own + dot_nn(attended, weights["attn"][:, 3 * width :])[:SEQS]
    middle_ref[...] = middle
    normed_two_ref[...] = low16(layer_norm(middle, gains[4], gains[5]))
    copies["up"].wait()

    def rise(j, carry):
        cols = pl.ds(pl.multiple_of(j * 512, 512), 512)
        upper = dot_nn(normed_two_ref[...], weights["up"][:, cols])[:SEQS]
        upper_ref[:, cols] = upper
        act_ref[:, cols] = low16(upper * jax.nn.sigmoid(1.702 * upper))
        return carry

    lax.fori_loop(0, 4 * width // 512, rise, 0)
    copies["down"].wait()

    def fall(j, carry):
        cols = pl.ds(pl.multiple_of(j * 256, 256), 256)
        output_ref[:, cols] = middle_ref[:, cols] + dot_nn(act_ref[...], weights["down"][:, cols])[:SEQS]
        return carry

    lax.fori_loop(0, width // 256, fall, 0)
    head_in = low16(layer_norm(output_ref[...], gains[6], gains[7]))
    head_ref[...] = head_in
    copies["proj"].wait()
    raw = dot_nn(head_in, weights["proj"][...])[:SEQS]
    raw_ref[...] = raw
    emb_ref[...] = raw * lax.rsqrt(jnp.sum(raw * raw, -1, keepdims=True) + 1e-06)


def tower_forward(tower, ends, gains, base, inputs, weights):
    width, rows = tower.width, tower.rows
    low, full = jnp.bfloat16, jnp.float32
    outs = [
        ((rows, width), full),
        ((rows, width), low),
        ((rows, 2 * width), low),
        ((GROUP, width), low),
        ((GROUP, width), low),
        ((tower.queries, rows), full),
        ((GROUP, width), low),
        ((SEQS, width), full),
        ((GROUP, width), low),
        ((SEQS, 4 * width), full),
        ((GROUP, 4 * width), low),
        ((SEQS, width), full),
        ((GROUP, width), low),
        ((SEQS, EMBED), full),
        ((SEQS, EMBED), full),
    ]
    vmem = pl.BlockSpec(memory_space=pltpu.VMEM)
    shapes = tower.shapes()
    return pl.pallas_call(
        functools.partial(tower_forward_kernel, tower),
        out_shape=[jax.ShapeDtypeStruct(shape, kind) for shape, kind in outs],
        in_specs=[pl.BlockSpec(memory_space=pltpu.SMEM)]
        + [vmem] * 3
        + [pl.BlockSpec(memory_space=pl.ANY)] * len(tower.names),
        out_specs=[vmem] * len(outs),
        scratch_shapes=[pltpu.VMEM((rows, width), full), pltpu.VMEM((tower.queries, width), full)]
        + [pltpu.VMEM(shapes[name], low) for name in tower.names]
        + [pltpu.SemaphoreType.DMA((len(tower.names),))],
        compiler_params=pltpu.CompilerParams(vmem_limit_bytes=58 << 20),
        name="image_forward" if tower.image else "text_forward",
    )(ends, gains, base, inputs, *[weights[name] for name in tower.names])


def tower_backward_kernel(tower, *refs):
    names = tower.names[-4:]
    count = len(names)
    ends_ref, gains_ref, grad_ref = refs[:3]
    (tokens_ref, normed_ref, pair_ref, normed_own_ref, query_ref, probs_ref, attended_ref, middle_ref, normed_two_ref,
     upper_ref, act_ref, output_ref, head_ref, raw_ref) = refs[3:17]
    sources = refs[17 : 17 + count]
    (grad_raw_ref, grad_mlp_ref, grad_upper_ref, grad_att_ref, grad_query_ref, grad_pair_ref, grad_rows_ref,
     places_ref, gain_grads_ref) = refs[17 + count : 26 + count]
    grad_ref_wide, wide_ref, grad_middle_ref = refs[26 + count : 29 + count]
    landed, sems = refs[29 + count : 29 + 2 * count], refs[29 + 2 * count]
    copies, weights = tower_fetch(names, sources, landed, sems)
    width, rows = tower.width, tower.rows
    scale = (width // tower.heads) ** (-0.5)
    gains = [gains_ref[i : i + 1, :] for i in range(8)]
    raw, grad_emb = raw_ref[...], grad_ref[...]
    norm = lax.rsqrt(jnp.sum(raw * raw, -1, keepdims=True) + 1e-06)
    along = jnp.sum(raw * grad_emb, -1, keepdims=True)
    grad_raw = low16(grad_emb * norm - raw * (norm * norm * norm * along))
    grad_raw_ref[...] = grad_raw
    copies["proj"].wait()
    grad_head = dot_nt(grad_raw, weights["proj"][...])[:SEQS]
    grad_out, gain_part = layer_norm_back(output_ref[...], gains[6], grad_head)
    gain_grads_ref[6:7, :] = sum_rows(gain_part)
    gain_grads_ref[7:8, :] = sum_rows(grad_head)
    grad_mlp_ref[...] = low16(grad_out)
    copies["down"].wait()

    def rise(j, carry):
        cols = pl.ds(pl.multiple_of(j * 512, 512), 512)
        grad_act = dot_nt(grad_mlp_ref[...], weights["down"][cols, :])[:SEQS]
        upper = upper_ref[:, cols]
        sig = jax.nn.sigmoid(1.702 * upper)
        grad_upper_ref[:, cols] = low16(grad_act * (sig + upper * (1.702 * (sig * (1.0 - sig)))))
        return carry

    lax.fori_loop(0, 4 * width // 512, rise, 0)
    copies["up"].wait()

    def fall(j, carry):
        cols = pl.ds(pl.multiple_of(j * 256, 256), 256)
        grad_middle_ref[:, cols] = dot_nt(grad_upper_ref[...], weights["up"][cols, :])[:SEQS]
        return carry

    lax.fori_loop(0, width // 256, fall, 0)
    grad_norm_two = grad_middle_ref[...]
    grad_mid, gain_part = layer_norm_back(middle_ref[...], gains[4], grad_norm_two)
    gain_grads_ref[4:5, :] = sum_rows(gain_part)
    gain_grads_ref[5:6, :] = sum_rows(grad_norm_two)
    grad_middle = grad_out + grad_mid
    grad_middle_ref[...] = grad_middle
    grad_att = low16(grad_middle)
    grad_att_ref[...] = grad_att
    copies["attn"].wait()
    grad_attended = dot_nt(grad_att, weights["attn"][:, 3 * width :]).astype(jnp.bfloat16)
    grads_heads = tower.spread_heads(grad_attended, wide_ref)
    queries = tower.spread_heads(query_ref[...], wide_ref)
    probs = probs_ref[...]
    grad_probs = dot_nt(grads_heads, pair_ref[:, width:])
    grad_scores = probs * (grad_probs - jnp.sum(grad_probs * probs, -1, keepdims=True))
    grad_scores = grad_scores.astype(jnp.bfloat16)
    grad_query = low16(tower.join_heads(dot_nn(grad_scores, pair_ref[:, :width]), wide_ref) * scale)
    grad_query_ref[...] = grad_query
    grad_pair_ref[:, :width] = (dot_tn(grad_scores, queries) * scale).astype(jnp.bfloat16)
    grad_pair_ref[:, width:] = dot_tn(probs.astype(jnp.bfloat16), grads_heads).astype(jnp.bfloat16)

    def inner(j, carry):
        at = pl.multiple_of(j * 256, 256)
        grad_ref_wide[:, pl.ds(at, 256)] = dot_nt(
            grad_pair_ref[...], weights["attn"][pl.ds(at, 256), width : 3 * width]
        )
        return carry

    lax.fori_loop(0, width // 256, inner, 0)
    grad_own = dot_nt(grad_query, weights["attn"][:, :width])
    for s in range(SEQS):
        grad_ref_wide[pl.ds(tower.row_of(s, ends_ref), 1), :] += grad_own[s : s + 1]

    def first(at, carry):
        grad = grad_ref_wide[at, :]
        hidden = tokens_ref[at, :]
        if tower.image:
            hidden = layer_norm(hidden, gains[0], gains[1])
        grad_in, gain_part = layer_norm_back(hidden, gains[2], grad)
        grad_ref_wide[at, :] = grad_in
        return carry[0] + sum_rows(gain_part), carry[1] + sum_rows(grad)

    nothing = jnp.zeros((1, width), jnp.float32)
    gain_one, shift_one = tower.each_block(first, (nothing, nothing))
    gain_grads_ref[2:3, :] = gain_one
    gain_grads_ref[3:4, :] = shift_one
    for s in range(SEQS):
        grad_ref_wide[pl.ds(tower.row_of(s, ends_ref), 1), :] += grad_middle_ref[s : s + 1, :]

    def second(at, carry):
        grad = grad_ref_wide[at, :]
        if not tower.image:
            grad_rows_ref[at, :] = grad.astype(jnp.bfloat16)
            return carry
        grad_in, gain_part = layer_norm_back(tokens_ref[at, :], gains[0], grad)
        grad_ref_wide[at, :] = grad_in
        grad_rows_ref[at, :] = grad_in.astype(jnp.bfloat16)
        return carry[0] + sum_rows(gain_part), carry[1] + sum_rows(grad)

    gain_pre, shift_pre = tower.each_block(second, (nothing, nothing))
    gain_grads_ref[0:1, :] = gain_pre
    gain_grads_ref[1:2, :] = shift_pre
    places = grad_ref_wide[0 : tower.length, :]
    for s in range(1, SEQS):
        places = places + grad_ref_wide[s * tower.length : (s + 1) * tower.length, :]
    places_ref[...] = places


def tower_backward(tower, ends, gains, grad_emb, kept, weights):
    width, rows = tower.width, tower.rows
    low, full = jnp.bfloat16, jnp.float32
    outs = [
        ((GROUP, EMBED), low),
        ((GROUP, width), low),
        ((GROUP, 4 * width), low),
        ((GROUP, width), low),
        ((GROUP, width), low),
        ((rows, 2 * width), low),
        ((rows, width), low),
        ((tower.length, width), full),
        ((8, width), full),
    ]
    vmem = pl.BlockSpec(memory_space=pltpu.VMEM)
    shapes, names = tower.shapes(), tower.names[-4:]
    return pl.pallas_call(
        functools.partial(tower_backward_kernel, tower),
        out_shape=[jax.ShapeDtypeStruct(shape, kind) for shape, kind in outs],
        in_specs=[pl.BlockSpec(memory_space=pltpu.SMEM)]
        + [vmem] * (2 + len(kept))
        + [pl.BlockSpec(memory_space=pl.ANY)] * len(names),
        out_specs=[vmem] * len(outs),
        scratch_shapes=[
            pltpu.VMEM((rows, width), full),
            pltpu.VMEM((tower.queries, width), full),
            pltpu.VMEM((SEQS, width), full),
        ]
        + [pltpu.VMEM(shapes[name], low) for name in names]
        + [pltpu.SemaphoreType.DMA((len(names),))],
        compiler_params=pltpu.CompilerParams(vmem_limit_bytes=58 << 20),
        name="image_backward" if tower.image else "text_backward",
    )(ends, gains, grad_emb, *kept, *[weights[name] for name in names])


def grad_pairs(kept, grads):
    (normed, normed_own, attended, normed_two, act_low, head_in) = (
        kept[1], kept[3], kept[6], kept[8], kept[10], kept[12]
    )
    grad_raw, grad_mlp, grad_upper, grad_att, grad_query, grad_pair = grads[:6]
    return (
        [(normed_own, grad_query), (normed, grad_pair), (attended, grad_att)],
        [(normed_two, grad_upper)],
        [(act_low, grad_mlp)],
        [(head_in, grad_raw)],
    )


def image_inputs(image_vec, pixels):
    pixels = jnp.pad(pixels, ((0, 0), (1, 0), (0, 0))).reshape(-1, PATCH_DIM)
    base = image_vec[1 : IMG_TOK + 1] + jnp.pad(image_vec[:1], ((0, IMG_TOK - 1), (0, 0)))
    return image_vec[IMG_TOK + 1 :], jnp.tile(base, (SEQS, 1)), pixels


def text_inputs(text_vec, token_rows):
    gains = jnp.pad(text_vec[CTX:], ((2, 0), (0, 0)))
    extra = TEXT.rows - SEQS * CTX
    base = jnp.pad(jnp.tile(text_vec[:CTX], (SEQS, 1)), ((0, extra), (0, 0)))
    return gains, base, jnp.pad(token_rows, ((0, extra), (0, 0)))


def adam_step(weight, first, second, grad, rate, decay):
    first = beta_one * first + (1.0 - beta_one) * grad
    second = beta_two * second + (1.0 - beta_two) * grad * grad
    first_hat = first / (1.0 - beta_one**STEP)
    second_hat = second / (1.0 - beta_two**STEP)
    weight = weight - rate * (first_hat / (jnp.sqrt(second_hat) + adam_eps) + decay * weight)
    return (weight, first, second)


IMAGE, TEXT = Tower(True), Tower(False)


def matrix_rows():
    return sum(seg_rows * seg_cols for seg_name, seg_rows, seg_cols in segment_list()[:9]) // LANES


def parameter_count():
    return sum(seg_rows * seg_cols for seg_name, seg_rows, seg_cols in segment_list())


def window_rows(shard, step=GROUP):
    need = -(-(GROUP * LANES - 1 + shard) // LANES)
    return -(-need // step) * step


def window_start(shard, index):
    return (shard * index // (GROUP * LANES)) * GROUP


def linear_index(gy_size):
    return lax.axis_index("gx") * gy_size + lax.axis_index("gy")


def place_kernel(shard, gy_size, flat_ref, out_ref, rolled):
    rows = flat_ref.shape[0]
    offset = lax.rem(shard * linear_index(gy_size), GROUP * LANES)
    down, right = offset // LANES, lax.rem(offset, LANES)
    pad = 2 * GROUP
    rolled[0:pad, :] = jnp.zeros((pad, LANES), jnp.float32)
    parts = 5 if rows % (5 * GROUP) == 0 else 1
    step = rows // parts

    def roll_rows(i, carry):
        at = pl.multiple_of(i * step, GROUP)
        rolled[pl.ds(pad + at, step), :] = pltpu.roll(flat_ref[pl.ds(at, step), :], right, 1)
        return carry

    lax.fori_loop(0, parts, roll_rows, 0)
    lane = lax.broadcasted_iota(jnp.int32, (step, LANES), 1)

    def put_rows(i, carry):
        at = pl.multiple_of(i * step, GROUP)
        upper = rolled[pl.ds(pad + at - down - 1, step), :]
        lower = rolled[pl.ds(pad + at - down, step), :]
        out_ref[pl.ds(at, step), :] = jnp.where(lane < right, upper, lower).astype(jnp.bfloat16)
        return carry

    lax.fori_loop(0, parts, put_rows, 0)


def place_window(flat, gy_size):
    shard = flat.shape[0]
    rows = window_rows(shard)
    padded = jnp.pad(flat, (0, rows * LANES - shard)).reshape(rows, LANES)
    return pl.pallas_call(
        functools.partial(place_kernel, shard, gy_size),
        out_shape=jax.ShapeDtypeStruct((rows, LANES), jnp.bfloat16),
        in_specs=[pl.BlockSpec(memory_space=pltpu.VMEM)],
        out_specs=pl.BlockSpec(memory_space=pltpu.VMEM),
        scratch_shapes=[pltpu.VMEM((rows + 2 * GROUP, LANES), jnp.float32)],
        compiler_params=pltpu.CompilerParams(vmem_limit_bytes=32 << 20),
        name="place_window",
    )(padded)


def lift_kernel(shard, gy_size, window_ref, out_ref, rolled):
    rows = window_ref.shape[0]
    offset = lax.rem(shard * linear_index(gy_size), GROUP * LANES)
    up, left = offset // LANES, lax.rem(offset, LANES)
    pad = 2 * GROUP
    step = rows // CHUNKS
    rolled[rows:, :] = jnp.zeros((pad, LANES), jnp.float32)

    def roll_rows(i, carry):
        at = pl.multiple_of(i * step, GROUP)
        rolled[pl.ds(at, step), :] = pltpu.roll(
            window_ref[pl.ds(at, step), :], lax.rem(LANES - left, LANES), 1
        )
        return carry

    lax.fori_loop(0, CHUNKS, roll_rows, 0)
    lane = lax.broadcasted_iota(jnp.int32, (step, LANES), 1)

    def put_rows(i, carry):
        at = pl.multiple_of(i * step, GROUP)
        first = rolled[pl.ds(at + up, step), :]
        second = rolled[pl.ds(at + up + 1, step), :]
        out_ref[pl.ds(at, step), :] = jnp.where(lane < LANES - left, first, second)
        return carry

    lax.fori_loop(0, CHUNKS, put_rows, 0)


def lift_window(window, shard, gy_size):
    rows = window.shape[0]
    lifted = pl.pallas_call(
        functools.partial(lift_kernel, shard, gy_size),
        out_shape=jax.ShapeDtypeStruct((rows, LANES), jnp.float32),
        in_specs=[pl.BlockSpec(memory_space=pltpu.VMEM)],
        out_specs=pl.BlockSpec(memory_space=pltpu.VMEM),
        scratch_shapes=[pltpu.VMEM((rows + 2 * GROUP, LANES), jnp.float32)],
        compiler_params=pltpu.CompilerParams(vmem_limit_bytes=32 << 20),
        name="lift_window",
    )(window)
    return lifted.reshape(-1)[:shard]


def spread_steps():
    steps = []
    base = 0
    for number, (seg_name, seg_rows, seg_cols) in enumerate(segment_list()[:9]):
        wide = seg_cols // LANES
        take = seg_rows
        while take * wide > 4608:
            take //= 2
        for start in range(0, seg_rows, take):
            steps.append((number, start, take, seg_cols, base + start * wide))
        base += seg_rows * wide
    return steps


def window_pieces(shard, count, stride, first, length):
    pieces, shared = [], []
    for index in range(count):
        low = window_start(shard, index)
        high = window_start(shard, index + 1) if index + 1 < count else low + window_rows(shard)
        start, stop = max(low, first), min(high, first + length)
        if start < stop:
            pieces.append((index * stride + start - low, start - first, stop - start))
        if index + 1 < count and first <= high < first + length:
            shared.append((index * stride + high - low, high - first))
    return pieces, shared


def spread_kernel(shard, count, vec_rows, gathered_ref, *refs):
    outs, vec_ref = refs[:9], refs[9]
    landed, edges, wide_rows, ready, in_sem, out_sem = refs[10:]
    rows = gathered_ref.shape[0] // count
    steps = spread_steps()
    steps.append((9, 0, vec_rows, LANES, matrix_rows()))

    def copies_in(number):
        seg, start, take, cols, base = steps[number]
        slot = number % 2
        pieces, shared = window_pieces(shard, count, rows, base, take * cols // LANES)
        found = [
            pltpu.make_async_copy(
                gathered_ref.at[pl.ds(src, size)], landed.at[slot, pl.ds(dst, size)], in_sem.at[slot]
            )
            for src, dst, size in pieces
        ]
        found += [
            pltpu.make_async_copy(
                gathered_ref.at[pl.ds(src, GROUP)], edges.at[slot, order], in_sem.at[slot]
            )
            for order, (src, dst) in enumerate(shared)
        ]
        return found, shared

    def copy_out(number):
        seg, start, take, cols, base = steps[number]
        slot = number % 2
        if seg == 9:
            return pltpu.make_async_copy(wide_rows.at[pl.ds(0, take)], vec_ref, out_sem.at[slot])
        return pltpu.make_async_copy(
            ready[cols].at[slot, pl.ds(0, take)], outs[seg].at[pl.ds(start, take)], out_sem.at[slot]
        )

    for copy in copies_in(0)[0]:
        copy.start()
    for number, (seg, start, take, cols, base) in enumerate(steps):
        slot = number % 2
        wide = cols // LANES
        total = take * wide
        if number + 1 < len(steps):
            for copy in copies_in(number + 1)[0]:
                copy.start()
        found, shared = copies_in(number)
        for copy in found:
            copy.wait()
        if number >= 2:
            copy_out(number - 2).wait()
        block = 256 if total % 256 == 0 else GROUP

        def widen(i, carry, slot=slot, block=block):
            at = pl.multiple_of(i * block, GROUP)
            wide_rows[pl.ds(at, block), :] = landed[slot, pl.ds(at, block), :].astype(jnp.float32)
            return carry

        lax.fori_loop(0, total // block, widen, 0)
        for order, (src, dst) in enumerate(shared):
            wide_rows[dst : dst + GROUP, :] += edges[slot, order].astype(jnp.float32)
        if seg < 9:

            def tile(i, carry, slot=slot, wide=wide, cols=cols):
                at = pl.multiple_of(i * GROUP, GROUP)
                for j in range(wide):
                    ready[cols][slot, pl.ds(at, GROUP), j * LANES : (j + 1) * LANES] = wide_rows[
                        pl.ds(at * wide + j, GROUP, stride=wide), :
                    ].astype(jnp.bfloat16)
                return carry

            lax.fori_loop(0, take // GROUP, tile, 0)
        copy_out(number).start()
    copy_out(len(steps) - 2).wait()
    copy_out(len(steps) - 1).wait()


def spread_entry(shard, gx_size, gy_size, vec_rows, gathered_ref, rows_ref, *refs):
    outs, landed_rows = refs[:10], refs[10]
    landed, edges, wide_rows, ready_a, ready_b, ready_c, ready_d, in_sem, out_sem = refs[11:20]
    ready = {D_IMG: ready_a, 4 * D_IMG: ready_b, D_TXT: ready_c, 4 * D_TXT: ready_d}
    share = Share(gx_size, gy_size, False, rows_ref, landed_rows, refs[20:])
    share.greet()
    share.begin()
    spread_kernel(
        shard, gx_size * gy_size, vec_rows, gathered_ref, *outs, landed, edges, wide_rows, ready, in_sem, out_sem
    )
    share.middle()
    share.finish()


def spread_weights(gathered, rows_to_send, shard, gx_size, gy_size, number):
    count = gx_size * gy_size
    rows = gathered.shape[0] // count
    steps = spread_steps()
    tallest = {}
    for seg, start, take, cols, base in steps:
        tallest[cols] = max(tallest.get(cols, 0), take)
    most = max(take * cols // LANES for seg, start, take, cols, base in steps)
    vec_rows = -(-(sum(r * c for name, r, c in segment_list()[9:])) // (LANES * GROUP)) * GROUP
    edge_count = max(
        len(window_pieces(shard, count, rows, base, take * cols // LANES)[1])
        for seg, start, take, cols, base in steps
    )
    ready = [
        pltpu.VMEM((2, tallest[cols], cols), jnp.bfloat16)
        for cols in (D_IMG, 4 * D_IMG, D_TXT, 4 * D_TXT)
    ]
    return pl.pallas_call(
        functools.partial(spread_entry, shard, gx_size, gy_size, vec_rows),
        out_shape=[
            jax.ShapeDtypeStruct((seg_rows, seg_cols), jnp.bfloat16)
            for seg_name, seg_rows, seg_cols in segment_list()[:9]
        ]
        + [
            jax.ShapeDtypeStruct((vec_rows, LANES), jnp.float32),
            jax.ShapeDtypeStruct((1,) + rows_to_send.shape, rows_to_send.dtype),
        ],
        in_specs=[pl.BlockSpec(memory_space=pl.ANY), pl.BlockSpec(memory_space=pltpu.VMEM)],
        out_specs=[pl.BlockSpec(memory_space=pl.ANY)] * 10 + [pl.BlockSpec(memory_space=pltpu.VMEM)],
        scratch_shapes=[
            pltpu.VMEM((2, most, LANES), jnp.bfloat16),
            pltpu.VMEM((2, edge_count + 1, GROUP, LANES), jnp.bfloat16),
            pltpu.VMEM((most, LANES), jnp.float32),
        ]
        + ready
        + [pltpu.SemaphoreType.DMA((2,)), pltpu.SemaphoreType.DMA((2,))]
        + share_sems(gx_size, gy_size),
        compiler_params=pltpu.CompilerParams(
            collective_id=number, has_side_effects=True, vmem_limit_bytes=48 << 20
        ),
        name="spread_weights",
    )(gathered, rows_to_send)


def split_vectors(vec_rows):
    image_count, text_count = (IMG_TOK + 9) * D_IMG // LANES, (CTX + 6) * D_TXT // LANES
    image_vec = vec_rows[:image_count].reshape(IMG_TOK + 9, D_IMG)
    text_vec = vec_rows[image_count : image_count + text_count].reshape(CTX + 6, D_TXT)
    return image_vec, text_vec, vec_rows[image_count + text_count, 0]


def grads_kernel(parts, gx_size, gy_size, *refs):
    operand_count = sum(2 * len(pairs) for seg_rows, seg_cols, take, pairs in parts)
    operands = refs[:operand_count]
    vec_ref, token_ref, out_ref, arrived_ref, flat_rows, vec_sem, out_sem = refs[operand_count : operand_count + 7]
    share = Share(gx_size, gy_size, True, token_ref, arrived_ref, refs[operand_count + 7 :])
    share.greet()
    share.begin()
    tail = pltpu.make_async_copy(vec_ref, out_ref.at[pl.ds(matrix_rows(), vec_ref.shape[0])], vec_sem)
    tail.start()
    base = 0
    steps_before = 0
    for number, (seg_rows, seg_cols, take, pairs) in enumerate(parts):
        if number == 2:
            share.middle()
        if number == 6:
            share.rest()
        wide = seg_cols // LANES
        size = take * wide
        count = seg_rows // take

        def step(i, carry, base=base, before=steps_before, size=size, take=take, wide=wide, pairs=pairs):
            slot = lax.rem(i + before, 2)

            def written(number):
                at = pl.multiple_of(base + number * size, 8)
                return pltpu.make_async_copy(
                    flat_rows.at[slot, pl.ds(0, size)], out_ref.at[pl.ds(at, size)], out_sem.at[slot]
                )

            @pl.when(i >= 2)
            def _():
                written(i - 2).wait()

            for left_number, right_number, first in pairs:
                left_ref, right_ref = operands[left_number], operands[right_number]
                at = pl.multiple_of(i * take, LANES)
                product = lax.dot_general(
                    left_ref[:, pl.ds(at, take)],
                    right_ref[...],
                    (((0,), (0,)), ((), ())),
                    preferred_element_type=jnp.float32,
                )
                for j in range(right_ref.shape[1] // LANES):
                    flat_rows[slot, pl.ds(first + j, take, stride=wide), :] = product[
                        :, j * LANES : (j + 1) * LANES
                    ]
            written(i).start()
            return carry

        lax.fori_loop(0, count, step, 0)
        for number in range(max(count - 2, 0), count):
            slot = (number + steps_before) % 2
            at = base + number * size
            pltpu.make_async_copy(
                flat_rows.at[slot, pl.ds(0, size)], out_ref.at[pl.ds(at, size)], out_sem.at[slot]
            ).wait()
        base += seg_rows * wide
        steps_before += count
    tail.wait()
    share.finish()


def weight_grads(pair_lists, vec_rows, token_grads, gx_size, gy_size, number):
    operands, parts = [], []
    for (seg_name, seg_rows, seg_cols), pairs in zip(segment_list()[:9], pair_lists):
        numbered, first = [], 0
        for left_side, right_side in pairs:
            numbered.append((len(operands), len(operands) + 1, first))
            for side in (left_side, right_side):
                side = side.reshape(-1, side.shape[-1])
                operands.append(jnp.pad(side, ((0, -side.shape[0] % GROUP), (0, 0))))
            first += right_side.shape[-1] // LANES
        parts.append((seg_rows, seg_cols, min(seg_rows, 256 if seg_cols <= 768 else 128), numbered))
    total_rows = matrix_rows() + vec_rows.shape[0]
    most = max(take * seg_cols // LANES for seg_rows, seg_cols, take, pairs in parts)
    return pl.pallas_call(
        functools.partial(grads_kernel, parts, gx_size, gy_size),
        out_shape=[
            jax.ShapeDtypeStruct((total_rows, LANES), jnp.float32),
            jax.ShapeDtypeStruct((gx_size,) + token_grads.shape, token_grads.dtype),
        ],
        in_specs=[pl.BlockSpec(memory_space=pltpu.VMEM)] * (len(operands) + 2),
        out_specs=[pl.BlockSpec(memory_space=pl.ANY)] * 2,
        scratch_shapes=[
            pltpu.VMEM((2, most, LANES), jnp.float32),
            pltpu.SemaphoreType.DMA,
            pltpu.SemaphoreType.DMA((2,)),
        ]
        + share_sems(gx_size, gy_size),
        compiler_params=pltpu.CompilerParams(
            collective_id=number, has_side_effects=True, vmem_limit_bytes=56 << 20
        ),
        name="weight_grads",
    )(*operands, vec_rows, token_grads)


def exchange_kernel(gx_size, gy_size, many, *refs):
    blocks, outs = refs[:many], refs[many : 2 * many]
    send_sem, recv_sem, own_sem = refs[2 * many :]
    count = gx_size * gy_size
    me = linear_index(gy_size)
    barrier = pltpu.get_barrier_semaphore()

    def device(step):
        other = lax.rem(me + step, count)
        return (other // gy_size, lax.rem(other, gy_size))

    def greet(step, carry):
        pl.semaphore_signal(barrier, inc=1, device_id=device(step), device_id_type=MESH)
        return carry

    lax.fori_loop(1, count, greet, 0)
    own = [
        pltpu.make_async_copy(block, out.at[me], own_sem.at[i])
        for i, (block, out) in enumerate(zip(blocks, outs))
    ]
    for copy in own:
        copy.start()
    pl.semaphore_wait(barrier, count - 1)

    def send(step, carry):
        for i, (block, out) in enumerate(zip(blocks, outs)):
            pltpu.make_async_remote_copy(
                src_ref=block,
                dst_ref=out.at[me],
                send_sem=send_sem.at[i],
                recv_sem=recv_sem.at[i],
                device_id=device(step),
                device_id_type=MESH,
            ).start()
        return carry

    lax.fori_loop(1, count, send, 0)
    for i, out in enumerate(outs):
        own[i].wait()
        others = out.at[pl.ds(0, count - 1)]
        both = pltpu.make_async_remote_copy(
            src_ref=others,
            dst_ref=others,
            send_sem=send_sem.at[i],
            recv_sem=recv_sem.at[i],
            device_id=device(1),
            device_id_type=MESH,
        )
        both.wait_send()
        both.wait_recv()


def exchange_all(blocks, gx_size, gy_size, number, name):
    count, many = gx_size * gy_size, len(blocks)
    return pl.pallas_call(
        functools.partial(exchange_kernel, gx_size, gy_size, many),
        out_shape=[jax.ShapeDtypeStruct((count,) + block.shape, block.dtype) for block in blocks],
        in_specs=[pl.BlockSpec(memory_space=pltpu.VMEM)] * many,
        out_specs=[pl.BlockSpec(memory_space=pltpu.VMEM)] * many,
        scratch_shapes=[pltpu.SemaphoreType.DMA((many,))] * 3,
        compiler_params=pltpu.CompilerParams(
            collective_id=number, has_side_effects=True, vmem_limit_bytes=32 << 20
        ),
        name=name,
    )(*blocks)


class Share:
    def __init__(self, gx_size, gy_size, everyone, send_ref, out_ref, sems):
        gx, self.gy = lax.axis_index("gx"), lax.axis_index("gy")
        self.x_size, self.send_ref, self.out_ref = gx_size // 2, send_ref, out_ref
        self.core, self.x = lax.rem(gx, 2), gx // 2
        (self.own_sem, self.row_send, self.row_recv, self.x_send, self.x_recv, self.core_send, self.core_recv) = sems
        self.rows = [(gx, lax.rem(self.gy + d, gy_size)) for d in range(1, gy_size)]
        self.along_x, self.sibling = [], []
        if everyone:
            self.along_x = [
                (lax.rem(self.x + d, self.x_size) * 2 + self.core, self.gy) for d in range(1, self.x_size)
            ]
            self.sibling = [(self.x * 2 + 1 - self.core, self.gy)]
        self.mine = out_ref.at[gx if everyone else 0]

    def greet(self):
        greet_all(self.rows + self.along_x + self.sibling)

    def own(self):
        return pltpu.make_async_copy(self.send_ref.at[self.gy], self.mine.at[self.gy], self.own_sem)

    def row(self, d):
        other = self.rows[d]
        return remote(self.send_ref.at[other[1]], self.mine.at[self.gy], self.row_send.at[d], self.row_recv.at[d], other)

    def group(self, d):
        return remote(self.mine, self.mine, self.x_send.at[d], self.x_recv.at[d], self.along_x[d])

    def across(self, i, source):
        return remote(source, source, self.core_send.at[i], self.core_recv.at[i], self.sibling[0])

    def begin(self):
        self.own().start()
        for d in range(len(self.rows)):
            self.row(d).start()

    def middle(self):
        self.own().wait()
        for d in range(len(self.rows)):
            self.row(d).wait_recv()
        for d in range(len(self.along_x)):
            self.group(d).start()
        if self.sibling:
            self.across(0, self.mine).start()

    def rest(self):
        for d in range(len(self.along_x)):
            self.group(d).wait_recv()
            sender = lax.rem(self.x + self.x_size - d - 1, self.x_size) * 2 + self.core
            self.across(d + 1, self.out_ref.at[sender]).start()

    def finish(self):
        for d in range(len(self.rows)):
            self.row(d).wait_send()
        for d in range(len(self.along_x)):
            self.group(d).wait_send()
        for i in range(self.x_size if self.sibling else 0):
            self.across(i, self.mine).wait_send()
            self.across(i, self.mine).wait_recv()


def share_sems(gx_size, gy_size):
    dma, x_size = pltpu.SemaphoreType.DMA, gx_size // 2
    return [dma, dma((gy_size - 1,)), dma((gy_size - 1,)), dma((x_size,)), dma((x_size,)), dma((x_size,)), dma((x_size,))]


class Places:
    def __init__(self, sizes):
        self.x_size, self.low_size, self.high_size = sizes
        self.mixed = self.x_size == self.low_size
        self.gy_size = self.high_size * self.low_size
        gx, gy = lax.axis_index("gx"), lax.axis_index("gy")
        self.core, x = lax.rem(gx, 2), gx // 2
        self.h, low = gy // self.low_size, lax.rem(gy, self.low_size)
        self.a, self.b = self.turned(self.core, x, low)
        self.a_size, self.b_size = self.x_size, self.low_size

    def turned(self, side, a, b):
        if not self.mixed:
            return a, b
        return a * (1 - side) + b * side, b * (1 - side) + a * side

    def device(self, side, a, b, h):
        dev_x, dev_low = self.turned(side, a, b)
        return (dev_x * 2 + side, h * self.low_size + dev_low)

    def linear(self, side, a, b, h):
        gx, gy = self.device(side, a, b, h)
        return gx * self.gy_size + gy

    def sibling(self):
        a, b = (self.b, self.a) if self.mixed else (self.a, self.b)
        return self.device(1 - self.core, a, b, self.h)

    def along_a(self):
        return [
            self.device(self.core, lax.rem(self.a + d, self.a_size), self.b, self.h)
            for d in range(1, self.a_size)
        ]

    def along_b(self):
        return [
            self.device(self.core, self.a, lax.rem(self.b + d, self.b_size), self.h)
            for d in range(1, self.b_size)
        ]

    def along_h(self):
        return [
            self.device(self.core, self.a, self.b, lax.rem(self.h + d, self.high_size))
            for d in range(1, self.high_size)
        ]


def greet_all(others):
    barrier = pltpu.get_barrier_semaphore()
    for other in others:
        pl.semaphore_signal(barrier, inc=1, device_id=other, device_id_type=MESH)
    pl.semaphore_wait(barrier, len(others))


def remote(src, dst, send_sem, recv_sem, other):
    return pltpu.make_async_remote_copy(
        src_ref=src, dst_ref=dst, send_sem=send_sem, recv_sem=recv_sem, device_id=other, device_id_type=MESH
    )


def axis_sizes(gx_size, gy_size):
    return gx_size // 2, gy_size // 4, 4


NO_TOKEN = 65535


def route_capacity(tokens, gy_size):
    return GROUP * (1 + 17 * tokens // (16 * gy_size * GROUP))


def table_sum_kernel(cap, counts_ref, index_ref, rows_ref, out_ref, square_ref, wide, row_sem):
    sources = rows_ref.shape[0]
    vocab = out_ref.shape[0] - 8

    def fetch(source):
        slot = lax.rem(source, 2)
        return pltpu.make_async_copy(rows_ref.at[source], wide.at[slot], row_sem.at[slot])

    fetch(0).start()
    block = 32 if vocab % 32 == 0 else 8

    def clear(i, carry):
        out_ref[pl.ds(pl.multiple_of(i * block, 8), block), :] = jnp.zeros((block, D_TXT), jnp.float32)
        return carry

    lax.fori_loop(0, vocab // block, clear, 0)
    out_ref[vocab:, :] = jnp.zeros((8, D_TXT), jnp.float32)

    def one_source(source, carry):
        slot = lax.rem(source, 2)

        @pl.when(source + 1 < sources)
        def _():
            fetch(source + 1).start()

        fetch(source).wait()
        widened = wide.at[slot]

        def add(group, carry):
            rows = widened[pl.ds(pl.multiple_of(group * GROUP, GROUP), GROUP), :].astype(jnp.float32)
            for half in range(0, GROUP, 8):
                places = [
                    pl.ds(index_ref[source * cap + group * GROUP + half + i], 1) for i in range(8)
                ]
                sums = [out_ref[place, :] + rows[half + i : half + i + 1, :] for i, place in enumerate(places)]
                for place, value in zip(places, sums):
                    out_ref[place, :] = value
            return carry

        lax.fori_loop(0, (counts_ref[source] + GROUP - 1) // GROUP, add, 0)
        return carry

    lax.fori_loop(0, sources, one_source, 0)

    def square(i, carry):
        part = out_ref[pl.ds(pl.multiple_of(i * block, 8), block), :]
        part = part * part
        total = carry
        for r in range(0, block, 8):
            total = total + part[r : r + 8]
        return total

    square_ref[...] = lax.fori_loop(0, vocab // block, square, jnp.zeros((8, D_TXT), jnp.float32))


def table_sum(counts, index, rows, vocab):
    sources, cap = rows.shape[0], rows.shape[1]
    return pl.pallas_call(
        functools.partial(table_sum_kernel, cap),
        out_shape=[
            jax.ShapeDtypeStruct((vocab + 8, D_TXT), jnp.float32),
            jax.ShapeDtypeStruct((8, D_TXT), jnp.float32),
        ],
        in_specs=[pl.BlockSpec(memory_space=pltpu.SMEM)] * 2 + [pl.BlockSpec(memory_space=pl.ANY)],
        out_specs=[pl.BlockSpec(memory_space=pltpu.VMEM)] * 2,
        scratch_shapes=[pltpu.VMEM((2, cap, D_TXT), jnp.bfloat16), pltpu.SemaphoreType.DMA((2,))],
        compiler_params=pltpu.CompilerParams(vmem_limit_bytes=40 << 20),
        name="table_sum",
    )(counts, index, rows)


def ranks(flags):
    tokens = flags.shape[-1]
    before = (jnp.arange(tokens)[:, None] < jnp.arange(tokens)[None, :]).astype(jnp.bfloat16)
    return fwd_dot(flags.astype(jnp.bfloat16), before).astype(jnp.int32)


def pick_matrix(slots, count):
    return (jnp.arange(count)[:, None] == slots[None, :]).astype(jnp.bfloat16)


def gather_kernel(sizes, chunks, window_ref, out_ref, own_sem, h_send, h_recv, b_send, b_recv, a_send, a_recv, core_send,
                  core_recv):
    at = Places(sizes)
    rows = window_ref.shape[0]
    chunk = rows // chunks
    me = at.linear(at.core, at.a, at.b, at.h)
    sibling, peers_a, peers_b, peers_h = at.sibling(), at.along_a(), at.along_b(), at.along_h()
    greet_all([sibling] + peers_a + peers_b + peers_h)

    def part(block, t):
        return out_ref.at[pl.ds(pl.multiple_of(block * rows + t * chunk, GROUP), chunk)]

    def many(count):
        return out_ref.at[pl.ds(0, count * chunk)]

    def own_copy(t):
        src = window_ref.at[pl.ds(pl.multiple_of(t * chunk, GROUP), chunk)]
        return src, pltpu.make_async_copy(src, part(me, t), own_sem.at[t])

    def stage_h(t):
        src, own = own_copy(t)
        for d, other in enumerate(peers_h):
            remote(src, part(me, t), h_send.at[d], h_recv.at[t, d], other).start()
        own.start()

    def stage_b(t):
        own_copy(t)[1].wait()
        for d, other in enumerate(peers_h):
            remote(many(1), many(1), h_send.at[d], h_recv.at[t, d], other).wait_recv()
        for d, other in enumerate(peers_b):
            for h in range(at.high_size):
                block = part(at.linear(at.core, at.a, at.b, h), t)
                remote(block, block, b_send.at[d], b_recv.at[t, d], other).start()

    def stage_a(t):
        for d, other in enumerate(peers_b):
            remote(many(at.high_size), many(at.high_size), b_send.at[d], b_recv.at[t, d], other).wait_recv()
        for d, other in enumerate(peers_a):
            for b in range(at.b_size):
                for h in range(at.high_size):
                    block = part(at.linear(at.core, at.a, b, h), t)
                    remote(block, block, a_send.at[d], a_recv.at[t, d], other).start()

    plane = at.b_size * at.high_size

    def stage_core(t):
        for d, other in enumerate(peers_a):
            remote(many(plane), many(plane), a_send.at[d], a_recv.at[t, d], other).wait_recv()
        for a in range(at.a_size):
            for b in range(at.b_size):
                for h in range(at.high_size):
                    block = part(at.linear(at.core, a, b, h), t)
                    remote(block, block, core_send, core_recv, sibling).start()

    def turn(t, carry):
        for depth, stage in enumerate((stage_h, stage_b, stage_a, stage_core)):
            @pl.when((t >= depth) & (t < chunks + depth))
            def _():
                stage(t - depth)

        return carry

    lax.fori_loop(0, chunks + 3, turn, 0)

    def whole(count):
        return out_ref.at[pl.ds(0, count * rows)]

    for d, other in enumerate(peers_h):
        remote(whole(1), whole(1), h_send.at[d], h_recv.at[0, d], other).wait_send()
    for d, other in enumerate(peers_b):
        remote(whole(at.high_size), whole(at.high_size), b_send.at[d], b_recv.at[0, d], other).wait_send()
    for d, other in enumerate(peers_a):
        remote(whole(plane), whole(plane), a_send.at[d], a_recv.at[0, d], other).wait_send()
    half = whole(at.a_size * plane)
    last = remote(half, half, core_send, core_recv, sibling)
    last.wait_send()
    last.wait_recv()


def gather_windows(window, gx_size, gy_size, chunks, number, name):
    sizes = axis_sizes(gx_size, gy_size)
    a, b, h = sizes[0] - 1, sizes[1] - 1, sizes[2] - 1
    dma = pltpu.SemaphoreType.DMA
    return pl.pallas_call(
        functools.partial(gather_kernel, sizes, chunks),
        out_shape=jax.ShapeDtypeStruct((gx_size * gy_size * window.shape[0], LANES), window.dtype),
        in_specs=[pl.BlockSpec(memory_space=pltpu.VMEM)],
        out_specs=pl.BlockSpec(memory_space=pl.ANY),
        scratch_shapes=[dma((chunks,)), dma((h,)), dma((chunks, h)), dma((b,)), dma((chunks, b)), dma((a,)),
                        dma((chunks, a)), dma, dma],
        compiler_params=pltpu.CompilerParams(
            collective_id=number, has_side_effects=True, vmem_limit_bytes=32 << 20
        ),
        name=name,
    )(window)


def reduce_kernel(shard, sizes, grads_ref, out_ref, own, landed, keep_one, send_one, recv_one, keep_two, send_two,
                  recv_two, keep_three, send_three, recv_three, load_sem, pair_send, pair_recv, credit,
                  one_send, one_recv, two_send, two_recv, three_send, three_recv):
    at = Places(sizes)
    a_size, b_size, high_size = at.a_size, at.b_size, at.high_size
    core, my_a, my_b, high = at.core, at.a, at.b, at.h
    plane = b_size * high_size
    chunk = own.shape[2]
    chunks = out_ref.shape[0] // chunk

    def start_row(side, number):
        a, rest = number // plane, lax.rem(number, plane)
        return window_start(shard, at.linear(side, a, rest // high_size, lax.rem(rest, high_size)))

    sibling, peers, peers_two, peers_three = at.sibling(), at.along_a(), at.along_b(), at.along_h()
    greet_all([sibling] + peers + peers_two + peers_three)
    blocks = a_size * plane

    def pair_stage(t):
        slot = lax.rem(t, 2)

        @pl.when(t >= 2)
        def _():
            pl.semaphore_wait(credit, 1)

        def each(number, carry):
            theirs = pl.multiple_of(start_row(1 - core, number) + t * chunk, GROUP)
            mine = pl.multiple_of(start_row(core, number) + t * chunk, GROUP)
            remote(
                grads_ref.at[pl.ds(theirs, chunk)], landed.at[slot, number], pair_send.at[slot], pair_recv.at[slot], sibling
            ).start()
            pltpu.make_async_copy(
                grads_ref.at[pl.ds(mine, chunk)], own.at[slot, number], load_sem.at[slot]
            ).start()
            return carry

        lax.fori_loop(0, blocks, each, 0)

    def first_stage(u):
        slot = lax.rem(u, 2)
        both = remote(landed.at[slot], landed.at[slot], pair_send.at[slot], pair_recv.at[slot], sibling)
        pltpu.make_async_copy(own.at[slot], own.at[slot], load_sem.at[slot]).wait()
        both.wait_send()
        both.wait_recv()
        for d in range(1, a_size):
            @pl.when(u >= 2)
            def _():
                remote(send_one.at[slot, d - 1], recv_one.at[u - 2, d - 1], one_send.at[slot, d - 1],
                       one_recv.at[u - 2, d - 1], peers[d - 1]).wait_send()

            first = lax.rem(my_a + d, a_size) * plane

            def give(i, carry):
                send_one[slot, d - 1, i] = (own[slot, first + i] + landed[slot, first + i]).astype(jnp.bfloat16)
                return carry

            lax.fori_loop(0, plane, give, 0)
            remote(send_one.at[slot, d - 1], recv_one.at[u, d - 1], one_send.at[slot, d - 1],
                   one_recv.at[u, d - 1], peers[d - 1]).start()

        def hold(i, carry):
            keep_one[slot, i] = own[slot, my_a * plane + i] + landed[slot, my_a * plane + i]
            return carry

        lax.fori_loop(0, plane, hold, 0)

        @pl.when(u < chunks - 2)
        def _():
            pl.semaphore_signal(credit, inc=1, device_id=sibling, device_id_type=MESH)

    def second_stage(u):
        slot = lax.rem(u, 2)
        for d in range(1, a_size):
            remote(recv_one.at[u, d - 1], recv_one.at[u, d - 1], one_send.at[slot, d - 1], one_recv.at[u, d - 1],
                   peers[d - 1]).wait_recv()

        def total(number):
            value = keep_one[slot, number]
            for d in range(1, a_size):
                value = value + recv_one[u, d - 1, number].astype(jnp.float32)
            return value

        for d in range(1, b_size):
            @pl.when(u >= 2)
            def _():
                remote(send_two.at[slot, d - 1], recv_two.at[u - 2, d - 1], two_send.at[slot, d - 1],
                       two_recv.at[u - 2, d - 1], peers_two[d - 1]).wait_send()

            first = lax.rem(my_b + d, b_size) * high_size

            def give(i, carry):
                send_two[slot, d - 1, i] = total(first + i).astype(jnp.bfloat16)
                return carry

            lax.fori_loop(0, high_size, give, 0)
            remote(send_two.at[slot, d - 1], recv_two.at[u, d - 1], two_send.at[slot, d - 1],
                   two_recv.at[u, d - 1], peers_two[d - 1]).start()

        def hold(i, carry):
            keep_two[slot, i] = total(my_b * high_size + i)
            return carry

        lax.fori_loop(0, high_size, hold, 0)

    def third_stage(u):
        slot = lax.rem(u, 2)
        for d in range(1, b_size):
            remote(recv_two.at[u, d - 1], recv_two.at[u, d - 1], two_send.at[slot, d - 1], two_recv.at[u, d - 1],
                   peers_two[d - 1]).wait_recv()

        def total(number):
            value = keep_two[slot, number]
            for d in range(1, b_size):
                value = value + recv_two[u, d - 1, number].astype(jnp.float32)
            return value

        for d in range(1, high_size):
            @pl.when(u >= 2)
            def _():
                remote(send_three.at[slot, d - 1], recv_three.at[u - 2, d - 1], three_send.at[slot, d - 1],
                       three_recv.at[u - 2, d - 1], peers_three[d - 1]).wait_send()

            send_three[slot, d - 1] = total(lax.rem(high + d, high_size)).astype(jnp.bfloat16)
            remote(send_three.at[slot, d - 1], recv_three.at[u, d - 1], three_send.at[slot, d - 1],
                   three_recv.at[u, d - 1], peers_three[d - 1]).start()
        keep_three[slot] = total(high)

    def last_stage(u):
        slot = lax.rem(u, 2)
        value = keep_three[slot]
        for d in range(1, high_size):
            remote(recv_three.at[u, d - 1], recv_three.at[u, d - 1], three_send.at[slot, d - 1],
                   three_recv.at[u, d - 1], peers_three[d - 1]).wait_recv()
            value = value + recv_three[u, d - 1].astype(jnp.float32)
        out_ref[pl.ds(pl.multiple_of(u * chunk, GROUP), chunk), :] = value

    def turn(t, carry):
        stages = (pair_stage, first_stage, second_stage, third_stage, last_stage)
        for depth, stage in enumerate(stages):
            @pl.when((t >= depth) & (t < chunks + depth))
            def _():
                stage(t - depth)

        return carry

    lax.fori_loop(0, chunks + 4, turn, 0)
    for u in range(max(chunks - 2, 0), chunks):
        slot = u % 2
        for d in range(1, a_size):
            remote(send_one.at[slot, d - 1], recv_one.at[u, d - 1], one_send.at[slot, d - 1],
                   one_recv.at[u, d - 1], peers[d - 1]).wait_send()
        for d in range(1, b_size):
            remote(send_two.at[slot, d - 1], recv_two.at[u, d - 1], two_send.at[slot, d - 1],
                   two_recv.at[u, d - 1], peers_two[d - 1]).wait_send()
        for d in range(1, high_size):
            remote(send_three.at[slot, d - 1], recv_three.at[u, d - 1], three_send.at[slot, d - 1],
                   three_recv.at[u, d - 1], peers_three[d - 1]).wait_send()


def reduce_windows(grads, shard, gx_size, gy_size, number):
    rows = window_rows(shard, GROUP * CHUNKS)
    chunk = rows // CHUNKS
    x_size, low_size, high_size = axis_sizes(gx_size, gy_size)
    plane = low_size * high_size
    blocks = x_size * plane
    low_type, dma = jnp.bfloat16, pltpu.SemaphoreType.DMA
    a, b, h = x_size - 1, low_size - 1, high_size - 1
    return pl.pallas_call(
        functools.partial(reduce_kernel, shard, (x_size, low_size, high_size)),
        out_shape=jax.ShapeDtypeStruct((rows, LANES), jnp.float32),
        in_specs=[pl.BlockSpec(memory_space=pl.ANY)],
        out_specs=pl.BlockSpec(memory_space=pltpu.VMEM),
        scratch_shapes=[
            pltpu.VMEM((2, blocks, chunk, LANES), jnp.float32),
            pltpu.VMEM((2, blocks, chunk, LANES), jnp.float32),
            pltpu.VMEM((2, plane, chunk, LANES), jnp.float32),
            pltpu.VMEM((2, a, plane, chunk, LANES), low_type),
            pltpu.VMEM((CHUNKS, a, plane, chunk, LANES), low_type),
            pltpu.VMEM((2, high_size, chunk, LANES), jnp.float32),
            pltpu.VMEM((2, b, high_size, chunk, LANES), low_type),
            pltpu.VMEM((CHUNKS, b, high_size, chunk, LANES), low_type),
            pltpu.VMEM((2, chunk, LANES), jnp.float32),
            pltpu.VMEM((2, h, chunk, LANES), low_type),
            pltpu.VMEM((CHUNKS, h, chunk, LANES), low_type),
            dma((2,)),
            dma((2,)),
            dma((2,)),
            pltpu.SemaphoreType.REGULAR,
            dma((2, a)),
            dma((CHUNKS, a)),
            dma((2, b)),
            dma((CHUNKS, b)),
            dma((2, h)),
            dma((CHUNKS, h)),
        ],
        compiler_params=pltpu.CompilerParams(
            collective_id=number, has_side_effects=True, vmem_limit_bytes=60 << 20
        ),
        name="reduce_windows",
    )(grads)


def log_sums(rows, columns, column_ok, logit_scale, matches, positives):
    total, taken = rows.shape[0], min(rows.shape[0], 256)

    def some(args):
        row_part, match_part, positive_part = args
        dots = back_dot(row_part, columns)
        logits = logit_scale * dots
        masked = jnp.where(column_ok[None, :], logits, -1e30)
        row_max = jnp.max(masked, 1, keepdims=True)
        log_total = row_max[:, 0] + jnp.log(jnp.sum(jnp.exp(masked - row_max), 1))
        gap = jnp.where(match_part > 0.0, logits[:, :total] - log_total[:, None], 0.0)
        pulled = jnp.sum(positive_part[:, None] * jnp.exp(masked - log_total[:, None]) * dots)
        return log_total, -jnp.sum(gap), pulled - jnp.sum(match_part * dots[:, :total])

    if taken == total:
        return some((rows, matches, positives))
    logs, parts, pulls = lax.map(
        some,
        (
            rows.reshape(-1, taken, rows.shape[1]),
            matches.reshape(-1, taken, total),
            positives.reshape(-1, taken),
        ),
    )
    return logs.reshape(-1), jnp.sum(parts), jnp.sum(pulls)


def side_grads(row_embed, columns, column_ok, same_own, positives_own, log_own, logit_scale, total_count):
    dot_vals = back_dot(row_embed, columns)
    masked = jnp.where(column_ok[None, :], logit_scale * dot_vals, -1e30)
    extra = columns.shape[0] - same_own.shape[1]
    weights_pos = jnp.concatenate(
        [same_own, jnp.zeros((same_own.shape[0], extra), jnp.float32)], 1
    )
    grad_logits = (
        positives_own[:, None] * jnp.exp(masked - log_own[:, None]) - weights_pos
    ) / total_count
    grad_dots = (logit_scale * grad_logits).astype(jnp.bfloat16)
    return fwd_dot(grad_dots, columns)


def cross_grads(rows, own, valid_own, same_own, positives_all, logs, logit_scale, total_count):
    logits = logit_scale * back_dot(rows, own)
    masked = jnp.where(valid_own[None, :], logits, -1e30)
    grad_logits = (
        positives_all[:, None] * jnp.exp(masked - logs[:, None]) - same_own.T
    ) / total_count
    grad_dots = (logit_scale * grad_logits).astype(jnp.bfloat16)
    return weight_grad(grad_dots, rows)


def body(
    flat_master,
    flat_first,
    flat_second,
    table,
    table_first,
    table_second,
    pixels,
    token_ids,
    end_pos,
    pair_counts,
    groups,
    cached_image,
    cached_text,
):
    gx_size, gy_size = lax.axis_size("gx"), lax.axis_size("gy")
    device_count = gx_size * gy_size
    my_index = linear_index(gy_size)
    pairs_dev = pixels.shape[0]
    shard = flat_master.shape[0]
    tokens = token_ids.size
    vocab_dev = table.shape[0]
    cap = route_capacity(tokens, gy_size)
    own_ids = token_ids.reshape(-1)
    same = own_ids[:, None] == own_ids[None, :]
    order = jnp.arange(tokens)
    leading = ~jnp.any(same & (order[None, :] < order[:, None]), 1)
    flat_ids = jnp.where(leading, own_ids, NO_TOKEN)
    flat_ids = jnp.pad(flat_ids, (0, ID_ROWS * LANES // 2 - tokens)).reshape(-1, LANES)
    payload = [
        place_window(flat_master, gy_size),
        jnp.concatenate([cached_image, cached_text], 0).reshape(CACHED_ROWS, LANES),
        jnp.concatenate([flat_ids // 256, flat_ids % 256], 0).astype(jnp.bfloat16),
    ]
    used = sum(part.shape[0] for part in payload)
    step = GROUP * GATHER_CHUNKS
    payload = jnp.pad(jnp.concatenate(payload, 0), ((0, -used % step), (0, 0)))
    gathered = gather_windows(payload, gx_size, gy_size, GATHER_CHUNKS, 4, "gather_weights")
    every_part = gathered.reshape(device_count, -1, LANES)
    cached = every_part[:, used - ID_ROWS - CACHED_ROWS : used - ID_ROWS].reshape(device_count, -1, EMBED)
    cache_img, cache_txt = lax.optimization_barrier((cached[:, :pairs_dev], cached[:, pairs_dev:]))
    cache_img, cache_txt = cache_img.reshape(-1, EMBED), cache_txt.reshape(-1, EMBED)
    coded = every_part[:, used - ID_ROWS : used].astype(jnp.int32)
    ids_all = coded[:, : ID_ROWS // 2] * 256 + coded[:, ID_ROWS // 2 :]
    ids_all = ids_all.reshape(device_count, -1)[:, :tokens]
    holders = ids_all // vocab_dev
    pair_rows = jnp.sum(holders[:, :, None] == jnp.arange(gy_size), 1)
    rounds = (jnp.max(pair_rows) + cap - 1) // cap
    me_y = lax.axis_index("gy")
    held = holders == me_y
    held_rank = jnp.where(held, ranks(held), -1)
    held_row = ids_all - me_y * vocab_dev
    held_count = jnp.sum(held, 1)
    own_flags = (jnp.arange(gy_size)[:, None] == own_ids[None, :] // vocab_dev) & leading[None, :]
    own_place = jnp.arange(gy_size)[:, None] * tokens + ranks(own_flags)
    own_place = jnp.sum(jnp.where(own_flags, own_place, 0), 0)
    own_place = jnp.sum(jnp.where(same & leading[None, :], own_place[None, :], 0), 1)
    own_holder, own_rank = own_place // tokens, own_place % tokens

    def held_rows(turn):
        slots = held_rank - turn * cap
        found = slots[:, None, :] == jnp.arange(cap)[None, :, None]
        return vocab_dev + jnp.sum(jnp.where(found, held_row[:, None, :] - vocab_dev, 0), 2)

    def own_slots(turn):
        rank = own_rank - turn * cap
        return jnp.where((rank >= 0) & (rank < cap), own_holder * cap + rank, -1)

    first_rows = held_rows(0)
    group_start = lax.axis_index("gx") * gy_size

    def rows_to_send(index):
        index = lax.dynamic_slice_in_dim(index, group_start, gy_size, 0)
        rows = jnp.take(table, index.reshape(-1), axis=0, mode="clip")
        return rows.reshape(gy_size, cap, D_TXT)

    sent = rows_to_send(first_rows).astype(jnp.bfloat16)
    slot_count = gy_size * cap

    def more_rows(turn, found):
        rows = lax.all_to_all(rows_to_send(held_rows(turn)), "gy", 0, 0, tiled=True)
        rows = rows.reshape(slot_count, D_TXT).astype(jnp.bfloat16)
        return found + weight_grad(pick_matrix(own_slots(turn), slot_count), rows).astype(jnp.bfloat16)

    nothing = jnp.zeros((tokens, D_TXT), jnp.bfloat16)
    extra_rows = lax.cond(
        rounds > 1, lambda rows: lax.fori_loop(1, rounds, more_rows, rows), lambda rows: rows, nothing
    )
    sent, extra_rows = lax.optimization_barrier((sent, extra_rows))
    *spread, landed = spread_weights(gathered, sent, shard, gx_size, gy_size, 5)
    picks = pick_matrix(own_slots(0), slot_count)
    token_rows = weight_grad(picks, landed.reshape(slot_count, D_TXT)).astype(jnp.bfloat16)

    token_rows = token_rows + extra_rows
    image_weights = dict(zip(IMAGE.names, spread[:5]))
    text_weights = dict(zip(TEXT.names, spread[5:9]))
    image_vec, text_vec, temper = split_vectors(spread[9])
    image_gains, image_base, image_rows = image_inputs(image_vec, pixels)
    text_gains, text_base, text_rows = text_inputs(text_vec, token_rows)
    image_kept = tower_forward(IMAGE, end_pos, image_gains, image_base, image_rows, image_weights)
    text_kept = tower_forward(TEXT, end_pos, text_gains, text_base, text_rows, text_weights)
    image_emb = image_kept[14].astype(jnp.bfloat16)
    text_emb = text_kept[14].astype(jnp.bfloat16)
    embeds = jnp.concatenate([image_emb, text_emb], 0).reshape(-1, LANES)
    embeds = gather_windows(embeds, gx_size, gy_size, 1, 0, "embeddings")
    embeds = embeds.reshape(device_count, 2 * pairs_dev, EMBED)
    all_img, all_txt = lax.optimization_barrier((embeds[:, :pairs_dev], embeds[:, pairs_dev:]))
    all_img, all_txt = all_img.reshape(-1, EMBED), all_txt.reshape(-1, EMBED)
    total_pairs = all_img.shape[0]
    valid_all = jnp.arange(total_pairs) % pairs_dev < jnp.repeat(pair_counts.reshape(-1), pairs_dev)
    matches = (
        (groups[:, None] == groups[None, :]) & valid_all[:, None] & valid_all[None, :]
    ).astype(jnp.float32)
    positives_all = jnp.sum(matches, 1)
    total_count = 2.0 * jnp.sum(positives_all)
    own_start = my_index * pairs_dev
    own_part = functools.partial(
        lax.dynamic_slice_in_dim, start_index=own_start, slice_size=pairs_dev, axis=0
    )
    same_own, positives_own, valid_own = own_part(matches), own_part(positives_all), own_part(valid_all)
    logit_scale = jnp.exp(temper)
    column_ok = jnp.concatenate([valid_all, jnp.ones((cache_img.shape[0],), jnp.bool_)])
    columns_txt = jnp.concatenate([all_txt, cache_txt])
    columns_img = jnp.concatenate([all_img, cache_img])
    log_img, loss_one, pull_one = log_sums(
        all_img, columns_txt, column_ok, logit_scale, matches, positives_all
    )
    log_txt, loss_two, pull_two = log_sums(
        all_txt, columns_img, column_ok, logit_scale, matches, positives_all
    )
    grad_temper = logit_scale * (pull_one + pull_two) / total_count
    loss_sum = loss_one + loss_two
    grad_img = side_grads(
        image_emb, columns_txt, column_ok, same_own, positives_own, own_part(log_img), logit_scale, total_count
    )
    grad_txt = side_grads(
        text_emb, columns_img, column_ok, same_own, positives_own, own_part(log_txt), logit_scale, total_count
    )
    grad_img = grad_img + cross_grads(
        all_txt, image_emb, valid_own, same_own, positives_all, log_txt, logit_scale, total_count
    )
    grad_txt = grad_txt + cross_grads(
        all_img, text_emb, valid_own, same_own, positives_all, log_img, logit_scale, total_count
    )
    text_grads = tower_backward(TEXT, end_pos, text_gains, grad_txt, text_kept[:14], text_weights)
    grad_rows = text_grads[6][: SEQS * CTX]
    to_holders = fwd_dot(picks, grad_rows).astype(jnp.bfloat16).reshape(gy_size, cap, D_TXT)
    image_grads = tower_backward(IMAGE, end_pos, image_gains, grad_img, image_kept[:14], image_weights)
    pair_lists = ([(image_rows, image_grads[6])],) + grad_pairs(image_kept, image_grads)
    pair_lists = pair_lists + grad_pairs(text_kept, text_grads)
    total_rows = window_start(shard, device_count - 1) + window_rows(shard, GROUP * CHUNKS)
    vec_rows = jnp.concatenate(
        [
            image_grads[7][:1].reshape(-1, LANES),
            image_grads[7].reshape(-1, LANES),
            image_grads[8].reshape(-1, LANES),
            text_grads[7].reshape(-1, LANES),
            text_grads[8][2:].reshape(-1, LANES),
        ]
    )
    vec_rows = jnp.pad(vec_rows, ((0, total_rows - matrix_rows() - vec_rows.shape[0]), (0, 0)))
    local_grads, arrived = weight_grads(pair_lists, vec_rows, to_holders, gx_size, gy_size, 6)
    table_grad, table_square = table_sum(
        jnp.minimum(held_count, cap),
        first_rows.reshape(-1),
        arrived.reshape(device_count, cap, D_TXT),
        vocab_dev,
    )

    def more_grads(turn, total):
        rows = fwd_dot(pick_matrix(own_slots(turn), slot_count), grad_rows).astype(jnp.bfloat16)
        rows = lax.all_to_all(rows.reshape(gy_size, cap, D_TXT), "gy", 0, 0, tiled=True)
        rows = lax.all_gather(rows, "gx", axis=0).reshape(device_count * cap, D_TXT).astype(jnp.float32)
        return total.at[held_rows(turn).reshape(-1)].add(rows)

    table_grad, table_squares = lax.cond(
        rounds > 1,
        lambda total, square: (
            lambda whole: (whole, jnp.sum(whole[:vocab_dev] * whole[:vocab_dev]))
        )(lax.fori_loop(1, rounds, more_grads, total)),
        lambda total, square: (total, jnp.sum(square)),
        table_grad,
        table_square,
    )
    grad_window = reduce_windows(local_grads, shard, gx_size, gy_size, 1)
    position = my_index * shard + jnp.arange(shard)
    grad_shard = lift_window(grad_window, shard, gy_size)
    grad_shard = jnp.where(position == parameter_count() - 1, grad_temper, grad_shard)
    table_squares = jnp.where(lax.axis_index("gx") == 0, table_squares, 0.0)
    squares = jnp.sum(grad_shard * grad_shard) + table_squares
    (every,) = exchange_all([jnp.full((8, LANES), squares)], gx_size, gy_size, 2, "squares")
    grad_norm = jnp.sqrt(jnp.sum(every[:, 0, 0]))
    factor = jnp.minimum(1.0, clip_limit / (grad_norm + 1e-06))
    matrix_stop = matrix_rows() * LANES
    is_matrix = position < matrix_stop
    rates = jnp.where(is_matrix, rate_matrix, rate_vector)
    decays = jnp.where(is_matrix, decay_rate, 0.0)
    master_out, first_out, second_out = adam_step(
        flat_master, flat_first, flat_second, grad_shard * factor, rates, decays
    )
    table_out, table_first_out, table_second_out = adam_step(
        table, table_first, table_second, table_grad[:vocab_dev] * factor, rate_table, 0.0
    )
    return (
        master_out,
        first_out,
        second_out,
        table_out,
        table_first_out,
        table_second_out,
        loss_sum,
        total_count,
        grad_norm,
    )


def solution(mesh):
    placed = (
        P(("gx", "gy")),
        P(("gx", "gy")),
        P(("gx", "gy")),
        P("gy", None),
        P("gy", None),
        P("gy", None),
        P(("gx", "gy"), None, None),
        P(("gx", "gy"), None),
        P(("gx", "gy")),
        P(),
        P(),
        P(("gx", "gy"), None),
        P(("gx", "gy"), None),
    )
    return jax.shard_map(
        body,
        mesh=mesh,
        in_specs=placed,
        out_specs=(
            P(("gx", "gy")),
            P(("gx", "gy")),
            P(("gx", "gy")),
            P("gy", None),
            P("gy", None),
            P("gy", None),
            P(),
            P(),
            P(),
        ),
        check_vma=False,
    )
```

```python
import functools

import jax
import jax.numpy as jnp
from jax import lax
from jax.experimental import pallas as pl
from jax.experimental.pallas import tpu as pltpu
from jax.sharding import PartitionSpec as P

D_IMG = 768
IMG_HEADS = 12
IMG_MLP = 3072
PATCH_DIM = 3072
D_TXT = 512
TXT_HEADS = 8
TXT_MLP = 2048
CTX = 77
EMBED = 512
STEP = 10
IMG_TOK = 50


clip_limit = 0.1
beta_one = 0.9
beta_two = 0.999
adam_eps = 1e-08
decay_rate = 0.1
rate_matrix = 0.01
rate_vector = 0.2
rate_table = 0.2
norm_eps = 1e-05


def segment_list():
    return [
        ("patch_embed", PATCH_DIM, D_IMG),
        ("image_attn", D_IMG, 4 * D_IMG),
        ("image_up", D_IMG, IMG_MLP),
        ("image_down", IMG_MLP, D_IMG),
        ("image_proj", D_IMG, EMBED),
        ("text_attn", D_TXT, 4 * D_TXT),
        ("text_up", D_TXT, TXT_MLP),
        ("text_down", TXT_MLP, D_TXT),
        ("text_proj", D_TXT, EMBED),
        ("image_vec", IMG_TOK + 9, D_IMG),
        ("text_vec", CTX + 6, D_TXT),
        ("temper", 1, 1),
    ]


LANES = 128
GROUP = 16
CHUNKS = 16
GATHER_CHUNKS = 14
CACHED_ROWS = 64
ID_ROWS = 16
MESH = pl.DeviceIdType.MESH


def dot_nn(left_side, right_side):
    return lax.dot_general(
        left_side, right_side, (((1,), (0,)), ((), ())), preferred_element_type=jnp.float32
    )


def dot_nt(left_side, right_side):
    return lax.dot_general(
        left_side, right_side, (((1,), (1,)), ((), ())), preferred_element_type=jnp.float32
    )


def dot_tn(left_side, right_side):
    return lax.dot_general(
        left_side, right_side, (((0,), (0,)), ((), ())), preferred_element_type=jnp.float32
    )


def back_dot(left_side, right_side):
    return dot_nt(left_side, right_side)


def fwd_dot(left_side, right_side):
    return dot_nn(left_side, right_side)


def weight_grad(left_side, right_side):
    return dot_tn(left_side, right_side)


def norm_parts(values):
    center = values - jnp.mean(values, -1, keepdims=True)
    scale = lax.rsqrt(jnp.mean(center * center, -1, keepdims=True) + norm_eps)
    return center * scale, scale


def layer_norm(values, gain_vec, shift_vec):
    return norm_parts(values)[0] * gain_vec + shift_vec


def layer_norm_back(values, gain_vec, grad):
    unit, scale = norm_parts(values)
    grad_unit = grad * gain_vec
    inner = jnp.mean(grad_unit, -1, keepdims=True)
    along = jnp.mean(grad_unit * unit, -1, keepdims=True)
    return scale * (grad_unit - inner - unit * along), grad * unit


def sum_rows(values):
    return jnp.sum(values, 0, keepdims=True)


def low16(values):
    return jnp.concatenate([values, jnp.zeros_like(values)], 0).astype(jnp.bfloat16)


SEQS = 8


class Tower:
    def __init__(self, image):
        self.image = image
        self.width = D_IMG if image else D_TXT
        self.heads = IMG_HEADS if image else TXT_HEADS
        self.length = IMG_TOK if image else CTX
        self.rows = -(-SEQS * self.length // GROUP) * GROUP
        self.lanes = 16 if image else 8
        self.queries = SEQS * self.lanes
        self.block = 80 if image else 48
        self.names = ("patch", "attn", "up", "down", "proj") if image else ("attn", "up", "down", "proj")

    def shapes(self):
        width = self.width
        found = dict(attn=(width, 4 * width), up=(width, 4 * width), down=(4 * width, width), proj=(width, EMBED))
        if self.image:
            found["patch"] = (PATCH_DIM, width)
        return found

    def head_mask(self):
        lane = lax.broadcasted_iota(jnp.int32, (self.lanes, self.width), 1)
        row = lax.broadcasted_iota(jnp.int32, (self.lanes, self.width), 0)
        return lane // (self.width // self.heads) == row

    def spread_heads(self, values, wide_ref):
        mask = self.head_mask()
        for s in range(SEQS):
            row = jnp.broadcast_to(values[s : s + 1].astype(jnp.float32), mask.shape)
            wide_ref[s * self.lanes : (s + 1) * self.lanes, :] = jnp.where(mask, row, 0.0)
        return wide_ref[...].astype(jnp.bfloat16)

    def join_heads(self, values, wide_ref):
        mask = self.head_mask()
        wide_ref[...] = values
        rows = [
            sum_rows(jnp.where(mask, wide_ref[s * self.lanes : (s + 1) * self.lanes, :], 0.0))
            for s in range(SEQS)
        ]
        return jnp.concatenate(rows, 0)

    def row_of(self, s, ends_ref):
        return s * self.length + (0 if self.image else ends_ref[s])

    def each_block(self, function, start):
        return lax.fori_loop(
            0,
            self.rows // self.block,
            lambda i, carry: function(pl.ds(pl.multiple_of(i * self.block, GROUP), self.block), carry),
            start,
        )


def tower_fetch(names, sources, landed, sems):
    copies = {
        name: pltpu.make_async_copy(source, ref, sems.at[i])
        for i, (name, source, ref) in enumerate(zip(names, sources, landed))
    }
    for copy in copies.values():
        copy.start()
    return copies, dict(zip(names, landed))


def tower_forward_kernel(tower, *refs):
    count = len(tower.names)
    ends_ref, gains_ref, base_ref, input_ref = refs[:4]
    sources = refs[4 : 4 + count]
    (tokens_ref, normed_ref, pair_ref, normed_own_ref, query_ref, probs_ref, attended_ref, middle_ref, normed_two_ref,
     upper_ref, act_ref, output_ref, head_ref, raw_ref, emb_ref) = refs[4 + count : 19 + count]
    hidden_ref, wide_ref = refs[19 + count : 21 + count]
    landed, sems = refs[21 + count : 21 + 2 * count], refs[21 + 2 * count]
    copies, weights = tower_fetch(tower.names, sources, landed, sems)
    width = tower.width
    gains = [gains_ref[i : i + 1, :] for i in range(8)]
    if tower.image:
        copies["patch"].wait()

        def patch(j, carry):
            cols = pl.ds(pl.multiple_of(j * 256, 256), 256)
            tokens_ref[:, cols] = dot_nn(input_ref[...], weights["patch"][:, cols]) + base_ref[:, cols]
            return carry

        lax.fori_loop(0, width // 256, patch, 0)

    def first(rows, carry):
        if tower.image:
            hidden = layer_norm(tokens_ref[rows, :], gains[0], gains[1])
        else:
            hidden = input_ref[rows, :].astype(jnp.float32) + base_ref[rows, :]
            tokens_ref[rows, :] = hidden
        hidden_ref[rows, :] = hidden
        normed_ref[rows, :] = layer_norm(hidden, gains[2], gains[3]).astype(jnp.bfloat16)
        return carry

    tower.each_block(first, 0)
    copies["attn"].wait()

    def pair(j, carry):
        at = pl.multiple_of(j * 256, 256)
        product = dot_nn(normed_ref[...], weights["attn"][:, pl.ds(width + at, 256)])
        pair_ref[:, pl.ds(at, 256)] = product.astype(jnp.bfloat16)
        return carry

    lax.fori_loop(0, 2 * width // 256, pair, 0)
    hidden_own = jnp.concatenate(
        [hidden_ref[pl.ds(tower.row_of(s, ends_ref), 1), :] for s in range(SEQS)], 0
    )
    normed_own = low16(layer_norm(hidden_own, gains[2], gains[3]))
    normed_own_ref[...] = normed_own
    query = dot_nn(normed_own, weights["attn"][:, :width]).astype(jnp.bfloat16)
    query_ref[...] = query
    queries = tower.spread_heads(query, wide_ref)
    scores = dot_nt(queries, pair_ref[:, :width]) * (width // tower.heads) ** (-0.5)
    row = lax.broadcasted_iota(jnp.int32, scores.shape, 0) // tower.lanes
    spot = lax.broadcasted_iota(jnp.int32, scores.shape, 1) - row * tower.length
    last = jnp.full(scores.shape, tower.length - 1, jnp.int32)
    if not tower.image:
        for s in range(SEQS):
            last = jnp.where(row == s, ends_ref[s], last)
    scores = jnp.where((spot >= 0) & (spot <= last), scores, -1e30)
    powers = jnp.exp(scores - jnp.max(scores, -1, keepdims=True))
    probs = powers / jnp.sum(powers, -1, keepdims=True)
    probs_ref[...] = probs
    attended = low16(tower.join_heads(dot_nn(probs.astype(jnp.bfloat16), pair_ref[:, width:]), wide_ref))
    attended_ref[...] = attended
    middle = hidden_own + dot_nn(attended, weights["attn"][:, 3 * width :])[:SEQS]
    middle_ref[...] = middle
    normed_two_ref[...] = low16(layer_norm(middle, gains[4], gains[5]))
    copies["up"].wait()

    def rise(j, carry):
        cols = pl.ds(pl.multiple_of(j * 512, 512), 512)
        upper = dot_nn(normed_two_ref[...], weights["up"][:, cols])[:SEQS]
        upper_ref[:, cols] = upper
        act_ref[:, cols] = low16(upper * jax.nn.sigmoid(1.702 * upper))
        return carry

    lax.fori_loop(0, 4 * width // 512, rise, 0)
    copies["down"].wait()

    def fall(j, carry):
        cols = pl.ds(pl.multiple_of(j * 256, 256), 256)
        output_ref[:, cols] = middle_ref[:, cols] + dot_nn(act_ref[...], weights["down"][:, cols])[:SEQS]
        return carry

    lax.fori_loop(0, width // 256, fall, 0)
    head_in = low16(layer_norm(output_ref[...], gains[6], gains[7]))
    head_ref[...] = head_in
    copies["proj"].wait()
    raw = dot_nn(head_in, weights["proj"][...])[:SEQS]
    raw_ref[...] = raw
    emb_ref[...] = raw * lax.rsqrt(jnp.sum(raw * raw, -1, keepdims=True) + 1e-06)


def tower_forward(tower, ends, gains, base, inputs, weights):
    width, rows = tower.width, tower.rows
    low, full = jnp.bfloat16, jnp.float32
    outs = [
        ((rows, width), full),
        ((rows, width), low),
        ((rows, 2 * width), low),
        ((GROUP, width), low),
        ((GROUP, width), low),
        ((tower.queries, rows), full),
        ((GROUP, width), low),
        ((SEQS, width), full),
        ((GROUP, width), low),
        ((SEQS, 4 * width), full),
        ((GROUP, 4 * width), low),
        ((SEQS, width), full),
        ((GROUP, width), low),
        ((SEQS, EMBED), full),
        ((SEQS, EMBED), full),
    ]
    vmem = pl.BlockSpec(memory_space=pltpu.VMEM)
    shapes = tower.shapes()
    return pl.pallas_call(
        functools.partial(tower_forward_kernel, tower),
        out_shape=[jax.ShapeDtypeStruct(shape, kind) for shape, kind in outs],
        in_specs=[pl.BlockSpec(memory_space=pltpu.SMEM)]
        + [vmem] * 3
        + [pl.BlockSpec(memory_space=pl.ANY)] * len(tower.names),
        out_specs=[vmem] * len(outs),
        scratch_shapes=[pltpu.VMEM((rows, width), full), pltpu.VMEM((tower.queries, width), full)]
        + [pltpu.VMEM(shapes[name], low) for name in tower.names]
        + [pltpu.SemaphoreType.DMA((len(tower.names),))],
        compiler_params=pltpu.CompilerParams(vmem_limit_bytes=58 << 20),
        name="image_forward" if tower.image else "text_forward",
    )(ends, gains, base, inputs, *[weights[name] for name in tower.names])


def tower_backward_kernel(tower, *refs):
    names = tower.names[-4:]
    count = len(names)
    ends_ref, gains_ref, grad_ref = refs[:3]
    (tokens_ref, normed_ref, pair_ref, normed_own_ref, query_ref, probs_ref, attended_ref, middle_ref, normed_two_ref,
     upper_ref, act_ref, output_ref, head_ref, raw_ref) = refs[3:17]
    sources = refs[17 : 17 + count]
    (grad_raw_ref, grad_mlp_ref, grad_upper_ref, grad_att_ref, grad_query_ref, grad_pair_ref, grad_rows_ref,
     places_ref, gain_grads_ref) = refs[17 + count : 26 + count]
    grad_ref_wide, wide_ref, grad_middle_ref = refs[26 + count : 29 + count]
    landed, sems = refs[29 + count : 29 + 2 * count], refs[29 + 2 * count]
    copies, weights = tower_fetch(names, sources, landed, sems)
    width, rows = tower.width, tower.rows
    scale = (width // tower.heads) ** (-0.5)
    gains = [gains_ref[i : i + 1, :] for i in range(8)]
    raw, grad_emb = raw_ref[...], grad_ref[...]
    norm = lax.rsqrt(jnp.sum(raw * raw, -1, keepdims=True) + 1e-06)
    along = jnp.sum(raw * grad_emb, -1, keepdims=True)
    grad_raw = low16(grad_emb * norm - raw * (norm * norm * norm * along))
    grad_raw_ref[...] = grad_raw
    copies["proj"].wait()
    grad_head = dot_nt(grad_raw, weights["proj"][...])[:SEQS]
    grad_out, gain_part = layer_norm_back(output_ref[...], gains[6], grad_head)
    gain_grads_ref[6:7, :] = sum_rows(gain_part)
    gain_grads_ref[7:8, :] = sum_rows(grad_head)
    grad_mlp_ref[...] = low16(grad_out)
    copies["down"].wait()

    def rise(j, carry):
        cols = pl.ds(pl.multiple_of(j * 512, 512), 512)
        grad_act = dot_nt(grad_mlp_ref[...], weights["down"][cols, :])[:SEQS]
        upper = upper_ref[:, cols]
        sig = jax.nn.sigmoid(1.702 * upper)
        grad_upper_ref[:, cols] = low16(grad_act * (sig + upper * (1.702 * (sig * (1.0 - sig)))))
        return carry

    lax.fori_loop(0, 4 * width // 512, rise, 0)
    copies["up"].wait()

    def fall(j, carry):
        cols = pl.ds(pl.multiple_of(j * 256, 256), 256)
        grad_middle_ref[:, cols] = dot_nt(grad_upper_ref[...], weights["up"][cols, :])[:SEQS]
        return carry

    lax.fori_loop(0, width // 256, fall, 0)
    grad_norm_two = grad_middle_ref[...]
    grad_mid, gain_part = layer_norm_back(middle_ref[...], gains[4], grad_norm_two)
    gain_grads_ref[4:5, :] = sum_rows(gain_part)
    gain_grads_ref[5:6, :] = sum_rows(grad_norm_two)
    grad_middle = grad_out + grad_mid
    grad_middle_ref[...] = grad_middle
    grad_att = low16(grad_middle)
    grad_att_ref[...] = grad_att
    copies["attn"].wait()
    grad_attended = dot_nt(grad_att, weights["attn"][:, 3 * width :]).astype(jnp.bfloat16)
    grads_heads = tower.spread_heads(grad_attended, wide_ref)
    queries = tower.spread_heads(query_ref[...], wide_ref)
    probs = probs_ref[...]
    grad_probs = dot_nt(grads_heads, pair_ref[:, width:])
    grad_scores = probs * (grad_probs - jnp.sum(grad_probs * probs, -1, keepdims=True))
    grad_scores = grad_scores.astype(jnp.bfloat16)
    grad_query = low16(tower.join_heads(dot_nn(grad_scores, pair_ref[:, :width]), wide_ref) * scale)
    grad_query_ref[...] = grad_query
    grad_pair_ref[:, :width] = (dot_tn(grad_scores, queries) * scale).astype(jnp.bfloat16)
    grad_pair_ref[:, width:] = dot_tn(probs.astype(jnp.bfloat16), grads_heads).astype(jnp.bfloat16)

    def inner(j, carry):
        at = pl.multiple_of(j * 256, 256)
        grad_ref_wide[:, pl.ds(at, 256)] = dot_nt(
            grad_pair_ref[...], weights["attn"][pl.ds(at, 256), width : 3 * width]
        )
        return carry

    lax.fori_loop(0, width // 256, inner, 0)
    grad_own = dot_nt(grad_query, weights["attn"][:, :width])
    for s in range(SEQS):
        grad_ref_wide[pl.ds(tower.row_of(s, ends_ref), 1), :] += grad_own[s : s + 1]

    def first(at, carry):
        grad = grad_ref_wide[at, :]
        hidden = tokens_ref[at, :]
        if tower.image:
            hidden = layer_norm(hidden, gains[0], gains[1])
        grad_in, gain_part = layer_norm_back(hidden, gains[2], grad)
        grad_ref_wide[at, :] = grad_in
        return carry[0] + sum_rows(gain_part), carry[1] + sum_rows(grad)

    nothing = jnp.zeros((1, width), jnp.float32)
    gain_one, shift_one = tower.each_block(first, (nothing, nothing))
    gain_grads_ref[2:3, :] = gain_one
    gain_grads_ref[3:4, :] = shift_one
    for s in range(SEQS):
        grad_ref_wide[pl.ds(tower.row_of(s, ends_ref), 1), :] += grad_middle_ref[s : s + 1, :]

    def second(at, carry):
        grad = grad_ref_wide[at, :]
        if not tower.image:
            grad_rows_ref[at, :] = grad.astype(jnp.bfloat16)
            return carry
        grad_in, gain_part = layer_norm_back(tokens_ref[at, :], gains[0], grad)
        grad_ref_wide[at, :] = grad_in
        grad_rows_ref[at, :] = grad_in.astype(jnp.bfloat16)
        return carry[0] + sum_rows(gain_part), carry[1] + sum_rows(grad)

    gain_pre, shift_pre = tower.each_block(second, (nothing, nothing))
    gain_grads_ref[0:1, :] = gain_pre
    gain_grads_ref[1:2, :] = shift_pre
    places = grad_ref_wide[0 : tower.length, :]
    for s in range(1, SEQS):
        places = places + grad_ref_wide[s * tower.length : (s + 1) * tower.length, :]
    places_ref[...] = places


def tower_backward(tower, ends, gains, grad_emb, kept, weights):
    width, rows = tower.width, tower.rows
    low, full = jnp.bfloat16, jnp.float32
    outs = [
        ((GROUP, EMBED), low),
        ((GROUP, width), low),
        ((GROUP, 4 * width), low),
        ((GROUP, width), low),
        ((GROUP, width), low),
        ((rows, 2 * width), low),
        ((rows, width), low),
        ((tower.length, width), full),
        ((8, width), full),
    ]
    vmem = pl.BlockSpec(memory_space=pltpu.VMEM)
    shapes, names = tower.shapes(), tower.names[-4:]
    return pl.pallas_call(
        functools.partial(tower_backward_kernel, tower),
        out_shape=[jax.ShapeDtypeStruct(shape, kind) for shape, kind in outs],
        in_specs=[pl.BlockSpec(memory_space=pltpu.SMEM)]
        + [vmem] * (2 + len(kept))
        + [pl.BlockSpec(memory_space=pl.ANY)] * len(names),
        out_specs=[vmem] * len(outs),
        scratch_shapes=[
            pltpu.VMEM((rows, width), full),
            pltpu.VMEM((tower.queries, width), full),
            pltpu.VMEM((SEQS, width), full),
        ]
        + [pltpu.VMEM(shapes[name], low) for name in names]
        + [pltpu.SemaphoreType.DMA((len(names),))],
        compiler_params=pltpu.CompilerParams(vmem_limit_bytes=58 << 20),
        name="image_backward" if tower.image else "text_backward",
    )(ends, gains, grad_emb, *kept, *[weights[name] for name in names])


def grad_pairs(kept, grads):
    (normed, normed_own, attended, normed_two, act_low, head_in) = (
        kept[1], kept[3], kept[6], kept[8], kept[10], kept[12]
    )
    grad_raw, grad_mlp, grad_upper, grad_att, grad_query, grad_pair = grads[:6]
    return (
        [(normed_own, grad_query), (normed, grad_pair), (attended, grad_att)],
        [(normed_two, grad_upper)],
        [(act_low, grad_mlp)],
        [(head_in, grad_raw)],
    )


def image_inputs(image_vec, pixels):
    pixels = jnp.pad(pixels, ((0, 0), (1, 0), (0, 0))).reshape(-1, PATCH_DIM)
    base = image_vec[1 : IMG_TOK + 1] + jnp.pad(image_vec[:1], ((0, IMG_TOK - 1), (0, 0)))
    return image_vec[IMG_TOK + 1 :], jnp.tile(base, (SEQS, 1)), pixels


def text_inputs(text_vec, token_rows):
    gains = jnp.pad(text_vec[CTX:], ((2, 0), (0, 0)))
    extra = TEXT.rows - SEQS * CTX
    base = jnp.pad(jnp.tile(text_vec[:CTX], (SEQS, 1)), ((0, extra), (0, 0)))
    return gains, base, jnp.pad(token_rows, ((0, extra), (0, 0)))


def adam_step(weight, first, second, grad, rate, decay):
    first = beta_one * first + (1.0 - beta_one) * grad
    second = beta_two * second + (1.0 - beta_two) * grad * grad
    first_hat = first / (1.0 - beta_one**STEP)
    second_hat = second / (1.0 - beta_two**STEP)
    weight = weight - rate * (first_hat / (jnp.sqrt(second_hat) + adam_eps) + decay * weight)
    return (weight, first, second)


IMAGE, TEXT = Tower(True), Tower(False)


def matrix_rows():
    return sum(seg_rows * seg_cols for seg_name, seg_rows, seg_cols in segment_list()[:9]) // LANES


def parameter_count():
    return sum(seg_rows * seg_cols for seg_name, seg_rows, seg_cols in segment_list())


def window_rows(shard, step=GROUP):
    need = -(-(GROUP * LANES - 1 + shard) // LANES)
    return -(-need // step) * step


def window_start(shard, index):
    return (shard * index // (GROUP * LANES)) * GROUP


def linear_index(gy_size):
    return lax.axis_index("gx") * gy_size + lax.axis_index("gy")


def place_kernel(shard, gy_size, flat_ref, out_ref, rolled):
    rows = flat_ref.shape[0]
    offset = lax.rem(shard * linear_index(gy_size), GROUP * LANES)
    down, right = offset // LANES, lax.rem(offset, LANES)
    pad = 2 * GROUP
    rolled[0:pad, :] = jnp.zeros((pad, LANES), jnp.float32)
    parts = 5 if rows % (5 * GROUP) == 0 else 1
    step = rows // parts

    def roll_rows(i, carry):
        at = pl.multiple_of(i * step, GROUP)
        rolled[pl.ds(pad + at, step), :] = pltpu.roll(flat_ref[pl.ds(at, step), :], right, 1)
        return carry

    lax.fori_loop(0, parts, roll_rows, 0)
    lane = lax.broadcasted_iota(jnp.int32, (step, LANES), 1)

    def put_rows(i, carry):
        at = pl.multiple_of(i * step, GROUP)
        upper = rolled[pl.ds(pad + at - down - 1, step), :]
        lower = rolled[pl.ds(pad + at - down, step), :]
        out_ref[pl.ds(at, step), :] = jnp.where(lane < right, upper, lower).astype(jnp.bfloat16)
        return carry

    lax.fori_loop(0, parts, put_rows, 0)


def place_window(flat, gy_size):
    shard = flat.shape[0]
    rows = window_rows(shard)
    padded = jnp.pad(flat, (0, rows * LANES - shard)).reshape(rows, LANES)
    return pl.pallas_call(
        functools.partial(place_kernel, shard, gy_size),
        out_shape=jax.ShapeDtypeStruct((rows, LANES), jnp.bfloat16),
        in_specs=[pl.BlockSpec(memory_space=pltpu.VMEM)],
        out_specs=pl.BlockSpec(memory_space=pltpu.VMEM),
        scratch_shapes=[pltpu.VMEM((rows + 2 * GROUP, LANES), jnp.float32)],
        compiler_params=pltpu.CompilerParams(vmem_limit_bytes=32 << 20),
        name="place_window",
    )(padded)


def lift_kernel(shard, gy_size, window_ref, out_ref, rolled):
    rows = window_ref.shape[0]
    offset = lax.rem(shard * linear_index(gy_size), GROUP * LANES)
    up, left = offset // LANES, lax.rem(offset, LANES)
    pad = 2 * GROUP
    step = rows // CHUNKS
    rolled[rows:, :] = jnp.zeros((pad, LANES), jnp.float32)

    def roll_rows(i, carry):
        at = pl.multiple_of(i * step, GROUP)
        rolled[pl.ds(at, step), :] = pltpu.roll(
            window_ref[pl.ds(at, step), :], lax.rem(LANES - left, LANES), 1
        )
        return carry

    lax.fori_loop(0, CHUNKS, roll_rows, 0)
    lane = lax.broadcasted_iota(jnp.int32, (step, LANES), 1)

    def put_rows(i, carry):
        at = pl.multiple_of(i * step, GROUP)
        first = rolled[pl.ds(at + up, step), :]
        second = rolled[pl.ds(at + up + 1, step), :]
        out_ref[pl.ds(at, step), :] = jnp.where(lane < LANES - left, first, second)
        return carry

    lax.fori_loop(0, CHUNKS, put_rows, 0)


def lift_window(window, shard, gy_size):
    rows = window.shape[0]
    lifted = pl.pallas_call(
        functools.partial(lift_kernel, shard, gy_size),
        out_shape=jax.ShapeDtypeStruct((rows, LANES), jnp.float32),
        in_specs=[pl.BlockSpec(memory_space=pltpu.VMEM)],
        out_specs=pl.BlockSpec(memory_space=pltpu.VMEM),
        scratch_shapes=[pltpu.VMEM((rows + 2 * GROUP, LANES), jnp.float32)],
        compiler_params=pltpu.CompilerParams(vmem_limit_bytes=32 << 20),
        name="lift_window",
    )(window)
    return lifted.reshape(-1)[:shard]


def spread_steps():
    steps = []
    base = 0
    for number, (seg_name, seg_rows, seg_cols) in enumerate(segment_list()[:9]):
        wide = seg_cols // LANES
        take = seg_rows
        while take * wide > 4608:
            take //= 2
        for start in range(0, seg_rows, take):
            steps.append((number, start, take, seg_cols, base + start * wide))
        base += seg_rows * wide
    return steps


def window_pieces(shard, count, stride, first, length):
    pieces, shared = [], []
    for index in range(count):
        low = window_start(shard, index)
        high = window_start(shard, index + 1) if index + 1 < count else low + window_rows(shard)
        start, stop = max(low, first), min(high, first + length)
        if start < stop:
            pieces.append((index * stride + start - low, start - first, stop - start))
        if index + 1 < count and first <= high < first + length:
            shared.append((index * stride + high - low, high - first))
    return pieces, shared


def spread_kernel(shard, count, vec_rows, share, gathered_ref, *refs):
    outs, vec_ref = refs[:9], refs[9]
    landed, edges, wide_rows, ready, in_sem, out_sem = refs[10:]
    rows = gathered_ref.shape[0] // count
    steps = spread_steps()
    steps.append((9, 0, vec_rows, LANES, matrix_rows()))

    def copies_in(number):
        seg, start, take, cols, base = steps[number]
        slot = number % 2
        pieces, shared = window_pieces(shard, count, rows, base, take * cols // LANES)
        found = [
            pltpu.make_async_copy(
                gathered_ref.at[pl.ds(src, size)], landed.at[slot, pl.ds(dst, size)], in_sem.at[slot]
            )
            for src, dst, size in pieces
        ]
        found += [
            pltpu.make_async_copy(
                gathered_ref.at[pl.ds(src, GROUP)], edges.at[slot, order], in_sem.at[slot]
            )
            for order, (src, dst) in enumerate(shared)
        ]
        return found, shared

    def copy_out(number):
        seg, start, take, cols, base = steps[number]
        slot = number % 2
        if seg == 9:
            return pltpu.make_async_copy(wide_rows.at[pl.ds(0, take)], vec_ref, out_sem.at[slot])
        return pltpu.make_async_copy(
            ready[cols].at[slot, pl.ds(0, take)], outs[seg].at[pl.ds(start, take)], out_sem.at[slot]
        )

    for copy in copies_in(0)[0]:
        copy.start()
    for number, (seg, start, take, cols, base) in enumerate(steps):
        if number == 4:
            share.greet()
            share.begin()
        slot = number % 2
        wide = cols // LANES
        total = take * wide
        if number + 1 < len(steps):
            for copy in copies_in(number + 1)[0]:
                copy.start()
        found, shared = copies_in(number)
        for copy in found:
            copy.wait()
        if number >= 2:
            copy_out(number - 2).wait()
        block = 256 if total % 256 == 0 else GROUP

        def widen(i, carry, slot=slot, block=block):
            at = pl.multiple_of(i * block, GROUP)
            wide_rows[pl.ds(at, block), :] = landed[slot, pl.ds(at, block), :].astype(jnp.float32)
            return carry

        lax.fori_loop(0, total // block, widen, 0)
        for order, (src, dst) in enumerate(shared):
            wide_rows[dst : dst + GROUP, :] += edges[slot, order].astype(jnp.float32)
        if seg < 9:

            def tile(i, carry, slot=slot, wide=wide, cols=cols):
                at = pl.multiple_of(i * GROUP, GROUP)
                for j in range(wide):
                    ready[cols][slot, pl.ds(at, GROUP), j * LANES : (j + 1) * LANES] = wide_rows[
                        pl.ds(at * wide + j, GROUP, stride=wide), :
                    ].astype(jnp.bfloat16)
                return carry

            lax.fori_loop(0, take // GROUP, tile, 0)
        copy_out(number).start()
    copy_out(len(steps) - 2).wait()
    copy_out(len(steps) - 1).wait()


def spread_entry(shard, gx_size, gy_size, vec_rows, gathered_ref, rows_ref, *refs):
    outs, landed_rows = refs[:10], refs[10]
    landed, edges, wide_rows, ready_a, ready_b, ready_c, ready_d, in_sem, out_sem = refs[11:20]
    ready = {D_IMG: ready_a, 4 * D_IMG: ready_b, D_TXT: ready_c, 4 * D_TXT: ready_d}
    share = Share(gx_size, gy_size, False, rows_ref, landed_rows, refs[20:])
    spread_kernel(
        shard, gx_size * gy_size, vec_rows, share, gathered_ref, *outs, landed, edges, wide_rows, ready, in_sem, out_sem
    )
    share.middle()
    share.finish()


def spread_weights(gathered, rows_to_send, shard, gx_size, gy_size, number):
    count = gx_size * gy_size
    rows = gathered.shape[0] // count
    steps = spread_steps()
    tallest = {}
    for seg, start, take, cols, base in steps:
        tallest[cols] = max(tallest.get(cols, 0), take)
    most = max(take * cols // LANES for seg, start, take, cols, base in steps)
    vec_rows = -(-(sum(r * c for name, r, c in segment_list()[9:])) // (LANES * GROUP)) * GROUP
    edge_count = max(
        len(window_pieces(shard, count, rows, base, take * cols // LANES)[1])
        for seg, start, take, cols, base in steps
    )
    ready = [
        pltpu.VMEM((2, tallest[cols], cols), jnp.bfloat16)
        for cols in (D_IMG, 4 * D_IMG, D_TXT, 4 * D_TXT)
    ]
    return pl.pallas_call(
        functools.partial(spread_entry, shard, gx_size, gy_size, vec_rows),
        out_shape=[
            jax.ShapeDtypeStruct((seg_rows, seg_cols), jnp.bfloat16)
            for seg_name, seg_rows, seg_cols in segment_list()[:9]
        ]
        + [
            jax.ShapeDtypeStruct((vec_rows, LANES), jnp.float32),
            jax.ShapeDtypeStruct((1,) + rows_to_send.shape, rows_to_send.dtype),
        ],
        in_specs=[pl.BlockSpec(memory_space=pl.ANY), pl.BlockSpec(memory_space=pltpu.VMEM)],
        out_specs=[pl.BlockSpec(memory_space=pl.ANY)] * 10 + [pl.BlockSpec(memory_space=pltpu.VMEM)],
        scratch_shapes=[
            pltpu.VMEM((2, most, LANES), jnp.bfloat16),
            pltpu.VMEM((2, edge_count + 1, GROUP, LANES), jnp.bfloat16),
            pltpu.VMEM((most, LANES), jnp.float32),
        ]
        + ready
        + [pltpu.SemaphoreType.DMA((2,)), pltpu.SemaphoreType.DMA((2,))]
        + share_sems(gx_size, gy_size),
        compiler_params=pltpu.CompilerParams(
            collective_id=number, has_side_effects=True, vmem_limit_bytes=48 << 20
        ),
        name="spread_weights",
    )(gathered, rows_to_send)


def split_vectors(vec_rows):
    image_count, text_count = (IMG_TOK + 9) * D_IMG // LANES, (CTX + 6) * D_TXT // LANES
    image_vec = vec_rows[:image_count].reshape(IMG_TOK + 9, D_IMG)
    text_vec = vec_rows[image_count : image_count + text_count].reshape(CTX + 6, D_TXT)
    return image_vec, text_vec, vec_rows[image_count + text_count, 0]


def grads_kernel(parts, gx_size, gy_size, *refs):
    operand_count = sum(2 * len(pairs) for seg_rows, seg_cols, take, pairs in parts)
    operands = refs[:operand_count]
    vec_ref, token_ref, out_ref, arrived_ref, flat_rows, vec_sem, out_sem = refs[operand_count : operand_count + 7]
    share = Share(gx_size, gy_size, True, token_ref, arrived_ref, refs[operand_count + 7 :])
    share.greet()
    share.begin()
    tail = pltpu.make_async_copy(vec_ref, out_ref.at[pl.ds(matrix_rows(), vec_ref.shape[0])], vec_sem)
    tail.start()
    base = 0
    steps_before = 0
    for number, (seg_rows, seg_cols, take, pairs) in enumerate(parts):
        if number == 2:
            share.middle()
        if number == 6:
            share.rest()
        wide = seg_cols // LANES
        size = take * wide
        count = seg_rows // take

        def step(i, carry, base=base, before=steps_before, size=size, take=take, wide=wide, pairs=pairs):
            slot = lax.rem(i + before, 2)

            def written(number):
                at = pl.multiple_of(base + number * size, 8)
                return pltpu.make_async_copy(
                    flat_rows.at[slot, pl.ds(0, size)], out_ref.at[pl.ds(at, size)], out_sem.at[slot]
                )

            @pl.when(i >= 2)
            def _():
                written(i - 2).wait()

            for left_number, right_number, first in pairs:
                left_ref, right_ref = operands[left_number], operands[right_number]
                at = pl.multiple_of(i * take, LANES)
                product = lax.dot_general(
                    left_ref[:, pl.ds(at, take)],
                    right_ref[...],
                    (((0,), (0,)), ((), ())),
                    preferred_element_type=jnp.float32,
                )
                for j in range(right_ref.shape[1] // LANES):
                    flat_rows[slot, pl.ds(first + j, take, stride=wide), :] = product[
                        :, j * LANES : (j + 1) * LANES
                    ]
            written(i).start()
            return carry

        lax.fori_loop(0, count, step, 0)
        for number in range(max(count - 2, 0), count):
            slot = (number + steps_before) % 2
            at = base + number * size
            pltpu.make_async_copy(
                flat_rows.at[slot, pl.ds(0, size)], out_ref.at[pl.ds(at, size)], out_sem.at[slot]
            ).wait()
        base += seg_rows * wide
        steps_before += count
    tail.wait()
    share.finish()


def weight_grads(pair_lists, vec_rows, token_grads, gx_size, gy_size, number):
    operands, parts = [], []
    for (seg_name, seg_rows, seg_cols), pairs in zip(segment_list()[:9], pair_lists):
        numbered, first = [], 0
        for left_side, right_side in pairs:
            numbered.append((len(operands), len(operands) + 1, first))
            for side in (left_side, right_side):
                side = side.reshape(-1, side.shape[-1])
                operands.append(jnp.pad(side, ((0, -side.shape[0] % GROUP), (0, 0))))
            first += right_side.shape[-1] // LANES
        parts.append((seg_rows, seg_cols, min(seg_rows, 256 if seg_cols <= 768 else 128), numbered))
    total_rows = matrix_rows() + vec_rows.shape[0]
    most = max(take * seg_cols // LANES for seg_rows, seg_cols, take, pairs in parts)
    return pl.pallas_call(
        functools.partial(grads_kernel, parts, gx_size, gy_size),
        out_shape=[
            jax.ShapeDtypeStruct((total_rows, LANES), jnp.float32),
            jax.ShapeDtypeStruct((gx_size,) + token_grads.shape, token_grads.dtype),
        ],
        in_specs=[pl.BlockSpec(memory_space=pltpu.VMEM)] * (len(operands) + 2),
        out_specs=[pl.BlockSpec(memory_space=pl.ANY)] * 2,
        scratch_shapes=[
            pltpu.VMEM((2, most, LANES), jnp.float32),
            pltpu.SemaphoreType.DMA,
            pltpu.SemaphoreType.DMA((2,)),
        ]
        + share_sems(gx_size, gy_size),
        compiler_params=pltpu.CompilerParams(
            collective_id=number, has_side_effects=True, vmem_limit_bytes=56 << 20
        ),
        name="weight_grads",
    )(*operands, vec_rows, token_grads)


class Share:
    def __init__(self, gx_size, gy_size, everyone, send_ref, out_ref, sems):
        gx, self.gy = lax.axis_index("gx"), lax.axis_index("gy")
        self.x_size, self.send_ref, self.out_ref = gx_size // 2, send_ref, out_ref
        self.core, self.x = lax.rem(gx, 2), gx // 2
        (self.own_sem, self.row_send, self.row_recv, self.x_send, self.x_recv, self.core_send, self.core_recv) = sems
        self.rows = [(gx, lax.rem(self.gy + d, gy_size)) for d in range(1, gy_size)]
        self.along_x, self.sibling = [], []
        if everyone:
            self.along_x = [
                (lax.rem(self.x + d, self.x_size) * 2 + self.core, self.gy) for d in range(1, self.x_size)
            ]
            self.sibling = [(self.x * 2 + 1 - self.core, self.gy)]
        self.mine = out_ref.at[gx if everyone else 0]

    def greet(self):
        greet_all(self.rows + self.along_x + self.sibling)

    def own(self):
        return pltpu.make_async_copy(self.send_ref.at[self.gy], self.mine.at[self.gy], self.own_sem)

    def row(self, d):
        other = self.rows[d]
        return remote(self.send_ref.at[other[1]], self.mine.at[self.gy], self.row_send.at[d], self.row_recv.at[d], other)

    def group(self, d):
        return remote(self.mine, self.mine, self.x_send.at[d], self.x_recv.at[d], self.along_x[d])

    def across(self, i, source):
        return remote(source, source, self.core_send.at[i], self.core_recv.at[i], self.sibling[0])

    def begin(self):
        self.own().start()
        for d in range(len(self.rows)):
            self.row(d).start()

    def middle(self):
        self.own().wait()
        for d in range(len(self.rows)):
            self.row(d).wait_recv()
        for d in range(len(self.along_x)):
            self.group(d).start()
        if self.sibling:
            self.across(0, self.mine).start()

    def rest(self):
        for d in range(len(self.along_x)):
            self.group(d).wait_recv()
            sender = lax.rem(self.x + self.x_size - d - 1, self.x_size) * 2 + self.core
            self.across(d + 1, self.out_ref.at[sender]).start()

    def finish(self):
        for d in range(len(self.rows)):
            self.row(d).wait_send()
        for d in range(len(self.along_x)):
            self.group(d).wait_send()
        for i in range(self.x_size if self.sibling else 0):
            self.across(i, self.mine).wait_send()
            self.across(i, self.mine).wait_recv()


def share_sems(gx_size, gy_size):
    dma, x_size = pltpu.SemaphoreType.DMA, gx_size // 2
    return [dma, dma((gy_size - 1,)), dma((gy_size - 1,)), dma((x_size,)), dma((x_size,)), dma((x_size,)), dma((x_size,))]


class Places:
    def __init__(self, sizes):
        self.x_size, self.low_size, self.high_size = sizes
        self.mixed = self.x_size == self.low_size
        self.gy_size = self.high_size * self.low_size
        gx, gy = lax.axis_index("gx"), lax.axis_index("gy")
        self.core, x = lax.rem(gx, 2), gx // 2
        self.h, low = gy // self.low_size, lax.rem(gy, self.low_size)
        self.a, self.b = self.turned(self.core, x, low)
        self.a_size, self.b_size = self.x_size, self.low_size

    def turned(self, side, a, b):
        if not self.mixed:
            return a, b
        return a * (1 - side) + b * side, b * (1 - side) + a * side

    def device(self, side, a, b, h):
        dev_x, dev_low = self.turned(side, a, b)
        return (dev_x * 2 + side, h * self.low_size + dev_low)

    def linear(self, side, a, b, h):
        gx, gy = self.device(side, a, b, h)
        return gx * self.gy_size + gy

    def sibling(self):
        a, b = (self.b, self.a) if self.mixed else (self.a, self.b)
        return self.device(1 - self.core, a, b, self.h)

    def along_a(self):
        return [
            self.device(self.core, lax.rem(self.a + d, self.a_size), self.b, self.h)
            for d in range(1, self.a_size)
        ]

    def along_b(self):
        return [
            self.device(self.core, self.a, lax.rem(self.b + d, self.b_size), self.h)
            for d in range(1, self.b_size)
        ]

    def along_h(self):
        return [
            self.device(self.core, self.a, self.b, lax.rem(self.h + d, self.high_size))
            for d in range(1, self.high_size)
        ]


def greet_all(others):
    barrier = pltpu.get_barrier_semaphore()
    for other in others:
        pl.semaphore_signal(barrier, inc=1, device_id=other, device_id_type=MESH)
    pl.semaphore_wait(barrier, len(others))


def remote(src, dst, send_sem, recv_sem, other):
    return pltpu.make_async_remote_copy(
        src_ref=src, dst_ref=dst, send_sem=send_sem, recv_sem=recv_sem, device_id=other, device_id_type=MESH
    )


def axis_sizes(gx_size, gy_size):
    return gx_size // 2, gy_size // 4, 4


NO_TOKEN = 65535


def route_capacity(tokens, gy_size):
    return GROUP * (1 + 17 * tokens // (16 * gy_size * GROUP))


def table_sum_kernel(cap, counts_ref, index_ref, rows_ref, out_ref, square_ref, wide, row_sem):
    sources = rows_ref.shape[0]
    vocab = out_ref.shape[0] - 8

    def fetch(source):
        slot = lax.rem(source, 2)
        return pltpu.make_async_copy(rows_ref.at[source], wide.at[slot], row_sem.at[slot])

    fetch(0).start()
    block = 32 if vocab % 32 == 0 else 8

    def clear(i, carry):
        out_ref[pl.ds(pl.multiple_of(i * block, 8), block), :] = jnp.zeros((block, D_TXT), jnp.float32)
        return carry

    lax.fori_loop(0, vocab // block, clear, 0)
    out_ref[vocab:, :] = jnp.zeros((8, D_TXT), jnp.float32)

    def one_source(source, carry):
        slot = lax.rem(source, 2)

        @pl.when(source + 1 < sources)
        def _():
            fetch(source + 1).start()

        fetch(source).wait()
        widened = wide.at[slot]

        def add(group, carry):
            rows = widened[pl.ds(pl.multiple_of(group * GROUP, GROUP), GROUP), :].astype(jnp.float32)
            for half in range(0, GROUP, 8):
                places = [
                    pl.ds(index_ref[source * cap + group * GROUP + half + i], 1) for i in range(8)
                ]
                sums = [out_ref[place, :] + rows[half + i : half + i + 1, :] for i, place in enumerate(places)]
                for place, value in zip(places, sums):
                    out_ref[place, :] = value
            return carry

        lax.fori_loop(0, (counts_ref[source] + GROUP - 1) // GROUP, add, 0)
        return carry

    lax.fori_loop(0, sources, one_source, 0)

    def square(i, carry):
        part = out_ref[pl.ds(pl.multiple_of(i * block, 8), block), :]
        part = part * part
        total = carry
        for r in range(0, block, 8):
            total = total + part[r : r + 8]
        return total

    square_ref[...] = lax.fori_loop(0, vocab // block, square, jnp.zeros((8, D_TXT), jnp.float32))


def table_sum(counts, index, rows, vocab):
    sources, cap = rows.shape[0], rows.shape[1]
    return pl.pallas_call(
        functools.partial(table_sum_kernel, cap),
        out_shape=[
            jax.ShapeDtypeStruct((vocab + 8, D_TXT), jnp.float32),
            jax.ShapeDtypeStruct((8, D_TXT), jnp.float32),
        ],
        in_specs=[pl.BlockSpec(memory_space=pltpu.SMEM)] * 2 + [pl.BlockSpec(memory_space=pl.ANY)],
        out_specs=[pl.BlockSpec(memory_space=pltpu.VMEM)] * 2,
        scratch_shapes=[pltpu.VMEM((2, cap, D_TXT), jnp.bfloat16), pltpu.SemaphoreType.DMA((2,))],
        compiler_params=pltpu.CompilerParams(vmem_limit_bytes=40 << 20),
        name="table_sum",
    )(counts, index, rows)


def ranks(flags):
    tokens = flags.shape[-1]
    before = (jnp.arange(tokens)[:, None] < jnp.arange(tokens)[None, :]).astype(jnp.bfloat16)
    return fwd_dot(flags.astype(jnp.bfloat16), before).astype(jnp.int32)


def pick_matrix(slots, count):
    return (jnp.arange(count)[:, None] == slots[None, :]).astype(jnp.bfloat16)


def gather_kernel(sizes, chunks, window_ref, out_ref, own_sem, h_send, h_recv, b_send, b_recv, a_send, a_recv, core_send,
                  core_recv):
    at = Places(sizes)
    rows = window_ref.shape[0]
    chunk = rows // chunks
    me = at.linear(at.core, at.a, at.b, at.h)
    sibling, peers_a, peers_b, peers_h = at.sibling(), at.along_a(), at.along_b(), at.along_h()
    greet_all([sibling] + peers_a + peers_b + peers_h)

    def part(block, t):
        return out_ref.at[pl.ds(pl.multiple_of(block * rows + t * chunk, GROUP), chunk)]

    def many(count):
        return out_ref.at[pl.ds(0, count * chunk)]

    def own_copy(t):
        src = window_ref.at[pl.ds(pl.multiple_of(t * chunk, GROUP), chunk)]
        return src, pltpu.make_async_copy(src, part(me, t), own_sem.at[t])

    def stage_h(t):
        src, own = own_copy(t)
        for d, other in enumerate(peers_h):
            remote(src, part(me, t), h_send.at[d], h_recv.at[t, d], other).start()
        own.start()

    def stage_b(t):
        own_copy(t)[1].wait()
        for d, other in enumerate(peers_h):
            remote(many(1), many(1), h_send.at[d], h_recv.at[t, d], other).wait_recv()
        for d, other in enumerate(peers_b):
            for h in range(at.high_size):
                block = part(at.linear(at.core, at.a, at.b, h), t)
                remote(block, block, b_send.at[d], b_recv.at[t, d], other).start()

    def stage_a(t):
        for d, other in enumerate(peers_b):
            remote(many(at.high_size), many(at.high_size), b_send.at[d], b_recv.at[t, d], other).wait_recv()
        for d, other in enumerate(peers_a):
            for b in range(at.b_size):
                for h in range(at.high_size):
                    block = part(at.linear(at.core, at.a, b, h), t)
                    remote(block, block, a_send.at[d], a_recv.at[t, d], other).start()

    plane = at.b_size * at.high_size

    def stage_core(t):
        for d, other in enumerate(peers_a):
            remote(many(plane), many(plane), a_send.at[d], a_recv.at[t, d], other).wait_recv()
        for a in range(at.a_size):
            for b in range(at.b_size):
                for h in range(at.high_size):
                    block = part(at.linear(at.core, a, b, h), t)
                    remote(block, block, core_send, core_recv, sibling).start()

    def turn(t, carry):
        for depth, stage in enumerate((stage_h, stage_b, stage_a, stage_core)):
            @pl.when((t >= depth) & (t < chunks + depth))
            def _():
                stage(t - depth)

        return carry

    lax.fori_loop(0, chunks + 3, turn, 0)

    def whole(count):
        return out_ref.at[pl.ds(0, count * rows)]

    for d, other in enumerate(peers_h):
        remote(whole(1), whole(1), h_send.at[d], h_recv.at[0, d], other).wait_send()
    for d, other in enumerate(peers_b):
        remote(whole(at.high_size), whole(at.high_size), b_send.at[d], b_recv.at[0, d], other).wait_send()
    for d, other in enumerate(peers_a):
        remote(whole(plane), whole(plane), a_send.at[d], a_recv.at[0, d], other).wait_send()
    half = whole(at.a_size * plane)
    last = remote(half, half, core_send, core_recv, sibling)
    last.wait_send()
    last.wait_recv()


def gather_windows(window, gx_size, gy_size, chunks, number, name):
    sizes = axis_sizes(gx_size, gy_size)
    a, b, h = sizes[0] - 1, sizes[1] - 1, sizes[2] - 1
    dma = pltpu.SemaphoreType.DMA
    return pl.pallas_call(
        functools.partial(gather_kernel, sizes, chunks),
        out_shape=jax.ShapeDtypeStruct((gx_size * gy_size * window.shape[0], LANES), window.dtype),
        in_specs=[pl.BlockSpec(memory_space=pltpu.VMEM)],
        out_specs=pl.BlockSpec(memory_space=pl.ANY),
        scratch_shapes=[dma((chunks,)), dma((h,)), dma((chunks, h)), dma((b,)), dma((chunks, b)), dma((a,)),
                        dma((chunks, a)), dma, dma],
        compiler_params=pltpu.CompilerParams(
            collective_id=number, has_side_effects=True, vmem_limit_bytes=32 << 20
        ),
        name=name,
    )(window)


def reduce_kernel(shard, sizes, grads_ref, square_ref, out_ref, squares_ref, own, landed, keep_one, send_one, recv_one, keep_two, send_two,
                  recv_two, keep_three, send_three, recv_three, partial, square_send, square_recv, load_sem, pair_send, pair_recv, credit,
                  one_send, one_recv, two_send, two_recv, three_send, three_recv):
    at = Places(sizes)
    a_size, b_size, high_size = at.a_size, at.b_size, at.high_size
    core, my_a, my_b, high = at.core, at.a, at.b, at.h
    plane = b_size * high_size
    chunk = own.shape[2]
    chunks = out_ref.shape[0] // chunk

    def start_row(side, number):
        a, rest = number // plane, lax.rem(number, plane)
        return window_start(shard, at.linear(side, a, rest // high_size, lax.rem(rest, high_size)))

    sibling, peers, peers_two, peers_three = at.sibling(), at.along_a(), at.along_b(), at.along_h()
    count = squares_ref.shape[0]
    me = linear_index(at.gy_size)

    def device(step):
        other = lax.rem(me + step, count)
        return (other // at.gy_size, lax.rem(other, at.gy_size))

    barrier = pltpu.get_barrier_semaphore()

    def greet(step, carry):
        pl.semaphore_signal(barrier, inc=1, device_id=device(step), device_id_type=MESH)
        return carry

    lax.fori_loop(1, count, greet, 0)
    pl.semaphore_wait(barrier, count - 1)
    table_part = square_ref[...]
    partial[...] = sum(table_part[:, j * LANES : (j + 1) * LANES] for j in range(D_TXT // LANES))
    spot = (lax.broadcasted_iota(jnp.int32, (chunk, LANES), 0) * LANES
            + lax.broadcasted_iota(jnp.int32, (chunk, LANES), 1))
    blocks = a_size * plane

    def pair_stage(t):
        slot = lax.rem(t, 2)

        @pl.when(t >= 2)
        def _():
            pl.semaphore_wait(credit, 1)

        def each(number, carry):
            theirs = pl.multiple_of(start_row(1 - core, number) + t * chunk, GROUP)
            mine = pl.multiple_of(start_row(core, number) + t * chunk, GROUP)
            remote(
                grads_ref.at[pl.ds(theirs, chunk)], landed.at[slot, number], pair_send.at[slot], pair_recv.at[slot], sibling
            ).start()
            pltpu.make_async_copy(
                grads_ref.at[pl.ds(mine, chunk)], own.at[slot, number], load_sem.at[slot]
            ).start()
            return carry

        lax.fori_loop(0, blocks, each, 0)

    def first_stage(u):
        slot = lax.rem(u, 2)
        both = remote(landed.at[slot], landed.at[slot], pair_send.at[slot], pair_recv.at[slot], sibling)
        pltpu.make_async_copy(own.at[slot], own.at[slot], load_sem.at[slot]).wait()
        both.wait_send()
        both.wait_recv()
        for d in range(1, a_size):
            @pl.when(u >= 2)
            def _():
                remote(send_one.at[slot, d - 1], recv_one.at[u - 2, d - 1], one_send.at[slot, d - 1],
                       one_recv.at[u - 2, d - 1], peers[d - 1]).wait_send()

            first = lax.rem(my_a + d, a_size) * plane

            def give(i, carry):
                send_one[slot, d - 1, i] = (own[slot, first + i] + landed[slot, first + i]).astype(jnp.bfloat16)
                return carry

            lax.fori_loop(0, plane, give, 0)
            remote(send_one.at[slot, d - 1], recv_one.at[u, d - 1], one_send.at[slot, d - 1],
                   one_recv.at[u, d - 1], peers[d - 1]).start()

        def hold(i, carry):
            keep_one[slot, i] = own[slot, my_a * plane + i] + landed[slot, my_a * plane + i]
            return carry

        lax.fori_loop(0, plane, hold, 0)

        @pl.when(u < chunks - 2)
        def _():
            pl.semaphore_signal(credit, inc=1, device_id=sibling, device_id_type=MESH)

    def second_stage(u):
        slot = lax.rem(u, 2)
        for d in range(1, a_size):
            remote(recv_one.at[u, d - 1], recv_one.at[u, d - 1], one_send.at[slot, d - 1], one_recv.at[u, d - 1],
                   peers[d - 1]).wait_recv()

        def total(number):
            value = keep_one[slot, number]
            for d in range(1, a_size):
                value = value + recv_one[u, d - 1, number].astype(jnp.float32)
            return value

        for d in range(1, b_size):
            @pl.when(u >= 2)
            def _():
                remote(send_two.at[slot, d - 1], recv_two.at[u - 2, d - 1], two_send.at[slot, d - 1],
                       two_recv.at[u - 2, d - 1], peers_two[d - 1]).wait_send()

            first = lax.rem(my_b + d, b_size) * high_size

            def give(i, carry):
                send_two[slot, d - 1, i] = total(first + i).astype(jnp.bfloat16)
                return carry

            lax.fori_loop(0, high_size, give, 0)
            remote(send_two.at[slot, d - 1], recv_two.at[u, d - 1], two_send.at[slot, d - 1],
                   two_recv.at[u, d - 1], peers_two[d - 1]).start()

        def hold(i, carry):
            keep_two[slot, i] = total(my_b * high_size + i)
            return carry

        lax.fori_loop(0, high_size, hold, 0)

    def third_stage(u):
        slot = lax.rem(u, 2)
        for d in range(1, b_size):
            remote(recv_two.at[u, d - 1], recv_two.at[u, d - 1], two_send.at[slot, d - 1], two_recv.at[u, d - 1],
                   peers_two[d - 1]).wait_recv()

        def total(number):
            value = keep_two[slot, number]
            for d in range(1, b_size):
                value = value + recv_two[u, d - 1, number].astype(jnp.float32)
            return value

        for d in range(1, high_size):
            @pl.when(u >= 2)
            def _():
                remote(send_three.at[slot, d - 1], recv_three.at[u - 2, d - 1], three_send.at[slot, d - 1],
                       three_recv.at[u - 2, d - 1], peers_three[d - 1]).wait_send()

            send_three[slot, d - 1] = total(lax.rem(high + d, high_size)).astype(jnp.bfloat16)
            remote(send_three.at[slot, d - 1], recv_three.at[u, d - 1], three_send.at[slot, d - 1],
                   three_recv.at[u, d - 1], peers_three[d - 1]).start()
        keep_three[slot] = total(high)

    def last_stage(u):
        slot = lax.rem(u, 2)
        value = keep_three[slot]
        for d in range(1, high_size):
            remote(recv_three.at[u, d - 1], recv_three.at[u, d - 1], three_send.at[slot, d - 1],
                   three_recv.at[u, d - 1], peers_three[d - 1]).wait_recv()
            value = value + recv_three[u, d - 1].astype(jnp.float32)
        out_ref[pl.ds(pl.multiple_of(u * chunk, GROUP), chunk), :] = value
        place = spot + (window_start(shard, me) + u * chunk) * LANES - me * shard
        square = jnp.where((place >= 0) & (place < shard), value * value, 0.0)
        partial[...] += sum(square[r : r + 8] for r in range(0, chunk, 8))

    def turn(t, carry):
        stages = (pair_stage, first_stage, second_stage, third_stage, last_stage)
        for depth, stage in enumerate(stages):
            @pl.when((t >= depth) & (t < chunks + depth))
            def _():
                stage(t - depth)

        return carry

    lax.fori_loop(0, chunks + 4, turn, 0)
    squares_ref[me] = partial[...]

    def send(step, carry):
        remote(partial, squares_ref.at[me], square_send, square_recv, device(step)).start()
        return carry

    lax.fori_loop(1, count, send, 0)
    others = squares_ref.at[pl.ds(0, count - 1)]
    both = remote(others, others, square_send, square_recv, device(1))
    both.wait_send()
    both.wait_recv()
    for u in range(max(chunks - 2, 0), chunks):
        slot = u % 2
        for d in range(1, a_size):
            remote(send_one.at[slot, d - 1], recv_one.at[u, d - 1], one_send.at[slot, d - 1],
                   one_recv.at[u, d - 1], peers[d - 1]).wait_send()
        for d in range(1, b_size):
            remote(send_two.at[slot, d - 1], recv_two.at[u, d - 1], two_send.at[slot, d - 1],
                   two_recv.at[u, d - 1], peers_two[d - 1]).wait_send()
        for d in range(1, high_size):
            remote(send_three.at[slot, d - 1], recv_three.at[u, d - 1], three_send.at[slot, d - 1],
                   three_recv.at[u, d - 1], peers_three[d - 1]).wait_send()


def reduce_windows(grads, square, shard, gx_size, gy_size, number):
    rows = window_rows(shard, GROUP * CHUNKS)
    chunk = rows // CHUNKS
    x_size, low_size, high_size = axis_sizes(gx_size, gy_size)
    plane = low_size * high_size
    blocks = x_size * plane
    low_type, dma = jnp.bfloat16, pltpu.SemaphoreType.DMA
    a, b, h = x_size - 1, low_size - 1, high_size - 1
    return pl.pallas_call(
        functools.partial(reduce_kernel, shard, (x_size, low_size, high_size)),
        out_shape=[
            jax.ShapeDtypeStruct((rows, LANES), jnp.float32),
            jax.ShapeDtypeStruct((gx_size * gy_size, 8, LANES), jnp.float32),
        ],
        in_specs=[pl.BlockSpec(memory_space=pl.ANY), pl.BlockSpec(memory_space=pltpu.VMEM)],
        out_specs=[pl.BlockSpec(memory_space=pltpu.VMEM)] * 2,
        scratch_shapes=[
            pltpu.VMEM((2, blocks, chunk, LANES), jnp.float32),
            pltpu.VMEM((2, blocks, chunk, LANES), jnp.float32),
            pltpu.VMEM((2, plane, chunk, LANES), jnp.float32),
            pltpu.VMEM((2, a, plane, chunk, LANES), low_type),
            pltpu.VMEM((CHUNKS, a, plane, chunk, LANES), low_type),
            pltpu.VMEM((2, high_size, chunk, LANES), jnp.float32),
            pltpu.VMEM((2, b, high_size, chunk, LANES), low_type),
            pltpu.VMEM((CHUNKS, b, high_size, chunk, LANES), low_type),
            pltpu.VMEM((2, chunk, LANES), jnp.float32),
            pltpu.VMEM((2, h, chunk, LANES), low_type),
            pltpu.VMEM((CHUNKS, h, chunk, LANES), low_type),
            pltpu.VMEM((8, LANES), jnp.float32),
            dma,
            dma,
            dma((2,)),
            dma((2,)),
            dma((2,)),
            pltpu.SemaphoreType.REGULAR,
            dma((2, a)),
            dma((CHUNKS, a)),
            dma((2, b)),
            dma((CHUNKS, b)),
            dma((2, h)),
            dma((CHUNKS, h)),
        ],
        compiler_params=pltpu.CompilerParams(
            collective_id=number, has_side_effects=True, vmem_limit_bytes=60 << 20
        ),
        name="reduce_windows",
    )(grads, square)


def log_sums(rows, columns, column_ok, logit_scale, matches, positives):
    total, taken = rows.shape[0], min(rows.shape[0], 256)

    def some(args):
        row_part, match_part, positive_part = args
        dots = back_dot(row_part, columns)
        logits = logit_scale * dots
        masked = jnp.where(column_ok[None, :], logits, -1e30)
        row_max = jnp.max(masked, 1, keepdims=True)
        log_total = row_max[:, 0] + jnp.log(jnp.sum(jnp.exp(masked - row_max), 1))
        gap = jnp.where(match_part > 0.0, logits[:, :total] - log_total[:, None], 0.0)
        pulled = jnp.sum(positive_part[:, None] * jnp.exp(masked - log_total[:, None]) * dots)
        return log_total, -jnp.sum(gap), pulled - jnp.sum(match_part * dots[:, :total])

    if taken == total:
        return some((rows, matches, positives))
    logs, parts, pulls = lax.map(
        some,
        (
            rows.reshape(-1, taken, rows.shape[1]),
            matches.reshape(-1, taken, total),
            positives.reshape(-1, taken),
        ),
    )
    return logs.reshape(-1), jnp.sum(parts), jnp.sum(pulls)


def side_grads(row_embed, columns, column_ok, same_own, positives_own, log_own, logit_scale, total_count):
    dot_vals = back_dot(row_embed, columns)
    masked = jnp.where(column_ok[None, :], logit_scale * dot_vals, -1e30)
    extra = columns.shape[0] - same_own.shape[1]
    weights_pos = jnp.concatenate(
        [same_own, jnp.zeros((same_own.shape[0], extra), jnp.float32)], 1
    )
    grad_logits = (
        positives_own[:, None] * jnp.exp(masked - log_own[:, None]) - weights_pos
    ) / total_count
    grad_dots = (logit_scale * grad_logits).astype(jnp.bfloat16)
    return fwd_dot(grad_dots, columns)


def cross_grads(rows, own, valid_own, same_own, positives_all, logs, logit_scale, total_count):
    logits = logit_scale * back_dot(rows, own)
    masked = jnp.where(valid_own[None, :], logits, -1e30)
    grad_logits = (
        positives_all[:, None] * jnp.exp(masked - logs[:, None]) - same_own.T
    ) / total_count
    grad_dots = (logit_scale * grad_logits).astype(jnp.bfloat16)
    return weight_grad(grad_dots, rows)


def body(
    flat_master,
    flat_first,
    flat_second,
    table,
    table_first,
    table_second,
    pixels,
    token_ids,
    end_pos,
    pair_counts,
    groups,
    cached_image,
    cached_text,
):
    gx_size, gy_size = lax.axis_size("gx"), lax.axis_size("gy")
    device_count = gx_size * gy_size
    my_index = linear_index(gy_size)
    pairs_dev = pixels.shape[0]
    shard = flat_master.shape[0]
    tokens = token_ids.size
    vocab_dev = table.shape[0]
    cap = route_capacity(tokens, gy_size)
    own_ids = token_ids.reshape(-1)
    same = own_ids[:, None] == own_ids[None, :]
    order = jnp.arange(tokens)
    leading = ~jnp.any(same & (order[None, :] < order[:, None]), 1)
    flat_ids = jnp.where(leading, own_ids, NO_TOKEN)
    flat_ids = jnp.pad(flat_ids, (0, ID_ROWS * LANES // 2 - tokens)).reshape(-1, LANES)
    payload = [
        place_window(flat_master, gy_size),
        jnp.concatenate([cached_image, cached_text], 0).reshape(CACHED_ROWS, LANES),
        jnp.concatenate([flat_ids // 256, flat_ids % 256], 0).astype(jnp.bfloat16),
    ]
    used = sum(part.shape[0] for part in payload)
    step = GROUP * GATHER_CHUNKS
    payload = jnp.pad(jnp.concatenate(payload, 0), ((0, -used % step), (0, 0)))
    gathered = gather_windows(payload, gx_size, gy_size, GATHER_CHUNKS, 4, "gather_weights")
    every_part = gathered.reshape(device_count, -1, LANES)
    cached = every_part[:, used - ID_ROWS - CACHED_ROWS : used - ID_ROWS].reshape(device_count, -1, EMBED)
    cache_img, cache_txt = lax.optimization_barrier((cached[:, :pairs_dev], cached[:, pairs_dev:]))
    cache_img, cache_txt = cache_img.reshape(-1, EMBED), cache_txt.reshape(-1, EMBED)
    coded = every_part[:, used - ID_ROWS : used].astype(jnp.int32)
    ids_all = coded[:, : ID_ROWS // 2] * 256 + coded[:, ID_ROWS // 2 :]
    ids_all = ids_all.reshape(device_count, -1)[:, :tokens]
    holders = ids_all // vocab_dev
    pair_rows = jnp.sum(holders[:, :, None] == jnp.arange(gy_size), 1)
    rounds = (jnp.max(pair_rows) + cap - 1) // cap
    me_y = lax.axis_index("gy")
    held = holders == me_y
    held_rank = jnp.where(held, ranks(held), -1)
    held_row = ids_all - me_y * vocab_dev
    held_count = jnp.sum(held, 1)
    own_flags = (jnp.arange(gy_size)[:, None] == own_ids[None, :] // vocab_dev) & leading[None, :]
    own_place = jnp.arange(gy_size)[:, None] * tokens + ranks(own_flags)
    own_place = jnp.sum(jnp.where(own_flags, own_place, 0), 0)
    own_place = jnp.sum(jnp.where(same & leading[None, :], own_place[None, :], 0), 1)
    own_holder, own_rank = own_place // tokens, own_place % tokens

    def held_rows(turn):
        slots = held_rank - turn * cap
        found = slots[:, None, :] == jnp.arange(cap)[None, :, None]
        return vocab_dev + jnp.sum(jnp.where(found, held_row[:, None, :] - vocab_dev, 0), 2)

    def own_slots(turn):
        rank = own_rank - turn * cap
        return jnp.where((rank >= 0) & (rank < cap), own_holder * cap + rank, -1)

    first_rows = held_rows(0)
    group_start = lax.axis_index("gx") * gy_size

    def rows_to_send(index):
        index = lax.dynamic_slice_in_dim(index, group_start, gy_size, 0)
        rows = jnp.take(table, index.reshape(-1), axis=0, mode="clip")
        return rows.reshape(gy_size, cap, D_TXT)

    sent = rows_to_send(first_rows).astype(jnp.bfloat16)
    slot_count = gy_size * cap

    def more_rows(turn, found):
        rows = lax.all_to_all(rows_to_send(held_rows(turn)), "gy", 0, 0, tiled=True)
        rows = rows.reshape(slot_count, D_TXT).astype(jnp.bfloat16)
        return found + weight_grad(pick_matrix(own_slots(turn), slot_count), rows).astype(jnp.bfloat16)

    nothing = jnp.zeros((tokens, D_TXT), jnp.bfloat16)
    extra_rows = lax.cond(
        rounds > 1, lambda rows: lax.fori_loop(1, rounds, more_rows, rows), lambda rows: rows, nothing
    )
    sent, extra_rows = lax.optimization_barrier((sent, extra_rows))
    *spread, landed = spread_weights(gathered, sent, shard, gx_size, gy_size, 5)
    picks = pick_matrix(own_slots(0), slot_count)
    token_rows = weight_grad(picks, landed.reshape(slot_count, D_TXT)).astype(jnp.bfloat16)

    token_rows = token_rows + extra_rows
    image_weights = dict(zip(IMAGE.names, spread[:5]))
    text_weights = dict(zip(TEXT.names, spread[5:9]))
    image_vec, text_vec, temper = split_vectors(spread[9])
    image_gains, image_base, image_rows = image_inputs(image_vec, pixels)
    text_gains, text_base, text_rows = text_inputs(text_vec, token_rows)
    image_kept = tower_forward(IMAGE, end_pos, image_gains, image_base, image_rows, image_weights)
    text_kept = tower_forward(TEXT, end_pos, text_gains, text_base, text_rows, text_weights)
    image_emb = image_kept[14].astype(jnp.bfloat16)
    text_emb = text_kept[14].astype(jnp.bfloat16)
    embeds = jnp.concatenate([image_emb, text_emb], 0).reshape(-1, LANES)
    embeds = gather_windows(embeds, gx_size, gy_size, 1, 0, "embeddings")
    embeds = embeds.reshape(device_count, 2 * pairs_dev, EMBED)
    all_img, all_txt = lax.optimization_barrier((embeds[:, :pairs_dev], embeds[:, pairs_dev:]))
    all_img, all_txt = all_img.reshape(-1, EMBED), all_txt.reshape(-1, EMBED)
    total_pairs = all_img.shape[0]
    valid_all = jnp.arange(total_pairs) % pairs_dev < jnp.repeat(pair_counts.reshape(-1), pairs_dev)
    matches = (
        (groups[:, None] == groups[None, :]) & valid_all[:, None] & valid_all[None, :]
    ).astype(jnp.float32)
    positives_all = jnp.sum(matches, 1)
    total_count = 2.0 * jnp.sum(positives_all)
    own_start = my_index * pairs_dev
    own_part = functools.partial(
        lax.dynamic_slice_in_dim, start_index=own_start, slice_size=pairs_dev, axis=0
    )
    same_own, positives_own, valid_own = own_part(matches), own_part(positives_all), own_part(valid_all)
    logit_scale = jnp.exp(temper)
    column_ok = jnp.concatenate([valid_all, jnp.ones((cache_img.shape[0],), jnp.bool_)])
    columns_txt = jnp.concatenate([all_txt, cache_txt])
    columns_img = jnp.concatenate([all_img, cache_img])
    log_img, loss_one, pull_one = log_sums(
        all_img, columns_txt, column_ok, logit_scale, matches, positives_all
    )
    log_txt, loss_two, pull_two = log_sums(
        all_txt, columns_img, column_ok, logit_scale, matches, positives_all
    )
    grad_temper = logit_scale * (pull_one + pull_two) / total_count
    loss_sum = loss_one + loss_two
    grad_img = side_grads(
        image_emb, columns_txt, column_ok, same_own, positives_own, own_part(log_img), logit_scale, total_count
    )
    grad_txt = side_grads(
        text_emb, columns_img, column_ok, same_own, positives_own, own_part(log_txt), logit_scale, total_count
    )
    grad_img = grad_img + cross_grads(
        all_txt, image_emb, valid_own, same_own, positives_all, log_txt, logit_scale, total_count
    )
    grad_txt = grad_txt + cross_grads(
        all_img, text_emb, valid_own, same_own, positives_all, log_img, logit_scale, total_count
    )
    text_grads = tower_backward(TEXT, end_pos, text_gains, grad_txt, text_kept[:14], text_weights)
    grad_rows = text_grads[6][: SEQS * CTX]
    to_holders = fwd_dot(picks, grad_rows).astype(jnp.bfloat16).reshape(gy_size, cap, D_TXT)
    image_grads = tower_backward(IMAGE, end_pos, image_gains, grad_img, image_kept[:14], image_weights)
    pair_lists = ([(image_rows, image_grads[6])],) + grad_pairs(image_kept, image_grads)
    pair_lists = pair_lists + grad_pairs(text_kept, text_grads)
    total_rows = window_start(shard, device_count - 1) + window_rows(shard, GROUP * CHUNKS)
    vec_rows = jnp.concatenate(
        [
            image_grads[7][:1].reshape(-1, LANES),
            image_grads[7].reshape(-1, LANES),
            image_grads[8].reshape(-1, LANES),
            text_grads[7].reshape(-1, LANES),
            text_grads[8][2:].reshape(-1, LANES),
        ]
    )
    vec_rows = jnp.pad(vec_rows, ((0, total_rows - matrix_rows() - vec_rows.shape[0]), (0, 0)))
    local_grads, arrived = weight_grads(pair_lists, vec_rows, to_holders, gx_size, gy_size, 6)
    table_grad, table_square = table_sum(
        jnp.minimum(held_count, cap),
        first_rows.reshape(-1),
        arrived.reshape(device_count, cap, D_TXT),
        vocab_dev,
    )

    def more_grads(turn, total):
        rows = fwd_dot(pick_matrix(own_slots(turn), slot_count), grad_rows).astype(jnp.bfloat16)
        rows = lax.all_to_all(rows.reshape(gy_size, cap, D_TXT), "gy", 0, 0, tiled=True)
        rows = lax.all_gather(rows, "gx", axis=0).reshape(device_count * cap, D_TXT).astype(jnp.float32)
        return total.at[held_rows(turn).reshape(-1)].add(rows)

    def whole_squares(total):
        return jnp.sum((total[:vocab_dev] * total[:vocab_dev]).reshape(-1, 8, D_TXT), 0)

    def more_turns(total, square):
        total = lax.fori_loop(1, rounds, more_grads, total)
        return total, whole_squares(total)

    table_grad, table_square = lax.cond(
        rounds > 1, more_turns, lambda total, square: (total, square), table_grad, table_square
    )
    table_square = jnp.where(lax.axis_index("gx") == 0, table_square, 0.0)
    grad_window, every = reduce_windows(local_grads, table_square, shard, gx_size, gy_size, 1)
    position = my_index * shard + jnp.arange(shard)
    grad_shard = lift_window(grad_window, shard, gy_size)
    grad_shard = jnp.where(position == parameter_count() - 1, grad_temper, grad_shard)
    total_square = jnp.sum(every) + grad_temper * grad_temper
    grad_norm = jnp.sqrt(total_square)
    factor = jnp.minimum(1.0, clip_limit / (grad_norm + 1e-06))
    matrix_stop = matrix_rows() * LANES
    is_matrix = position < matrix_stop
    rates = jnp.where(is_matrix, rate_matrix, rate_vector)
    decays = jnp.where(is_matrix, decay_rate, 0.0)
    master_out, first_out, second_out = adam_step(
        flat_master, flat_first, flat_second, grad_shard * factor, rates, decays
    )
    table_out, table_first_out, table_second_out = adam_step(
        table, table_first, table_second, table_grad[:vocab_dev] * factor, rate_table, 0.0
    )
    return (
        master_out,
        first_out,
        second_out,
        table_out,
        table_first_out,
        table_second_out,
        loss_sum,
        total_count,
        grad_norm,
    )


def solution(mesh):
    placed = (
        P(("gx", "gy")),
        P(("gx", "gy")),
        P(("gx", "gy")),
        P("gy", None),
        P("gy", None),
        P("gy", None),
        P(("gx", "gy"), None, None),
        P(("gx", "gy"), None),
        P(("gx", "gy")),
        P(),
        P(),
        P(("gx", "gy"), None),
        P(("gx", "gy"), None),
    )
    return jax.shard_map(
        body,
        mesh=mesh,
        in_specs=placed,
        out_specs=(
            P(("gx", "gy")),
            P(("gx", "gy")),
            P(("gx", "gy")),
            P("gy", None),
            P("gy", None),
            P("gy", None),
            P(),
            P(),
            P(),
        ),
        check_vma=False,
    )
```

```python
import functools

import jax
import jax.numpy as jnp
from jax import lax
from jax.experimental import pallas as pl
from jax.experimental.pallas import tpu as pltpu
from jax.sharding import PartitionSpec as P

D_IMG = 768
IMG_HEADS = 12
IMG_MLP = 3072
PATCH_DIM = 3072
D_TXT = 512
TXT_HEADS = 8
TXT_MLP = 2048
CTX = 77
EMBED = 512
STEP = 10
IMG_TOK = 50


clip_limit = 0.1
beta_one = 0.9
beta_two = 0.999
adam_eps = 1e-08
decay_rate = 0.1
rate_matrix = 0.01
rate_vector = 0.2
rate_table = 0.2
norm_eps = 1e-05


def segment_list():
    return [
        ("patch_embed", PATCH_DIM, D_IMG),
        ("image_attn", D_IMG, 4 * D_IMG),
        ("image_up", D_IMG, IMG_MLP),
        ("image_down", IMG_MLP, D_IMG),
        ("image_proj", D_IMG, EMBED),
        ("text_attn", D_TXT, 4 * D_TXT),
        ("text_up", D_TXT, TXT_MLP),
        ("text_down", TXT_MLP, D_TXT),
        ("text_proj", D_TXT, EMBED),
        ("image_vec", IMG_TOK + 9, D_IMG),
        ("text_vec", CTX + 6, D_TXT),
        ("temper", 1, 1),
    ]


LANES = 128
GROUP = 16
CHUNKS = 16
GATHER_CHUNKS = 14
TURNED = 6
CACHED_ROWS = 64
ID_ROWS = 16
MESH = pl.DeviceIdType.MESH


def dot_nn(left_side, right_side):
    return lax.dot_general(
        left_side, right_side, (((1,), (0,)), ((), ())), preferred_element_type=jnp.float32
    )


def dot_nt(left_side, right_side):
    return lax.dot_general(
        left_side, right_side, (((1,), (1,)), ((), ())), preferred_element_type=jnp.float32
    )


def dot_tn(left_side, right_side):
    return lax.dot_general(
        left_side, right_side, (((0,), (0,)), ((), ())), preferred_element_type=jnp.float32
    )


def back_dot(left_side, right_side):
    return dot_nt(left_side, right_side)


def fwd_dot(left_side, right_side):
    return dot_nn(left_side, right_side)


def weight_grad(left_side, right_side):
    return dot_tn(left_side, right_side)


def norm_parts(values):
    center = values - jnp.mean(values, -1, keepdims=True)
    scale = lax.rsqrt(jnp.mean(center * center, -1, keepdims=True) + norm_eps)
    return center * scale, scale


def layer_norm(values, gain_vec, shift_vec):
    return norm_parts(values)[0] * gain_vec + shift_vec


def layer_norm_back(values, gain_vec, grad):
    unit, scale = norm_parts(values)
    grad_unit = grad * gain_vec
    inner = jnp.mean(grad_unit, -1, keepdims=True)
    along = jnp.mean(grad_unit * unit, -1, keepdims=True)
    return scale * (grad_unit - inner - unit * along), grad * unit


def sum_rows(values):
    return jnp.sum(values, 0, keepdims=True)


def low16(values):
    return jnp.concatenate([values, jnp.zeros_like(values)], 0).astype(jnp.bfloat16)


SEQS = 8


class Tower:
    def __init__(self, image):
        self.image = image
        self.width = D_IMG if image else D_TXT
        self.heads = IMG_HEADS if image else TXT_HEADS
        self.length = IMG_TOK if image else CTX
        self.rows = -(-SEQS * self.length // GROUP) * GROUP
        self.lanes = 16 if image else 8
        self.queries = SEQS * self.lanes
        self.block = 80 if image else 48
        self.names = ("patch", "attn", "up", "down", "proj") if image else ("attn", "up", "down", "proj")

    def shapes(self):
        width = self.width
        found = dict(attn=(width, 4 * width), up=(width, 4 * width), down=(4 * width, width), proj=(width, EMBED))
        if self.image:
            found["patch"] = (PATCH_DIM, width)
        return found

    def head_mask(self):
        lane = lax.broadcasted_iota(jnp.int32, (self.lanes, self.width), 1)
        row = lax.broadcasted_iota(jnp.int32, (self.lanes, self.width), 0)
        return lane // (self.width // self.heads) == row

    def spread_heads(self, values, wide_ref):
        mask = self.head_mask()
        for s in range(SEQS):
            row = jnp.broadcast_to(values[s : s + 1].astype(jnp.float32), mask.shape)
            wide_ref[s * self.lanes : (s + 1) * self.lanes, :] = jnp.where(mask, row, 0.0)
        return wide_ref[...].astype(jnp.bfloat16)

    def join_heads(self, values, wide_ref):
        mask = self.head_mask()
        wide_ref[...] = values
        rows = [
            sum_rows(jnp.where(mask, wide_ref[s * self.lanes : (s + 1) * self.lanes, :], 0.0))
            for s in range(SEQS)
        ]
        return jnp.concatenate(rows, 0)

    def row_of(self, s, ends_ref):
        return s * self.length + (0 if self.image else ends_ref[s])

    def each_block(self, function, start):
        return lax.fori_loop(
            0,
            self.rows // self.block,
            lambda i, carry: function(pl.ds(pl.multiple_of(i * self.block, GROUP), self.block), carry),
            start,
        )


def tower_fetch(names, sources, landed, sems):
    copies = {
        name: pltpu.make_async_copy(source, ref, sems.at[i])
        for i, (name, source, ref) in enumerate(zip(names, sources, landed))
    }
    for copy in copies.values():
        copy.start()
    return copies, dict(zip(names, landed))


def tower_forward_kernel(tower, *refs):
    count = len(tower.names)
    ends_ref, gains_ref, base_ref, input_ref = refs[:4]
    sources = refs[4 : 4 + count]
    (tokens_ref, normed_ref, pair_ref, normed_own_ref, query_ref, probs_ref, attended_ref, middle_ref, normed_two_ref,
     upper_ref, act_ref, output_ref, head_ref, raw_ref, emb_ref) = refs[4 + count : 19 + count]
    hidden_ref, wide_ref = refs[19 + count : 21 + count]
    landed, sems = refs[21 + count : 21 + 2 * count], refs[21 + 2 * count]
    copies, weights = tower_fetch(tower.names, sources, landed, sems)
    width = tower.width
    gains = [gains_ref[i : i + 1, :] for i in range(8)]
    if tower.image:
        copies["patch"].wait()

        def patch(j, carry):
            cols = pl.ds(pl.multiple_of(j * 256, 256), 256)
            tokens_ref[:, cols] = dot_nn(input_ref[...], weights["patch"][:, cols]) + base_ref[:, cols]
            return carry

        lax.fori_loop(0, width // 256, patch, 0)

    def first(rows, carry):
        if tower.image:
            hidden = layer_norm(tokens_ref[rows, :], gains[0], gains[1])
        else:
            hidden = input_ref[rows, :].astype(jnp.float32) + base_ref[rows, :]
            tokens_ref[rows, :] = hidden
        hidden_ref[rows, :] = hidden
        normed_ref[rows, :] = layer_norm(hidden, gains[2], gains[3]).astype(jnp.bfloat16)
        return carry

    tower.each_block(first, 0)
    copies["attn"].wait()

    def pair(j, carry):
        at = pl.multiple_of(j * 256, 256)
        product = dot_nn(normed_ref[...], weights["attn"][:, pl.ds(width + at, 256)])
        pair_ref[:, pl.ds(at, 256)] = product.astype(jnp.bfloat16)
        return carry

    lax.fori_loop(0, 2 * width // 256, pair, 0)
    hidden_own = jnp.concatenate(
        [hidden_ref[pl.ds(tower.row_of(s, ends_ref), 1), :] for s in range(SEQS)], 0
    )
    normed_own = low16(layer_norm(hidden_own, gains[2], gains[3]))
    normed_own_ref[...] = normed_own
    query = dot_nn(normed_own, weights["attn"][:, :width]).astype(jnp.bfloat16)
    query_ref[...] = query
    queries = tower.spread_heads(query, wide_ref)
    scores = dot_nt(queries, pair_ref[:, :width]) * (width // tower.heads) ** (-0.5)
    row = lax.broadcasted_iota(jnp.int32, scores.shape, 0) // tower.lanes
    spot = lax.broadcasted_iota(jnp.int32, scores.shape, 1) - row * tower.length
    last = jnp.full(scores.shape, tower.length - 1, jnp.int32)
    if not tower.image:
        for s in range(SEQS):
            last = jnp.where(row == s, ends_ref[s], last)
    scores = jnp.where((spot >= 0) & (spot <= last), scores, -1e30)
    powers = jnp.exp(scores - jnp.max(scores, -1, keepdims=True))
    probs = powers / jnp.sum(powers, -1, keepdims=True)
    probs_ref[...] = probs
    attended = low16(tower.join_heads(dot_nn(probs.astype(jnp.bfloat16), pair_ref[:, width:]), wide_ref))
    attended_ref[...] = attended
    middle = hidden_own + dot_nn(attended, weights["attn"][:, 3 * width :])[:SEQS]
    middle_ref[...] = middle
    normed_two_ref[...] = low16(layer_norm(middle, gains[4], gains[5]))
    copies["up"].wait()

    def rise(j, carry):
        cols = pl.ds(pl.multiple_of(j * 512, 512), 512)
        upper = dot_nn(normed_two_ref[...], weights["up"][:, cols])[:SEQS]
        upper_ref[:, cols] = upper
        act_ref[:, cols] = low16(upper * jax.nn.sigmoid(1.702 * upper))
        return carry

    lax.fori_loop(0, 4 * width // 512, rise, 0)
    copies["down"].wait()

    def fall(j, carry):
        cols = pl.ds(pl.multiple_of(j * 256, 256), 256)
        output_ref[:, cols] = middle_ref[:, cols] + dot_nn(act_ref[...], weights["down"][:, cols])[:SEQS]
        return carry

    lax.fori_loop(0, width // 256, fall, 0)
    head_in = low16(layer_norm(output_ref[...], gains[6], gains[7]))
    head_ref[...] = head_in
    copies["proj"].wait()
    raw = dot_nn(head_in, weights["proj"][...])[:SEQS]
    raw_ref[...] = raw
    emb_ref[...] = raw * lax.rsqrt(jnp.sum(raw * raw, -1, keepdims=True) + 1e-06)


def tower_forward(tower, ends, gains, base, inputs, weights):
    width, rows = tower.width, tower.rows
    low, full = jnp.bfloat16, jnp.float32
    outs = [
        ((rows, width), full),
        ((rows, width), low),
        ((rows, 2 * width), low),
        ((GROUP, width), low),
        ((GROUP, width), low),
        ((tower.queries, rows), full),
        ((GROUP, width), low),
        ((SEQS, width), full),
        ((GROUP, width), low),
        ((SEQS, 4 * width), full),
        ((GROUP, 4 * width), low),
        ((SEQS, width), full),
        ((GROUP, width), low),
        ((SEQS, EMBED), full),
        ((SEQS, EMBED), full),
    ]
    vmem = pl.BlockSpec(memory_space=pltpu.VMEM)
    shapes = tower.shapes()
    return pl.pallas_call(
        functools.partial(tower_forward_kernel, tower),
        out_shape=[jax.ShapeDtypeStruct(shape, kind) for shape, kind in outs],
        in_specs=[pl.BlockSpec(memory_space=pltpu.SMEM)]
        + [vmem] * 3
        + [pl.BlockSpec(memory_space=pl.ANY)] * len(tower.names),
        out_specs=[vmem] * len(outs),
        scratch_shapes=[pltpu.VMEM((rows, width), full), pltpu.VMEM((tower.queries, width), full)]
        + [pltpu.VMEM(shapes[name], low) for name in tower.names]
        + [pltpu.SemaphoreType.DMA((len(tower.names),))],
        compiler_params=pltpu.CompilerParams(vmem_limit_bytes=58 << 20),
        name="image_forward" if tower.image else "text_forward",
    )(ends, gains, base, inputs, *[weights[name] for name in tower.names])


def tower_backward_kernel(tower, *refs):
    names = tower.names[-4:]
    count = len(names)
    ends_ref, gains_ref, grad_ref = refs[:3]
    (tokens_ref, normed_ref, pair_ref, normed_own_ref, query_ref, probs_ref, attended_ref, middle_ref, normed_two_ref,
     upper_ref, act_ref, output_ref, head_ref, raw_ref) = refs[3:17]
    sources = refs[17 : 17 + count]
    (grad_raw_ref, grad_mlp_ref, grad_upper_ref, grad_att_ref, grad_query_ref, grad_pair_ref, grad_rows_ref,
     places_ref, gain_grads_ref) = refs[17 + count : 26 + count]
    grad_ref_wide, wide_ref, grad_middle_ref = refs[26 + count : 29 + count]
    landed, sems = refs[29 + count : 29 + 2 * count], refs[29 + 2 * count]
    copies, weights = tower_fetch(names, sources, landed, sems)
    width, rows = tower.width, tower.rows
    scale = (width // tower.heads) ** (-0.5)
    gains = [gains_ref[i : i + 1, :] for i in range(8)]
    raw, grad_emb = raw_ref[...], grad_ref[...]
    norm = lax.rsqrt(jnp.sum(raw * raw, -1, keepdims=True) + 1e-06)
    along = jnp.sum(raw * grad_emb, -1, keepdims=True)
    grad_raw = low16(grad_emb * norm - raw * (norm * norm * norm * along))
    grad_raw_ref[...] = grad_raw
    copies["proj"].wait()
    grad_head = dot_nt(grad_raw, weights["proj"][...])[:SEQS]
    grad_out, gain_part = layer_norm_back(output_ref[...], gains[6], grad_head)
    gain_grads_ref[6:7, :] = sum_rows(gain_part)
    gain_grads_ref[7:8, :] = sum_rows(grad_head)
    grad_mlp_ref[...] = low16(grad_out)
    copies["down"].wait()

    def rise(j, carry):
        cols = pl.ds(pl.multiple_of(j * 512, 512), 512)
        grad_act = dot_nt(grad_mlp_ref[...], weights["down"][cols, :])[:SEQS]
        upper = upper_ref[:, cols]
        sig = jax.nn.sigmoid(1.702 * upper)
        grad_upper_ref[:, cols] = low16(grad_act * (sig + upper * (1.702 * (sig * (1.0 - sig)))))
        return carry

    lax.fori_loop(0, 4 * width // 512, rise, 0)
    copies["up"].wait()

    def fall(j, carry):
        cols = pl.ds(pl.multiple_of(j * 256, 256), 256)
        grad_middle_ref[:, cols] = dot_nt(grad_upper_ref[...], weights["up"][cols, :])[:SEQS]
        return carry

    lax.fori_loop(0, width // 256, fall, 0)
    grad_norm_two = grad_middle_ref[...]
    grad_mid, gain_part = layer_norm_back(middle_ref[...], gains[4], grad_norm_two)
    gain_grads_ref[4:5, :] = sum_rows(gain_part)
    gain_grads_ref[5:6, :] = sum_rows(grad_norm_two)
    grad_middle = grad_out + grad_mid
    grad_middle_ref[...] = grad_middle
    grad_att = low16(grad_middle)
    grad_att_ref[...] = grad_att
    copies["attn"].wait()
    grad_attended = dot_nt(grad_att, weights["attn"][:, 3 * width :]).astype(jnp.bfloat16)
    grads_heads = tower.spread_heads(grad_attended, wide_ref)
    queries = tower.spread_heads(query_ref[...], wide_ref)
    probs = probs_ref[...]
    grad_probs = dot_nt(grads_heads, pair_ref[:, width:])
    grad_scores = probs * (grad_probs - jnp.sum(grad_probs * probs, -1, keepdims=True))
    grad_scores = grad_scores.astype(jnp.bfloat16)
    grad_query = low16(tower.join_heads(dot_nn(grad_scores, pair_ref[:, :width]), wide_ref) * scale)
    grad_query_ref[...] = grad_query
    grad_pair_ref[:, :width] = (dot_tn(grad_scores, queries) * scale).astype(jnp.bfloat16)
    grad_pair_ref[:, width:] = dot_tn(probs.astype(jnp.bfloat16), grads_heads).astype(jnp.bfloat16)

    def inner(j, carry):
        at = pl.multiple_of(j * 256, 256)
        grad_ref_wide[:, pl.ds(at, 256)] = dot_nt(
            grad_pair_ref[...], weights["attn"][pl.ds(at, 256), width : 3 * width]
        )
        return carry

    lax.fori_loop(0, width // 256, inner, 0)
    grad_own = dot_nt(grad_query, weights["attn"][:, :width])
    for s in range(SEQS):
        grad_ref_wide[pl.ds(tower.row_of(s, ends_ref), 1), :] += grad_own[s : s + 1]

    def first(at, carry):
        grad = grad_ref_wide[at, :]
        hidden = tokens_ref[at, :]
        if tower.image:
            hidden = layer_norm(hidden, gains[0], gains[1])
        grad_in, gain_part = layer_norm_back(hidden, gains[2], grad)
        grad_ref_wide[at, :] = grad_in
        return carry[0] + sum_rows(gain_part), carry[1] + sum_rows(grad)

    nothing = jnp.zeros((1, width), jnp.float32)
    gain_one, shift_one = tower.each_block(first, (nothing, nothing))
    gain_grads_ref[2:3, :] = gain_one
    gain_grads_ref[3:4, :] = shift_one
    for s in range(SEQS):
        grad_ref_wide[pl.ds(tower.row_of(s, ends_ref), 1), :] += grad_middle_ref[s : s + 1, :]

    def second(at, carry):
        grad = grad_ref_wide[at, :]
        if not tower.image:
            grad_rows_ref[at, :] = grad.astype(jnp.bfloat16)
            return carry
        grad_in, gain_part = layer_norm_back(tokens_ref[at, :], gains[0], grad)
        grad_ref_wide[at, :] = grad_in
        grad_rows_ref[at, :] = grad_in.astype(jnp.bfloat16)
        return carry[0] + sum_rows(gain_part), carry[1] + sum_rows(grad)

    gain_pre, shift_pre = tower.each_block(second, (nothing, nothing))
    gain_grads_ref[0:1, :] = gain_pre
    gain_grads_ref[1:2, :] = shift_pre
    places = grad_ref_wide[0 : tower.length, :]
    for s in range(1, SEQS):
        places = places + grad_ref_wide[s * tower.length : (s + 1) * tower.length, :]
    places_ref[...] = places


def tower_backward(tower, ends, gains, grad_emb, kept, weights):
    width, rows = tower.width, tower.rows
    low, full = jnp.bfloat16, jnp.float32
    outs = [
        ((GROUP, EMBED), low),
        ((GROUP, width), low),
        ((GROUP, 4 * width), low),
        ((GROUP, width), low),
        ((GROUP, width), low),
        ((rows, 2 * width), low),
        ((rows, width), low),
        ((tower.length, width), full),
        ((8, width), full),
    ]
    vmem = pl.BlockSpec(memory_space=pltpu.VMEM)
    shapes, names = tower.shapes(), tower.names[-4:]
    return pl.pallas_call(
        functools.partial(tower_backward_kernel, tower),
        out_shape=[jax.ShapeDtypeStruct(shape, kind) for shape, kind in outs],
        in_specs=[pl.BlockSpec(memory_space=pltpu.SMEM)]
        + [vmem] * (2 + len(kept))
        + [pl.BlockSpec(memory_space=pl.ANY)] * len(names),
        out_specs=[vmem] * len(outs),
        scratch_shapes=[
            pltpu.VMEM((rows, width), full),
            pltpu.VMEM((tower.queries, width), full),
            pltpu.VMEM((SEQS, width), full),
        ]
        + [pltpu.VMEM(shapes[name], low) for name in names]
        + [pltpu.SemaphoreType.DMA((len(names),))],
        compiler_params=pltpu.CompilerParams(vmem_limit_bytes=58 << 20),
        name="image_backward" if tower.image else "text_backward",
    )(ends, gains, grad_emb, *kept, *[weights[name] for name in names])


def grad_pairs(kept, grads):
    (normed, normed_own, attended, normed_two, act_low, head_in) = (
        kept[1], kept[3], kept[6], kept[8], kept[10], kept[12]
    )
    grad_raw, grad_mlp, grad_upper, grad_att, grad_query, grad_pair = grads[:6]
    return (
        [(normed_own, grad_query), (normed, grad_pair), (attended, grad_att)],
        [(normed_two, grad_upper)],
        [(act_low, grad_mlp)],
        [(head_in, grad_raw)],
    )


def image_inputs(image_vec, pixels):
    pixels = jnp.pad(pixels, ((0, 0), (1, 0), (0, 0))).reshape(-1, PATCH_DIM)
    base = image_vec[1 : IMG_TOK + 1] + jnp.pad(image_vec[:1], ((0, IMG_TOK - 1), (0, 0)))
    return image_vec[IMG_TOK + 1 :], jnp.tile(base, (SEQS, 1)), pixels


def text_inputs(text_vec, token_rows):
    gains = jnp.pad(text_vec[CTX:], ((2, 0), (0, 0)))
    extra = TEXT.rows - SEQS * CTX
    base = jnp.pad(jnp.tile(text_vec[:CTX], (SEQS, 1)), ((0, extra), (0, 0)))
    return gains, base, jnp.pad(token_rows, ((0, extra), (0, 0)))


def adam_step(weight, first, second, grad, rate, decay):
    first = beta_one * first + (1.0 - beta_one) * grad
    second = beta_two * second + (1.0 - beta_two) * grad * grad
    first_hat = first / (1.0 - beta_one**STEP)
    second_hat = second / (1.0 - beta_two**STEP)
    weight = weight - rate * (first_hat / (jnp.sqrt(second_hat) + adam_eps) + decay * weight)
    return (weight, first, second)


IMAGE, TEXT = Tower(True), Tower(False)


def matrix_rows():
    return sum(seg_rows * seg_cols for seg_name, seg_rows, seg_cols in segment_list()[:9]) // LANES


def parameter_count():
    return sum(seg_rows * seg_cols for seg_name, seg_rows, seg_cols in segment_list())


def window_rows(shard, step=GROUP):
    need = -(-(GROUP * LANES - 1 + shard) // LANES)
    return -(-need // step) * step


def window_start(shard, index):
    return (shard * index // (GROUP * LANES)) * GROUP


def linear_index(gy_size):
    return lax.axis_index("gx") * gy_size + lax.axis_index("gy")


def place_kernel(shard, gy_size, flat_ref, out_ref, rolled):
    rows = flat_ref.shape[0]
    offset = lax.rem(shard * linear_index(gy_size), GROUP * LANES)
    down, right = offset // LANES, lax.rem(offset, LANES)
    pad = 2 * GROUP
    rolled[0:pad, :] = jnp.zeros((pad, LANES), jnp.float32)
    parts = 5 if rows % (5 * GROUP) == 0 else 1
    step = rows // parts

    def roll_rows(i, carry):
        at = pl.multiple_of(i * step, GROUP)
        rolled[pl.ds(pad + at, step), :] = pltpu.roll(flat_ref[pl.ds(at, step), :], right, 1)
        return carry

    lax.fori_loop(0, parts, roll_rows, 0)
    lane = lax.broadcasted_iota(jnp.int32, (step, LANES), 1)

    def put_rows(i, carry):
        at = pl.multiple_of(i * step, GROUP)
        upper = rolled[pl.ds(pad + at - down - 1, step), :]
        lower = rolled[pl.ds(pad + at - down, step), :]
        out_ref[pl.ds(at, step), :] = jnp.where(lane < right, upper, lower).astype(jnp.bfloat16)
        return carry

    lax.fori_loop(0, parts, put_rows, 0)


def place_window(flat, gy_size):
    shard = flat.shape[0]
    rows = window_rows(shard)
    padded = jnp.pad(flat, (0, rows * LANES - shard)).reshape(rows, LANES)
    return pl.pallas_call(
        functools.partial(place_kernel, shard, gy_size),
        out_shape=jax.ShapeDtypeStruct((rows, LANES), jnp.bfloat16),
        in_specs=[pl.BlockSpec(memory_space=pltpu.VMEM)],
        out_specs=pl.BlockSpec(memory_space=pltpu.VMEM),
        scratch_shapes=[pltpu.VMEM((rows + 2 * GROUP, LANES), jnp.float32)],
        compiler_params=pltpu.CompilerParams(vmem_limit_bytes=32 << 20),
        name="place_window",
    )(padded)


def lift_kernel(shard, gy_size, window_ref, out_ref, rolled):
    rows = window_ref.shape[0]
    offset = lax.rem(shard * linear_index(gy_size), GROUP * LANES)
    up, left = offset // LANES, lax.rem(offset, LANES)
    pad = 2 * GROUP
    step = rows // CHUNKS
    rolled[rows:, :] = jnp.zeros((pad, LANES), jnp.float32)

    def roll_rows(i, carry):
        at = pl.multiple_of(i * step, GROUP)
        rolled[pl.ds(at, step), :] = pltpu.roll(
            window_ref[pl.ds(at, step), :], lax.rem(LANES - left, LANES), 1
        )
        return carry

    lax.fori_loop(0, CHUNKS, roll_rows, 0)
    lane = lax.broadcasted_iota(jnp.int32, (step, LANES), 1)

    def put_rows(i, carry):
        at = pl.multiple_of(i * step, GROUP)
        first = rolled[pl.ds(at + up, step), :]
        second = rolled[pl.ds(at + up + 1, step), :]
        out_ref[pl.ds(at, step), :] = jnp.where(lane < LANES - left, first, second)
        return carry

    lax.fori_loop(0, CHUNKS, put_rows, 0)


def lift_window(window, shard, gy_size):
    rows = window.shape[0]
    lifted = pl.pallas_call(
        functools.partial(lift_kernel, shard, gy_size),
        out_shape=jax.ShapeDtypeStruct((rows, LANES), jnp.float32),
        in_specs=[pl.BlockSpec(memory_space=pltpu.VMEM)],
        out_specs=pl.BlockSpec(memory_space=pltpu.VMEM),
        scratch_shapes=[pltpu.VMEM((rows + 2 * GROUP, LANES), jnp.float32)],
        compiler_params=pltpu.CompilerParams(vmem_limit_bytes=32 << 20),
        name="lift_window",
    )(window)
    return lifted.reshape(-1)[:shard]


def spread_steps():
    steps = []
    base = 0
    for number, (seg_name, seg_rows, seg_cols) in enumerate(segment_list()[:9]):
        wide = seg_cols // LANES
        take = seg_rows
        while take * wide > 4608:
            take //= 2
        for start in range(0, seg_rows, take):
            steps.append((number, start, take, seg_cols, base + start * wide))
        base += seg_rows * wide
    return steps


def window_pieces(shard, count, stride, first, length):
    pieces, shared = [], []
    for index in range(count):
        low = window_start(shard, index)
        high = window_start(shard, index + 1) if index + 1 < count else low + window_rows(shard)
        start, stop = max(low, first), min(high, first + length)
        if start < stop:
            pieces.append((index * stride + start - low, start - first, stop - start))
        if index + 1 < count and first <= high < first + length:
            shared.append((index * stride + high - low, high - first))
    return pieces, shared


def spread_kernel(shard, count, vec_rows, share, gathered_ref, *refs):
    outs, vec_ref = refs[:9], refs[9]
    landed, edges, wide_rows, ready, in_sem, out_sem = refs[10:]
    rows = gathered_ref.shape[0] // count
    steps = spread_steps()
    steps.append((9, 0, vec_rows, LANES, matrix_rows()))

    def copies_in(number):
        seg, start, take, cols, base = steps[number]
        slot = number % 2
        pieces, shared = window_pieces(shard, count, rows, base, take * cols // LANES)
        found = [
            pltpu.make_async_copy(
                gathered_ref.at[pl.ds(src, size)], landed.at[slot, pl.ds(dst, size)], in_sem.at[slot]
            )
            for src, dst, size in pieces
        ]
        found += [
            pltpu.make_async_copy(
                gathered_ref.at[pl.ds(src, GROUP)], edges.at[slot, order], in_sem.at[slot]
            )
            for order, (src, dst) in enumerate(shared)
        ]
        return found, shared

    def copy_out(number):
        seg, start, take, cols, base = steps[number]
        slot = number % 2
        if seg == 9:
            return pltpu.make_async_copy(wide_rows.at[pl.ds(0, take)], vec_ref, out_sem.at[slot])
        return pltpu.make_async_copy(
            ready[cols].at[slot, pl.ds(0, take)], outs[seg].at[pl.ds(start, take)], out_sem.at[slot]
        )

    for copy in copies_in(0)[0]:
        copy.start()
    for number, (seg, start, take, cols, base) in enumerate(steps):
        if number == 4:
            share.greet()
            share.begin()
        slot = number % 2
        wide = cols // LANES
        total = take * wide
        if number + 1 < len(steps):
            for copy in copies_in(number + 1)[0]:
                copy.start()
        found, shared = copies_in(number)
        for copy in found:
            copy.wait()
        if number >= 2:
            copy_out(number - 2).wait()
        block = 256 if total % 256 == 0 else GROUP

        def widen(i, carry, slot=slot, block=block):
            at = pl.multiple_of(i * block, GROUP)
            wide_rows[pl.ds(at, block), :] = landed[slot, pl.ds(at, block), :].astype(jnp.float32)
            return carry

        lax.fori_loop(0, total // block, widen, 0)
        for order, (src, dst) in enumerate(shared):
            wide_rows[dst : dst + GROUP, :] += edges[slot, order].astype(jnp.float32)
        if seg < 9:

            def tile(i, carry, slot=slot, wide=wide, cols=cols):
                at = pl.multiple_of(i * GROUP, GROUP)
                for j in range(wide):
                    ready[cols][slot, pl.ds(at, GROUP), j * LANES : (j + 1) * LANES] = wide_rows[
                        pl.ds(at * wide + j, GROUP, stride=wide), :
                    ].astype(jnp.bfloat16)
                return carry

            lax.fori_loop(0, take // GROUP, tile, 0)
        copy_out(number).start()
    copy_out(len(steps) - 2).wait()
    copy_out(len(steps) - 1).wait()


def spread_entry(shard, gx_size, gy_size, vec_rows, gathered_ref, rows_ref, *refs):
    outs, landed_rows = refs[:10], refs[10]
    landed, edges, wide_rows, ready_a, ready_b, ready_c, ready_d, in_sem, out_sem = refs[11:20]
    ready = {D_IMG: ready_a, 4 * D_IMG: ready_b, D_TXT: ready_c, 4 * D_TXT: ready_d}
    share = Share(gx_size, gy_size, False, rows_ref, landed_rows, refs[20:])
    spread_kernel(
        shard, gx_size * gy_size, vec_rows, share, gathered_ref, *outs, landed, edges, wide_rows, ready, in_sem, out_sem
    )
    share.middle()
    share.finish()


def spread_weights(gathered, rows_to_send, shard, gx_size, gy_size, number):
    count = gx_size * gy_size
    rows = gathered.shape[0] // count
    steps = spread_steps()
    tallest = {}
    for seg, start, take, cols, base in steps:
        tallest[cols] = max(tallest.get(cols, 0), take)
    most = max(take * cols // LANES for seg, start, take, cols, base in steps)
    vec_rows = -(-(sum(r * c for name, r, c in segment_list()[9:])) // (LANES * GROUP)) * GROUP
    edge_count = max(
        len(window_pieces(shard, count, rows, base, take * cols // LANES)[1])
        for seg, start, take, cols, base in steps
    )
    ready = [
        pltpu.VMEM((2, tallest[cols], cols), jnp.bfloat16)
        for cols in (D_IMG, 4 * D_IMG, D_TXT, 4 * D_TXT)
    ]
    return pl.pallas_call(
        functools.partial(spread_entry, shard, gx_size, gy_size, vec_rows),
        out_shape=[
            jax.ShapeDtypeStruct((seg_rows, seg_cols), jnp.bfloat16)
            for seg_name, seg_rows, seg_cols in segment_list()[:9]
        ]
        + [
            jax.ShapeDtypeStruct((vec_rows, LANES), jnp.float32),
            jax.ShapeDtypeStruct((1,) + rows_to_send.shape, rows_to_send.dtype),
        ],
        in_specs=[pl.BlockSpec(memory_space=pl.ANY), pl.BlockSpec(memory_space=pltpu.VMEM)],
        out_specs=[pl.BlockSpec(memory_space=pl.ANY)] * 10 + [pl.BlockSpec(memory_space=pltpu.VMEM)],
        scratch_shapes=[
            pltpu.VMEM((2, most, LANES), jnp.bfloat16),
            pltpu.VMEM((2, edge_count + 1, GROUP, LANES), jnp.bfloat16),
            pltpu.VMEM((most, LANES), jnp.float32),
        ]
        + ready
        + [pltpu.SemaphoreType.DMA((2,)), pltpu.SemaphoreType.DMA((2,))]
        + share_sems(gx_size, gy_size),
        compiler_params=pltpu.CompilerParams(
            collective_id=number, has_side_effects=True, vmem_limit_bytes=48 << 20
        ),
        name="spread_weights",
    )(gathered, rows_to_send)


def split_vectors(vec_rows):
    image_count, text_count = (IMG_TOK + 9) * D_IMG // LANES, (CTX + 6) * D_TXT // LANES
    image_vec = vec_rows[:image_count].reshape(IMG_TOK + 9, D_IMG)
    text_vec = vec_rows[image_count : image_count + text_count].reshape(CTX + 6, D_TXT)
    return image_vec, text_vec, vec_rows[image_count + text_count, 0]


def grads_kernel(parts, gx_size, gy_size, *refs):
    operand_count = sum(2 * len(pairs) for seg_rows, seg_cols, take, pairs in parts)
    operands = refs[:operand_count]
    vec_ref, token_ref, out_ref, arrived_ref, flat_rows, vec_sem, out_sem = refs[operand_count : operand_count + 7]
    share = Share(gx_size, gy_size, True, token_ref, arrived_ref, refs[operand_count + 7 :])
    share.greet()
    share.begin()
    tail = pltpu.make_async_copy(vec_ref, out_ref.at[pl.ds(matrix_rows(), vec_ref.shape[0])], vec_sem)
    tail.start()
    base = 0
    steps_before = 0
    for number, (seg_rows, seg_cols, take, pairs) in enumerate(parts):
        if number == 2:
            share.middle()
        if number == 6:
            share.rest()
        wide = seg_cols // LANES
        size = take * wide
        count = seg_rows // take

        def step(i, carry, base=base, before=steps_before, size=size, take=take, wide=wide, pairs=pairs):
            slot = lax.rem(i + before, 2)

            def written(number):
                at = pl.multiple_of(base + number * size, 8)
                return pltpu.make_async_copy(
                    flat_rows.at[slot, pl.ds(0, size)], out_ref.at[pl.ds(at, size)], out_sem.at[slot]
                )

            @pl.when(i >= 2)
            def _():
                written(i - 2).wait()

            for left_number, right_number, first in pairs:
                left_ref, right_ref = operands[left_number], operands[right_number]
                at = pl.multiple_of(i * take, LANES)
                product = lax.dot_general(
                    left_ref[:, pl.ds(at, take)],
                    right_ref[...],
                    (((0,), (0,)), ((), ())),
                    preferred_element_type=jnp.float32,
                )
                for j in range(right_ref.shape[1] // LANES):
                    flat_rows[slot, pl.ds(first + j, take, stride=wide), :] = product[
                        :, j * LANES : (j + 1) * LANES
                    ]
            written(i).start()
            return carry

        lax.fori_loop(0, count, step, 0)
        for number in range(max(count - 2, 0), count):
            slot = (number + steps_before) % 2
            at = base + number * size
            pltpu.make_async_copy(
                flat_rows.at[slot, pl.ds(0, size)], out_ref.at[pl.ds(at, size)], out_sem.at[slot]
            ).wait()
        base += seg_rows * wide
        steps_before += count
    tail.wait()
    share.finish()


def weight_grads(pair_lists, vec_rows, token_grads, gx_size, gy_size, number):
    operands, parts = [], []
    for (seg_name, seg_rows, seg_cols), pairs in zip(segment_list()[:9], pair_lists):
        numbered, first = [], 0
        for left_side, right_side in pairs:
            numbered.append((len(operands), len(operands) + 1, first))
            for side in (left_side, right_side):
                side = side.reshape(-1, side.shape[-1])
                operands.append(jnp.pad(side, ((0, -side.shape[0] % GROUP), (0, 0))))
            first += right_side.shape[-1] // LANES
        parts.append((seg_rows, seg_cols, min(seg_rows, 256 if seg_cols <= 768 else 128), numbered))
    total_rows = matrix_rows() + vec_rows.shape[0]
    most = max(take * seg_cols // LANES for seg_rows, seg_cols, take, pairs in parts)
    return pl.pallas_call(
        functools.partial(grads_kernel, parts, gx_size, gy_size),
        out_shape=[
            jax.ShapeDtypeStruct((total_rows, LANES), jnp.float32),
            jax.ShapeDtypeStruct((gx_size,) + token_grads.shape, token_grads.dtype),
        ],
        in_specs=[pl.BlockSpec(memory_space=pltpu.VMEM)] * (len(operands) + 2),
        out_specs=[pl.BlockSpec(memory_space=pl.ANY)] * 2,
        scratch_shapes=[
            pltpu.VMEM((2, most, LANES), jnp.float32),
            pltpu.SemaphoreType.DMA,
            pltpu.SemaphoreType.DMA((2,)),
        ]
        + share_sems(gx_size, gy_size),
        compiler_params=pltpu.CompilerParams(
            collective_id=number, has_side_effects=True, vmem_limit_bytes=56 << 20
        ),
        name="weight_grads",
    )(*operands, vec_rows, token_grads)


class Share:
    def __init__(self, gx_size, gy_size, everyone, send_ref, out_ref, sems):
        gx, self.gy = lax.axis_index("gx"), lax.axis_index("gy")
        self.x_size, self.send_ref, self.out_ref = gx_size // 2, send_ref, out_ref
        self.core, self.x = lax.rem(gx, 2), gx // 2
        (self.own_sem, self.row_send, self.row_recv, self.x_send, self.x_recv, self.core_send, self.core_recv) = sems
        self.rows = [(gx, lax.rem(self.gy + d, gy_size)) for d in range(1, gy_size)]
        self.along_x, self.sibling = [], []
        if everyone:
            self.along_x = [
                (lax.rem(self.x + d, self.x_size) * 2 + self.core, self.gy) for d in range(1, self.x_size)
            ]
            self.sibling = [(self.x * 2 + 1 - self.core, self.gy)]
        self.mine = out_ref.at[gx if everyone else 0]

    def greet(self):
        greet_all(self.rows + self.along_x + self.sibling)

    def own(self):
        return pltpu.make_async_copy(self.send_ref.at[self.gy], self.mine.at[self.gy], self.own_sem)

    def row(self, d):
        other = self.rows[d]
        return remote(self.send_ref.at[other[1]], self.mine.at[self.gy], self.row_send.at[d], self.row_recv.at[d], other)

    def group(self, d):
        return remote(self.mine, self.mine, self.x_send.at[d], self.x_recv.at[d], self.along_x[d])

    def across(self, i, source):
        return remote(source, source, self.core_send.at[i], self.core_recv.at[i], self.sibling[0])

    def begin(self):
        self.own().start()
        for d in range(len(self.rows)):
            self.row(d).start()

    def middle(self):
        self.own().wait()
        for d in range(len(self.rows)):
            self.row(d).wait_recv()
        for d in range(len(self.along_x)):
            self.group(d).start()
        if self.sibling:
            self.across(0, self.mine).start()

    def rest(self):
        for d in range(len(self.along_x)):
            self.group(d).wait_recv()
            sender = lax.rem(self.x + self.x_size - d - 1, self.x_size) * 2 + self.core
            self.across(d + 1, self.out_ref.at[sender]).start()

    def finish(self):
        for d in range(len(self.rows)):
            self.row(d).wait_send()
        for d in range(len(self.along_x)):
            self.group(d).wait_send()
        for i in range(self.x_size if self.sibling else 0):
            self.across(i, self.mine).wait_send()
            self.across(i, self.mine).wait_recv()


def share_sems(gx_size, gy_size):
    dma, x_size = pltpu.SemaphoreType.DMA, gx_size // 2
    return [dma, dma((gy_size - 1,)), dma((gy_size - 1,)), dma((x_size,)), dma((x_size,)), dma((x_size,)), dma((x_size,))]


class Places:
    def __init__(self, sizes):
        self.x_size, self.low_size, self.high_size = sizes
        self.mixed = self.x_size == self.low_size
        self.gy_size = self.high_size * self.low_size
        gx, gy = lax.axis_index("gx"), lax.axis_index("gy")
        self.core, x = lax.rem(gx, 2), gx // 2
        self.h, low = gy // self.low_size, lax.rem(gy, self.low_size)
        self.a, self.b = self.turned(self.core, x, low)
        self.a_size, self.b_size = self.x_size, self.low_size

    def turned(self, side, a, b):
        if not self.mixed:
            return a, b
        return a * (1 - side) + b * side, b * (1 - side) + a * side

    def device(self, side, a, b, h):
        dev_x, dev_low = self.turned(side, a, b)
        return (dev_x * 2 + side, h * self.low_size + dev_low)

    def linear(self, side, a, b, h):
        gx, gy = self.device(side, a, b, h)
        return gx * self.gy_size + gy

    def sibling(self):
        a, b = (self.b, self.a) if self.mixed else (self.a, self.b)
        return self.device(1 - self.core, a, b, self.h)

    def along_a(self):
        return [
            self.device(self.core, lax.rem(self.a + d, self.a_size), self.b, self.h)
            for d in range(1, self.a_size)
        ]

    def along_b(self):
        return [
            self.device(self.core, self.a, lax.rem(self.b + d, self.b_size), self.h)
            for d in range(1, self.b_size)
        ]

    def along_h(self):
        return [
            self.device(self.core, self.a, self.b, lax.rem(self.h + d, self.high_size))
            for d in range(1, self.high_size)
        ]


def greet_all(others):
    barrier = pltpu.get_barrier_semaphore()
    for other in others:
        pl.semaphore_signal(barrier, inc=1, device_id=other, device_id_type=MESH)
    pl.semaphore_wait(barrier, len(others))


def remote(src, dst, send_sem, recv_sem, other):
    return pltpu.make_async_remote_copy(
        src_ref=src, dst_ref=dst, send_sem=send_sem, recv_sem=recv_sem, device_id=other, device_id_type=MESH
    )


def axis_sizes(gx_size, gy_size):
    return gx_size // 2, gy_size // 4, 4


NO_TOKEN = 65535


def route_capacity(tokens, gy_size):
    return GROUP * (1 + 17 * tokens // (16 * gy_size * GROUP))


def table_sum_kernel(cap, counts_ref, index_ref, rows_ref, out_ref, square_ref, wide, row_sem):
    sources = rows_ref.shape[0]
    vocab = out_ref.shape[0] - 8

    def fetch(source):
        slot = lax.rem(source, 2)
        return pltpu.make_async_copy(rows_ref.at[source], wide.at[slot], row_sem.at[slot])

    fetch(0).start()
    block = 32 if vocab % 32 == 0 else 8

    def clear(i, carry):
        out_ref[pl.ds(pl.multiple_of(i * block, 8), block), :] = jnp.zeros((block, D_TXT), jnp.float32)
        return carry

    lax.fori_loop(0, vocab // block, clear, 0)
    out_ref[vocab:, :] = jnp.zeros((8, D_TXT), jnp.float32)

    def one_source(source, carry):
        slot = lax.rem(source, 2)

        @pl.when(source + 1 < sources)
        def _():
            fetch(source + 1).start()

        fetch(source).wait()
        widened = wide.at[slot]

        def add(group, carry):
            rows = widened[pl.ds(pl.multiple_of(group * GROUP, GROUP), GROUP), :].astype(jnp.float32)
            for half in range(0, GROUP, 8):
                places = [
                    pl.ds(index_ref[source * cap + group * GROUP + half + i], 1) for i in range(8)
                ]
                sums = [out_ref[place, :] + rows[half + i : half + i + 1, :] for i, place in enumerate(places)]
                for place, value in zip(places, sums):
                    out_ref[place, :] = value
            return carry

        lax.fori_loop(0, (counts_ref[source] + GROUP - 1) // GROUP, add, 0)
        return carry

    lax.fori_loop(0, sources, one_source, 0)

    def square(i, carry):
        part = out_ref[pl.ds(pl.multiple_of(i * block, 8), block), :]
        part = part * part
        total = carry
        for r in range(0, block, 8):
            total = total + part[r : r + 8]
        return total

    square_ref[...] = lax.fori_loop(0, vocab // block, square, jnp.zeros((8, D_TXT), jnp.float32))


def table_sum(counts, index, rows, vocab):
    sources, cap = rows.shape[0], rows.shape[1]
    return pl.pallas_call(
        functools.partial(table_sum_kernel, cap),
        out_shape=[
            jax.ShapeDtypeStruct((vocab + 8, D_TXT), jnp.float32),
            jax.ShapeDtypeStruct((8, D_TXT), jnp.float32),
        ],
        in_specs=[pl.BlockSpec(memory_space=pltpu.SMEM)] * 2 + [pl.BlockSpec(memory_space=pl.ANY)],
        out_specs=[pl.BlockSpec(memory_space=pltpu.VMEM)] * 2,
        scratch_shapes=[pltpu.VMEM((2, cap, D_TXT), jnp.bfloat16), pltpu.SemaphoreType.DMA((2,))],
        compiler_params=pltpu.CompilerParams(vmem_limit_bytes=40 << 20),
        name="table_sum",
    )(counts, index, rows)


def ranks(flags):
    tokens = flags.shape[-1]
    before = (jnp.arange(tokens)[:, None] < jnp.arange(tokens)[None, :]).astype(jnp.bfloat16)
    return fwd_dot(flags.astype(jnp.bfloat16), before).astype(jnp.int32)


def pick_matrix(slots, count):
    return (jnp.arange(count)[:, None] == slots[None, :]).astype(jnp.bfloat16)


def turned_rows(chunk):
    return TURNED * chunk // (16 * GROUP) * GROUP


def gather_kernel(sizes, chunks, window_ref, out_ref, own_sem, h_send, h_recv, b_send, b_recv, a_send, a_recv, core_send,
                  core_recv):
    at = Places(sizes)
    rows = window_ref.shape[0]
    chunk = rows // chunks
    changed = turned_rows(chunk)
    ways = (False, True) if changed else (False,)
    spans = {False: (0, chunk - changed), True: (chunk - changed, changed)}
    me = at.linear(at.core, at.a, at.b, at.h)
    sibling, peers_a, peers_b, peers_h = at.sibling(), at.along_a(), at.along_b(), at.along_h()
    greet_all([sibling] + peers_a + peers_b + peers_h)
    along_h, along_b = (peers_h, h_send, h_recv), (peers_b, b_send, b_recv)

    def part(block, t, span=(0, chunk)):
        return out_ref.at[pl.ds(pl.multiple_of(block * rows + t * chunk + span[0], GROUP), span[1])]

    def many(count):
        return out_ref.at[pl.ds(0, count)]

    def own_copy(t):
        src = window_ref.at[pl.ds(pl.multiple_of(t * chunk, GROUP), chunk)]
        return pltpu.make_async_copy(src, part(me, t), own_sem.at[t])

    def first(t):
        for turned in ways:
            peers, send, recv = along_b if turned else along_h
            start, size = spans[turned]
            src = window_ref.at[pl.ds(pl.multiple_of(t * chunk + start, GROUP), size)]
            for d, other in enumerate(peers):
                remote(src, part(me, t, spans[turned]), send.at[d], recv.at[int(turned), t, d], other).start()
        own_copy(t).start()

    def second(t):
        own_copy(t).wait()
        for turned in ways:
            size = many(spans[turned][1])
            peers, send, recv = along_b if turned else along_h
            for d, other in enumerate(peers):
                remote(size, size, send.at[d], recv.at[int(turned), t, d], other).wait_recv()
            if turned:
                blocks = [at.linear(at.core, at.a, b, at.h) for b in range(at.b_size)]
            else:
                blocks = [at.linear(at.core, at.a, at.b, h) for h in range(at.high_size)]
            peers, send, recv = along_h if turned else along_b
            for d, other in enumerate(peers):
                for block in blocks:
                    block = part(block, t, spans[turned])
                    remote(block, block, send.at[d], recv.at[int(turned), t, d], other).start()

    def third(t):
        for turned in ways:
            count = at.b_size if turned else at.high_size
            size = many(count * spans[turned][1])
            peers, send, recv = along_h if turned else along_b
            for d, other in enumerate(peers):
                remote(size, size, send.at[d], recv.at[int(turned), t, d], other).wait_recv()
        for d, other in enumerate(peers_a):
            for b in range(at.b_size):
                for h in range(at.high_size):
                    block = part(at.linear(at.core, at.a, b, h), t)
                    remote(block, block, a_send.at[d], a_recv.at[t, d], other).start()

    plane = at.b_size * at.high_size

    def fourth(t):
        size = many(plane * chunk)
        for d, other in enumerate(peers_a):
            remote(size, size, a_send.at[d], a_recv.at[t, d], other).wait_recv()
        for a in range(at.a_size):
            for b in range(at.b_size):
                for h in range(at.high_size):
                    block = part(at.linear(at.core, a, b, h), t)
                    remote(block, block, core_send, core_recv, sibling).start()

    def turn(t, carry):
        for depth, stage in enumerate((first, second, third, fourth)):
            active = (t >= depth) & (t < chunks + depth)
            pl.when(active)(functools.partial(stage, t - depth))
        return carry

    lax.fori_loop(0, chunks + 3, turn, 0)
    straight = chunk - changed
    for peers, send, sent in (
        (peers_h, h_send, straight + changed * at.b_size),
        (peers_b, b_send, straight * at.high_size + changed),
        (peers_a, a_send, chunk * plane),
    ):
        size = many(chunks * sent)
        for d, other in enumerate(peers):
            remote(size, size, send.at[d], core_recv, other).wait_send()
    half = many(at.a_size * plane * rows)
    last = remote(half, half, core_send, core_recv, sibling)
    last.wait_send()
    last.wait_recv()


def gather_windows(window, gx_size, gy_size, chunks, number, name):
    sizes = axis_sizes(gx_size, gy_size)
    a, b, h = sizes[0] - 1, sizes[1] - 1, sizes[2] - 1
    dma = pltpu.SemaphoreType.DMA
    return pl.pallas_call(
        functools.partial(gather_kernel, sizes, chunks),
        out_shape=jax.ShapeDtypeStruct((gx_size * gy_size * window.shape[0], LANES), window.dtype),
        in_specs=[pl.BlockSpec(memory_space=pltpu.VMEM)],
        out_specs=pl.BlockSpec(memory_space=pl.ANY),
        scratch_shapes=[dma((chunks,)), dma((h,)), dma((2, chunks, h)), dma((b,)), dma((2, chunks, b)), dma((a,)),
                        dma((chunks, a)), dma, dma],
        compiler_params=pltpu.CompilerParams(
            collective_id=number, has_side_effects=True, vmem_limit_bytes=32 << 20
        ),
        name=name,
    )(window)


class Way:
    def __init__(self, at, turned, span, refs):
        self.start, self.size = span
        (self.keep_two, self.send_two, self.recv_two, self.keep_three, self.send_three, self.recv_three,
         self.two_send, self.two_recv, self.three_send, self.three_recv) = refs
        along_b, along_h = (at.along_b(), at.b, at.b_size), (at.along_h(), at.h, at.high_size)
        high = at.high_size
        if turned:
            (self.peers, self.place, self.count), (self.last_peers, self.last_place, self.inner) = along_h, along_b
            self.number = lambda other, i: i * high + other
        else:
            (self.peers, self.place, self.count), (self.last_peers, self.last_place, self.inner) = along_b, along_h
            self.number = lambda other, i: other * high + i

    def two(self, u, d):
        slot = lax.rem(u, 2)
        return remote(self.send_two.at[slot, d - 1], self.recv_two.at[u, d - 1], self.two_send.at[slot, d - 1],
                      self.two_recv.at[u, d - 1], self.peers[d - 1])

    def three(self, u, d):
        slot = lax.rem(u, 2)
        return remote(self.send_three.at[slot, d - 1], self.recv_three.at[u, d - 1], self.three_send.at[slot, d - 1],
                      self.three_recv.at[u, d - 1], self.last_peers[d - 1])

    def second(self, u, total):
        slot, rows = lax.rem(u, 2), pl.ds(self.start, self.size)
        for d in range(1, self.count):
            pl.when(u >= 2)(lambda d=d: self.two(u - 2, d).wait_send())
            other = lax.rem(self.place + d, self.count)

            def give(i, carry):
                self.send_two[slot, d - 1, i] = total(self.number(other, i), rows).astype(jnp.bfloat16)
                return carry

            lax.fori_loop(0, self.inner, give, 0)
            self.two(u, d).start()

        def hold(i, carry):
            self.keep_two[slot, i] = total(self.number(self.place, i), rows)
            return carry

        lax.fori_loop(0, self.inner, hold, 0)

    def third(self, u):
        slot = lax.rem(u, 2)
        for d in range(1, self.count):
            self.two(u, d).wait_recv()

        def total(i):
            value = self.keep_two[slot, i]
            for d in range(1, self.count):
                value = value + self.recv_two[u, d - 1, i].astype(jnp.float32)
            return value

        for d in range(1, self.inner):
            pl.when(u >= 2)(lambda d=d: self.three(u - 2, d).wait_send())
            self.send_three[slot, d - 1] = total(lax.rem(self.last_place + d, self.inner)).astype(jnp.bfloat16)
            self.three(u, d).start()
        self.keep_three[slot] = total(self.last_place)

    def last(self, u):
        value = self.keep_three[lax.rem(u, 2)]
        for d in range(1, self.inner):
            self.three(u, d).wait_recv()
            value = value + self.recv_three[u, d - 1].astype(jnp.float32)
        return value

    def drain(self, u):
        for d in range(1, self.count):
            self.two(u, d).wait_send()
        for d in range(1, self.inner):
            self.three(u, d).wait_send()


def way_scratch(chunks, count, inner, size):
    low, dma = jnp.bfloat16, pltpu.SemaphoreType.DMA
    return [
        pltpu.VMEM((2, inner, size, LANES), jnp.float32),
        pltpu.VMEM((2, count - 1, inner, size, LANES), low),
        pltpu.VMEM((chunks, count - 1, inner, size, LANES), low),
        pltpu.VMEM((2, size, LANES), jnp.float32),
        pltpu.VMEM((2, inner - 1, size, LANES), low),
        pltpu.VMEM((chunks, inner - 1, size, LANES), low),
        dma((2, count - 1)),
        dma((chunks, count - 1)),
        dma((2, inner - 1)),
        dma((chunks, inner - 1)),
    ]


def reduce_kernel(shard, sizes, grads_ref, square_ref, out_ref, squares_ref, own, landed, keep_one, send_one, recv_one,
                  partial, square_send, square_recv, load_sem, pair_send, pair_recv, credit, one_send, one_recv, *more):
    at = Places(sizes)
    a_size, b_size, high_size = at.a_size, at.b_size, at.high_size
    core, my_a, my_b, high = at.core, at.a, at.b, at.h
    plane = b_size * high_size
    chunk = own.shape[2]
    chunks = out_ref.shape[0] // chunk

    def start_row(side, number):
        a, rest = number // plane, lax.rem(number, plane)
        return window_start(shard, at.linear(side, a, rest // high_size, lax.rem(rest, high_size)))

    sibling, peers = at.sibling(), at.along_a()
    changed = turned_rows(chunk)
    straight = chunk - changed
    ways = [Way(at, False, (0, straight), more[:10])]
    if changed:
        ways.append(Way(at, True, (straight, changed), more[10:]))
    count = squares_ref.shape[0]
    me = linear_index(at.gy_size)

    def device(step):
        other = lax.rem(me + step, count)
        return (other // at.gy_size, lax.rem(other, at.gy_size))

    barrier = pltpu.get_barrier_semaphore()

    def greet(step, carry):
        pl.semaphore_signal(barrier, inc=1, device_id=device(step), device_id_type=MESH)
        return carry

    lax.fori_loop(1, count, greet, 0)
    pl.semaphore_wait(barrier, count - 1)
    table_part = square_ref[...]
    partial[...] = sum(table_part[:, j * LANES : (j + 1) * LANES] for j in range(D_TXT // LANES))
    spot = (lax.broadcasted_iota(jnp.int32, (chunk, LANES), 0) * LANES
            + lax.broadcasted_iota(jnp.int32, (chunk, LANES), 1))
    blocks = a_size * plane

    def pair_stage(t):
        slot = lax.rem(t, 2)

        @pl.when(t >= 2)
        def _():
            pl.semaphore_wait(credit, 1)

        def each(number, carry):
            theirs = pl.multiple_of(start_row(1 - core, number) + t * chunk, GROUP)
            mine = pl.multiple_of(start_row(core, number) + t * chunk, GROUP)
            remote(
                grads_ref.at[pl.ds(theirs, chunk)], landed.at[slot, number], pair_send.at[slot], pair_recv.at[slot], sibling
            ).start()
            pltpu.make_async_copy(
                grads_ref.at[pl.ds(mine, chunk)], own.at[slot, number], load_sem.at[slot]
            ).start()
            return carry

        lax.fori_loop(0, blocks, each, 0)

    def first_stage(u):
        slot = lax.rem(u, 2)
        both = remote(landed.at[slot], landed.at[slot], pair_send.at[slot], pair_recv.at[slot], sibling)
        pltpu.make_async_copy(own.at[slot], own.at[slot], load_sem.at[slot]).wait()
        both.wait_send()
        both.wait_recv()
        for d in range(1, a_size):
            @pl.when(u >= 2)
            def _():
                remote(send_one.at[slot, d - 1], recv_one.at[u - 2, d - 1], one_send.at[slot, d - 1],
                       one_recv.at[u - 2, d - 1], peers[d - 1]).wait_send()

            first = lax.rem(my_a + d, a_size) * plane

            def give(i, carry):
                send_one[slot, d - 1, i] = (own[slot, first + i] + landed[slot, first + i]).astype(jnp.bfloat16)
                return carry

            lax.fori_loop(0, plane, give, 0)
            remote(send_one.at[slot, d - 1], recv_one.at[u, d - 1], one_send.at[slot, d - 1],
                   one_recv.at[u, d - 1], peers[d - 1]).start()

        def hold(i, carry):
            keep_one[slot, i] = own[slot, my_a * plane + i] + landed[slot, my_a * plane + i]
            return carry

        lax.fori_loop(0, plane, hold, 0)

        @pl.when(u < chunks - 2)
        def _():
            pl.semaphore_signal(credit, inc=1, device_id=sibling, device_id_type=MESH)

    def second_stage(u):
        slot = lax.rem(u, 2)
        for d in range(1, a_size):
            remote(recv_one.at[u, d - 1], recv_one.at[u, d - 1], one_send.at[slot, d - 1], one_recv.at[u, d - 1],
                   peers[d - 1]).wait_recv()

        def total(number, rows):
            value = keep_one[slot, number, rows, :]
            for d in range(1, a_size):
                value = value + recv_one[u, d - 1, number, rows, :].astype(jnp.float32)
            return value

        for way in ways:
            way.second(u, total)

    def third_stage(u):
        for way in ways:
            way.third(u)

    def last_stage(u):
        for way in ways:
            value = way.last(u)
            row = u * chunk + way.start
            out_ref[pl.ds(pl.multiple_of(row, GROUP), way.size), :] = value
            place = spot[: way.size] + (window_start(shard, me) + row) * LANES - me * shard
            square = jnp.where((place >= 0) & (place < shard), value * value, 0.0)
            partial[...] += sum(square[r : r + 8] for r in range(0, way.size, 8))

    def turn(t, carry):
        stages = (pair_stage, first_stage, second_stage, third_stage, last_stage)
        for depth, stage in enumerate(stages):
            @pl.when((t >= depth) & (t < chunks + depth))
            def _():
                stage(t - depth)

        return carry

    lax.fori_loop(0, chunks + 4, turn, 0)
    squares_ref[me] = partial[...]

    def send(step, carry):
        remote(partial, squares_ref.at[me], square_send, square_recv, device(step)).start()
        return carry

    lax.fori_loop(1, count, send, 0)
    others = squares_ref.at[pl.ds(0, count - 1)]
    both = remote(others, others, square_send, square_recv, device(1))
    both.wait_send()
    both.wait_recv()
    for u in range(max(chunks - 2, 0), chunks):
        slot = u % 2
        for d in range(1, a_size):
            remote(send_one.at[slot, d - 1], recv_one.at[u, d - 1], one_send.at[slot, d - 1],
                   one_recv.at[u, d - 1], peers[d - 1]).wait_send()
        for way in ways:
            way.drain(u)


def reduce_windows(grads, square, shard, gx_size, gy_size, number):
    rows = window_rows(shard, GROUP * CHUNKS)
    chunk = rows // CHUNKS
    x_size, low_size, high_size = axis_sizes(gx_size, gy_size)
    plane = low_size * high_size
    blocks = x_size * plane
    low_type, dma = jnp.bfloat16, pltpu.SemaphoreType.DMA
    a = x_size - 1
    return pl.pallas_call(
        functools.partial(reduce_kernel, shard, (x_size, low_size, high_size)),
        out_shape=[
            jax.ShapeDtypeStruct((rows, LANES), jnp.float32),
            jax.ShapeDtypeStruct((gx_size * gy_size, 8, LANES), jnp.float32),
        ],
        in_specs=[pl.BlockSpec(memory_space=pl.ANY), pl.BlockSpec(memory_space=pltpu.VMEM)],
        out_specs=[pl.BlockSpec(memory_space=pltpu.VMEM)] * 2,
        scratch_shapes=[
            pltpu.VMEM((2, blocks, chunk, LANES), jnp.float32),
            pltpu.VMEM((2, blocks, chunk, LANES), jnp.float32),
            pltpu.VMEM((2, plane, chunk, LANES), jnp.float32),
            pltpu.VMEM((2, a, plane, chunk, LANES), low_type),
            pltpu.VMEM((CHUNKS, a, plane, chunk, LANES), low_type),
            pltpu.VMEM((8, LANES), jnp.float32),
            dma,
            dma,
            dma((2,)),
            dma((2,)),
            dma((2,)),
            pltpu.SemaphoreType.REGULAR,
            dma((2, a)),
            dma((CHUNKS, a)),
        ]
        + way_scratch(CHUNKS, low_size, high_size, chunk - turned_rows(chunk))
        + (way_scratch(CHUNKS, high_size, low_size, turned_rows(chunk)) if turned_rows(chunk) else []),
        compiler_params=pltpu.CompilerParams(
            collective_id=number, has_side_effects=True, vmem_limit_bytes=60 << 20
        ),
        name="reduce_windows",
    )(grads, square)


def log_sums(rows, columns, column_ok, logit_scale, matches, positives):
    total, taken = rows.shape[0], min(rows.shape[0], 256)

    def some(args):
        row_part, match_part, positive_part = args
        dots = back_dot(row_part, columns)
        logits = logit_scale * dots
        masked = jnp.where(column_ok[None, :], logits, -1e30)
        row_max = jnp.max(masked, 1, keepdims=True)
        log_total = row_max[:, 0] + jnp.log(jnp.sum(jnp.exp(masked - row_max), 1))
        gap = jnp.where(match_part > 0.0, logits[:, :total] - log_total[:, None], 0.0)
        pulled = jnp.sum(positive_part[:, None] * jnp.exp(masked - log_total[:, None]) * dots)
        return log_total, -jnp.sum(gap), pulled - jnp.sum(match_part * dots[:, :total])

    if taken == total:
        return some((rows, matches, positives))
    logs, parts, pulls = lax.map(
        some,
        (
            rows.reshape(-1, taken, rows.shape[1]),
            matches.reshape(-1, taken, total),
            positives.reshape(-1, taken),
        ),
    )
    return logs.reshape(-1), jnp.sum(parts), jnp.sum(pulls)


def side_grads(row_embed, columns, column_ok, same_own, positives_own, log_own, logit_scale, total_count):
    dot_vals = back_dot(row_embed, columns)
    masked = jnp.where(column_ok[None, :], logit_scale * dot_vals, -1e30)
    extra = columns.shape[0] - same_own.shape[1]
    weights_pos = jnp.concatenate(
        [same_own, jnp.zeros((same_own.shape[0], extra), jnp.float32)], 1
    )
    grad_logits = (
        positives_own[:, None] * jnp.exp(masked - log_own[:, None]) - weights_pos
    ) / total_count
    grad_dots = (logit_scale * grad_logits).astype(jnp.bfloat16)
    return fwd_dot(grad_dots, columns)


def cross_grads(rows, own, valid_own, same_own, positives_all, logs, logit_scale, total_count):
    logits = logit_scale * back_dot(rows, own)
    masked = jnp.where(valid_own[None, :], logits, -1e30)
    grad_logits = (
        positives_all[:, None] * jnp.exp(masked - logs[:, None]) - same_own.T
    ) / total_count
    grad_dots = (logit_scale * grad_logits).astype(jnp.bfloat16)
    return weight_grad(grad_dots, rows)


def body(
    flat_master,
    flat_first,
    flat_second,
    table,
    table_first,
    table_second,
    pixels,
    token_ids,
    end_pos,
    pair_counts,
    groups,
    cached_image,
    cached_text,
):
    gx_size, gy_size = lax.axis_size("gx"), lax.axis_size("gy")
    device_count = gx_size * gy_size
    my_index = linear_index(gy_size)
    pairs_dev = pixels.shape[0]
    shard = flat_master.shape[0]
    tokens = token_ids.size
    vocab_dev = table.shape[0]
    cap = route_capacity(tokens, gy_size)
    own_ids = token_ids.reshape(-1)
    same = own_ids[:, None] == own_ids[None, :]
    order = jnp.arange(tokens)
    leading = ~jnp.any(same & (order[None, :] < order[:, None]), 1)
    flat_ids = jnp.where(leading, own_ids, NO_TOKEN)
    flat_ids = jnp.pad(flat_ids, (0, ID_ROWS * LANES // 2 - tokens)).reshape(-1, LANES)
    payload = [
        place_window(flat_master, gy_size),
        jnp.concatenate([cached_image, cached_text], 0).reshape(CACHED_ROWS, LANES),
        jnp.concatenate([flat_ids // 256, flat_ids % 256], 0).astype(jnp.bfloat16),
    ]
    used = sum(part.shape[0] for part in payload)
    step = GROUP * GATHER_CHUNKS
    payload = jnp.pad(jnp.concatenate(payload, 0), ((0, -used % step), (0, 0)))
    gathered = gather_windows(payload, gx_size, gy_size, GATHER_CHUNKS, 4, "gather_weights")
    every_part = gathered.reshape(device_count, -1, LANES)
    cached = every_part[:, used - ID_ROWS - CACHED_ROWS : used - ID_ROWS].reshape(device_count, -1, EMBED)
    cache_img, cache_txt = lax.optimization_barrier((cached[:, :pairs_dev], cached[:, pairs_dev:]))
    cache_img, cache_txt = cache_img.reshape(-1, EMBED), cache_txt.reshape(-1, EMBED)
    coded = every_part[:, used - ID_ROWS : used].astype(jnp.int32)
    ids_all = coded[:, : ID_ROWS // 2] * 256 + coded[:, ID_ROWS // 2 :]
    ids_all = ids_all.reshape(device_count, -1)[:, :tokens]
    holders = ids_all // vocab_dev
    pair_rows = jnp.sum(holders[:, :, None] == jnp.arange(gy_size), 1)
    rounds = (jnp.max(pair_rows) + cap - 1) // cap
    me_y = lax.axis_index("gy")
    held = holders == me_y
    held_rank = jnp.where(held, ranks(held), -1)
    held_row = ids_all - me_y * vocab_dev
    held_count = jnp.sum(held, 1)
    own_flags = (jnp.arange(gy_size)[:, None] == own_ids[None, :] // vocab_dev) & leading[None, :]
    own_place = jnp.arange(gy_size)[:, None] * tokens + ranks(own_flags)
    own_place = jnp.sum(jnp.where(own_flags, own_place, 0), 0)
    own_place = jnp.sum(jnp.where(same & leading[None, :], own_place[None, :], 0), 1)
    own_holder, own_rank = own_place // tokens, own_place % tokens

    def held_rows(turn):
        slots = held_rank - turn * cap
        found = slots[:, None, :] == jnp.arange(cap)[None, :, None]
        return vocab_dev + jnp.sum(jnp.where(found, held_row[:, None, :] - vocab_dev, 0), 2)

    def own_slots(turn):
        rank = own_rank - turn * cap
        return jnp.where((rank >= 0) & (rank < cap), own_holder * cap + rank, -1)

    first_rows = held_rows(0)
    group_start = lax.axis_index("gx") * gy_size

    def rows_to_send(index):
        index = lax.dynamic_slice_in_dim(index, group_start, gy_size, 0)
        rows = jnp.take(table, index.reshape(-1), axis=0, mode="clip")
        return rows.reshape(gy_size, cap, D_TXT)

    sent = rows_to_send(first_rows).astype(jnp.bfloat16)
    slot_count = gy_size * cap

    def more_rows(turn, found):
        rows = lax.all_to_all(rows_to_send(held_rows(turn)), "gy", 0, 0, tiled=True)
        rows = rows.reshape(slot_count, D_TXT).astype(jnp.bfloat16)
        return found + weight_grad(pick_matrix(own_slots(turn), slot_count), rows).astype(jnp.bfloat16)

    nothing = jnp.zeros((tokens, D_TXT), jnp.bfloat16)
    extra_rows = lax.cond(
        rounds > 1, lambda rows: lax.fori_loop(1, rounds, more_rows, rows), lambda rows: rows, nothing
    )
    sent, extra_rows = lax.optimization_barrier((sent, extra_rows))
    *spread, landed = spread_weights(gathered, sent, shard, gx_size, gy_size, 5)
    picks = pick_matrix(own_slots(0), slot_count)
    token_rows = weight_grad(picks, landed.reshape(slot_count, D_TXT)).astype(jnp.bfloat16)

    token_rows = token_rows + extra_rows
    image_weights = dict(zip(IMAGE.names, spread[:5]))
    text_weights = dict(zip(TEXT.names, spread[5:9]))
    image_vec, text_vec, temper = split_vectors(spread[9])
    image_gains, image_base, image_rows = image_inputs(image_vec, pixels)
    text_gains, text_base, text_rows = text_inputs(text_vec, token_rows)
    image_kept = tower_forward(IMAGE, end_pos, image_gains, image_base, image_rows, image_weights)
    text_kept = tower_forward(TEXT, end_pos, text_gains, text_base, text_rows, text_weights)
    image_emb = image_kept[14].astype(jnp.bfloat16)
    text_emb = text_kept[14].astype(jnp.bfloat16)
    embeds = jnp.concatenate([image_emb, text_emb], 0).reshape(-1, LANES)
    embeds = gather_windows(embeds, gx_size, gy_size, 1, 0, "embeddings")
    embeds = embeds.reshape(device_count, 2 * pairs_dev, EMBED)
    all_img, all_txt = lax.optimization_barrier((embeds[:, :pairs_dev], embeds[:, pairs_dev:]))
    all_img, all_txt = all_img.reshape(-1, EMBED), all_txt.reshape(-1, EMBED)
    total_pairs = all_img.shape[0]
    valid_all = jnp.arange(total_pairs) % pairs_dev < jnp.repeat(pair_counts.reshape(-1), pairs_dev)
    matches = (
        (groups[:, None] == groups[None, :]) & valid_all[:, None] & valid_all[None, :]
    ).astype(jnp.float32)
    positives_all = jnp.sum(matches, 1)
    total_count = 2.0 * jnp.sum(positives_all)
    own_start = my_index * pairs_dev
    own_part = functools.partial(
        lax.dynamic_slice_in_dim, start_index=own_start, slice_size=pairs_dev, axis=0
    )
    same_own, positives_own, valid_own = own_part(matches), own_part(positives_all), own_part(valid_all)
    logit_scale = jnp.exp(temper)
    column_ok = jnp.concatenate([valid_all, jnp.ones((cache_img.shape[0],), jnp.bool_)])
    columns_txt = jnp.concatenate([all_txt, cache_txt])
    columns_img = jnp.concatenate([all_img, cache_img])
    log_img, loss_one, pull_one = log_sums(
        all_img, columns_txt, column_ok, logit_scale, matches, positives_all
    )
    log_txt, loss_two, pull_two = log_sums(
        all_txt, columns_img, column_ok, logit_scale, matches, positives_all
    )
    grad_temper = logit_scale * (pull_one + pull_two) / total_count
    loss_sum = loss_one + loss_two
    grad_img = side_grads(
        image_emb, columns_txt, column_ok, same_own, positives_own, own_part(log_img), logit_scale, total_count
    )
    grad_txt = side_grads(
        text_emb, columns_img, column_ok, same_own, positives_own, own_part(log_txt), logit_scale, total_count
    )
    grad_img = grad_img + cross_grads(
        all_txt, image_emb, valid_own, same_own, positives_all, log_txt, logit_scale, total_count
    )
    grad_txt = grad_txt + cross_grads(
        all_img, text_emb, valid_own, same_own, positives_all, log_img, logit_scale, total_count
    )
    text_grads = tower_backward(TEXT, end_pos, text_gains, grad_txt, text_kept[:14], text_weights)
    grad_rows = text_grads[6][: SEQS * CTX]
    to_holders = fwd_dot(picks, grad_rows).astype(jnp.bfloat16).reshape(gy_size, cap, D_TXT)
    image_grads = tower_backward(IMAGE, end_pos, image_gains, grad_img, image_kept[:14], image_weights)
    pair_lists = ([(image_rows, image_grads[6])],) + grad_pairs(image_kept, image_grads)
    pair_lists = pair_lists + grad_pairs(text_kept, text_grads)
    total_rows = window_start(shard, device_count - 1) + window_rows(shard, GROUP * CHUNKS)
    vec_rows = jnp.concatenate(
        [
            image_grads[7][:1].reshape(-1, LANES),
            image_grads[7].reshape(-1, LANES),
            image_grads[8].reshape(-1, LANES),
            text_grads[7].reshape(-1, LANES),
            text_grads[8][2:].reshape(-1, LANES),
        ]
    )
    vec_rows = jnp.pad(vec_rows, ((0, total_rows - matrix_rows() - vec_rows.shape[0]), (0, 0)))
    local_grads, arrived = weight_grads(pair_lists, vec_rows, to_holders, gx_size, gy_size, 6)
    table_grad, table_square = table_sum(
        jnp.minimum(held_count, cap),
        first_rows.reshape(-1),
        arrived.reshape(device_count, cap, D_TXT),
        vocab_dev,
    )

    def more_grads(turn, total):
        rows = fwd_dot(pick_matrix(own_slots(turn), slot_count), grad_rows).astype(jnp.bfloat16)
        rows = lax.all_to_all(rows.reshape(gy_size, cap, D_TXT), "gy", 0, 0, tiled=True)
        rows = lax.all_gather(rows, "gx", axis=0).reshape(device_count * cap, D_TXT).astype(jnp.float32)
        return total.at[held_rows(turn).reshape(-1)].add(rows)

    def whole_squares(total):
        return jnp.sum((total[:vocab_dev] * total[:vocab_dev]).reshape(-1, 8, D_TXT), 0)

    def more_turns(total, square):
        total = lax.fori_loop(1, rounds, more_grads, total)
        return total, whole_squares(total)

    table_grad, table_square = lax.cond(
        rounds > 1, more_turns, lambda total, square: (total, square), table_grad, table_square
    )
    table_square = jnp.where(lax.axis_index("gx") == 0, table_square, 0.0)
    grad_window, every = reduce_windows(local_grads, table_square, shard, gx_size, gy_size, 1)
    position = my_index * shard + jnp.arange(shard)
    grad_shard = lift_window(grad_window, shard, gy_size)
    grad_shard = jnp.where(position == parameter_count() - 1, grad_temper, grad_shard)
    total_square = jnp.sum(every) + grad_temper * grad_temper
    grad_norm = jnp.sqrt(total_square)
    factor = jnp.minimum(1.0, clip_limit / (grad_norm + 1e-06))
    matrix_stop = matrix_rows() * LANES
    is_matrix = position < matrix_stop
    rates = jnp.where(is_matrix, rate_matrix, rate_vector)
    decays = jnp.where(is_matrix, decay_rate, 0.0)
    master_out, first_out, second_out = adam_step(
        flat_master, flat_first, flat_second, grad_shard * factor, rates, decays
    )
    table_out, table_first_out, table_second_out = adam_step(
        table, table_first, table_second, table_grad[:vocab_dev] * factor, rate_table, 0.0
    )
    return (
        master_out,
        first_out,
        second_out,
        table_out,
        table_first_out,
        table_second_out,
        loss_sum,
        total_count,
        grad_norm,
    )


def solution(mesh):
    placed = (
        P(("gx", "gy")),
        P(("gx", "gy")),
        P(("gx", "gy")),
        P("gy", None),
        P("gy", None),
        P("gy", None),
        P(("gx", "gy"), None, None),
        P(("gx", "gy"), None),
        P(("gx", "gy")),
        P(),
        P(),
        P(("gx", "gy"), None),
        P(("gx", "gy"), None),
    )
    return jax.shard_map(
        body,
        mesh=mesh,
        in_specs=placed,
        out_specs=(
            P(("gx", "gy")),
            P(("gx", "gy")),
            P(("gx", "gy")),
            P("gy", None),
            P("gy", None),
            P("gy", None),
            P(),
            P(),
            P(),
        ),
        check_vma=False,
    )
```

```python
import functools

import jax
import jax.numpy as jnp
from jax import lax
from jax.experimental import pallas as pl
from jax.experimental.pallas import tpu as pltpu
from jax.sharding import PartitionSpec as P

D_IMG = 768
IMG_HEADS = 12
IMG_MLP = 3072
PATCH_DIM = 3072
D_TXT = 512
TXT_HEADS = 8
TXT_MLP = 2048
CTX = 77
EMBED = 512
STEP = 10
IMG_TOK = 50


clip_limit = 0.1
beta_one = 0.9
beta_two = 0.999
adam_eps = 1e-08
decay_rate = 0.1
rate_matrix = 0.01
rate_vector = 0.2
rate_table = 0.2
norm_eps = 1e-05


def segment_list():
    return [
        ("patch_embed", PATCH_DIM, D_IMG),
        ("image_attn", D_IMG, 4 * D_IMG),
        ("image_up", D_IMG, IMG_MLP),
        ("image_down", IMG_MLP, D_IMG),
        ("image_proj", D_IMG, EMBED),
        ("text_attn", D_TXT, 4 * D_TXT),
        ("text_up", D_TXT, TXT_MLP),
        ("text_down", TXT_MLP, D_TXT),
        ("text_proj", D_TXT, EMBED),
        ("image_vec", IMG_TOK + 9, D_IMG),
        ("text_vec", CTX + 6, D_TXT),
        ("temper", 1, 1),
    ]


LANES = 128
GROUP = 16
CHUNKS = 16
GATHER_CHUNKS = 14
TURNED = 6
CACHED_ROWS = 64
ID_ROWS = 16
MESH = pl.DeviceIdType.MESH


def dot_nn(left_side, right_side):
    return lax.dot_general(
        left_side, right_side, (((1,), (0,)), ((), ())), preferred_element_type=jnp.float32
    )


def dot_nt(left_side, right_side):
    return lax.dot_general(
        left_side, right_side, (((1,), (1,)), ((), ())), preferred_element_type=jnp.float32
    )


def dot_tn(left_side, right_side):
    return lax.dot_general(
        left_side, right_side, (((0,), (0,)), ((), ())), preferred_element_type=jnp.float32
    )


def back_dot(left_side, right_side):
    return dot_nt(left_side, right_side)


def fwd_dot(left_side, right_side):
    return dot_nn(left_side, right_side)


def weight_grad(left_side, right_side):
    return dot_tn(left_side, right_side)


def norm_parts(values):
    center = values - jnp.mean(values, -1, keepdims=True)
    scale = lax.rsqrt(jnp.mean(center * center, -1, keepdims=True) + norm_eps)
    return center * scale, scale


def layer_norm(values, gain_vec, shift_vec):
    return norm_parts(values)[0] * gain_vec + shift_vec


def layer_norm_back(values, gain_vec, grad):
    unit, scale = norm_parts(values)
    grad_unit = grad * gain_vec
    inner = jnp.mean(grad_unit, -1, keepdims=True)
    along = jnp.mean(grad_unit * unit, -1, keepdims=True)
    return scale * (grad_unit - inner - unit * along), grad * unit


def sum_rows(values):
    return jnp.sum(values, 0, keepdims=True)


def low16(values):
    return jnp.concatenate([values, jnp.zeros_like(values)], 0).astype(jnp.bfloat16)


SEQS = 8


class Tower:
    def __init__(self, image):
        self.image = image
        self.width = D_IMG if image else D_TXT
        self.heads = IMG_HEADS if image else TXT_HEADS
        self.length = IMG_TOK if image else CTX
        self.rows = -(-SEQS * self.length // GROUP) * GROUP
        self.lanes = 16 if image else 8
        self.queries = SEQS * self.lanes
        self.block = 80 if image else 48
        self.names = ("patch", "attn", "up", "down", "proj") if image else ("attn", "up", "down", "proj")

    def shapes(self):
        width = self.width
        found = dict(attn=(width, 4 * width), up=(width, 4 * width), down=(4 * width, width), proj=(width, EMBED))
        if self.image:
            found["patch"] = (PATCH_DIM, width)
        return found

    def head_mask(self):
        lane = lax.broadcasted_iota(jnp.int32, (self.lanes, self.width), 1)
        row = lax.broadcasted_iota(jnp.int32, (self.lanes, self.width), 0)
        return lane // (self.width // self.heads) == row

    def spread_heads(self, values, wide_ref):
        mask = self.head_mask()
        for s in range(SEQS):
            row = jnp.broadcast_to(values[s : s + 1].astype(jnp.float32), mask.shape)
            wide_ref[s * self.lanes : (s + 1) * self.lanes, :] = jnp.where(mask, row, 0.0)
        return wide_ref[...].astype(jnp.bfloat16)

    def join_heads(self, values, wide_ref):
        mask = self.head_mask()
        wide_ref[...] = values
        rows = [
            sum_rows(jnp.where(mask, wide_ref[s * self.lanes : (s + 1) * self.lanes, :], 0.0))
            for s in range(SEQS)
        ]
        return jnp.concatenate(rows, 0)

    def row_of(self, s, ends_ref):
        return s if self.image else s * self.length + ends_ref[s]

    def each_block(self, function, start):
        return lax.fori_loop(
            0,
            self.rows // self.block,
            lambda i, carry: function(pl.ds(pl.multiple_of(i * self.block, GROUP), self.block), carry),
            start,
        )


def tower_fetch(names, sources, landed, sems):
    copies = {
        name: pltpu.make_async_copy(source, ref, sems.at[i])
        for i, (name, source, ref) in enumerate(zip(names, sources, landed))
    }
    for copy in copies.values():
        copy.start()
    return copies, dict(zip(names, landed))


def tower_forward_kernel(tower, *refs):
    count = len(tower.names)
    ends_ref, gains_ref, base_ref, input_ref = refs[:4]
    sources = refs[4 : 4 + count]
    (tokens_ref, normed_ref, pair_ref, normed_own_ref, query_ref, probs_ref, attended_ref, middle_ref, normed_two_ref,
     upper_ref, act_ref, output_ref, head_ref, raw_ref, emb_ref) = refs[4 + count : 19 + count]
    hidden_ref, wide_ref = refs[19 + count : 21 + count]
    landed, sems = refs[21 + count : 21 + 2 * count], refs[21 + 2 * count]
    copies, weights = tower_fetch(tower.names, sources, landed, sems)
    width = tower.width
    gains = [gains_ref[i : i + 1, :] for i in range(8)]
    if tower.image:
        copies["patch"].wait()

        def patch(j, carry):
            cols = pl.ds(pl.multiple_of(j * 256, 256), 256)
            tokens_ref[:, cols] = dot_nn(input_ref[...], weights["patch"][:, cols]) + base_ref[:, cols]
            return carry

        lax.fori_loop(0, width // 256, patch, 0)

    def first(rows, carry):
        if tower.image:
            hidden = layer_norm(tokens_ref[rows, :], gains[0], gains[1])
        else:
            hidden = input_ref[rows, :].astype(jnp.float32) + base_ref[rows, :]
            tokens_ref[rows, :] = hidden
        hidden_ref[rows, :] = hidden
        normed_ref[rows, :] = layer_norm(hidden, gains[2], gains[3]).astype(jnp.bfloat16)
        return carry

    tower.each_block(first, 0)
    copies["attn"].wait()

    def pair(j, carry):
        at = pl.multiple_of(j * 256, 256)
        product = dot_nn(normed_ref[...], weights["attn"][:, pl.ds(width + at, 256)])
        pair_ref[:, pl.ds(at, 256)] = product.astype(jnp.bfloat16)
        return carry

    lax.fori_loop(0, 2 * width // 256, pair, 0)
    hidden_own = jnp.concatenate(
        [hidden_ref[pl.ds(tower.row_of(s, ends_ref), 1), :] for s in range(SEQS)], 0
    )
    normed_own = low16(layer_norm(hidden_own, gains[2], gains[3]))
    normed_own_ref[...] = normed_own
    query = dot_nn(normed_own, weights["attn"][:, :width]).astype(jnp.bfloat16)
    query_ref[...] = query
    queries = tower.spread_heads(query, wide_ref)
    scores = dot_nt(queries, pair_ref[:, :width]) * (width // tower.heads) ** (-0.5)
    row = lax.broadcasted_iota(jnp.int32, scores.shape, 0) // tower.lanes
    spot = lax.broadcasted_iota(jnp.int32, scores.shape, 1)
    if tower.image:
        allowed = lax.rem(spot, SEQS) == row
    else:
        spot = spot - row * tower.length
        last = jnp.zeros(scores.shape, jnp.int32)
        for s in range(SEQS):
            last = jnp.where(row == s, ends_ref[s], last)
        allowed = (spot >= 0) & (spot <= last)
    scores = jnp.where(allowed, scores, -1e30)
    powers = jnp.exp(scores - jnp.max(scores, -1, keepdims=True))
    probs = powers / jnp.sum(powers, -1, keepdims=True)
    probs_ref[...] = probs
    attended = low16(tower.join_heads(dot_nn(probs.astype(jnp.bfloat16), pair_ref[:, width:]), wide_ref))
    attended_ref[...] = attended
    middle = hidden_own + dot_nn(attended, weights["attn"][:, 3 * width :])[:SEQS]
    middle_ref[...] = middle
    normed_two_ref[...] = low16(layer_norm(middle, gains[4], gains[5]))
    copies["up"].wait()

    def rise(j, carry):
        cols = pl.ds(pl.multiple_of(j * 512, 512), 512)
        upper = dot_nn(normed_two_ref[...], weights["up"][:, cols])[:SEQS]
        upper_ref[:, cols] = upper
        act_ref[:, cols] = low16(upper * jax.nn.sigmoid(1.702 * upper))
        return carry

    lax.fori_loop(0, 4 * width // 512, rise, 0)
    copies["down"].wait()

    def fall(j, carry):
        cols = pl.ds(pl.multiple_of(j * 256, 256), 256)
        output_ref[:, cols] = middle_ref[:, cols] + dot_nn(act_ref[...], weights["down"][:, cols])[:SEQS]
        return carry

    lax.fori_loop(0, width // 256, fall, 0)
    head_in = low16(layer_norm(output_ref[...], gains[6], gains[7]))
    head_ref[...] = head_in
    copies["proj"].wait()
    raw = dot_nn(head_in, weights["proj"][...])[:SEQS]
    raw_ref[...] = raw
    emb_ref[...] = raw * lax.rsqrt(jnp.sum(raw * raw, -1, keepdims=True) + 1e-06)


def tower_forward(tower, ends, gains, base, inputs, weights):
    width, rows = tower.width, tower.rows
    low, full = jnp.bfloat16, jnp.float32
    outs = [
        ((rows, width), full),
        ((rows, width), low),
        ((rows, 2 * width), low),
        ((GROUP, width), low),
        ((GROUP, width), low),
        ((tower.queries, rows), full),
        ((GROUP, width), low),
        ((SEQS, width), full),
        ((GROUP, width), low),
        ((SEQS, 4 * width), full),
        ((GROUP, 4 * width), low),
        ((SEQS, width), full),
        ((GROUP, width), low),
        ((SEQS, EMBED), full),
        ((SEQS, EMBED), full),
    ]
    vmem = pl.BlockSpec(memory_space=pltpu.VMEM)
    shapes = tower.shapes()
    return pl.pallas_call(
        functools.partial(tower_forward_kernel, tower),
        out_shape=[jax.ShapeDtypeStruct(shape, kind) for shape, kind in outs],
        in_specs=[pl.BlockSpec(memory_space=pltpu.SMEM)]
        + [vmem] * 3
        + [pl.BlockSpec(memory_space=pl.ANY)] * len(tower.names),
        out_specs=[vmem] * len(outs),
        scratch_shapes=[pltpu.VMEM((rows, width), full), pltpu.VMEM((tower.queries, width), full)]
        + [pltpu.VMEM(shapes[name], low) for name in tower.names]
        + [pltpu.SemaphoreType.DMA((len(tower.names),))],
        compiler_params=pltpu.CompilerParams(vmem_limit_bytes=58 << 20),
        name="image_forward" if tower.image else "text_forward",
    )(ends, gains, base, inputs, *[weights[name] for name in tower.names])


def tower_backward_kernel(tower, *refs):
    names = tower.names[-4:]
    count = len(names)
    ends_ref, gains_ref, grad_ref = refs[:3]
    (tokens_ref, normed_ref, pair_ref, normed_own_ref, query_ref, probs_ref, attended_ref, middle_ref, normed_two_ref,
     upper_ref, act_ref, output_ref, head_ref, raw_ref) = refs[3:17]
    sources = refs[17 : 17 + count]
    (grad_raw_ref, grad_mlp_ref, grad_upper_ref, grad_att_ref, grad_query_ref, grad_pair_ref, grad_rows_ref,
     places_ref, gain_grads_ref) = refs[17 + count : 26 + count]
    grad_ref_wide, wide_ref, grad_middle_ref = refs[26 + count : 29 + count]
    landed, sems = refs[29 + count : 29 + 2 * count], refs[29 + 2 * count]
    copies, weights = tower_fetch(names, sources, landed, sems)
    width, rows = tower.width, tower.rows
    scale = (width // tower.heads) ** (-0.5)
    gains = [gains_ref[i : i + 1, :] for i in range(8)]
    raw, grad_emb = raw_ref[...], grad_ref[...]
    norm = lax.rsqrt(jnp.sum(raw * raw, -1, keepdims=True) + 1e-06)
    along = jnp.sum(raw * grad_emb, -1, keepdims=True)
    grad_raw = low16(grad_emb * norm - raw * (norm * norm * norm * along))
    grad_raw_ref[...] = grad_raw
    copies["proj"].wait()
    grad_head = dot_nt(grad_raw, weights["proj"][...])[:SEQS]
    grad_out, gain_part = layer_norm_back(output_ref[...], gains[6], grad_head)
    gain_grads_ref[6:7, :] = sum_rows(gain_part)
    gain_grads_ref[7:8, :] = sum_rows(grad_head)
    grad_mlp_ref[...] = low16(grad_out)
    copies["down"].wait()

    def rise(j, carry):
        cols = pl.ds(pl.multiple_of(j * 512, 512), 512)
        grad_act = dot_nt(grad_mlp_ref[...], weights["down"][cols, :])[:SEQS]
        upper = upper_ref[:, cols]
        sig = jax.nn.sigmoid(1.702 * upper)
        grad_upper_ref[:, cols] = low16(grad_act * (sig + upper * (1.702 * (sig * (1.0 - sig)))))
        return carry

    lax.fori_loop(0, 4 * width // 512, rise, 0)
    copies["up"].wait()

    def fall(j, carry):
        cols = pl.ds(pl.multiple_of(j * 256, 256), 256)
        grad_middle_ref[:, cols] = dot_nt(grad_upper_ref[...], weights["up"][cols, :])[:SEQS]
        return carry

    lax.fori_loop(0, width // 256, fall, 0)
    grad_norm_two = grad_middle_ref[...]
    grad_mid, gain_part = layer_norm_back(middle_ref[...], gains[4], grad_norm_two)
    gain_grads_ref[4:5, :] = sum_rows(gain_part)
    gain_grads_ref[5:6, :] = sum_rows(grad_norm_two)
    grad_middle = grad_out + grad_mid
    grad_middle_ref[...] = grad_middle
    grad_att = low16(grad_middle)
    grad_att_ref[...] = grad_att
    copies["attn"].wait()
    grad_attended = dot_nt(grad_att, weights["attn"][:, 3 * width :]).astype(jnp.bfloat16)
    grads_heads = tower.spread_heads(grad_attended, wide_ref)
    queries = tower.spread_heads(query_ref[...], wide_ref)
    probs = probs_ref[...]
    grad_probs = dot_nt(grads_heads, pair_ref[:, width:])
    grad_scores = probs * (grad_probs - jnp.sum(grad_probs * probs, -1, keepdims=True))
    grad_scores = grad_scores.astype(jnp.bfloat16)
    grad_query = low16(tower.join_heads(dot_nn(grad_scores, pair_ref[:, :width]), wide_ref) * scale)
    grad_query_ref[...] = grad_query
    grad_pair_ref[:, :width] = (dot_tn(grad_scores, queries) * scale).astype(jnp.bfloat16)
    grad_pair_ref[:, width:] = dot_tn(probs.astype(jnp.bfloat16), grads_heads).astype(jnp.bfloat16)

    def inner(j, carry):
        at = pl.multiple_of(j * 256, 256)
        grad_ref_wide[:, pl.ds(at, 256)] = dot_nt(
            grad_pair_ref[...], weights["attn"][pl.ds(at, 256), width : 3 * width]
        )
        return carry

    lax.fori_loop(0, width // 256, inner, 0)
    grad_own = dot_nt(grad_query, weights["attn"][:, :width])
    for s in range(SEQS):
        grad_ref_wide[pl.ds(tower.row_of(s, ends_ref), 1), :] += grad_own[s : s + 1]

    def first(at, carry):
        grad = grad_ref_wide[at, :]
        hidden = tokens_ref[at, :]
        if tower.image:
            hidden = layer_norm(hidden, gains[0], gains[1])
        grad_in, gain_part = layer_norm_back(hidden, gains[2], grad)
        grad_ref_wide[at, :] = grad_in
        return carry[0] + sum_rows(gain_part), carry[1] + sum_rows(grad)

    nothing = jnp.zeros((1, width), jnp.float32)
    gain_one, shift_one = tower.each_block(first, (nothing, nothing))
    gain_grads_ref[2:3, :] = gain_one
    gain_grads_ref[3:4, :] = shift_one
    for s in range(SEQS):
        grad_ref_wide[pl.ds(tower.row_of(s, ends_ref), 1), :] += grad_middle_ref[s : s + 1, :]

    def second(at, carry):
        grad = grad_ref_wide[at, :]
        if not tower.image:
            grad_rows_ref[at, :] = grad.astype(jnp.bfloat16)
            return carry
        grad_in, gain_part = layer_norm_back(tokens_ref[at, :], gains[0], grad)
        grad_ref_wide[at, :] = grad_in
        grad_rows_ref[at, :] = grad_in.astype(jnp.bfloat16)
        return carry[0] + sum_rows(gain_part), carry[1] + sum_rows(grad)

    gain_pre, shift_pre = tower.each_block(second, (nothing, nothing))
    gain_grads_ref[0:1, :] = gain_pre
    gain_grads_ref[1:2, :] = shift_pre
    if tower.image:
        for p in range(tower.length):
            places_ref[p : p + 1, :] = sum_rows(grad_ref_wide[p * SEQS : (p + 1) * SEQS, :])
        return
    places = grad_ref_wide[0 : tower.length, :]
    for s in range(1, SEQS):
        places = places + grad_ref_wide[s * tower.length : (s + 1) * tower.length, :]
    places_ref[...] = places


def tower_backward(tower, ends, gains, grad_emb, kept, weights):
    width, rows = tower.width, tower.rows
    low, full = jnp.bfloat16, jnp.float32
    outs = [
        ((GROUP, EMBED), low),
        ((GROUP, width), low),
        ((GROUP, 4 * width), low),
        ((GROUP, width), low),
        ((GROUP, width), low),
        ((rows, 2 * width), low),
        ((rows, width), low),
        ((tower.length, width), full),
        ((8, width), full),
    ]
    vmem = pl.BlockSpec(memory_space=pltpu.VMEM)
    shapes, names = tower.shapes(), tower.names[-4:]
    return pl.pallas_call(
        functools.partial(tower_backward_kernel, tower),
        out_shape=[jax.ShapeDtypeStruct(shape, kind) for shape, kind in outs],
        in_specs=[pl.BlockSpec(memory_space=pltpu.SMEM)]
        + [vmem] * (2 + len(kept))
        + [pl.BlockSpec(memory_space=pl.ANY)] * len(names),
        out_specs=[vmem] * len(outs),
        scratch_shapes=[
            pltpu.VMEM((rows, width), full),
            pltpu.VMEM((tower.queries, width), full),
            pltpu.VMEM((SEQS, width), full),
        ]
        + [pltpu.VMEM(shapes[name], low) for name in names]
        + [pltpu.SemaphoreType.DMA((len(names),))],
        compiler_params=pltpu.CompilerParams(vmem_limit_bytes=58 << 20),
        name="image_backward" if tower.image else "text_backward",
    )(ends, gains, grad_emb, *kept, *[weights[name] for name in names])


def grad_pairs(kept, grads):
    (normed, normed_own, attended, normed_two, act_low, head_in) = (
        kept[1], kept[3], kept[6], kept[8], kept[10], kept[12]
    )
    grad_raw, grad_mlp, grad_upper, grad_att, grad_query, grad_pair = grads[:6]
    return (
        [(normed_own, grad_query), (normed, grad_pair), (attended, grad_att)],
        [(normed_two, grad_upper)],
        [(act_low, grad_mlp)],
        [(head_in, grad_raw)],
    )


def image_inputs(image_vec, pixels):
    pixels = jnp.pad(pixels.transpose(1, 0, 2), ((1, 0), (0, 0), (0, 0))).reshape(-1, PATCH_DIM)
    base = image_vec[1 : IMG_TOK + 1] + jnp.pad(image_vec[:1], ((0, IMG_TOK - 1), (0, 0)))
    return image_vec[IMG_TOK + 1 :], jnp.repeat(base, SEQS, axis=0), pixels


def text_inputs(text_vec, token_rows):
    gains = jnp.pad(text_vec[CTX:], ((2, 0), (0, 0)))
    extra = TEXT.rows - SEQS * CTX
    base = jnp.pad(jnp.tile(text_vec[:CTX], (SEQS, 1)), ((0, extra), (0, 0)))
    return gains, base, jnp.pad(token_rows, ((0, extra), (0, 0)))


def adam_step(weight, first, second, grad, rate, decay):
    first = beta_one * first + (1.0 - beta_one) * grad
    second = beta_two * second + (1.0 - beta_two) * grad * grad
    first_hat = first / (1.0 - beta_one**STEP)
    second_hat = second / (1.0 - beta_two**STEP)
    weight = weight - rate * (first_hat / (jnp.sqrt(second_hat) + adam_eps) + decay * weight)
    return (weight, first, second)


IMAGE, TEXT = Tower(True), Tower(False)


def matrix_rows():
    return sum(seg_rows * seg_cols for seg_name, seg_rows, seg_cols in segment_list()[:9]) // LANES


def parameter_count():
    return sum(seg_rows * seg_cols for seg_name, seg_rows, seg_cols in segment_list())


def window_rows(shard, step=GROUP):
    need = -(-(GROUP * LANES - 1 + shard) // LANES)
    return -(-need // step) * step


def window_start(shard, index):
    return (shard * index // (GROUP * LANES)) * GROUP


def linear_index(gy_size):
    return lax.axis_index("gx") * gy_size + lax.axis_index("gy")


def place_kernel(shard, gy_size, flat_ref, out_ref, rolled):
    rows = flat_ref.shape[0]
    offset = lax.rem(shard * linear_index(gy_size), GROUP * LANES)
    down, right = offset // LANES, lax.rem(offset, LANES)
    pad = 2 * GROUP
    rolled[0:pad, :] = jnp.zeros((pad, LANES), jnp.float32)
    parts = 5 if rows % (5 * GROUP) == 0 else 1
    step = rows // parts

    def roll_rows(i, carry):
        at = pl.multiple_of(i * step, GROUP)
        rolled[pl.ds(pad + at, step), :] = pltpu.roll(flat_ref[pl.ds(at, step), :], right, 1)
        return carry

    lax.fori_loop(0, parts, roll_rows, 0)
    lane = lax.broadcasted_iota(jnp.int32, (step, LANES), 1)

    def put_rows(i, carry):
        at = pl.multiple_of(i * step, GROUP)
        upper = rolled[pl.ds(pad + at - down - 1, step), :]
        lower = rolled[pl.ds(pad + at - down, step), :]
        out_ref[pl.ds(at, step), :] = jnp.where(lane < right, upper, lower).astype(jnp.bfloat16)
        return carry

    lax.fori_loop(0, parts, put_rows, 0)


def place_window(flat, gy_size):
    shard = flat.shape[0]
    rows = window_rows(shard)
    padded = jnp.pad(flat, (0, rows * LANES - shard)).reshape(rows, LANES)
    return pl.pallas_call(
        functools.partial(place_kernel, shard, gy_size),
        out_shape=jax.ShapeDtypeStruct((rows, LANES), jnp.bfloat16),
        in_specs=[pl.BlockSpec(memory_space=pltpu.VMEM)],
        out_specs=pl.BlockSpec(memory_space=pltpu.VMEM),
        scratch_shapes=[pltpu.VMEM((rows + 2 * GROUP, LANES), jnp.float32)],
        compiler_params=pltpu.CompilerParams(vmem_limit_bytes=32 << 20),
        name="place_window",
    )(padded)


def lift_kernel(shard, gy_size, window_ref, out_ref, rolled):
    rows = window_ref.shape[0]
    offset = lax.rem(shard * linear_index(gy_size), GROUP * LANES)
    up, left = offset // LANES, lax.rem(offset, LANES)
    pad = 2 * GROUP
    step = rows // CHUNKS
    rolled[rows:, :] = jnp.zeros((pad, LANES), jnp.float32)

    def roll_rows(i, carry):
        at = pl.multiple_of(i * step, GROUP)
        rolled[pl.ds(at, step), :] = pltpu.roll(
            window_ref[pl.ds(at, step), :], lax.rem(LANES - left, LANES), 1
        )
        return carry

    lax.fori_loop(0, CHUNKS, roll_rows, 0)
    lane = lax.broadcasted_iota(jnp.int32, (step, LANES), 1)

    def put_rows(i, carry):
        at = pl.multiple_of(i * step, GROUP)
        first = rolled[pl.ds(at + up, step), :]
        second = rolled[pl.ds(at + up + 1, step), :]
        out_ref[pl.ds(at, step), :] = jnp.where(lane < LANES - left, first, second)
        return carry

    lax.fori_loop(0, CHUNKS, put_rows, 0)


def lift_window(window, shard, gy_size):
    rows = window.shape[0]
    lifted = pl.pallas_call(
        functools.partial(lift_kernel, shard, gy_size),
        out_shape=jax.ShapeDtypeStruct((rows, LANES), jnp.float32),
        in_specs=[pl.BlockSpec(memory_space=pltpu.VMEM)],
        out_specs=pl.BlockSpec(memory_space=pltpu.VMEM),
        scratch_shapes=[pltpu.VMEM((rows + 2 * GROUP, LANES), jnp.float32)],
        compiler_params=pltpu.CompilerParams(vmem_limit_bytes=32 << 20),
        name="lift_window",
    )(window)
    return lifted.reshape(-1)[:shard]


def spread_steps():
    steps = []
    base = 0
    for number, (seg_name, seg_rows, seg_cols) in enumerate(segment_list()[:9]):
        wide = seg_cols // LANES
        take = seg_rows
        while take * wide > 4608:
            take //= 2
        for start in range(0, seg_rows, take):
            steps.append((number, start, take, seg_cols, base + start * wide))
        base += seg_rows * wide
    return steps


def window_pieces(shard, count, stride, first, length):
    pieces, shared = [], []
    for index in range(count):
        low = window_start(shard, index)
        high = window_start(shard, index + 1) if index + 1 < count else low + window_rows(shard)
        start, stop = max(low, first), min(high, first + length)
        if start < stop:
            pieces.append((index * stride + start - low, start - first, stop - start))
        if index + 1 < count and first <= high < first + length:
            shared.append((index * stride + high - low, high - first))
    return pieces, shared


def spread_kernel(shard, count, vec_rows, share, gathered_ref, *refs):
    outs, vec_ref = refs[:9], refs[9]
    landed, edges, wide_rows, ready, in_sem, out_sem = refs[10:]
    rows = gathered_ref.shape[0] // count
    steps = spread_steps()
    steps.append((9, 0, vec_rows, LANES, matrix_rows()))

    def copies_in(number):
        seg, start, take, cols, base = steps[number]
        slot = number % 2
        pieces, shared = window_pieces(shard, count, rows, base, take * cols // LANES)
        found = [
            pltpu.make_async_copy(
                gathered_ref.at[pl.ds(src, size)], landed.at[slot, pl.ds(dst, size)], in_sem.at[slot]
            )
            for src, dst, size in pieces
        ]
        found += [
            pltpu.make_async_copy(
                gathered_ref.at[pl.ds(src, GROUP)], edges.at[slot, order], in_sem.at[slot]
            )
            for order, (src, dst) in enumerate(shared)
        ]
        return found, shared

    def copy_out(number):
        seg, start, take, cols, base = steps[number]
        slot = number % 2
        if seg == 9:
            return pltpu.make_async_copy(wide_rows.at[pl.ds(0, take)], vec_ref, out_sem.at[slot])
        return pltpu.make_async_copy(
            ready[cols].at[slot, pl.ds(0, take)], outs[seg].at[pl.ds(start, take)], out_sem.at[slot]
        )

    for copy in copies_in(0)[0]:
        copy.start()
    for number, (seg, start, take, cols, base) in enumerate(steps):
        if number == 4:
            share.greet()
            share.begin()
        slot = number % 2
        wide = cols // LANES
        total = take * wide
        if number + 1 < len(steps):
            for copy in copies_in(number + 1)[0]:
                copy.start()
        found, shared = copies_in(number)
        for copy in found:
            copy.wait()
        if number >= 2:
            copy_out(number - 2).wait()
        block = 256 if total % 256 == 0 else GROUP

        def widen(i, carry, slot=slot, block=block):
            at = pl.multiple_of(i * block, GROUP)
            wide_rows[pl.ds(at, block), :] = landed[slot, pl.ds(at, block), :].astype(jnp.float32)
            return carry

        lax.fori_loop(0, total // block, widen, 0)
        for order, (src, dst) in enumerate(shared):
            wide_rows[dst : dst + GROUP, :] += edges[slot, order].astype(jnp.float32)
        if seg < 9:

            def tile(i, carry, slot=slot, wide=wide, cols=cols):
                at = pl.multiple_of(i * GROUP, GROUP)
                for j in range(wide):
                    ready[cols][slot, pl.ds(at, GROUP), j * LANES : (j + 1) * LANES] = wide_rows[
                        pl.ds(at * wide + j, GROUP, stride=wide), :
                    ].astype(jnp.bfloat16)
                return carry

            lax.fori_loop(0, take // GROUP, tile, 0)
        copy_out(number).start()
    copy_out(len(steps) - 2).wait()
    copy_out(len(steps) - 1).wait()


def spread_entry(shard, gx_size, gy_size, vec_rows, gathered_ref, rows_ref, *refs):
    outs, landed_rows = refs[:10], refs[10]
    landed, edges, wide_rows, ready_a, ready_b, ready_c, ready_d, in_sem, out_sem = refs[11:20]
    ready = {D_IMG: ready_a, 4 * D_IMG: ready_b, D_TXT: ready_c, 4 * D_TXT: ready_d}
    share = Share(gx_size, gy_size, False, rows_ref, landed_rows, refs[20:])
    spread_kernel(
        shard, gx_size * gy_size, vec_rows, share, gathered_ref, *outs, landed, edges, wide_rows, ready, in_sem, out_sem
    )
    share.middle()
    share.finish()


def spread_weights(gathered, rows_to_send, shard, gx_size, gy_size, number):
    count = gx_size * gy_size
    rows = gathered.shape[0] // count
    steps = spread_steps()
    tallest = {}
    for seg, start, take, cols, base in steps:
        tallest[cols] = max(tallest.get(cols, 0), take)
    most = max(take * cols // LANES for seg, start, take, cols, base in steps)
    vec_rows = -(-(sum(r * c for name, r, c in segment_list()[9:])) // (LANES * GROUP)) * GROUP
    edge_count = max(
        len(window_pieces(shard, count, rows, base, take * cols // LANES)[1])
        for seg, start, take, cols, base in steps
    )
    ready = [
        pltpu.VMEM((2, tallest[cols], cols), jnp.bfloat16)
        for cols in (D_IMG, 4 * D_IMG, D_TXT, 4 * D_TXT)
    ]
    return pl.pallas_call(
        functools.partial(spread_entry, shard, gx_size, gy_size, vec_rows),
        out_shape=[
            jax.ShapeDtypeStruct((seg_rows, seg_cols), jnp.bfloat16)
            for seg_name, seg_rows, seg_cols in segment_list()[:9]
        ]
        + [
            jax.ShapeDtypeStruct((vec_rows, LANES), jnp.float32),
            jax.ShapeDtypeStruct((1,) + rows_to_send.shape, rows_to_send.dtype),
        ],
        in_specs=[pl.BlockSpec(memory_space=pl.ANY), pl.BlockSpec(memory_space=pltpu.VMEM)],
        out_specs=[pl.BlockSpec(memory_space=pl.ANY)] * 10 + [pl.BlockSpec(memory_space=pltpu.VMEM)],
        scratch_shapes=[
            pltpu.VMEM((2, most, LANES), jnp.bfloat16),
            pltpu.VMEM((2, edge_count + 1, GROUP, LANES), jnp.bfloat16),
            pltpu.VMEM((most, LANES), jnp.float32),
        ]
        + ready
        + [pltpu.SemaphoreType.DMA((2,)), pltpu.SemaphoreType.DMA((2,))]
        + share_sems(gx_size, gy_size),
        compiler_params=pltpu.CompilerParams(
            collective_id=number, has_side_effects=True, vmem_limit_bytes=48 << 20
        ),
        name="spread_weights",
    )(gathered, rows_to_send)


def split_vectors(vec_rows):
    image_count, text_count = (IMG_TOK + 9) * D_IMG // LANES, (CTX + 6) * D_TXT // LANES
    image_vec = vec_rows[:image_count].reshape(IMG_TOK + 9, D_IMG)
    text_vec = vec_rows[image_count : image_count + text_count].reshape(CTX + 6, D_TXT)
    return image_vec, text_vec, vec_rows[image_count + text_count, 0]


def grads_kernel(parts, gx_size, gy_size, *refs):
    operand_count = sum(2 * len(pairs) for seg_rows, seg_cols, take, pairs in parts)
    operands = refs[:operand_count]
    vec_ref, token_ref, out_ref, arrived_ref, flat_rows, vec_sem, out_sem = refs[operand_count : operand_count + 7]
    share = Share(gx_size, gy_size, True, token_ref, arrived_ref, refs[operand_count + 7 :])
    share.greet()
    share.begin()
    tail = pltpu.make_async_copy(vec_ref, out_ref.at[pl.ds(matrix_rows(), vec_ref.shape[0])], vec_sem)
    tail.start()
    base = 0
    steps_before = 0
    for number, (seg_rows, seg_cols, take, pairs) in enumerate(parts):
        if number == 2:
            share.middle()
        if number == 6:
            share.rest()
        wide = seg_cols // LANES
        size = take * wide
        count = seg_rows // take

        def step(i, carry, base=base, before=steps_before, size=size, take=take, wide=wide, pairs=pairs):
            slot = lax.rem(i + before, 2)

            def written(number):
                at = pl.multiple_of(base + number * size, 8)
                return pltpu.make_async_copy(
                    flat_rows.at[slot, pl.ds(0, size)], out_ref.at[pl.ds(at, size)], out_sem.at[slot]
                )

            @pl.when(i >= 2)
            def _():
                written(i - 2).wait()

            for left_number, right_number, first in pairs:
                left_ref, right_ref = operands[left_number], operands[right_number]
                at = pl.multiple_of(i * take, LANES)
                product = lax.dot_general(
                    left_ref[:, pl.ds(at, take)],
                    right_ref[...],
                    (((0,), (0,)), ((), ())),
                    preferred_element_type=jnp.float32,
                )
                for j in range(right_ref.shape[1] // LANES):
                    flat_rows[slot, pl.ds(first + j, take, stride=wide), :] = product[
                        :, j * LANES : (j + 1) * LANES
                    ]
            written(i).start()
            return carry

        lax.fori_loop(0, count, step, 0)
        for number in range(max(count - 2, 0), count):
            slot = (number + steps_before) % 2
            at = base + number * size
            pltpu.make_async_copy(
                flat_rows.at[slot, pl.ds(0, size)], out_ref.at[pl.ds(at, size)], out_sem.at[slot]
            ).wait()
        base += seg_rows * wide
        steps_before += count
    tail.wait()
    share.finish()


def weight_grads(pair_lists, vec_rows, token_grads, gx_size, gy_size, number):
    operands, parts = [], []
    for (seg_name, seg_rows, seg_cols), pairs in zip(segment_list()[:9], pair_lists):
        numbered, first = [], 0
        for left_side, right_side in pairs:
            numbered.append((len(operands), len(operands) + 1, first))
            for side in (left_side, right_side):
                side = side.reshape(-1, side.shape[-1])
                operands.append(jnp.pad(side, ((0, -side.shape[0] % GROUP), (0, 0))))
            first += right_side.shape[-1] // LANES
        parts.append((seg_rows, seg_cols, min(seg_rows, 256 if seg_cols <= 768 else 128), numbered))
    total_rows = matrix_rows() + vec_rows.shape[0]
    most = max(take * seg_cols // LANES for seg_rows, seg_cols, take, pairs in parts)
    return pl.pallas_call(
        functools.partial(grads_kernel, parts, gx_size, gy_size),
        out_shape=[
            jax.ShapeDtypeStruct((total_rows, LANES), jnp.float32),
            jax.ShapeDtypeStruct((gx_size,) + token_grads.shape, token_grads.dtype),
        ],
        in_specs=[pl.BlockSpec(memory_space=pltpu.VMEM)] * (len(operands) + 2),
        out_specs=[pl.BlockSpec(memory_space=pl.ANY)] * 2,
        scratch_shapes=[
            pltpu.VMEM((2, most, LANES), jnp.float32),
            pltpu.SemaphoreType.DMA,
            pltpu.SemaphoreType.DMA((2,)),
        ]
        + share_sems(gx_size, gy_size),
        compiler_params=pltpu.CompilerParams(
            collective_id=number, has_side_effects=True, vmem_limit_bytes=56 << 20
        ),
        name="weight_grads",
    )(*operands, vec_rows, token_grads)


class Share:
    def __init__(self, gx_size, gy_size, everyone, send_ref, out_ref, sems):
        gx, self.gy = lax.axis_index("gx"), lax.axis_index("gy")
        self.x_size, self.send_ref, self.out_ref = gx_size // 2, send_ref, out_ref
        self.core, self.x = lax.rem(gx, 2), gx // 2
        (self.own_sem, self.row_send, self.row_recv, self.x_send, self.x_recv, self.core_send, self.core_recv) = sems
        self.rows = [(gx, lax.rem(self.gy + d, gy_size)) for d in range(1, gy_size)]
        self.along_x, self.sibling = [], []
        if everyone:
            self.along_x = [
                (lax.rem(self.x + d, self.x_size) * 2 + self.core, self.gy) for d in range(1, self.x_size)
            ]
            self.sibling = [(self.x * 2 + 1 - self.core, self.gy)]
        self.mine = out_ref.at[gx if everyone else 0]

    def greet(self):
        greet_all(self.rows + self.along_x + self.sibling)

    def own(self):
        return pltpu.make_async_copy(self.send_ref.at[self.gy], self.mine.at[self.gy], self.own_sem)

    def row(self, d):
        other = self.rows[d]
        return remote(self.send_ref.at[other[1]], self.mine.at[self.gy], self.row_send.at[d], self.row_recv.at[d], other)

    def group(self, d):
        return remote(self.mine, self.mine, self.x_send.at[d], self.x_recv.at[d], self.along_x[d])

    def across(self, i, source):
        return remote(source, source, self.core_send.at[i], self.core_recv.at[i], self.sibling[0])

    def begin(self):
        self.own().start()
        for d in range(len(self.rows)):
            self.row(d).start()

    def middle(self):
        self.own().wait()
        for d in range(len(self.rows)):
            self.row(d).wait_recv()
        for d in range(len(self.along_x)):
            self.group(d).start()
        if self.sibling:
            self.across(0, self.mine).start()

    def rest(self):
        for d in range(len(self.along_x)):
            self.group(d).wait_recv()
            sender = lax.rem(self.x + self.x_size - d - 1, self.x_size) * 2 + self.core
            self.across(d + 1, self.out_ref.at[sender]).start()

    def finish(self):
        for d in range(len(self.rows)):
            self.row(d).wait_send()
        for d in range(len(self.along_x)):
            self.group(d).wait_send()
        for i in range(self.x_size if self.sibling else 0):
            self.across(i, self.mine).wait_send()
            self.across(i, self.mine).wait_recv()


def share_sems(gx_size, gy_size):
    dma, x_size = pltpu.SemaphoreType.DMA, gx_size // 2
    return [dma, dma((gy_size - 1,)), dma((gy_size - 1,)), dma((x_size,)), dma((x_size,)), dma((x_size,)), dma((x_size,))]


class Places:
    def __init__(self, sizes):
        self.x_size, self.low_size, self.high_size = sizes
        self.mixed = self.x_size == self.low_size
        self.gy_size = self.high_size * self.low_size
        gx, gy = lax.axis_index("gx"), lax.axis_index("gy")
        self.core, x = lax.rem(gx, 2), gx // 2
        self.h, low = gy // self.low_size, lax.rem(gy, self.low_size)
        self.a, self.b = self.turned(self.core, x, low)
        self.a_size, self.b_size = self.x_size, self.low_size

    def turned(self, side, a, b):
        if not self.mixed:
            return a, b
        return a * (1 - side) + b * side, b * (1 - side) + a * side

    def device(self, side, a, b, h):
        dev_x, dev_low = self.turned(side, a, b)
        return (dev_x * 2 + side, h * self.low_size + dev_low)

    def linear(self, side, a, b, h):
        gx, gy = self.device(side, a, b, h)
        return gx * self.gy_size + gy

    def sibling(self):
        a, b = (self.b, self.a) if self.mixed else (self.a, self.b)
        return self.device(1 - self.core, a, b, self.h)

    def along_a(self):
        return [
            self.device(self.core, lax.rem(self.a + d, self.a_size), self.b, self.h)
            for d in range(1, self.a_size)
        ]

    def along_b(self):
        return [
            self.device(self.core, self.a, lax.rem(self.b + d, self.b_size), self.h)
            for d in range(1, self.b_size)
        ]

    def along_h(self):
        return [
            self.device(self.core, self.a, self.b, lax.rem(self.h + d, self.high_size))
            for d in range(1, self.high_size)
        ]


def greet_all(others):
    barrier = pltpu.get_barrier_semaphore()
    for other in others:
        pl.semaphore_signal(barrier, inc=1, device_id=other, device_id_type=MESH)
    pl.semaphore_wait(barrier, len(others))


def remote(src, dst, send_sem, recv_sem, other):
    return pltpu.make_async_remote_copy(
        src_ref=src, dst_ref=dst, send_sem=send_sem, recv_sem=recv_sem, device_id=other, device_id_type=MESH
    )


def axis_sizes(gx_size, gy_size):
    return gx_size // 2, gy_size // 4, 4


NO_TOKEN = 65535


def route_capacity(tokens, gy_size):
    return GROUP * (1 + 17 * tokens // (16 * gy_size * GROUP))


def table_sum_kernel(cap, counts_ref, index_ref, rows_ref, out_ref, square_ref, wide, row_sem):
    sources = rows_ref.shape[0]
    vocab = out_ref.shape[0] - 8

    def fetch(source):
        slot = lax.rem(source, 2)
        return pltpu.make_async_copy(rows_ref.at[source], wide.at[slot], row_sem.at[slot])

    fetch(0).start()
    block = 32 if vocab % 32 == 0 else 8

    def clear(i, carry):
        out_ref[pl.ds(pl.multiple_of(i * block, 8), block), :] = jnp.zeros((block, D_TXT), jnp.float32)
        return carry

    lax.fori_loop(0, vocab // block, clear, 0)
    out_ref[vocab:, :] = jnp.zeros((8, D_TXT), jnp.float32)

    def one_source(source, carry):
        slot = lax.rem(source, 2)

        @pl.when(source + 1 < sources)
        def _():
            fetch(source + 1).start()

        fetch(source).wait()
        widened = wide.at[slot]

        def add(group, carry):
            rows = widened[pl.ds(pl.multiple_of(group * GROUP, GROUP), GROUP), :].astype(jnp.float32)
            for half in range(0, GROUP, 8):
                places = [
                    pl.ds(index_ref[source * cap + group * GROUP + half + i], 1) for i in range(8)
                ]
                sums = [out_ref[place, :] + rows[half + i : half + i + 1, :] for i, place in enumerate(places)]
                for place, value in zip(places, sums):
                    out_ref[place, :] = value
            return carry

        lax.fori_loop(0, (counts_ref[source] + GROUP - 1) // GROUP, add, 0)
        return carry

    lax.fori_loop(0, sources, one_source, 0)

    def square(i, carry):
        part = out_ref[pl.ds(pl.multiple_of(i * block, 8), block), :]
        part = part * part
        total = carry
        for r in range(0, block, 8):
            total = total + part[r : r + 8]
        return total

    square_ref[...] = lax.fori_loop(0, vocab // block, square, jnp.zeros((8, D_TXT), jnp.float32))


def table_sum(counts, index, rows, vocab):
    sources, cap = rows.shape[0], rows.shape[1]
    return pl.pallas_call(
        functools.partial(table_sum_kernel, cap),
        out_shape=[
            jax.ShapeDtypeStruct((vocab + 8, D_TXT), jnp.float32),
            jax.ShapeDtypeStruct((8, D_TXT), jnp.float32),
        ],
        in_specs=[pl.BlockSpec(memory_space=pltpu.SMEM)] * 2 + [pl.BlockSpec(memory_space=pl.ANY)],
        out_specs=[pl.BlockSpec(memory_space=pltpu.VMEM)] * 2,
        scratch_shapes=[pltpu.VMEM((2, cap, D_TXT), jnp.bfloat16), pltpu.SemaphoreType.DMA((2,))],
        compiler_params=pltpu.CompilerParams(vmem_limit_bytes=40 << 20),
        name="table_sum",
    )(counts, index, rows)


def ranks(flags):
    tokens = flags.shape[-1]
    before = (jnp.arange(tokens)[:, None] < jnp.arange(tokens)[None, :]).astype(jnp.bfloat16)
    return fwd_dot(flags.astype(jnp.bfloat16), before).astype(jnp.int32)


def pick_matrix(slots, count):
    return (jnp.arange(count)[:, None] == slots[None, :]).astype(jnp.bfloat16)


def turned_rows(chunk):
    return TURNED * chunk // (16 * GROUP) * GROUP


def gather_kernel(sizes, chunks, window_ref, out_ref, own_sem, h_send, h_recv, b_send, b_recv, a_send, a_recv, core_send,
                  core_recv):
    at = Places(sizes)
    rows = window_ref.shape[0]
    chunk = rows // chunks
    changed = turned_rows(chunk)
    ways = (False, True) if changed else (False,)
    spans = {False: (0, chunk - changed), True: (chunk - changed, changed)}
    me = at.linear(at.core, at.a, at.b, at.h)
    sibling, peers_a, peers_b, peers_h = at.sibling(), at.along_a(), at.along_b(), at.along_h()
    greet_all([sibling] + peers_a + peers_b + peers_h)
    along_h, along_b = (peers_h, h_send, h_recv), (peers_b, b_send, b_recv)

    def part(block, t, span=(0, chunk)):
        return out_ref.at[pl.ds(pl.multiple_of(block * rows + t * chunk + span[0], GROUP), span[1])]

    def many(count):
        return out_ref.at[pl.ds(0, count)]

    def own_copy(t):
        src = window_ref.at[pl.ds(pl.multiple_of(t * chunk, GROUP), chunk)]
        return pltpu.make_async_copy(src, part(me, t), own_sem.at[t])

    def first(t):
        for turned in ways:
            peers, send, recv = along_b if turned else along_h
            start, size = spans[turned]
            src = window_ref.at[pl.ds(pl.multiple_of(t * chunk + start, GROUP), size)]
            for d, other in enumerate(peers):
                remote(src, part(me, t, spans[turned]), send.at[d], recv.at[int(turned), t, d], other).start()
        own_copy(t).start()

    def second(t):
        own_copy(t).wait()
        for turned in ways:
            size = many(spans[turned][1])
            peers, send, recv = along_b if turned else along_h
            for d, other in enumerate(peers):
                remote(size, size, send.at[d], recv.at[int(turned), t, d], other).wait_recv()
            if turned:
                blocks = [at.linear(at.core, at.a, b, at.h) for b in range(at.b_size)]
            else:
                blocks = [at.linear(at.core, at.a, at.b, h) for h in range(at.high_size)]
            peers, send, recv = along_h if turned else along_b
            for d, other in enumerate(peers):
                for block in blocks:
                    block = part(block, t, spans[turned])
                    remote(block, block, send.at[d], recv.at[int(turned), t, d], other).start()

    def third(t):
        for turned in ways:
            count = at.b_size if turned else at.high_size
            size = many(count * spans[turned][1])
            peers, send, recv = along_h if turned else along_b
            for d, other in enumerate(peers):
                remote(size, size, send.at[d], recv.at[int(turned), t, d], other).wait_recv()
        for d, other in enumerate(peers_a):
            for b in range(at.b_size):
                for h in range(at.high_size):
                    block = part(at.linear(at.core, at.a, b, h), t)
                    remote(block, block, a_send.at[d], a_recv.at[t, d], other).start()

    plane = at.b_size * at.high_size

    def fourth(t):
        size = many(plane * chunk)
        for d, other in enumerate(peers_a):
            remote(size, size, a_send.at[d], a_recv.at[t, d], other).wait_recv()
        for a in range(at.a_size):
            for b in range(at.b_size):
                for h in range(at.high_size):
                    block = part(at.linear(at.core, a, b, h), t)
                    remote(block, block, core_send, core_recv, sibling).start()

    def turn(t, carry):
        for depth, stage in enumerate((first, second, third, fourth)):
            active = (t >= depth) & (t < chunks + depth)
            pl.when(active)(functools.partial(stage, t - depth))
        return carry

    lax.fori_loop(0, chunks + 3, turn, 0)
    straight = chunk - changed
    for peers, send, sent in (
        (peers_h, h_send, straight + changed * at.b_size),
        (peers_b, b_send, straight * at.high_size + changed),
        (peers_a, a_send, chunk * plane),
    ):
        size = many(chunks * sent)
        for d, other in enumerate(peers):
            remote(size, size, send.at[d], core_recv, other).wait_send()
    half = many(at.a_size * plane * rows)
    last = remote(half, half, core_send, core_recv, sibling)
    last.wait_send()
    last.wait_recv()


def gather_windows(window, gx_size, gy_size, chunks, number, name):
    sizes = axis_sizes(gx_size, gy_size)
    a, b, h = sizes[0] - 1, sizes[1] - 1, sizes[2] - 1
    dma = pltpu.SemaphoreType.DMA
    return pl.pallas_call(
        functools.partial(gather_kernel, sizes, chunks),
        out_shape=jax.ShapeDtypeStruct((gx_size * gy_size * window.shape[0], LANES), window.dtype),
        in_specs=[pl.BlockSpec(memory_space=pltpu.VMEM)],
        out_specs=pl.BlockSpec(memory_space=pl.ANY),
        scratch_shapes=[dma((chunks,)), dma((h,)), dma((2, chunks, h)), dma((b,)), dma((2, chunks, b)), dma((a,)),
                        dma((chunks, a)), dma, dma],
        compiler_params=pltpu.CompilerParams(
            collective_id=number, has_side_effects=True, vmem_limit_bytes=32 << 20
        ),
        name=name,
    )(window)


class Way:
    def __init__(self, at, turned, span, refs):
        self.start, self.size = span
        (self.keep_two, self.send_two, self.recv_two, self.keep_three, self.send_three, self.recv_three,
         self.two_send, self.two_recv, self.three_send, self.three_recv) = refs
        along_b, along_h = (at.along_b(), at.b, at.b_size), (at.along_h(), at.h, at.high_size)
        high = at.high_size
        if turned:
            (self.peers, self.place, self.count), (self.last_peers, self.last_place, self.inner) = along_h, along_b
            self.number = lambda other, i: i * high + other
        else:
            (self.peers, self.place, self.count), (self.last_peers, self.last_place, self.inner) = along_b, along_h
            self.number = lambda other, i: other * high + i

    def two(self, u, d):
        slot = lax.rem(u, 2)
        return remote(self.send_two.at[slot, d - 1], self.recv_two.at[u, d - 1], self.two_send.at[slot, d - 1],
                      self.two_recv.at[u, d - 1], self.peers[d - 1])

    def three(self, u, d):
        slot = lax.rem(u, 2)
        return remote(self.send_three.at[slot, d - 1], self.recv_three.at[u, d - 1], self.three_send.at[slot, d - 1],
                      self.three_recv.at[u, d - 1], self.last_peers[d - 1])

    def second(self, u, total):
        slot, rows = lax.rem(u, 2), pl.ds(self.start, self.size)
        for d in range(1, self.count):
            pl.when(u >= 2)(lambda d=d: self.two(u - 2, d).wait_send())
            other = lax.rem(self.place + d, self.count)

            def give(i, carry):
                self.send_two[slot, d - 1, i] = total(self.number(other, i), rows).astype(jnp.bfloat16)
                return carry

            lax.fori_loop(0, self.inner, give, 0)
            self.two(u, d).start()

        def hold(i, carry):
            self.keep_two[slot, i] = total(self.number(self.place, i), rows)
            return carry

        lax.fori_loop(0, self.inner, hold, 0)

    def third(self, u):
        slot = lax.rem(u, 2)
        for d in range(1, self.count):
            self.two(u, d).wait_recv()

        def total(i):
            value = self.keep_two[slot, i]
            for d in range(1, self.count):
                value = value + self.recv_two[u, d - 1, i].astype(jnp.float32)
            return value

        for d in range(1, self.inner):
            pl.when(u >= 2)(lambda d=d: self.three(u - 2, d).wait_send())
            self.send_three[slot, d - 1] = total(lax.rem(self.last_place + d, self.inner)).astype(jnp.bfloat16)
            self.three(u, d).start()
        self.keep_three[slot] = total(self.last_place)

    def last(self, u):
        value = self.keep_three[lax.rem(u, 2)]
        for d in range(1, self.inner):
            self.three(u, d).wait_recv()
            value = value + self.recv_three[u, d - 1].astype(jnp.float32)
        return value

    def drain(self, u):
        for d in range(1, self.count):
            self.two(u, d).wait_send()
        for d in range(1, self.inner):
            self.three(u, d).wait_send()


def way_scratch(chunks, count, inner, size):
    low, dma = jnp.bfloat16, pltpu.SemaphoreType.DMA
    return [
        pltpu.VMEM((2, inner, size, LANES), jnp.float32),
        pltpu.VMEM((2, count - 1, inner, size, LANES), low),
        pltpu.VMEM((chunks, count - 1, inner, size, LANES), low),
        pltpu.VMEM((2, size, LANES), jnp.float32),
        pltpu.VMEM((2, inner - 1, size, LANES), low),
        pltpu.VMEM((chunks, inner - 1, size, LANES), low),
        dma((2, count - 1)),
        dma((chunks, count - 1)),
        dma((2, inner - 1)),
        dma((chunks, inner - 1)),
    ]


def reduce_kernel(shard, sizes, grads_ref, square_ref, out_ref, squares_ref, own, landed, keep_one, send_one, recv_one,
                  partial, square_send, square_recv, load_sem, pair_send, pair_recv, credit, one_send, one_recv, *more):
    at = Places(sizes)
    a_size, b_size, high_size = at.a_size, at.b_size, at.high_size
    core, my_a, my_b, high = at.core, at.a, at.b, at.h
    plane = b_size * high_size
    chunk = own.shape[2]
    chunks = out_ref.shape[0] // chunk

    def start_row(side, number):
        a, rest = number // plane, lax.rem(number, plane)
        return window_start(shard, at.linear(side, a, rest // high_size, lax.rem(rest, high_size)))

    sibling, peers = at.sibling(), at.along_a()
    changed = turned_rows(chunk)
    straight = chunk - changed
    ways = [Way(at, False, (0, straight), more[:10])]
    if changed:
        ways.append(Way(at, True, (straight, changed), more[10:]))
    count = squares_ref.shape[0]
    me = linear_index(at.gy_size)

    def device(step):
        other = lax.rem(me + step, count)
        return (other // at.gy_size, lax.rem(other, at.gy_size))

    barrier = pltpu.get_barrier_semaphore()

    def greet(step, carry):
        pl.semaphore_signal(barrier, inc=1, device_id=device(step), device_id_type=MESH)
        return carry

    lax.fori_loop(1, count, greet, 0)
    pl.semaphore_wait(barrier, count - 1)
    table_part = square_ref[...]
    partial[...] = sum(table_part[:, j * LANES : (j + 1) * LANES] for j in range(D_TXT // LANES))
    spot = (lax.broadcasted_iota(jnp.int32, (chunk, LANES), 0) * LANES
            + lax.broadcasted_iota(jnp.int32, (chunk, LANES), 1))
    blocks = a_size * plane

    def pair_stage(t):
        slot = lax.rem(t, 2)

        @pl.when(t >= 2)
        def _():
            pl.semaphore_wait(credit, 1)

        def each(number, carry):
            theirs = pl.multiple_of(start_row(1 - core, number) + t * chunk, GROUP)
            mine = pl.multiple_of(start_row(core, number) + t * chunk, GROUP)
            remote(
                grads_ref.at[pl.ds(theirs, chunk)], landed.at[slot, number], pair_send.at[slot], pair_recv.at[slot], sibling
            ).start()
            pltpu.make_async_copy(
                grads_ref.at[pl.ds(mine, chunk)], own.at[slot, number], load_sem.at[slot]
            ).start()
            return carry

        lax.fori_loop(0, blocks, each, 0)

    def first_stage(u):
        slot = lax.rem(u, 2)
        both = remote(landed.at[slot], landed.at[slot], pair_send.at[slot], pair_recv.at[slot], sibling)
        pltpu.make_async_copy(own.at[slot], own.at[slot], load_sem.at[slot]).wait()
        both.wait_send()
        both.wait_recv()
        for d in range(1, a_size):
            @pl.when(u >= 2)
            def _():
                remote(send_one.at[slot, d - 1], recv_one.at[u - 2, d - 1], one_send.at[slot, d - 1],
                       one_recv.at[u - 2, d - 1], peers[d - 1]).wait_send()

            first = lax.rem(my_a + d, a_size) * plane

            def give(i, carry):
                send_one[slot, d - 1, i] = (own[slot, first + i] + landed[slot, first + i]).astype(jnp.bfloat16)
                return carry

            lax.fori_loop(0, plane, give, 0)
            remote(send_one.at[slot, d - 1], recv_one.at[u, d - 1], one_send.at[slot, d - 1],
                   one_recv.at[u, d - 1], peers[d - 1]).start()

        def hold(i, carry):
            keep_one[slot, i] = own[slot, my_a * plane + i] + landed[slot, my_a * plane + i]
            return carry

        lax.fori_loop(0, plane, hold, 0)

        @pl.when(u < chunks - 2)
        def _():
            pl.semaphore_signal(credit, inc=1, device_id=sibling, device_id_type=MESH)

    def second_stage(u):
        slot = lax.rem(u, 2)
        for d in range(1, a_size):
            remote(recv_one.at[u, d - 1], recv_one.at[u, d - 1], one_send.at[slot, d - 1], one_recv.at[u, d - 1],
                   peers[d - 1]).wait_recv()

        def total(number, rows):
            value = keep_one[slot, number, rows, :]
            for d in range(1, a_size):
                value = value + recv_one[u, d - 1, number, rows, :].astype(jnp.float32)
            return value

        for way in ways:
            way.second(u, total)

    def third_stage(u):
        for way in ways:
            way.third(u)

    def last_stage(u):
        for way in ways:
            value = way.last(u)
            row = u * chunk + way.start
            out_ref[pl.ds(pl.multiple_of(row, GROUP), way.size), :] = value
            place = spot[: way.size] + (window_start(shard, me) + row) * LANES - me * shard
            square = jnp.where((place >= 0) & (place < shard), value * value, 0.0)
            partial[...] += sum(square[r : r + 8] for r in range(0, way.size, 8))

    def turn(t, carry):
        stages = (pair_stage, first_stage, second_stage, third_stage, last_stage)
        for depth, stage in enumerate(stages):
            @pl.when((t >= depth) & (t < chunks + depth))
            def _():
                stage(t - depth)

        return carry

    lax.fori_loop(0, chunks + 4, turn, 0)
    squares_ref[me] = partial[...]

    def send(step, carry):
        remote(partial, squares_ref.at[me], square_send, square_recv, device(step)).start()
        return carry

    lax.fori_loop(1, count, send, 0)
    others = squares_ref.at[pl.ds(0, count - 1)]
    both = remote(others, others, square_send, square_recv, device(1))
    both.wait_send()
    both.wait_recv()
    for u in range(max(chunks - 2, 0), chunks):
        slot = u % 2
        for d in range(1, a_size):
            remote(send_one.at[slot, d - 1], recv_one.at[u, d - 1], one_send.at[slot, d - 1],
                   one_recv.at[u, d - 1], peers[d - 1]).wait_send()
        for way in ways:
            way.drain(u)


def reduce_windows(grads, square, shard, gx_size, gy_size, number):
    rows = window_rows(shard, GROUP * CHUNKS)
    chunk = rows // CHUNKS
    x_size, low_size, high_size = axis_sizes(gx_size, gy_size)
    plane = low_size * high_size
    blocks = x_size * plane
    low_type, dma = jnp.bfloat16, pltpu.SemaphoreType.DMA
    a = x_size - 1
    return pl.pallas_call(
        functools.partial(reduce_kernel, shard, (x_size, low_size, high_size)),
        out_shape=[
            jax.ShapeDtypeStruct((rows, LANES), jnp.float32),
            jax.ShapeDtypeStruct((gx_size * gy_size, 8, LANES), jnp.float32),
        ],
        in_specs=[pl.BlockSpec(memory_space=pl.ANY), pl.BlockSpec(memory_space=pltpu.VMEM)],
        out_specs=[pl.BlockSpec(memory_space=pltpu.VMEM)] * 2,
        scratch_shapes=[
            pltpu.VMEM((2, blocks, chunk, LANES), jnp.float32),
            pltpu.VMEM((2, blocks, chunk, LANES), jnp.float32),
            pltpu.VMEM((2, plane, chunk, LANES), jnp.float32),
            pltpu.VMEM((2, a, plane, chunk, LANES), low_type),
            pltpu.VMEM((CHUNKS, a, plane, chunk, LANES), low_type),
            pltpu.VMEM((8, LANES), jnp.float32),
            dma,
            dma,
            dma((2,)),
            dma((2,)),
            dma((2,)),
            pltpu.SemaphoreType.REGULAR,
            dma((2, a)),
            dma((CHUNKS, a)),
        ]
        + way_scratch(CHUNKS, low_size, high_size, chunk - turned_rows(chunk))
        + (way_scratch(CHUNKS, high_size, low_size, turned_rows(chunk)) if turned_rows(chunk) else []),
        compiler_params=pltpu.CompilerParams(
            collective_id=number, has_side_effects=True, vmem_limit_bytes=60 << 20
        ),
        name="reduce_windows",
    )(grads, square)


def log_sums(rows, columns, column_ok, logit_scale, matches, positives):
    total, taken = rows.shape[0], min(rows.shape[0], 256)

    def some(args):
        row_part, match_part, positive_part = args
        dots = back_dot(row_part, columns)
        logits = logit_scale * dots
        masked = jnp.where(column_ok[None, :], logits, -1e30)
        row_max = jnp.max(masked, 1, keepdims=True)
        log_total = row_max[:, 0] + jnp.log(jnp.sum(jnp.exp(masked - row_max), 1))
        gap = jnp.where(match_part > 0.0, logits[:, :total] - log_total[:, None], 0.0)
        pulled = jnp.sum(positive_part[:, None] * jnp.exp(masked - log_total[:, None]) * dots)
        return log_total, -jnp.sum(gap), pulled - jnp.sum(match_part * dots[:, :total])

    if taken == total:
        return some((rows, matches, positives))
    logs, parts, pulls = lax.map(
        some,
        (
            rows.reshape(-1, taken, rows.shape[1]),
            matches.reshape(-1, taken, total),
            positives.reshape(-1, taken),
        ),
    )
    return logs.reshape(-1), jnp.sum(parts), jnp.sum(pulls)


def side_grads(row_embed, columns, column_ok, same_own, positives_own, log_own, logit_scale, total_count):
    dot_vals = back_dot(row_embed, columns)
    masked = jnp.where(column_ok[None, :], logit_scale * dot_vals, -1e30)
    extra = columns.shape[0] - same_own.shape[1]
    weights_pos = jnp.concatenate(
        [same_own, jnp.zeros((same_own.shape[0], extra), jnp.float32)], 1
    )
    grad_logits = (
        positives_own[:, None] * jnp.exp(masked - log_own[:, None]) - weights_pos
    ) / total_count
    grad_dots = (logit_scale * grad_logits).astype(jnp.bfloat16)
    return fwd_dot(grad_dots, columns)


def cross_grads(rows, own, valid_own, same_own, positives_all, logs, logit_scale, total_count):
    logits = logit_scale * back_dot(rows, own)
    masked = jnp.where(valid_own[None, :], logits, -1e30)
    grad_logits = (
        positives_all[:, None] * jnp.exp(masked - logs[:, None]) - same_own.T
    ) / total_count
    grad_dots = (logit_scale * grad_logits).astype(jnp.bfloat16)
    return weight_grad(grad_dots, rows)


def body(
    flat_master,
    flat_first,
    flat_second,
    table,
    table_first,
    table_second,
    pixels,
    token_ids,
    end_pos,
    pair_counts,
    groups,
    cached_image,
    cached_text,
):
    gx_size, gy_size = lax.axis_size("gx"), lax.axis_size("gy")
    device_count = gx_size * gy_size
    my_index = linear_index(gy_size)
    pairs_dev = pixels.shape[0]
    shard = flat_master.shape[0]
    tokens = token_ids.size
    vocab_dev = table.shape[0]
    cap = route_capacity(tokens, gy_size)
    own_ids = token_ids.reshape(-1)
    same = own_ids[:, None] == own_ids[None, :]
    order = jnp.arange(tokens)
    leading = ~jnp.any(same & (order[None, :] < order[:, None]), 1)
    flat_ids = jnp.where(leading, own_ids, NO_TOKEN)
    flat_ids = jnp.pad(flat_ids, (0, ID_ROWS * LANES // 2 - tokens)).reshape(-1, LANES)
    payload = [
        place_window(flat_master, gy_size),
        jnp.concatenate([cached_image, cached_text], 0).reshape(CACHED_ROWS, LANES),
        jnp.concatenate([flat_ids // 256, flat_ids % 256], 0).astype(jnp.bfloat16),
    ]
    used = sum(part.shape[0] for part in payload)
    step = GROUP * GATHER_CHUNKS
    payload = jnp.pad(jnp.concatenate(payload, 0), ((0, -used % step), (0, 0)))
    gathered = gather_windows(payload, gx_size, gy_size, GATHER_CHUNKS, 4, "gather_weights")
    every_part = gathered.reshape(device_count, -1, LANES)
    cached = every_part[:, used - ID_ROWS - CACHED_ROWS : used - ID_ROWS].reshape(device_count, -1, EMBED)
    cache_img, cache_txt = lax.optimization_barrier((cached[:, :pairs_dev], cached[:, pairs_dev:]))
    cache_img, cache_txt = cache_img.reshape(-1, EMBED), cache_txt.reshape(-1, EMBED)
    coded = every_part[:, used - ID_ROWS : used].astype(jnp.int32)
    ids_all = coded[:, : ID_ROWS // 2] * 256 + coded[:, ID_ROWS // 2 :]
    ids_all = ids_all.reshape(device_count, -1)[:, :tokens]
    holders = ids_all // vocab_dev
    pair_rows = jnp.sum(holders[:, :, None] == jnp.arange(gy_size), 1)
    rounds = (jnp.max(pair_rows) + cap - 1) // cap
    me_y = lax.axis_index("gy")
    held = holders == me_y
    held_rank = jnp.where(held, ranks(held), -1)
    held_row = ids_all - me_y * vocab_dev
    held_count = jnp.sum(held, 1)
    own_flags = (jnp.arange(gy_size)[:, None] == own_ids[None, :] // vocab_dev) & leading[None, :]
    own_place = jnp.arange(gy_size)[:, None] * tokens + ranks(own_flags)
    own_place = jnp.sum(jnp.where(own_flags, own_place, 0), 0)
    own_place = jnp.sum(jnp.where(same & leading[None, :], own_place[None, :], 0), 1)
    own_holder, own_rank = own_place // tokens, own_place % tokens

    def held_rows(turn):
        slots = held_rank - turn * cap
        found = slots[:, None, :] == jnp.arange(cap)[None, :, None]
        return vocab_dev + jnp.sum(jnp.where(found, held_row[:, None, :] - vocab_dev, 0), 2)

    def own_slots(turn):
        rank = own_rank - turn * cap
        return jnp.where((rank >= 0) & (rank < cap), own_holder * cap + rank, -1)

    first_rows = held_rows(0)
    group_start = lax.axis_index("gx") * gy_size

    def rows_to_send(index):
        index = lax.dynamic_slice_in_dim(index, group_start, gy_size, 0)
        rows = jnp.take(table, index.reshape(-1), axis=0, mode="clip")
        return rows.reshape(gy_size, cap, D_TXT)

    sent = rows_to_send(first_rows).astype(jnp.bfloat16)
    slot_count = gy_size * cap

    def more_rows(turn, found):
        rows = lax.all_to_all(rows_to_send(held_rows(turn)), "gy", 0, 0, tiled=True)
        rows = rows.reshape(slot_count, D_TXT).astype(jnp.bfloat16)
        return found + weight_grad(pick_matrix(own_slots(turn), slot_count), rows).astype(jnp.bfloat16)

    nothing = jnp.zeros((tokens, D_TXT), jnp.bfloat16)
    extra_rows = lax.cond(
        rounds > 1, lambda rows: lax.fori_loop(1, rounds, more_rows, rows), lambda rows: rows, nothing
    )
    sent, extra_rows = lax.optimization_barrier((sent, extra_rows))
    *spread, landed = spread_weights(gathered, sent, shard, gx_size, gy_size, 5)
    picks = pick_matrix(own_slots(0), slot_count)
    token_rows = weight_grad(picks, landed.reshape(slot_count, D_TXT)).astype(jnp.bfloat16)

    token_rows = token_rows + extra_rows
    image_weights = dict(zip(IMAGE.names, spread[:5]))
    text_weights = dict(zip(TEXT.names, spread[5:9]))
    image_vec, text_vec, temper = split_vectors(spread[9])
    image_gains, image_base, image_rows = image_inputs(image_vec, pixels)
    text_gains, text_base, text_rows = text_inputs(text_vec, token_rows)
    image_kept = tower_forward(IMAGE, end_pos, image_gains, image_base, image_rows, image_weights)
    text_kept = tower_forward(TEXT, end_pos, text_gains, text_base, text_rows, text_weights)
    image_emb = image_kept[14].astype(jnp.bfloat16)
    text_emb = text_kept[14].astype(jnp.bfloat16)
    embeds = jnp.concatenate([image_emb, text_emb], 0).reshape(-1, LANES)
    embeds = gather_windows(embeds, gx_size, gy_size, 1, 0, "embeddings")
    embeds = embeds.reshape(device_count, 2 * pairs_dev, EMBED)
    all_img, all_txt = lax.optimization_barrier((embeds[:, :pairs_dev], embeds[:, pairs_dev:]))
    all_img, all_txt = all_img.reshape(-1, EMBED), all_txt.reshape(-1, EMBED)
    total_pairs = all_img.shape[0]
    valid_all = jnp.arange(total_pairs) % pairs_dev < jnp.repeat(pair_counts.reshape(-1), pairs_dev)
    matches = (
        (groups[:, None] == groups[None, :]) & valid_all[:, None] & valid_all[None, :]
    ).astype(jnp.float32)
    positives_all = jnp.sum(matches, 1)
    total_count = 2.0 * jnp.sum(positives_all)
    own_start = my_index * pairs_dev
    own_part = functools.partial(
        lax.dynamic_slice_in_dim, start_index=own_start, slice_size=pairs_dev, axis=0
    )
    same_own, positives_own, valid_own = own_part(matches), own_part(positives_all), own_part(valid_all)
    logit_scale = jnp.exp(temper)
    column_ok = jnp.concatenate([valid_all, jnp.ones((cache_img.shape[0],), jnp.bool_)])
    columns_txt = jnp.concatenate([all_txt, cache_txt])
    columns_img = jnp.concatenate([all_img, cache_img])
    log_img, loss_one, pull_one = log_sums(
        all_img, columns_txt, column_ok, logit_scale, matches, positives_all
    )
    log_txt, loss_two, pull_two = log_sums(
        all_txt, columns_img, column_ok, logit_scale, matches, positives_all
    )
    grad_temper = logit_scale * (pull_one + pull_two) / total_count
    loss_sum = loss_one + loss_two
    grad_img = side_grads(
        image_emb, columns_txt, column_ok, same_own, positives_own, own_part(log_img), logit_scale, total_count
    )
    grad_txt = side_grads(
        text_emb, columns_img, column_ok, same_own, positives_own, own_part(log_txt), logit_scale, total_count
    )
    grad_img = grad_img + cross_grads(
        all_txt, image_emb, valid_own, same_own, positives_all, log_txt, logit_scale, total_count
    )
    grad_txt = grad_txt + cross_grads(
        all_img, text_emb, valid_own, same_own, positives_all, log_img, logit_scale, total_count
    )
    text_grads = tower_backward(TEXT, end_pos, text_gains, grad_txt, text_kept[:14], text_weights)
    grad_rows = text_grads[6][: SEQS * CTX]
    to_holders = fwd_dot(picks, grad_rows).astype(jnp.bfloat16).reshape(gy_size, cap, D_TXT)
    image_grads = tower_backward(IMAGE, end_pos, image_gains, grad_img, image_kept[:14], image_weights)
    pair_lists = ([(image_rows, image_grads[6])],) + grad_pairs(image_kept, image_grads)
    pair_lists = pair_lists + grad_pairs(text_kept, text_grads)
    total_rows = window_start(shard, device_count - 1) + window_rows(shard, GROUP * CHUNKS)
    vec_rows = jnp.concatenate(
        [
            image_grads[7][:1].reshape(-1, LANES),
            image_grads[7].reshape(-1, LANES),
            image_grads[8].reshape(-1, LANES),
            text_grads[7].reshape(-1, LANES),
            text_grads[8][2:].reshape(-1, LANES),
        ]
    )
    vec_rows = jnp.pad(vec_rows, ((0, total_rows - matrix_rows() - vec_rows.shape[0]), (0, 0)))
    local_grads, arrived = weight_grads(pair_lists, vec_rows, to_holders, gx_size, gy_size, 6)
    table_grad, table_square = table_sum(
        jnp.minimum(held_count, cap),
        first_rows.reshape(-1),
        arrived.reshape(device_count, cap, D_TXT),
        vocab_dev,
    )

    def more_grads(turn, total):
        rows = fwd_dot(pick_matrix(own_slots(turn), slot_count), grad_rows).astype(jnp.bfloat16)
        rows = lax.all_to_all(rows.reshape(gy_size, cap, D_TXT), "gy", 0, 0, tiled=True)
        rows = lax.all_gather(rows, "gx", axis=0).reshape(device_count * cap, D_TXT).astype(jnp.float32)
        return total.at[held_rows(turn).reshape(-1)].add(rows)

    def whole_squares(total):
        return jnp.sum((total[:vocab_dev] * total[:vocab_dev]).reshape(-1, 8, D_TXT), 0)

    def more_turns(total, square):
        total = lax.fori_loop(1, rounds, more_grads, total)
        return total, whole_squares(total)

    table_grad, table_square = lax.cond(
        rounds > 1, more_turns, lambda total, square: (total, square), table_grad, table_square
    )
    table_square = jnp.where(lax.axis_index("gx") == 0, table_square, 0.0)
    grad_window, every = reduce_windows(local_grads, table_square, shard, gx_size, gy_size, 1)
    position = my_index * shard + jnp.arange(shard)
    grad_shard = lift_window(grad_window, shard, gy_size)
    grad_shard = jnp.where(position == parameter_count() - 1, grad_temper, grad_shard)
    total_square = jnp.sum(every) + grad_temper * grad_temper
    grad_norm = jnp.sqrt(total_square)
    factor = jnp.minimum(1.0, clip_limit / (grad_norm + 1e-06))
    matrix_stop = matrix_rows() * LANES
    is_matrix = position < matrix_stop
    rates = jnp.where(is_matrix, rate_matrix, rate_vector)
    decays = jnp.where(is_matrix, decay_rate, 0.0)
    master_out, first_out, second_out = adam_step(
        flat_master, flat_first, flat_second, grad_shard * factor, rates, decays
    )
    table_out, table_first_out, table_second_out = adam_step(
        table, table_first, table_second, table_grad[:vocab_dev] * factor, rate_table, 0.0
    )
    return (
        master_out,
        first_out,
        second_out,
        table_out,
        table_first_out,
        table_second_out,
        loss_sum,
        total_count,
        grad_norm,
    )


def solution(mesh):
    placed = (
        P(("gx", "gy")),
        P(("gx", "gy")),
        P(("gx", "gy")),
        P("gy", None),
        P("gy", None),
        P("gy", None),
        P(("gx", "gy"), None, None),
        P(("gx", "gy"), None),
        P(("gx", "gy")),
        P(),
        P(),
        P(("gx", "gy"), None),
        P(("gx", "gy"), None),
    )
    return jax.shard_map(
        body,
        mesh=mesh,
        in_specs=placed,
        out_specs=(
            P(("gx", "gy")),
            P(("gx", "gy")),
            P(("gx", "gy")),
            P("gy", None),
            P("gy", None),
            P("gy", None),
            P(),
            P(),
            P(),
        ),
        check_vma=False,
    )
```

```python
import functools

import jax
import jax.numpy as jnp
from jax import lax
from jax.experimental import pallas as pl
from jax.experimental.pallas import tpu as pltpu
from jax.sharding import PartitionSpec as P

D_IMG = 768
IMG_HEADS = 12
IMG_MLP = 3072
PATCH_DIM = 3072
D_TXT = 512
TXT_HEADS = 8
TXT_MLP = 2048
CTX = 77
EMBED = 512
STEP = 10
IMG_TOK = 50


clip_limit = 0.1
beta_one = 0.9
beta_two = 0.999
adam_eps = 1e-08
decay_rate = 0.1
rate_matrix = 0.01
rate_vector = 0.2
rate_table = 0.2
norm_eps = 1e-05


def segment_list():
    return [
        ("patch_embed", PATCH_DIM, D_IMG),
        ("image_attn", D_IMG, 4 * D_IMG),
        ("image_up", D_IMG, IMG_MLP),
        ("image_down", IMG_MLP, D_IMG),
        ("image_proj", D_IMG, EMBED),
        ("text_attn", D_TXT, 4 * D_TXT),
        ("text_up", D_TXT, TXT_MLP),
        ("text_down", TXT_MLP, D_TXT),
        ("text_proj", D_TXT, EMBED),
        ("image_vec", IMG_TOK + 9, D_IMG),
        ("text_vec", CTX + 6, D_TXT),
        ("temper", 1, 1),
    ]


LANES = 128
GROUP = 16
CHUNKS = 16
GATHER_CHUNKS = 21
TURNED = 6
CACHED_ROWS = 64
ID_ROWS = 16
MESH = pl.DeviceIdType.MESH


def dot_nn(left_side, right_side):
    return lax.dot_general(
        left_side, right_side, (((1,), (0,)), ((), ())), preferred_element_type=jnp.float32
    )


def dot_nt(left_side, right_side):
    return lax.dot_general(
        left_side, right_side, (((1,), (1,)), ((), ())), preferred_element_type=jnp.float32
    )


def dot_tn(left_side, right_side):
    return lax.dot_general(
        left_side, right_side, (((0,), (0,)), ((), ())), preferred_element_type=jnp.float32
    )


def back_dot(left_side, right_side):
    return dot_nt(left_side, right_side)


def fwd_dot(left_side, right_side):
    return dot_nn(left_side, right_side)


def weight_grad(left_side, right_side):
    return dot_tn(left_side, right_side)


def norm_parts(values):
    center = values - jnp.mean(values, -1, keepdims=True)
    scale = lax.rsqrt(jnp.mean(center * center, -1, keepdims=True) + norm_eps)
    return center * scale, scale


def layer_norm(values, gain_vec, shift_vec):
    return norm_parts(values)[0] * gain_vec + shift_vec


def layer_norm_back(values, gain_vec, grad):
    unit, scale = norm_parts(values)
    grad_unit = grad * gain_vec
    inner = jnp.mean(grad_unit, -1, keepdims=True)
    along = jnp.mean(grad_unit * unit, -1, keepdims=True)
    return scale * (grad_unit - inner - unit * along), grad * unit


def sum_rows(values):
    return jnp.sum(values, 0, keepdims=True)


def low16(values):
    return jnp.concatenate([values, jnp.zeros_like(values)], 0).astype(jnp.bfloat16)


SEQS = 8


class Tower:
    def __init__(self, image):
        self.image = image
        self.width = D_IMG if image else D_TXT
        self.heads = IMG_HEADS if image else TXT_HEADS
        self.length = IMG_TOK if image else CTX
        self.rows = -(-SEQS * self.length // GROUP) * GROUP
        self.lanes = 16 if image else 8
        self.queries = SEQS * self.lanes
        self.block = 80 if image else 48
        self.names = ("patch", "attn", "up", "down", "proj") if image else ("attn", "up", "down", "proj")

    def shapes(self):
        width = self.width
        found = dict(attn=(width, 4 * width), up=(width, 4 * width), down=(4 * width, width), proj=(width, EMBED))
        if self.image:
            found["patch"] = (PATCH_DIM, width)
        return found

    def head_mask(self):
        lane = lax.broadcasted_iota(jnp.int32, (self.lanes, self.width), 1)
        row = lax.broadcasted_iota(jnp.int32, (self.lanes, self.width), 0)
        return lane // (self.width // self.heads) == row

    def spread_heads(self, values, wide_ref):
        mask = self.head_mask()
        for s in range(SEQS):
            row = jnp.broadcast_to(values[s : s + 1].astype(jnp.float32), mask.shape)
            wide_ref[s * self.lanes : (s + 1) * self.lanes, :] = jnp.where(mask, row, 0.0)
        return wide_ref[...].astype(jnp.bfloat16)

    def join_heads(self, values, wide_ref):
        mask = self.head_mask()
        wide_ref[...] = values
        rows = [
            sum_rows(jnp.where(mask, wide_ref[s * self.lanes : (s + 1) * self.lanes, :], 0.0))
            for s in range(SEQS)
        ]
        return jnp.concatenate(rows, 0)

    def row_of(self, s, ends_ref):
        return s if self.image else s * self.length + ends_ref[s]

    def each_block(self, function, start):
        return lax.fori_loop(
            0,
            self.rows // self.block,
            lambda i, carry: function(pl.ds(pl.multiple_of(i * self.block, GROUP), self.block), carry),
            start,
        )


def tower_fetch(names, sources, landed, sems):
    copies = {
        name: pltpu.make_async_copy(source, ref, sems.at[i])
        for i, (name, source, ref) in enumerate(zip(names, sources, landed))
    }
    for copy in copies.values():
        copy.start()
    return copies, dict(zip(names, landed))


def tower_forward_kernel(tower, *refs):
    count = len(tower.names)
    ends_ref, gains_ref, base_ref, input_ref = refs[:4]
    sources = refs[4 : 4 + count]
    (tokens_ref, normed_ref, pair_ref, normed_own_ref, query_ref, probs_ref, attended_ref, middle_ref, normed_two_ref,
     upper_ref, act_ref, output_ref, head_ref, raw_ref, emb_ref) = refs[4 + count : 19 + count]
    hidden_ref, wide_ref = refs[19 + count : 21 + count]
    landed, sems = refs[21 + count : 21 + 2 * count], refs[21 + 2 * count]
    copies, weights = tower_fetch(tower.names, sources, landed, sems)
    width = tower.width
    gains = [gains_ref[i : i + 1, :] for i in range(8)]
    if tower.image:
        copies["patch"].wait()

        def patch(j, carry):
            cols = pl.ds(pl.multiple_of(j * 256, 256), 256)
            tokens_ref[:, cols] = dot_nn(input_ref[...], weights["patch"][:, cols]) + base_ref[:, cols]
            return carry

        lax.fori_loop(0, width // 256, patch, 0)

    def first(rows, carry):
        if tower.image:
            hidden = layer_norm(tokens_ref[rows, :], gains[0], gains[1])
        else:
            hidden = input_ref[rows, :].astype(jnp.float32) + base_ref[rows, :]
            tokens_ref[rows, :] = hidden
        hidden_ref[rows, :] = hidden
        normed_ref[rows, :] = layer_norm(hidden, gains[2], gains[3]).astype(jnp.bfloat16)
        return carry

    tower.each_block(first, 0)
    copies["attn"].wait()

    def pair(j, carry):
        at = pl.multiple_of(j * 256, 256)
        product = dot_nn(normed_ref[...], weights["attn"][:, pl.ds(width + at, 256)])
        pair_ref[:, pl.ds(at, 256)] = product.astype(jnp.bfloat16)
        return carry

    lax.fori_loop(0, 2 * width // 256, pair, 0)
    hidden_own = jnp.concatenate(
        [hidden_ref[pl.ds(tower.row_of(s, ends_ref), 1), :] for s in range(SEQS)], 0
    )
    normed_own = low16(layer_norm(hidden_own, gains[2], gains[3]))
    normed_own_ref[...] = normed_own
    query = dot_nn(normed_own, weights["attn"][:, :width]).astype(jnp.bfloat16)
    query_ref[...] = query
    queries = tower.spread_heads(query, wide_ref)
    scores = dot_nt(queries, pair_ref[:, :width]) * (width // tower.heads) ** (-0.5)
    row = lax.broadcasted_iota(jnp.int32, scores.shape, 0) // tower.lanes
    spot = lax.broadcasted_iota(jnp.int32, scores.shape, 1)
    if tower.image:
        allowed = lax.rem(spot, SEQS) == row
    else:
        spot = spot - row * tower.length
        last = jnp.zeros(scores.shape, jnp.int32)
        for s in range(SEQS):
            last = jnp.where(row == s, ends_ref[s], last)
        allowed = (spot >= 0) & (spot <= last)
    scores = jnp.where(allowed, scores, -1e30)
    powers = jnp.exp(scores - jnp.max(scores, -1, keepdims=True))
    probs = powers / jnp.sum(powers, -1, keepdims=True)
    probs_ref[...] = probs
    attended = low16(tower.join_heads(dot_nn(probs.astype(jnp.bfloat16), pair_ref[:, width:]), wide_ref))
    attended_ref[...] = attended
    middle = hidden_own + dot_nn(attended, weights["attn"][:, 3 * width :])[:SEQS]
    middle_ref[...] = middle
    normed_two_ref[...] = low16(layer_norm(middle, gains[4], gains[5]))
    copies["up"].wait()

    def rise(j, carry):
        cols = pl.ds(pl.multiple_of(j * 512, 512), 512)
        upper = dot_nn(normed_two_ref[...], weights["up"][:, cols])[:SEQS]
        upper_ref[:, cols] = upper
        act_ref[:, cols] = low16(upper * jax.nn.sigmoid(1.702 * upper))
        return carry

    lax.fori_loop(0, 4 * width // 512, rise, 0)
    copies["down"].wait()

    def fall(j, carry):
        cols = pl.ds(pl.multiple_of(j * 256, 256), 256)
        output_ref[:, cols] = middle_ref[:, cols] + dot_nn(act_ref[...], weights["down"][:, cols])[:SEQS]
        return carry

    lax.fori_loop(0, width // 256, fall, 0)
    head_in = low16(layer_norm(output_ref[...], gains[6], gains[7]))
    head_ref[...] = head_in
    copies["proj"].wait()
    raw = dot_nn(head_in, weights["proj"][...])[:SEQS]
    raw_ref[...] = raw
    emb_ref[...] = raw * lax.rsqrt(jnp.sum(raw * raw, -1, keepdims=True) + 1e-06)


def tower_forward(tower, ends, gains, base, inputs, weights):
    width, rows = tower.width, tower.rows
    low, full = jnp.bfloat16, jnp.float32
    outs = [
        ((rows, width), full),
        ((rows, width), low),
        ((rows, 2 * width), low),
        ((GROUP, width), low),
        ((GROUP, width), low),
        ((tower.queries, rows), full),
        ((GROUP, width), low),
        ((SEQS, width), full),
        ((GROUP, width), low),
        ((SEQS, 4 * width), full),
        ((GROUP, 4 * width), low),
        ((SEQS, width), full),
        ((GROUP, width), low),
        ((SEQS, EMBED), full),
        ((SEQS, EMBED), full),
    ]
    vmem = pl.BlockSpec(memory_space=pltpu.VMEM)
    shapes = tower.shapes()
    return pl.pallas_call(
        functools.partial(tower_forward_kernel, tower),
        out_shape=[jax.ShapeDtypeStruct(shape, kind) for shape, kind in outs],
        in_specs=[pl.BlockSpec(memory_space=pltpu.SMEM)]
        + [vmem] * 3
        + [pl.BlockSpec(memory_space=pl.ANY)] * len(tower.names),
        out_specs=[vmem] * len(outs),
        scratch_shapes=[pltpu.VMEM((rows, width), full), pltpu.VMEM((tower.queries, width), full)]
        + [pltpu.VMEM(shapes[name], low) for name in tower.names]
        + [pltpu.SemaphoreType.DMA((len(tower.names),))],
        compiler_params=pltpu.CompilerParams(vmem_limit_bytes=58 << 20),
        name="image_forward" if tower.image else "text_forward",
    )(ends, gains, base, inputs, *[weights[name] for name in tower.names])


def tower_backward_kernel(tower, *refs):
    names = tower.names[-4:]
    count = len(names)
    ends_ref, gains_ref, grad_ref = refs[:3]
    (tokens_ref, normed_ref, pair_ref, normed_own_ref, query_ref, probs_ref, attended_ref, middle_ref, normed_two_ref,
     upper_ref, act_ref, output_ref, head_ref, raw_ref) = refs[3:17]
    sources = refs[17 : 17 + count]
    (grad_raw_ref, grad_mlp_ref, grad_upper_ref, grad_att_ref, grad_query_ref, grad_pair_ref, grad_rows_ref,
     places_ref, gain_grads_ref) = refs[17 + count : 26 + count]
    grad_ref_wide, wide_ref, grad_middle_ref = refs[26 + count : 29 + count]
    landed, sems = refs[29 + count : 29 + 2 * count], refs[29 + 2 * count]
    copies, weights = tower_fetch(names, sources, landed, sems)
    width, rows = tower.width, tower.rows
    scale = (width // tower.heads) ** (-0.5)
    gains = [gains_ref[i : i + 1, :] for i in range(8)]
    raw, grad_emb = raw_ref[...], grad_ref[...]
    norm = lax.rsqrt(jnp.sum(raw * raw, -1, keepdims=True) + 1e-06)
    along = jnp.sum(raw * grad_emb, -1, keepdims=True)
    grad_raw = low16(grad_emb * norm - raw * (norm * norm * norm * along))
    grad_raw_ref[...] = grad_raw
    copies["proj"].wait()
    grad_head = dot_nt(grad_raw, weights["proj"][...])[:SEQS]
    grad_out, gain_part = layer_norm_back(output_ref[...], gains[6], grad_head)
    gain_grads_ref[6:7, :] = sum_rows(gain_part)
    gain_grads_ref[7:8, :] = sum_rows(grad_head)
    grad_mlp_ref[...] = low16(grad_out)
    copies["down"].wait()

    def rise(j, carry):
        cols = pl.ds(pl.multiple_of(j * 512, 512), 512)
        grad_act = dot_nt(grad_mlp_ref[...], weights["down"][cols, :])[:SEQS]
        upper = upper_ref[:, cols]
        sig = jax.nn.sigmoid(1.702 * upper)
        grad_upper_ref[:, cols] = low16(grad_act * (sig + upper * (1.702 * (sig * (1.0 - sig)))))
        return carry

    lax.fori_loop(0, 4 * width // 512, rise, 0)
    copies["up"].wait()

    def fall(j, carry):
        cols = pl.ds(pl.multiple_of(j * 256, 256), 256)
        grad_middle_ref[:, cols] = dot_nt(grad_upper_ref[...], weights["up"][cols, :])[:SEQS]
        return carry

    lax.fori_loop(0, width // 256, fall, 0)
    grad_norm_two = grad_middle_ref[...]
    grad_mid, gain_part = layer_norm_back(middle_ref[...], gains[4], grad_norm_two)
    gain_grads_ref[4:5, :] = sum_rows(gain_part)
    gain_grads_ref[5:6, :] = sum_rows(grad_norm_two)
    grad_middle = grad_out + grad_mid
    grad_middle_ref[...] = grad_middle
    grad_att = low16(grad_middle)
    grad_att_ref[...] = grad_att
    copies["attn"].wait()
    grad_attended = dot_nt(grad_att, weights["attn"][:, 3 * width :]).astype(jnp.bfloat16)
    grads_heads = tower.spread_heads(grad_attended, wide_ref)
    queries = tower.spread_heads(query_ref[...], wide_ref)
    probs = probs_ref[...]
    grad_probs = dot_nt(grads_heads, pair_ref[:, width:])
    grad_scores = probs * (grad_probs - jnp.sum(grad_probs * probs, -1, keepdims=True))
    grad_scores = grad_scores.astype(jnp.bfloat16)
    grad_query = low16(tower.join_heads(dot_nn(grad_scores, pair_ref[:, :width]), wide_ref) * scale)
    grad_query_ref[...] = grad_query
    grad_pair_ref[:, :width] = (dot_tn(grad_scores, queries) * scale).astype(jnp.bfloat16)
    grad_pair_ref[:, width:] = dot_tn(probs.astype(jnp.bfloat16), grads_heads).astype(jnp.bfloat16)

    def inner(j, carry):
        at = pl.multiple_of(j * 256, 256)
        grad_ref_wide[:, pl.ds(at, 256)] = dot_nt(
            grad_pair_ref[...], weights["attn"][pl.ds(at, 256), width : 3 * width]
        )
        return carry

    lax.fori_loop(0, width // 256, inner, 0)
    grad_own = dot_nt(grad_query, weights["attn"][:, :width])
    for s in range(SEQS):
        grad_ref_wide[pl.ds(tower.row_of(s, ends_ref), 1), :] += grad_own[s : s + 1]

    def first(at, carry):
        grad = grad_ref_wide[at, :]
        hidden = tokens_ref[at, :]
        if tower.image:
            hidden = layer_norm(hidden, gains[0], gains[1])
        grad_in, gain_part = layer_norm_back(hidden, gains[2], grad)
        grad_ref_wide[at, :] = grad_in
        return carry[0] + sum_rows(gain_part), carry[1] + sum_rows(grad)

    nothing = jnp.zeros((1, width), jnp.float32)
    gain_one, shift_one = tower.each_block(first, (nothing, nothing))
    gain_grads_ref[2:3, :] = gain_one
    gain_grads_ref[3:4, :] = shift_one
    for s in range(SEQS):
        grad_ref_wide[pl.ds(tower.row_of(s, ends_ref), 1), :] += grad_middle_ref[s : s + 1, :]

    def second(at, carry):
        grad = grad_ref_wide[at, :]
        if not tower.image:
            grad_rows_ref[at, :] = grad.astype(jnp.bfloat16)
            return carry
        grad_in, gain_part = layer_norm_back(tokens_ref[at, :], gains[0], grad)
        grad_ref_wide[at, :] = grad_in
        grad_rows_ref[at, :] = grad_in.astype(jnp.bfloat16)
        return carry[0] + sum_rows(gain_part), carry[1] + sum_rows(grad)

    gain_pre, shift_pre = tower.each_block(second, (nothing, nothing))
    gain_grads_ref[0:1, :] = gain_pre
    gain_grads_ref[1:2, :] = shift_pre
    if tower.image:
        for p in range(tower.length):
            places_ref[p : p + 1, :] = sum_rows(grad_ref_wide[p * SEQS : (p + 1) * SEQS, :])
        return
    places = grad_ref_wide[0 : tower.length, :]
    for s in range(1, SEQS):
        places = places + grad_ref_wide[s * tower.length : (s + 1) * tower.length, :]
    places_ref[...] = places


def tower_backward(tower, ends, gains, grad_emb, kept, weights):
    width, rows = tower.width, tower.rows
    low, full = jnp.bfloat16, jnp.float32
    outs = [
        ((GROUP, EMBED), low),
        ((GROUP, width), low),
        ((GROUP, 4 * width), low),
        ((GROUP, width), low),
        ((GROUP, width), low),
        ((rows, 2 * width), low),
        ((rows, width), low),
        ((tower.length, width), full),
        ((8, width), full),
    ]
    vmem = pl.BlockSpec(memory_space=pltpu.VMEM)
    shapes, names = tower.shapes(), tower.names[-4:]
    return pl.pallas_call(
        functools.partial(tower_backward_kernel, tower),
        out_shape=[jax.ShapeDtypeStruct(shape, kind) for shape, kind in outs],
        in_specs=[pl.BlockSpec(memory_space=pltpu.SMEM)]
        + [vmem] * (2 + len(kept))
        + [pl.BlockSpec(memory_space=pl.ANY)] * len(names),
        out_specs=[vmem] * len(outs),
        scratch_shapes=[
            pltpu.VMEM((rows, width), full),
            pltpu.VMEM((tower.queries, width), full),
            pltpu.VMEM((SEQS, width), full),
        ]
        + [pltpu.VMEM(shapes[name], low) for name in names]
        + [pltpu.SemaphoreType.DMA((len(names),))],
        compiler_params=pltpu.CompilerParams(vmem_limit_bytes=58 << 20),
        name="image_backward" if tower.image else "text_backward",
    )(ends, gains, grad_emb, *kept, *[weights[name] for name in names])


def grad_pairs(kept, grads):
    (normed, normed_own, attended, normed_two, act_low, head_in) = (
        kept[1], kept[3], kept[6], kept[8], kept[10], kept[12]
    )
    grad_raw, grad_mlp, grad_upper, grad_att, grad_query, grad_pair = grads[:6]
    return (
        [(normed_own, grad_query), (normed, grad_pair), (attended, grad_att)],
        [(normed_two, grad_upper)],
        [(act_low, grad_mlp)],
        [(head_in, grad_raw)],
    )


def image_inputs(image_vec, pixels):
    pixels = jnp.pad(pixels.transpose(1, 0, 2), ((1, 0), (0, 0), (0, 0))).reshape(-1, PATCH_DIM)
    base = image_vec[1 : IMG_TOK + 1] + jnp.pad(image_vec[:1], ((0, IMG_TOK - 1), (0, 0)))
    return image_vec[IMG_TOK + 1 :], jnp.repeat(base, SEQS, axis=0), pixels


def text_inputs(text_vec, token_rows):
    gains = jnp.pad(text_vec[CTX:], ((2, 0), (0, 0)))
    extra = TEXT.rows - SEQS * CTX
    base = jnp.pad(jnp.tile(text_vec[:CTX], (SEQS, 1)), ((0, extra), (0, 0)))
    return gains, base, jnp.pad(token_rows, ((0, extra), (0, 0)))


def adam_step(weight, first, second, grad, rate, decay):
    first = beta_one * first + (1.0 - beta_one) * grad
    second = beta_two * second + (1.0 - beta_two) * grad * grad
    first_hat = first / (1.0 - beta_one**STEP)
    second_hat = second / (1.0 - beta_two**STEP)
    weight = weight - rate * (first_hat / (jnp.sqrt(second_hat) + adam_eps) + decay * weight)
    return (weight, first, second)


IMAGE, TEXT = Tower(True), Tower(False)


def matrix_rows():
    return sum(seg_rows * seg_cols for seg_name, seg_rows, seg_cols in segment_list()[:9]) // LANES


def parameter_count():
    return sum(seg_rows * seg_cols for seg_name, seg_rows, seg_cols in segment_list())


def window_rows(shard, step=GROUP):
    need = -(-(GROUP * LANES - 1 + shard) // LANES)
    return -(-need // step) * step


def window_start(shard, index):
    return (shard * index // (GROUP * LANES)) * GROUP


def linear_index(gy_size):
    return lax.axis_index("gx") * gy_size + lax.axis_index("gy")


def place_kernel(shard, gy_size, flat_ref, out_ref, rolled):
    rows = flat_ref.shape[0]
    offset = lax.rem(shard * linear_index(gy_size), GROUP * LANES)
    down, right = offset // LANES, lax.rem(offset, LANES)
    pad = 2 * GROUP
    rolled[0:pad, :] = jnp.zeros((pad, LANES), jnp.float32)
    parts = 5 if rows % (5 * GROUP) == 0 else 1
    step = rows // parts

    def roll_rows(i, carry):
        at = pl.multiple_of(i * step, GROUP)
        rolled[pl.ds(pad + at, step), :] = pltpu.roll(flat_ref[pl.ds(at, step), :], right, 1)
        return carry

    lax.fori_loop(0, parts, roll_rows, 0)
    lane = lax.broadcasted_iota(jnp.int32, (step, LANES), 1)

    def put_rows(i, carry):
        at = pl.multiple_of(i * step, GROUP)
        upper = rolled[pl.ds(pad + at - down - 1, step), :]
        lower = rolled[pl.ds(pad + at - down, step), :]
        out_ref[pl.ds(at, step), :] = jnp.where(lane < right, upper, lower).astype(jnp.bfloat16)
        return carry

    lax.fori_loop(0, parts, put_rows, 0)


def place_window(flat, gy_size):
    shard = flat.shape[0]
    rows = window_rows(shard)
    padded = jnp.pad(flat, (0, rows * LANES - shard)).reshape(rows, LANES)
    return pl.pallas_call(
        functools.partial(place_kernel, shard, gy_size),
        out_shape=jax.ShapeDtypeStruct((rows, LANES), jnp.bfloat16),
        in_specs=[pl.BlockSpec(memory_space=pltpu.VMEM)],
        out_specs=pl.BlockSpec(memory_space=pltpu.VMEM),
        scratch_shapes=[pltpu.VMEM((rows + 2 * GROUP, LANES), jnp.float32)],
        compiler_params=pltpu.CompilerParams(vmem_limit_bytes=32 << 20),
        name="place_window",
    )(padded)


def lift_kernel(shard, gy_size, window_ref, out_ref, rolled):
    rows = window_ref.shape[0]
    offset = lax.rem(shard * linear_index(gy_size), GROUP * LANES)
    up, left = offset // LANES, lax.rem(offset, LANES)
    pad = 2 * GROUP
    step = rows // CHUNKS
    rolled[rows:, :] = jnp.zeros((pad, LANES), jnp.float32)

    def roll_rows(i, carry):
        at = pl.multiple_of(i * step, GROUP)
        rolled[pl.ds(at, step), :] = pltpu.roll(
            window_ref[pl.ds(at, step), :], lax.rem(LANES - left, LANES), 1
        )
        return carry

    lax.fori_loop(0, CHUNKS, roll_rows, 0)
    lane = lax.broadcasted_iota(jnp.int32, (step, LANES), 1)

    def put_rows(i, carry):
        at = pl.multiple_of(i * step, GROUP)
        first = rolled[pl.ds(at + up, step), :]
        second = rolled[pl.ds(at + up + 1, step), :]
        out_ref[pl.ds(at, step), :] = jnp.where(lane < LANES - left, first, second)
        return carry

    lax.fori_loop(0, CHUNKS, put_rows, 0)


def lift_window(window, shard, gy_size):
    rows = window.shape[0]
    lifted = pl.pallas_call(
        functools.partial(lift_kernel, shard, gy_size),
        out_shape=jax.ShapeDtypeStruct((rows, LANES), jnp.float32),
        in_specs=[pl.BlockSpec(memory_space=pltpu.VMEM)],
        out_specs=pl.BlockSpec(memory_space=pltpu.VMEM),
        scratch_shapes=[pltpu.VMEM((rows + 2 * GROUP, LANES), jnp.float32)],
        compiler_params=pltpu.CompilerParams(vmem_limit_bytes=32 << 20),
        name="lift_window",
    )(window)
    return lifted.reshape(-1)[:shard]


def spread_steps():
    steps = []
    base = 0
    for number, (seg_name, seg_rows, seg_cols) in enumerate(segment_list()[:9]):
        wide = seg_cols // LANES
        take = seg_rows
        while take * wide > 4608:
            take //= 2
        for start in range(0, seg_rows, take):
            steps.append((number, start, take, seg_cols, base + start * wide))
        base += seg_rows * wide
    return steps


def window_pieces(shard, count, stride, first, length):
    pieces, shared = [], []
    for index in range(count):
        low = window_start(shard, index)
        high = window_start(shard, index + 1) if index + 1 < count else low + window_rows(shard)
        start, stop = max(low, first), min(high, first + length)
        if start < stop:
            pieces.append((index * stride + start - low, start - first, stop - start))
        if index + 1 < count and first <= high < first + length:
            shared.append((index * stride + high - low, high - first))
    return pieces, shared


def spread_kernel(shard, count, vec_rows, share, gathered_ref, *refs):
    outs, vec_ref = refs[:9], refs[9]
    landed, edges, wide_rows, ready, in_sem, out_sem = refs[10:]
    rows = gathered_ref.shape[0] // count
    steps = spread_steps()
    steps.append((9, 0, vec_rows, LANES, matrix_rows()))

    def copies_in(number):
        seg, start, take, cols, base = steps[number]
        slot = number % 2
        pieces, shared = window_pieces(shard, count, rows, base, take * cols // LANES)
        found = [
            pltpu.make_async_copy(
                gathered_ref.at[pl.ds(src, size)], landed.at[slot, pl.ds(dst, size)], in_sem.at[slot]
            )
            for src, dst, size in pieces
        ]
        found += [
            pltpu.make_async_copy(
                gathered_ref.at[pl.ds(src, GROUP)], edges.at[slot, order], in_sem.at[slot]
            )
            for order, (src, dst) in enumerate(shared)
        ]
        return found, shared

    def copy_out(number):
        seg, start, take, cols, base = steps[number]
        slot = number % 2
        if seg == 9:
            return pltpu.make_async_copy(wide_rows.at[pl.ds(0, take)], vec_ref, out_sem.at[slot])
        return pltpu.make_async_copy(
            ready[cols].at[slot, pl.ds(0, take)], outs[seg].at[pl.ds(start, take)], out_sem.at[slot]
        )

    for copy in copies_in(0)[0]:
        copy.start()
    for number, (seg, start, take, cols, base) in enumerate(steps):
        if number == 4:
            share.greet()
            share.begin()
        slot = number % 2
        wide = cols // LANES
        total = take * wide
        if number + 1 < len(steps):
            for copy in copies_in(number + 1)[0]:
                copy.start()
        found, shared = copies_in(number)
        for copy in found:
            copy.wait()
        if number >= 2:
            copy_out(number - 2).wait()
        block = 256 if total % 256 == 0 else GROUP

        def widen(i, carry, slot=slot, block=block):
            at = pl.multiple_of(i * block, GROUP)
            wide_rows[pl.ds(at, block), :] = landed[slot, pl.ds(at, block), :].astype(jnp.float32)
            return carry

        lax.fori_loop(0, total // block, widen, 0)
        for order, (src, dst) in enumerate(shared):
            wide_rows[dst : dst + GROUP, :] += edges[slot, order].astype(jnp.float32)
        if seg < 9:

            def tile(i, carry, slot=slot, wide=wide, cols=cols):
                at = pl.multiple_of(i * GROUP, GROUP)
                for j in range(wide):
                    ready[cols][slot, pl.ds(at, GROUP), j * LANES : (j + 1) * LANES] = wide_rows[
                        pl.ds(at * wide + j, GROUP, stride=wide), :
                    ].astype(jnp.bfloat16)
                return carry

            lax.fori_loop(0, take // GROUP, tile, 0)
        copy_out(number).start()
    copy_out(len(steps) - 2).wait()
    copy_out(len(steps) - 1).wait()


def spread_entry(shard, gx_size, gy_size, vec_rows, gathered_ref, rows_ref, *refs):
    outs, landed_rows = refs[:10], refs[10]
    landed, edges, wide_rows, ready_a, ready_b, ready_c, ready_d, in_sem, out_sem = refs[11:20]
    ready = {D_IMG: ready_a, 4 * D_IMG: ready_b, D_TXT: ready_c, 4 * D_TXT: ready_d}
    share = Share(gx_size, gy_size, False, rows_ref, landed_rows, refs[20:])
    spread_kernel(
        shard, gx_size * gy_size, vec_rows, share, gathered_ref, *outs, landed, edges, wide_rows, ready, in_sem, out_sem
    )
    share.middle()
    share.finish()


def spread_weights(gathered, rows_to_send, shard, gx_size, gy_size, number):
    count = gx_size * gy_size
    rows = gathered.shape[0] // count
    steps = spread_steps()
    tallest = {}
    for seg, start, take, cols, base in steps:
        tallest[cols] = max(tallest.get(cols, 0), take)
    most = max(take * cols // LANES for seg, start, take, cols, base in steps)
    vec_rows = -(-(sum(r * c for name, r, c in segment_list()[9:])) // (LANES * GROUP)) * GROUP
    edge_count = max(
        len(window_pieces(shard, count, rows, base, take * cols // LANES)[1])
        for seg, start, take, cols, base in steps
    )
    ready = [
        pltpu.VMEM((2, tallest[cols], cols), jnp.bfloat16)
        for cols in (D_IMG, 4 * D_IMG, D_TXT, 4 * D_TXT)
    ]
    return pl.pallas_call(
        functools.partial(spread_entry, shard, gx_size, gy_size, vec_rows),
        out_shape=[
            jax.ShapeDtypeStruct((seg_rows, seg_cols), jnp.bfloat16)
            for seg_name, seg_rows, seg_cols in segment_list()[:9]
        ]
        + [
            jax.ShapeDtypeStruct((vec_rows, LANES), jnp.float32),
            jax.ShapeDtypeStruct((1,) + rows_to_send.shape, rows_to_send.dtype),
        ],
        in_specs=[pl.BlockSpec(memory_space=pl.ANY), pl.BlockSpec(memory_space=pltpu.VMEM)],
        out_specs=[pl.BlockSpec(memory_space=pl.ANY)] * 10 + [pl.BlockSpec(memory_space=pltpu.VMEM)],
        scratch_shapes=[
            pltpu.VMEM((2, most, LANES), jnp.bfloat16),
            pltpu.VMEM((2, edge_count + 1, GROUP, LANES), jnp.bfloat16),
            pltpu.VMEM((most, LANES), jnp.float32),
        ]
        + ready
        + [pltpu.SemaphoreType.DMA((2,)), pltpu.SemaphoreType.DMA((2,))]
        + share_sems(gx_size, gy_size),
        compiler_params=pltpu.CompilerParams(
            collective_id=number, has_side_effects=True, vmem_limit_bytes=48 << 20
        ),
        name="spread_weights",
    )(gathered, rows_to_send)


def split_vectors(vec_rows):
    image_count, text_count = (IMG_TOK + 9) * D_IMG // LANES, (CTX + 6) * D_TXT // LANES
    image_vec = vec_rows[:image_count].reshape(IMG_TOK + 9, D_IMG)
    text_vec = vec_rows[image_count : image_count + text_count].reshape(CTX + 6, D_TXT)
    return image_vec, text_vec, vec_rows[image_count + text_count, 0]


def grads_kernel(parts, gx_size, gy_size, *refs):
    operand_count = sum(2 * len(pairs) for seg_rows, seg_cols, take, pairs in parts)
    operands = refs[:operand_count]
    vec_ref, token_ref, out_ref, arrived_ref, flat_rows, vec_sem, out_sem = refs[operand_count : operand_count + 7]
    share = Share(gx_size, gy_size, True, token_ref, arrived_ref, refs[operand_count + 7 :])
    share.greet()
    share.begin()
    tail = pltpu.make_async_copy(vec_ref, out_ref.at[pl.ds(matrix_rows(), vec_ref.shape[0])], vec_sem)
    tail.start()
    base = 0
    steps_before = 0
    for number, (seg_rows, seg_cols, take, pairs) in enumerate(parts):
        if number == 2:
            share.middle()
        if number == 6:
            share.rest()
        wide = seg_cols // LANES
        size = take * wide
        count = seg_rows // take

        def step(i, carry, base=base, before=steps_before, size=size, take=take, wide=wide, pairs=pairs):
            slot = lax.rem(i + before, 2)

            def written(number):
                at = pl.multiple_of(base + number * size, 8)
                return pltpu.make_async_copy(
                    flat_rows.at[slot, pl.ds(0, size)], out_ref.at[pl.ds(at, size)], out_sem.at[slot]
                )

            @pl.when(i >= 2)
            def _():
                written(i - 2).wait()

            for left_number, right_number, first in pairs:
                left_ref, right_ref = operands[left_number], operands[right_number]
                at = pl.multiple_of(i * take, LANES)
                product = lax.dot_general(
                    left_ref[:, pl.ds(at, take)],
                    right_ref[...],
                    (((0,), (0,)), ((), ())),
                    preferred_element_type=jnp.float32,
                )
                for j in range(right_ref.shape[1] // LANES):
                    flat_rows[slot, pl.ds(first + j, take, stride=wide), :] = product[
                        :, j * LANES : (j + 1) * LANES
                    ]
            written(i).start()
            return carry

        lax.fori_loop(0, count, step, 0)
        for number in range(max(count - 2, 0), count):
            slot = (number + steps_before) % 2
            at = base + number * size
            pltpu.make_async_copy(
                flat_rows.at[slot, pl.ds(0, size)], out_ref.at[pl.ds(at, size)], out_sem.at[slot]
            ).wait()
        base += seg_rows * wide
        steps_before += count
    tail.wait()
    share.finish()


def weight_grads(pair_lists, vec_rows, token_grads, gx_size, gy_size, number):
    operands, parts = [], []
    for (seg_name, seg_rows, seg_cols), pairs in zip(segment_list()[:9], pair_lists):
        numbered, first = [], 0
        for left_side, right_side in pairs:
            numbered.append((len(operands), len(operands) + 1, first))
            for side in (left_side, right_side):
                side = side.reshape(-1, side.shape[-1])
                operands.append(jnp.pad(side, ((0, -side.shape[0] % GROUP), (0, 0))))
            first += right_side.shape[-1] // LANES
        parts.append((seg_rows, seg_cols, min(seg_rows, 256 if seg_cols <= 768 else 128), numbered))
    total_rows = matrix_rows() + vec_rows.shape[0]
    most = max(take * seg_cols // LANES for seg_rows, seg_cols, take, pairs in parts)
    return pl.pallas_call(
        functools.partial(grads_kernel, parts, gx_size, gy_size),
        out_shape=[
            jax.ShapeDtypeStruct((total_rows, LANES), jnp.float32),
            jax.ShapeDtypeStruct((gx_size,) + token_grads.shape, token_grads.dtype),
        ],
        in_specs=[pl.BlockSpec(memory_space=pltpu.VMEM)] * (len(operands) + 2),
        out_specs=[pl.BlockSpec(memory_space=pl.ANY)] * 2,
        scratch_shapes=[
            pltpu.VMEM((2, most, LANES), jnp.float32),
            pltpu.SemaphoreType.DMA,
            pltpu.SemaphoreType.DMA((2,)),
        ]
        + share_sems(gx_size, gy_size),
        compiler_params=pltpu.CompilerParams(
            collective_id=number, has_side_effects=True, vmem_limit_bytes=56 << 20
        ),
        name="weight_grads",
    )(*operands, vec_rows, token_grads)


class Share:
    def __init__(self, gx_size, gy_size, everyone, send_ref, out_ref, sems):
        gx, self.gy = lax.axis_index("gx"), lax.axis_index("gy")
        self.x_size, self.send_ref, self.out_ref = gx_size // 2, send_ref, out_ref
        self.core, self.x = lax.rem(gx, 2), gx // 2
        (self.own_sem, self.row_send, self.row_recv, self.x_send, self.x_recv, self.core_send, self.core_recv) = sems
        self.rows = [(gx, lax.rem(self.gy + d, gy_size)) for d in range(1, gy_size)]
        self.along_x, self.sibling = [], []
        if everyone:
            self.along_x = [
                (lax.rem(self.x + d, self.x_size) * 2 + self.core, self.gy) for d in range(1, self.x_size)
            ]
            self.sibling = [(self.x * 2 + 1 - self.core, self.gy)]
        self.mine = out_ref.at[gx if everyone else 0]

    def greet(self):
        greet_all(self.rows + self.along_x + self.sibling)

    def own(self):
        return pltpu.make_async_copy(self.send_ref.at[self.gy], self.mine.at[self.gy], self.own_sem)

    def row(self, d):
        other = self.rows[d]
        return remote(self.send_ref.at[other[1]], self.mine.at[self.gy], self.row_send.at[d], self.row_recv.at[d], other)

    def group(self, d):
        return remote(self.mine, self.mine, self.x_send.at[d], self.x_recv.at[d], self.along_x[d])

    def across(self, i, source):
        return remote(source, source, self.core_send.at[i], self.core_recv.at[i], self.sibling[0])

    def begin(self):
        self.own().start()
        for d in range(len(self.rows)):
            self.row(d).start()

    def middle(self):
        self.own().wait()
        for d in range(len(self.rows)):
            self.row(d).wait_recv()
        for d in range(len(self.along_x)):
            self.group(d).start()
        if self.sibling:
            self.across(0, self.mine).start()

    def rest(self):
        for d in range(len(self.along_x)):
            self.group(d).wait_recv()
            sender = lax.rem(self.x + self.x_size - d - 1, self.x_size) * 2 + self.core
            self.across(d + 1, self.out_ref.at[sender]).start()

    def finish(self):
        for d in range(len(self.rows)):
            self.row(d).wait_send()
        for d in range(len(self.along_x)):
            self.group(d).wait_send()
        for i in range(self.x_size if self.sibling else 0):
            self.across(i, self.mine).wait_send()
            self.across(i, self.mine).wait_recv()


def share_sems(gx_size, gy_size):
    dma, x_size = pltpu.SemaphoreType.DMA, gx_size // 2
    return [dma, dma((gy_size - 1,)), dma((gy_size - 1,)), dma((x_size,)), dma((x_size,)), dma((x_size,)), dma((x_size,))]


class Places:
    def __init__(self, sizes):
        self.x_size, self.low_size, self.high_size = sizes
        self.mixed = self.x_size == self.low_size
        self.gy_size = self.high_size * self.low_size
        gx, gy = lax.axis_index("gx"), lax.axis_index("gy")
        self.core, x = lax.rem(gx, 2), gx // 2
        self.h, low = gy // self.low_size, lax.rem(gy, self.low_size)
        self.a, self.b = self.turned(self.core, x, low)
        self.a_size, self.b_size = self.x_size, self.low_size

    def turned(self, side, a, b):
        if not self.mixed:
            return a, b
        return a * (1 - side) + b * side, b * (1 - side) + a * side

    def device(self, side, a, b, h):
        dev_x, dev_low = self.turned(side, a, b)
        return (dev_x * 2 + side, h * self.low_size + dev_low)

    def linear(self, side, a, b, h):
        gx, gy = self.device(side, a, b, h)
        return gx * self.gy_size + gy

    def sibling(self):
        a, b = (self.b, self.a) if self.mixed else (self.a, self.b)
        return self.device(1 - self.core, a, b, self.h)

    def along_a(self):
        return [
            self.device(self.core, lax.rem(self.a + d, self.a_size), self.b, self.h)
            for d in range(1, self.a_size)
        ]

    def along_b(self):
        return [
            self.device(self.core, self.a, lax.rem(self.b + d, self.b_size), self.h)
            for d in range(1, self.b_size)
        ]

    def along_h(self):
        return [
            self.device(self.core, self.a, self.b, lax.rem(self.h + d, self.high_size))
            for d in range(1, self.high_size)
        ]


def greet_all(others):
    barrier = pltpu.get_barrier_semaphore()
    for other in others:
        pl.semaphore_signal(barrier, inc=1, device_id=other, device_id_type=MESH)
    pl.semaphore_wait(barrier, len(others))


def remote(src, dst, send_sem, recv_sem, other):
    return pltpu.make_async_remote_copy(
        src_ref=src, dst_ref=dst, send_sem=send_sem, recv_sem=recv_sem, device_id=other, device_id_type=MESH
    )


def axis_sizes(gx_size, gy_size):
    return gx_size // 2, gy_size // 4, 4


NO_TOKEN = 65535


def route_capacity(tokens, gy_size):
    return GROUP * (1 + 17 * tokens // (16 * gy_size * GROUP))


def table_sum_kernel(cap, counts_ref, index_ref, rows_ref, out_ref, square_ref, wide, row_sem):
    sources = rows_ref.shape[0]
    vocab = out_ref.shape[0] - 8

    def fetch(source):
        slot = lax.rem(source, 2)
        return pltpu.make_async_copy(rows_ref.at[source], wide.at[slot], row_sem.at[slot])

    fetch(0).start()
    block = 32 if vocab % 32 == 0 else 8

    def clear(i, carry):
        out_ref[pl.ds(pl.multiple_of(i * block, 8), block), :] = jnp.zeros((block, D_TXT), jnp.float32)
        return carry

    lax.fori_loop(0, vocab // block, clear, 0)
    out_ref[vocab:, :] = jnp.zeros((8, D_TXT), jnp.float32)

    def one_source(source, carry):
        slot = lax.rem(source, 2)

        @pl.when(source + 1 < sources)
        def _():
            fetch(source + 1).start()

        fetch(source).wait()
        widened = wide.at[slot]

        def add(group, carry):
            rows = widened[pl.ds(pl.multiple_of(group * GROUP, GROUP), GROUP), :].astype(jnp.float32)
            for half in range(0, GROUP, 8):
                places = [
                    pl.ds(index_ref[source * cap + group * GROUP + half + i], 1) for i in range(8)
                ]
                sums = [out_ref[place, :] + rows[half + i : half + i + 1, :] for i, place in enumerate(places)]
                for place, value in zip(places, sums):
                    out_ref[place, :] = value
            return carry

        lax.fori_loop(0, (counts_ref[source] + GROUP - 1) // GROUP, add, 0)
        return carry

    lax.fori_loop(0, sources, one_source, 0)

    def square(i, carry):
        part = out_ref[pl.ds(pl.multiple_of(i * block, 8), block), :]
        part = part * part
        total = carry
        for r in range(0, block, 8):
            total = total + part[r : r + 8]
        return total

    square_ref[...] = lax.fori_loop(0, vocab // block, square, jnp.zeros((8, D_TXT), jnp.float32))


def table_sum(counts, index, rows, vocab):
    sources, cap = rows.shape[0], rows.shape[1]
    return pl.pallas_call(
        functools.partial(table_sum_kernel, cap),
        out_shape=[
            jax.ShapeDtypeStruct((vocab + 8, D_TXT), jnp.float32),
            jax.ShapeDtypeStruct((8, D_TXT), jnp.float32),
        ],
        in_specs=[pl.BlockSpec(memory_space=pltpu.SMEM)] * 2 + [pl.BlockSpec(memory_space=pl.ANY)],
        out_specs=[pl.BlockSpec(memory_space=pltpu.VMEM)] * 2,
        scratch_shapes=[pltpu.VMEM((2, cap, D_TXT), jnp.bfloat16), pltpu.SemaphoreType.DMA((2,))],
        compiler_params=pltpu.CompilerParams(vmem_limit_bytes=40 << 20),
        name="table_sum",
    )(counts, index, rows)


def ranks(flags):
    tokens = flags.shape[-1]
    before = (jnp.arange(tokens)[:, None] < jnp.arange(tokens)[None, :]).astype(jnp.bfloat16)
    return fwd_dot(flags.astype(jnp.bfloat16), before).astype(jnp.int32)


def pick_matrix(slots, count):
    return (jnp.arange(count)[:, None] == slots[None, :]).astype(jnp.bfloat16)


def turned_rows(chunk):
    return TURNED * chunk // (16 * GROUP) * GROUP


def gather_kernel(sizes, chunks, window_ref, out_ref, own_sem, h_send, h_recv, b_send, b_recv, a_send, a_recv, core_send,
                  core_recv):
    at = Places(sizes)
    rows = window_ref.shape[0]
    chunk = rows // chunks
    changed = turned_rows(chunk)
    ways = (False, True) if changed else (False,)
    spans = {False: (0, chunk - changed), True: (chunk - changed, changed)}
    me = at.linear(at.core, at.a, at.b, at.h)
    sibling, peers_a, peers_b, peers_h = at.sibling(), at.along_a(), at.along_b(), at.along_h()
    greet_all([sibling] + peers_a + peers_b + peers_h)
    along_h, along_b = (peers_h, h_send, h_recv), (peers_b, b_send, b_recv)

    def part(block, t, span=(0, chunk)):
        return out_ref.at[pl.ds(pl.multiple_of(block * rows + t * chunk + span[0], GROUP), span[1])]

    def many(count):
        return out_ref.at[pl.ds(0, count)]

    def own_copy(t):
        src = window_ref.at[pl.ds(pl.multiple_of(t * chunk, GROUP), chunk)]
        return pltpu.make_async_copy(src, part(me, t), own_sem.at[t])

    def first(t):
        for turned in ways:
            peers, send, recv = along_b if turned else along_h
            start, size = spans[turned]
            src = window_ref.at[pl.ds(pl.multiple_of(t * chunk + start, GROUP), size)]
            for d, other in enumerate(peers):
                remote(src, part(me, t, spans[turned]), send.at[d], recv.at[int(turned), t, d], other).start()
        own_copy(t).start()

    def second(t):
        own_copy(t).wait()
        for turned in ways:
            size = many(spans[turned][1])
            peers, send, recv = along_b if turned else along_h
            for d, other in enumerate(peers):
                remote(size, size, send.at[d], recv.at[int(turned), t, d], other).wait_recv()
            if turned:
                blocks = [at.linear(at.core, at.a, b, at.h) for b in range(at.b_size)]
            else:
                blocks = [at.linear(at.core, at.a, at.b, h) for h in range(at.high_size)]
            peers, send, recv = along_h if turned else along_b
            for d, other in enumerate(peers):
                for block in blocks:
                    block = part(block, t, spans[turned])
                    remote(block, block, send.at[d], recv.at[int(turned), t, d], other).start()

    def third(t):
        for turned in ways:
            count = at.b_size if turned else at.high_size
            size = many(count * spans[turned][1])
            peers, send, recv = along_h if turned else along_b
            for d, other in enumerate(peers):
                remote(size, size, send.at[d], recv.at[int(turned), t, d], other).wait_recv()
        for d, other in enumerate(peers_a):
            for b in range(at.b_size):
                for h in range(at.high_size):
                    block = part(at.linear(at.core, at.a, b, h), t)
                    remote(block, block, a_send.at[d], a_recv.at[t, d], other).start()

    plane = at.b_size * at.high_size

    def fourth(t):
        size = many(plane * chunk)
        for d, other in enumerate(peers_a):
            remote(size, size, a_send.at[d], a_recv.at[t, d], other).wait_recv()
        for a in range(at.a_size):
            for b in range(at.b_size):
                for h in range(at.high_size):
                    block = part(at.linear(at.core, a, b, h), t)
                    remote(block, block, core_send, core_recv, sibling).start()

    def turn(t, carry):
        for depth, stage in enumerate((first, second, third, fourth)):
            active = (t >= depth) & (t < chunks + depth)
            pl.when(active)(functools.partial(stage, t - depth))
        return carry

    lax.fori_loop(0, chunks + 3, turn, 0)
    straight = chunk - changed
    for peers, send, sent in (
        (peers_h, h_send, straight + changed * at.b_size),
        (peers_b, b_send, straight * at.high_size + changed),
        (peers_a, a_send, chunk * plane),
    ):
        size = many(chunks * sent)
        for d, other in enumerate(peers):
            remote(size, size, send.at[d], core_recv, other).wait_send()
    half = many(at.a_size * plane * rows)
    last = remote(half, half, core_send, core_recv, sibling)
    last.wait_send()
    last.wait_recv()


def gather_windows(window, gx_size, gy_size, chunks, number, name):
    sizes = axis_sizes(gx_size, gy_size)
    a, b, h = sizes[0] - 1, sizes[1] - 1, sizes[2] - 1
    dma = pltpu.SemaphoreType.DMA
    return pl.pallas_call(
        functools.partial(gather_kernel, sizes, chunks),
        out_shape=jax.ShapeDtypeStruct((gx_size * gy_size * window.shape[0], LANES), window.dtype),
        in_specs=[pl.BlockSpec(memory_space=pltpu.VMEM)],
        out_specs=pl.BlockSpec(memory_space=pl.ANY),
        scratch_shapes=[dma((chunks,)), dma((h,)), dma((2, chunks, h)), dma((b,)), dma((2, chunks, b)), dma((a,)),
                        dma((chunks, a)), dma, dma],
        compiler_params=pltpu.CompilerParams(
            collective_id=number, has_side_effects=True, vmem_limit_bytes=32 << 20
        ),
        name=name,
    )(window)


class Way:
    def __init__(self, at, turned, span, refs):
        self.start, self.size = span
        (self.keep_two, self.send_two, self.recv_two, self.keep_three, self.send_three, self.recv_three,
         self.two_send, self.two_recv, self.three_send, self.three_recv) = refs
        along_b, along_h = (at.along_b(), at.b, at.b_size), (at.along_h(), at.h, at.high_size)
        high = at.high_size
        if turned:
            (self.peers, self.place, self.count), (self.last_peers, self.last_place, self.inner) = along_h, along_b
            self.number = lambda other, i: i * high + other
        else:
            (self.peers, self.place, self.count), (self.last_peers, self.last_place, self.inner) = along_b, along_h
            self.number = lambda other, i: other * high + i

    def two(self, u, d):
        slot = lax.rem(u, 2)
        return remote(self.send_two.at[slot, d - 1], self.recv_two.at[u, d - 1], self.two_send.at[slot, d - 1],
                      self.two_recv.at[u, d - 1], self.peers[d - 1])

    def three(self, u, d):
        slot = lax.rem(u, 2)
        return remote(self.send_three.at[slot, d - 1], self.recv_three.at[u, d - 1], self.three_send.at[slot, d - 1],
                      self.three_recv.at[u, d - 1], self.last_peers[d - 1])

    def second(self, u, total):
        slot, rows = lax.rem(u, 2), pl.ds(self.start, self.size)
        for d in range(1, self.count):
            pl.when(u >= 2)(lambda d=d: self.two(u - 2, d).wait_send())
            other = lax.rem(self.place + d, self.count)

            def give(i, carry):
                self.send_two[slot, d - 1, i] = total(self.number(other, i), rows).astype(jnp.bfloat16)
                return carry

            lax.fori_loop(0, self.inner, give, 0)
            self.two(u, d).start()

        def hold(i, carry):
            self.keep_two[slot, i] = total(self.number(self.place, i), rows)
            return carry

        lax.fori_loop(0, self.inner, hold, 0)

    def third(self, u):
        slot = lax.rem(u, 2)
        for d in range(1, self.count):
            self.two(u, d).wait_recv()

        def total(i):
            value = self.keep_two[slot, i]
            for d in range(1, self.count):
                value = value + self.recv_two[u, d - 1, i].astype(jnp.float32)
            return value

        for d in range(1, self.inner):
            pl.when(u >= 2)(lambda d=d: self.three(u - 2, d).wait_send())
            self.send_three[slot, d - 1] = total(lax.rem(self.last_place + d, self.inner)).astype(jnp.bfloat16)
            self.three(u, d).start()
        self.keep_three[slot] = total(self.last_place)

    def last(self, u):
        value = self.keep_three[lax.rem(u, 2)]
        for d in range(1, self.inner):
            self.three(u, d).wait_recv()
            value = value + self.recv_three[u, d - 1].astype(jnp.float32)
        return value

    def drain(self, u):
        for d in range(1, self.count):
            self.two(u, d).wait_send()
        for d in range(1, self.inner):
            self.three(u, d).wait_send()


def way_scratch(chunks, count, inner, size):
    low, dma = jnp.bfloat16, pltpu.SemaphoreType.DMA
    return [
        pltpu.VMEM((2, inner, size, LANES), jnp.float32),
        pltpu.VMEM((2, count - 1, inner, size, LANES), low),
        pltpu.VMEM((chunks, count - 1, inner, size, LANES), low),
        pltpu.VMEM((2, size, LANES), jnp.float32),
        pltpu.VMEM((2, inner - 1, size, LANES), low),
        pltpu.VMEM((chunks, inner - 1, size, LANES), low),
        dma((2, count - 1)),
        dma((chunks, count - 1)),
        dma((2, inner - 1)),
        dma((chunks, inner - 1)),
    ]


def reduce_kernel(shard, sizes, grads_ref, square_ref, out_ref, squares_ref, own, landed, keep_one, send_one, recv_one,
                  partial, square_send, square_recv, load_sem, pair_send, pair_recv, credit, one_send, one_recv, *more):
    at = Places(sizes)
    a_size, b_size, high_size = at.a_size, at.b_size, at.high_size
    core, my_a, my_b, high = at.core, at.a, at.b, at.h
    plane = b_size * high_size
    chunk = own.shape[2]
    chunks = out_ref.shape[0] // chunk

    def start_row(side, number):
        a, rest = number // plane, lax.rem(number, plane)
        return window_start(shard, at.linear(side, a, rest // high_size, lax.rem(rest, high_size)))

    sibling, peers = at.sibling(), at.along_a()
    changed = turned_rows(chunk)
    straight = chunk - changed
    ways = [Way(at, False, (0, straight), more[:10])]
    if changed:
        ways.append(Way(at, True, (straight, changed), more[10:]))
    count = squares_ref.shape[0]
    me = linear_index(at.gy_size)

    def device(step):
        other = lax.rem(me + step, count)
        return (other // at.gy_size, lax.rem(other, at.gy_size))

    barrier = pltpu.get_barrier_semaphore()

    def greet(step, carry):
        pl.semaphore_signal(barrier, inc=1, device_id=device(step), device_id_type=MESH)
        return carry

    lax.fori_loop(1, count, greet, 0)
    pl.semaphore_wait(barrier, count - 1)
    table_part = square_ref[...]
    partial[...] = sum(table_part[:, j * LANES : (j + 1) * LANES] for j in range(D_TXT // LANES))
    spot = (lax.broadcasted_iota(jnp.int32, (chunk, LANES), 0) * LANES
            + lax.broadcasted_iota(jnp.int32, (chunk, LANES), 1))
    blocks = a_size * plane

    def pair_stage(t):
        slot = lax.rem(t, 2)

        @pl.when(t >= 2)
        def _():
            pl.semaphore_wait(credit, 1)

        def each(number, carry):
            theirs = pl.multiple_of(start_row(1 - core, number) + t * chunk, GROUP)
            mine = pl.multiple_of(start_row(core, number) + t * chunk, GROUP)
            remote(
                grads_ref.at[pl.ds(theirs, chunk)], landed.at[slot, number], pair_send.at[slot], pair_recv.at[slot], sibling
            ).start()
            pltpu.make_async_copy(
                grads_ref.at[pl.ds(mine, chunk)], own.at[slot, number], load_sem.at[slot]
            ).start()
            return carry

        lax.fori_loop(0, blocks, each, 0)

    def first_stage(u):
        slot = lax.rem(u, 2)
        both = remote(landed.at[slot], landed.at[slot], pair_send.at[slot], pair_recv.at[slot], sibling)
        pltpu.make_async_copy(own.at[slot], own.at[slot], load_sem.at[slot]).wait()
        both.wait_send()
        both.wait_recv()
        for d in range(1, a_size):
            @pl.when(u >= 2)
            def _():
                remote(send_one.at[slot, d - 1], recv_one.at[u - 2, d - 1], one_send.at[slot, d - 1],
                       one_recv.at[u - 2, d - 1], peers[d - 1]).wait_send()

            first = lax.rem(my_a + d, a_size) * plane

            def give(i, carry):
                send_one[slot, d - 1, i] = (own[slot, first + i] + landed[slot, first + i]).astype(jnp.bfloat16)
                return carry

            lax.fori_loop(0, plane, give, 0)
            remote(send_one.at[slot, d - 1], recv_one.at[u, d - 1], one_send.at[slot, d - 1],
                   one_recv.at[u, d - 1], peers[d - 1]).start()

        def hold(i, carry):
            keep_one[slot, i] = own[slot, my_a * plane + i] + landed[slot, my_a * plane + i]
            return carry

        lax.fori_loop(0, plane, hold, 0)

        @pl.when(u < chunks - 2)
        def _():
            pl.semaphore_signal(credit, inc=1, device_id=sibling, device_id_type=MESH)

    def second_stage(u):
        slot = lax.rem(u, 2)
        for d in range(1, a_size):
            remote(recv_one.at[u, d - 1], recv_one.at[u, d - 1], one_send.at[slot, d - 1], one_recv.at[u, d - 1],
                   peers[d - 1]).wait_recv()

        def total(number, rows):
            value = keep_one[slot, number, rows, :]
            for d in range(1, a_size):
                value = value + recv_one[u, d - 1, number, rows, :].astype(jnp.float32)
            return value

        for way in ways:
            way.second(u, total)

    def third_stage(u):
        for way in ways:
            way.third(u)

    def last_stage(u):
        for way in ways:
            value = way.last(u)
            row = u * chunk + way.start
            out_ref[pl.ds(pl.multiple_of(row, GROUP), way.size), :] = value
            place = spot[: way.size] + (window_start(shard, me) + row) * LANES - me * shard
            square = jnp.where((place >= 0) & (place < shard), value * value, 0.0)
            partial[...] += sum(square[r : r + 8] for r in range(0, way.size, 8))

    def turn(t, carry):
        stages = (pair_stage, first_stage, second_stage, third_stage, last_stage)
        for depth, stage in enumerate(stages):
            @pl.when((t >= depth) & (t < chunks + depth))
            def _():
                stage(t - depth)

        return carry

    lax.fori_loop(0, chunks + 4, turn, 0)
    squares_ref[me] = partial[...]

    def send(step, carry):
        remote(partial, squares_ref.at[me], square_send, square_recv, device(step)).start()
        return carry

    lax.fori_loop(1, count, send, 0)
    others = squares_ref.at[pl.ds(0, count - 1)]
    both = remote(others, others, square_send, square_recv, device(1))
    both.wait_send()
    both.wait_recv()
    for u in range(max(chunks - 2, 0), chunks):
        slot = u % 2
        for d in range(1, a_size):
            remote(send_one.at[slot, d - 1], recv_one.at[u, d - 1], one_send.at[slot, d - 1],
                   one_recv.at[u, d - 1], peers[d - 1]).wait_send()
        for way in ways:
            way.drain(u)


def reduce_windows(grads, square, shard, gx_size, gy_size, number):
    rows = window_rows(shard, GROUP * CHUNKS)
    chunk = rows // CHUNKS
    x_size, low_size, high_size = axis_sizes(gx_size, gy_size)
    plane = low_size * high_size
    blocks = x_size * plane
    low_type, dma = jnp.bfloat16, pltpu.SemaphoreType.DMA
    a = x_size - 1
    return pl.pallas_call(
        functools.partial(reduce_kernel, shard, (x_size, low_size, high_size)),
        out_shape=[
            jax.ShapeDtypeStruct((rows, LANES), jnp.float32),
            jax.ShapeDtypeStruct((gx_size * gy_size, 8, LANES), jnp.float32),
        ],
        in_specs=[pl.BlockSpec(memory_space=pl.ANY), pl.BlockSpec(memory_space=pltpu.VMEM)],
        out_specs=[pl.BlockSpec(memory_space=pltpu.VMEM)] * 2,
        scratch_shapes=[
            pltpu.VMEM((2, blocks, chunk, LANES), jnp.float32),
            pltpu.VMEM((2, blocks, chunk, LANES), jnp.float32),
            pltpu.VMEM((2, plane, chunk, LANES), jnp.float32),
            pltpu.VMEM((2, a, plane, chunk, LANES), low_type),
            pltpu.VMEM((CHUNKS, a, plane, chunk, LANES), low_type),
            pltpu.VMEM((8, LANES), jnp.float32),
            dma,
            dma,
            dma((2,)),
            dma((2,)),
            dma((2,)),
            pltpu.SemaphoreType.REGULAR,
            dma((2, a)),
            dma((CHUNKS, a)),
        ]
        + way_scratch(CHUNKS, low_size, high_size, chunk - turned_rows(chunk))
        + (way_scratch(CHUNKS, high_size, low_size, turned_rows(chunk)) if turned_rows(chunk) else []),
        compiler_params=pltpu.CompilerParams(
            collective_id=number, has_side_effects=True, vmem_limit_bytes=60 << 20
        ),
        name="reduce_windows",
    )(grads, square)


def log_sums(rows, columns, column_ok, logit_scale, matches, positives):
    total, taken = rows.shape[0], min(rows.shape[0], 256)

    def some(args):
        row_part, match_part, positive_part = args
        dots = back_dot(row_part, columns)
        logits = logit_scale * dots
        masked = jnp.where(column_ok[None, :], logits, -1e30)
        row_max = jnp.max(masked, 1, keepdims=True)
        log_total = row_max[:, 0] + jnp.log(jnp.sum(jnp.exp(masked - row_max), 1))
        gap = jnp.where(match_part > 0.0, logits[:, :total] - log_total[:, None], 0.0)
        pulled = jnp.sum(positive_part[:, None] * jnp.exp(masked - log_total[:, None]) * dots)
        return log_total, -jnp.sum(gap), pulled - jnp.sum(match_part * dots[:, :total])

    if taken == total:
        return some((rows, matches, positives))
    logs, parts, pulls = lax.map(
        some,
        (
            rows.reshape(-1, taken, rows.shape[1]),
            matches.reshape(-1, taken, total),
            positives.reshape(-1, taken),
        ),
    )
    return logs.reshape(-1), jnp.sum(parts), jnp.sum(pulls)


def side_grads(row_embed, columns, column_ok, same_own, positives_own, log_own, logit_scale, total_count):
    dot_vals = back_dot(row_embed, columns)
    masked = jnp.where(column_ok[None, :], logit_scale * dot_vals, -1e30)
    extra = columns.shape[0] - same_own.shape[1]
    weights_pos = jnp.concatenate(
        [same_own, jnp.zeros((same_own.shape[0], extra), jnp.float32)], 1
    )
    grad_logits = (
        positives_own[:, None] * jnp.exp(masked - log_own[:, None]) - weights_pos
    ) / total_count
    grad_dots = (logit_scale * grad_logits).astype(jnp.bfloat16)
    return fwd_dot(grad_dots, columns)


def cross_grads(rows, own, valid_own, same_own, positives_all, logs, logit_scale, total_count):
    logits = logit_scale * back_dot(rows, own)
    masked = jnp.where(valid_own[None, :], logits, -1e30)
    grad_logits = (
        positives_all[:, None] * jnp.exp(masked - logs[:, None]) - same_own.T
    ) / total_count
    grad_dots = (logit_scale * grad_logits).astype(jnp.bfloat16)
    return weight_grad(grad_dots, rows)


def body(
    flat_master,
    flat_first,
    flat_second,
    table,
    table_first,
    table_second,
    pixels,
    token_ids,
    end_pos,
    pair_counts,
    groups,
    cached_image,
    cached_text,
):
    gx_size, gy_size = lax.axis_size("gx"), lax.axis_size("gy")
    device_count = gx_size * gy_size
    my_index = linear_index(gy_size)
    pairs_dev = pixels.shape[0]
    shard = flat_master.shape[0]
    tokens = token_ids.size
    vocab_dev = table.shape[0]
    cap = route_capacity(tokens, gy_size)
    own_ids = token_ids.reshape(-1)
    same = own_ids[:, None] == own_ids[None, :]
    order = jnp.arange(tokens)
    leading = ~jnp.any(same & (order[None, :] < order[:, None]), 1)
    flat_ids = jnp.where(leading, own_ids, NO_TOKEN)
    flat_ids = jnp.pad(flat_ids, (0, ID_ROWS * LANES // 2 - tokens)).reshape(-1, LANES)
    payload = [
        place_window(flat_master, gy_size),
        jnp.concatenate([cached_image, cached_text], 0).reshape(CACHED_ROWS, LANES),
        jnp.concatenate([flat_ids // 256, flat_ids % 256], 0).astype(jnp.bfloat16),
    ]
    used = sum(part.shape[0] for part in payload)
    step = GROUP * GATHER_CHUNKS
    payload = jnp.pad(jnp.concatenate(payload, 0), ((0, -used % step), (0, 0)))
    gathered = gather_windows(payload, gx_size, gy_size, GATHER_CHUNKS, 4, "gather_weights")
    every_part = gathered.reshape(device_count, -1, LANES)
    cached = every_part[:, used - ID_ROWS - CACHED_ROWS : used - ID_ROWS].reshape(device_count, -1, EMBED)
    cache_img, cache_txt = lax.optimization_barrier((cached[:, :pairs_dev], cached[:, pairs_dev:]))
    cache_img, cache_txt = cache_img.reshape(-1, EMBED), cache_txt.reshape(-1, EMBED)
    coded = every_part[:, used - ID_ROWS : used].astype(jnp.int32)
    ids_all = coded[:, : ID_ROWS // 2] * 256 + coded[:, ID_ROWS // 2 :]
    ids_all = ids_all.reshape(device_count, -1)[:, :tokens]
    holders = ids_all // vocab_dev
    pair_rows = jnp.sum(holders[:, :, None] == jnp.arange(gy_size), 1)
    rounds = (jnp.max(pair_rows) + cap - 1) // cap
    me_y = lax.axis_index("gy")
    held = holders == me_y
    held_rank = jnp.where(held, ranks(held), -1)
    held_row = ids_all - me_y * vocab_dev
    held_count = jnp.sum(held, 1)
    own_flags = (jnp.arange(gy_size)[:, None] == own_ids[None, :] // vocab_dev) & leading[None, :]
    own_place = jnp.arange(gy_size)[:, None] * tokens + ranks(own_flags)
    own_place = jnp.sum(jnp.where(own_flags, own_place, 0), 0)
    own_place = jnp.sum(jnp.where(same & leading[None, :], own_place[None, :], 0), 1)
    own_holder, own_rank = own_place // tokens, own_place % tokens

    def held_rows(turn):
        slots = held_rank - turn * cap
        found = slots[:, None, :] == jnp.arange(cap)[None, :, None]
        return vocab_dev + jnp.sum(jnp.where(found, held_row[:, None, :] - vocab_dev, 0), 2)

    def own_slots(turn):
        rank = own_rank - turn * cap
        return jnp.where((rank >= 0) & (rank < cap), own_holder * cap + rank, -1)

    first_rows = held_rows(0)
    group_start = lax.axis_index("gx") * gy_size

    def rows_to_send(index):
        index = lax.dynamic_slice_in_dim(index, group_start, gy_size, 0)
        rows = jnp.take(table, index.reshape(-1), axis=0, mode="clip")
        return rows.reshape(gy_size, cap, D_TXT)

    sent = rows_to_send(first_rows).astype(jnp.bfloat16)
    slot_count = gy_size * cap

    def more_rows(turn, found):
        rows = lax.all_to_all(rows_to_send(held_rows(turn)), "gy", 0, 0, tiled=True)
        rows = rows.reshape(slot_count, D_TXT).astype(jnp.bfloat16)
        return found + weight_grad(pick_matrix(own_slots(turn), slot_count), rows).astype(jnp.bfloat16)

    nothing = jnp.zeros((tokens, D_TXT), jnp.bfloat16)
    extra_rows = lax.cond(
        rounds > 1, lambda rows: lax.fori_loop(1, rounds, more_rows, rows), lambda rows: rows, nothing
    )
    sent, extra_rows = lax.optimization_barrier((sent, extra_rows))
    *spread, landed = spread_weights(gathered, sent, shard, gx_size, gy_size, 5)
    picks = pick_matrix(own_slots(0), slot_count)
    token_rows = weight_grad(picks, landed.reshape(slot_count, D_TXT)).astype(jnp.bfloat16)

    token_rows = token_rows + extra_rows
    image_weights = dict(zip(IMAGE.names, spread[:5]))
    text_weights = dict(zip(TEXT.names, spread[5:9]))
    image_vec, text_vec, temper = split_vectors(spread[9])
    image_gains, image_base, image_rows = image_inputs(image_vec, pixels)
    text_gains, text_base, text_rows = text_inputs(text_vec, token_rows)
    image_kept = tower_forward(IMAGE, end_pos, image_gains, image_base, image_rows, image_weights)
    text_kept = tower_forward(TEXT, end_pos, text_gains, text_base, text_rows, text_weights)
    image_emb = image_kept[14].astype(jnp.bfloat16)
    text_emb = text_kept[14].astype(jnp.bfloat16)
    embeds = jnp.concatenate([image_emb, text_emb], 0).reshape(-1, LANES)
    embeds = gather_windows(embeds, gx_size, gy_size, 1, 0, "embeddings")
    embeds = embeds.reshape(device_count, 2 * pairs_dev, EMBED)
    all_img, all_txt = lax.optimization_barrier((embeds[:, :pairs_dev], embeds[:, pairs_dev:]))
    all_img, all_txt = all_img.reshape(-1, EMBED), all_txt.reshape(-1, EMBED)
    total_pairs = all_img.shape[0]
    valid_all = jnp.arange(total_pairs) % pairs_dev < jnp.repeat(pair_counts.reshape(-1), pairs_dev)
    matches = (
        (groups[:, None] == groups[None, :]) & valid_all[:, None] & valid_all[None, :]
    ).astype(jnp.float32)
    positives_all = jnp.sum(matches, 1)
    total_count = 2.0 * jnp.sum(positives_all)
    own_start = my_index * pairs_dev
    own_part = functools.partial(
        lax.dynamic_slice_in_dim, start_index=own_start, slice_size=pairs_dev, axis=0
    )
    same_own, positives_own, valid_own = own_part(matches), own_part(positives_all), own_part(valid_all)
    logit_scale = jnp.exp(temper)
    column_ok = jnp.concatenate([valid_all, jnp.ones((cache_img.shape[0],), jnp.bool_)])
    columns_txt = jnp.concatenate([all_txt, cache_txt])
    columns_img = jnp.concatenate([all_img, cache_img])
    log_img, loss_one, pull_one = log_sums(
        all_img, columns_txt, column_ok, logit_scale, matches, positives_all
    )
    log_txt, loss_two, pull_two = log_sums(
        all_txt, columns_img, column_ok, logit_scale, matches, positives_all
    )
    grad_temper = logit_scale * (pull_one + pull_two) / total_count
    loss_sum = loss_one + loss_two
    grad_img = side_grads(
        image_emb, columns_txt, column_ok, same_own, positives_own, own_part(log_img), logit_scale, total_count
    )
    grad_txt = side_grads(
        text_emb, columns_img, column_ok, same_own, positives_own, own_part(log_txt), logit_scale, total_count
    )
    grad_img = grad_img + cross_grads(
        all_txt, image_emb, valid_own, same_own, positives_all, log_txt, logit_scale, total_count
    )
    grad_txt = grad_txt + cross_grads(
        all_img, text_emb, valid_own, same_own, positives_all, log_img, logit_scale, total_count
    )
    text_grads = tower_backward(TEXT, end_pos, text_gains, grad_txt, text_kept[:14], text_weights)
    grad_rows = text_grads[6][: SEQS * CTX]
    to_holders = fwd_dot(picks, grad_rows).astype(jnp.bfloat16).reshape(gy_size, cap, D_TXT)
    image_grads = tower_backward(IMAGE, end_pos, image_gains, grad_img, image_kept[:14], image_weights)
    pair_lists = ([(image_rows, image_grads[6])],) + grad_pairs(image_kept, image_grads)
    pair_lists = pair_lists + grad_pairs(text_kept, text_grads)
    total_rows = window_start(shard, device_count - 1) + window_rows(shard, GROUP * CHUNKS)
    vec_rows = jnp.concatenate(
        [
            image_grads[7][:1].reshape(-1, LANES),
            image_grads[7].reshape(-1, LANES),
            image_grads[8].reshape(-1, LANES),
            text_grads[7].reshape(-1, LANES),
            text_grads[8][2:].reshape(-1, LANES),
        ]
    )
    vec_rows = jnp.pad(vec_rows, ((0, total_rows - matrix_rows() - vec_rows.shape[0]), (0, 0)))
    local_grads, arrived = weight_grads(pair_lists, vec_rows, to_holders, gx_size, gy_size, 6)
    table_grad, table_square = table_sum(
        jnp.minimum(held_count, cap),
        first_rows.reshape(-1),
        arrived.reshape(device_count, cap, D_TXT),
        vocab_dev,
    )

    def more_grads(turn, total):
        rows = fwd_dot(pick_matrix(own_slots(turn), slot_count), grad_rows).astype(jnp.bfloat16)
        rows = lax.all_to_all(rows.reshape(gy_size, cap, D_TXT), "gy", 0, 0, tiled=True)
        rows = lax.all_gather(rows, "gx", axis=0).reshape(device_count * cap, D_TXT).astype(jnp.float32)
        return total.at[held_rows(turn).reshape(-1)].add(rows)

    def whole_squares(total):
        return jnp.sum((total[:vocab_dev] * total[:vocab_dev]).reshape(-1, 8, D_TXT), 0)

    def more_turns(total, square):
        total = lax.fori_loop(1, rounds, more_grads, total)
        return total, whole_squares(total)

    table_grad, table_square = lax.cond(
        rounds > 1, more_turns, lambda total, square: (total, square), table_grad, table_square
    )
    table_square = jnp.where(lax.axis_index("gx") == 0, table_square, 0.0)
    grad_window, every = reduce_windows(local_grads, table_square, shard, gx_size, gy_size, 1)
    position = my_index * shard + jnp.arange(shard)
    grad_shard = lift_window(grad_window, shard, gy_size)
    grad_shard = jnp.where(position == parameter_count() - 1, grad_temper, grad_shard)
    total_square = jnp.sum(every) + grad_temper * grad_temper
    grad_norm = jnp.sqrt(total_square)
    factor = jnp.minimum(1.0, clip_limit / (grad_norm + 1e-06))
    matrix_stop = matrix_rows() * LANES
    is_matrix = position < matrix_stop
    rates = jnp.where(is_matrix, rate_matrix, rate_vector)
    decays = jnp.where(is_matrix, decay_rate, 0.0)
    master_out, first_out, second_out = adam_step(
        flat_master, flat_first, flat_second, grad_shard * factor, rates, decays
    )
    table_out, table_first_out, table_second_out = adam_step(
        table, table_first, table_second, table_grad[:vocab_dev] * factor, rate_table, 0.0
    )
    return (
        master_out,
        first_out,
        second_out,
        table_out,
        table_first_out,
        table_second_out,
        loss_sum,
        total_count,
        grad_norm,
    )


def solution(mesh):
    placed = (
        P(("gx", "gy")),
        P(("gx", "gy")),
        P(("gx", "gy")),
        P("gy", None),
        P("gy", None),
        P("gy", None),
        P(("gx", "gy"), None, None),
        P(("gx", "gy"), None),
        P(("gx", "gy")),
        P(),
        P(),
        P(("gx", "gy"), None),
        P(("gx", "gy"), None),
    )
    return jax.shard_map(
        body,
        mesh=mesh,
        in_specs=placed,
        out_specs=(
            P(("gx", "gy")),
            P(("gx", "gy")),
            P(("gx", "gy")),
            P("gy", None),
            P("gy", None),
            P("gy", None),
            P(),
            P(),
            P(),
        ),
        check_vma=False,
    )
```
